32 devices in a mesh: blk: 8 (over y, x, core), tp: 4 (over z).
Axes of the slice: x: 2, y: 2, z: 4, core: 2. Of those that a mesh axis runs over, the one named last changes fastest.
Arguments:
- text_emb: bfloat16 [12288, 1024], P('blk', 'tp'), may hold values from -4 to 4
- image_emb: bfloat16 [12288, 1024], P(('blk', 'tp')), may hold values from -4 to 4
- logit_scale: float32 [1], replicated, may hold values from 4 to 12
- logit_bias: float32 [1], replicated, may hold values from -3 to -1
- bucket: int32 [12288], replicated, may hold values from 0 to 3
- positive: int32 [12288], replicated, may hold values from 0 to 12287, as said below
- blocks: int32 [96, 8, 3], replicated, may hold values from -1 to 2, as said below
Outputs:
- text_grad: bfloat16 [12288, 1024], P('blk', 'tp')
- image_grad: bfloat16 [12288, 1024], P(('blk', 'tp'))
The draws below stay inside these ranges and needn't reach their ends.
Inputs may be any that keep to these rules, and one draw needn't show every extreme that they name: positive[i] lies in the same 128-row tile as i, and within each tile the entries are a permutation of that tile's rows. `blocks`: each entry is a tile of the named shard or -1 for an unused slot; slot 0 is never -1; the used slots of one text tile and shard name different tiles; for the text tile's own blk index, slot 0 names the text tile's own tile.
All inputs are finite; a program needn't handle non-finite values.
Results may differ from the reference program's by a relative error of at most 0.015.
Values may be sent and summed in bfloat16 or wider, within the bound.
No kernel may reach another device: no remote copies, remote signals or barrier semaphores. Data moves between devices by JAX's collectives and lax.ppermute only.
A program may use at most 128 MiB of HBM per device.

```python
import math
import jax
import jax.numpy as jnp
from jax import lax

E = 1024
TILE = 128
TILE_DEV = 3
SLOTS = 3
BUCKETS = 4
SHARDS = 8
GROUPS = 4
N = 12288
TILES = 96


def embed_draw(key_value):
    first, second, third = jax.random.split(key_value, 3)
    row_scale = jnp.exp(jax.random.uniform(first, (N, 1), jnp.float32) * math.log(10.0))
    col_scale = jnp.exp(jax.random.uniform(second, (1, E), jnp.float32) * math.log(10.0))
    base_values = jnp.clip(jax.random.normal(third, (N, E), jnp.float32), -4.0, 4.0)
    return 0.01 * row_scale * col_scale * base_values


def draw_text_emb(key, part):
    return embed_draw(jax.random.fold_in(key, 11)).astype(jnp.bfloat16)


def draw_image_emb(key, part):
    return embed_draw(jax.random.fold_in(key, 23)).astype(jnp.bfloat16)


def draw_positive(key, part):
    scores = jax.random.randint(jax.random.fold_in(key, 31), (TILES, TILE), 0, 65536) * TILE + jnp.arange(TILE, dtype=jnp.int32)[None, :]
    within = jnp.argsort(scores, axis=1, stable=True).astype(jnp.int32)
    return (jnp.arange(TILES, dtype=jnp.int32)[:, None] * TILE + within).reshape(-1).astype(jnp.int32)


def draw_blocks(key, part):
    first, second, third, fourth = jax.random.split(jax.random.fold_in(key, 37), 4)
    scores = jax.random.randint(first, (TILES, SHARDS, TILE_DEV), 0, 65536) * TILE_DEV + jnp.arange(TILE_DEV, dtype=jnp.int32)
    listing = jnp.argsort(scores, axis=-1, stable=True)[..., :SLOTS].astype(jnp.int32)
    others = jax.random.randint(second, (TILES, TILE_DEV - 1), 0, 65536) * TILE_DEV + jnp.arange(TILE_DEV - 1, dtype=jnp.int32)
    other_order = jnp.argsort(others, axis=-1, stable=True).astype(jnp.int32) + 1
    tile_ids = jnp.arange(TILES, dtype=jnp.int32)
    device_ids = tile_ids // TILE_DEV
    own_shard = device_ids // GROUPS
    own_tile = tile_ids % TILE_DEV
    offsets = jnp.concatenate([jnp.zeros((TILES, 1), jnp.int32), other_order[:, :SLOTS - 1]], axis=1)
    own_list = (own_tile[:, None] + offsets) % TILE_DEV
    is_own = jnp.arange(SHARDS, dtype=jnp.int32)[None, :] == own_shard[:, None]
    listing = jnp.where(is_own[:, :, None], own_list[:, None, :], listing)
    levels = jax.random.randint(third, (SHARDS * GROUPS,), 0, 5)[device_ids]
    live_mask = jax.random.randint(fourth, (TILES, SHARDS, SLOTS), 0, 4) < levels[:, None, None]
    live_mask = jnp.logical_or(live_mask, (jnp.arange(SLOTS, dtype=jnp.int32) == 0)[None, None, :])
    return jnp.where(live_mask, listing, -1).astype(jnp.int32)


def place_ends(result, key, low, top_value):
    longest = result.shape.index(max(result.shape))
    spots = []
    for shift in (0, 1):
        where = [jax.random.randint(jax.random.fold_in(key, axis), (), 0, length) for axis, length in enumerate(result.shape)]
        where[longest] = (where[longest] + shift) % result.shape[longest]
        spots.append(tuple(where))
    return result.at[spots[0]].set(low).at[spots[1]].set(top_value)


def setup_inputs(seed: int = 0) -> dict:
    keys = jax.random.split(jax.random.key(seed), 8)
    text_emb = draw_text_emb(jax.random.fold_in(keys[7], 71), 0)
    image_emb = draw_image_emb(jax.random.fold_in(keys[7], 71), 0)
    logit_scale = jnp.clip(jnp.exp(jax.random.uniform(keys[2], (1,), jnp.float32, math.log(4.0), math.log(12.0))), 4.0, 12.0)
    logit_bias = jnp.clip(jax.random.uniform(keys[3], (1,), jnp.float32, -3.0, -1.0), -3.0, -1.0)
    bucket = place_ends(jax.random.randint(keys[4], (N,), 0, BUCKETS), jax.random.fold_in(keys[4], 1), 0, BUCKETS - 1).astype(jnp.int32)
    positive = draw_positive(jax.random.fold_in(keys[7], 71), 0)
    blocks = draw_blocks(jax.random.fold_in(keys[7], 71), 0)
    return {"text_emb": text_emb, "image_emb": image_emb, "logit_scale": logit_scale, "logit_bias": logit_bias, "bucket": bucket, "positive": positive, "blocks": blocks}


def unit_rows(raw_rows):
    values = raw_rows.astype(jnp.float32)
    scales = lax.rsqrt(lax.optimization_barrier(jnp.sum(values * values, axis=-1, keepdims=True)) + 1e-06)
    return (values * scales, scales)

def grad_rows(raw_rows, scales, upstream):
    unit_float = raw_rows.astype(jnp.float32) * scales
    return (scales * (upstream - unit_float * lax.optimization_barrier(jnp.sum(unit_float * upstream, axis=-1, keepdims=True)))).astype(jnp.bfloat16)

def pair_weights(text_part, text_ids, image_part, image_ids, live_mask, scale_value, bias_value, positive, bucket):
    products = jnp.einsum('cid,cjd->cij', text_part.astype(jnp.float32), image_part.astype(jnp.float32))
    logits = scale_value * products + bias_value
    columns = image_ids[:, None] * TILE + jnp.arange(TILE, dtype=jnp.int32)[None, :]
    row_positive = positive.reshape(-1, TILE)[text_ids]
    row_bucket = bucket.reshape(-1, TILE)[text_ids]
    col_bucket = bucket.reshape(-1, TILE)[image_ids]
    matched = row_positive[:, :, None] == columns[:, None, :]
    labels = jnp.where(matched, 1.0, -1.0).astype(jnp.float32)
    kept_pairs = jnp.logical_or(matched, row_bucket[:, :, None] == col_bucket[:, None, :])
    pair_mask = jnp.where(kept_pairs, 1.0, 0.0).astype(jnp.float32) * jnp.where(live_mask, 1.0, 0.0).astype(jnp.float32)[:, None, None]
    return (scale_value * pair_mask * -labels * jax.nn.sigmoid(-labels * logits)).astype(jnp.bfloat16)

def reference(text_emb, image_emb, logit_scale, logit_bias, bucket, positive, blocks):
    text_float, text_scales = unit_rows(text_emb)
    image_float, image_scales = unit_rows(image_emb)
    text_unit = text_float.astype(jnp.bfloat16)
    image_unit = image_float.astype(jnp.bfloat16)
    image_tiles = image_unit.reshape(TILES, TILE, E)
    scale_value = logit_scale[0]
    bias_value = logit_bias[0]
    shard_base = jnp.arange(SHARDS, dtype=jnp.int32)[:, None] * GROUPS

    def per_tile(image_acc, tile_index):
        group = tile_index // TILE_DEV % GROUPS
        listed = lax.dynamic_index_in_dim(blocks, tile_index, 0, keepdims=False)
        live_mask = (listed >= 0).reshape(-1)
        image_ids = ((shard_base + group) * TILE_DEV + jnp.maximum(listed, 0)).reshape(-1).astype(jnp.int32)
        chosen = image_tiles[image_ids]
        text_part = lax.dynamic_slice_in_dim(text_unit, (tile_index * TILE).astype(jnp.int32), TILE, 0)
        text_rep = jnp.broadcast_to(text_part[None], (SHARDS * SLOTS, TILE, E))
        text_ids = jnp.full((SHARDS * SLOTS,), tile_index, dtype=jnp.int32)
        weights = pair_weights(text_rep, text_ids, chosen, image_ids, live_mask, scale_value, bias_value, positive, bucket)
        text_update = jnp.einsum('cij,cjd->id', weights.astype(jnp.float32), chosen.astype(jnp.float32))
        image_update = jnp.einsum('cij,id->cjd', weights.astype(jnp.float32), text_part.astype(jnp.float32))
        image_acc = image_acc.at[image_ids].add(image_update)
        return (image_acc, text_update)
    image_acc, text_acc = lax.scan(per_tile, jnp.zeros((TILES, TILE, E), jnp.float32), jnp.arange(TILES, dtype=jnp.int32))
    text_grad = grad_rows(text_emb, text_scales, text_acc.reshape(N, E))
    image_grad = grad_rows(image_emb, image_scales, image_acc.reshape(N, E))
    return (text_grad, image_grad)
```

```python
import functools
import math

import jax
import jax.numpy as jnp
from jax import lax
from jax.experimental import pallas as pl
from jax.experimental.pallas import tpu as pltpu
from jax.sharding import PartitionSpec as P

TILE = 128
SLOTS = 3
CORES = 2
EPS = 1e-06
LOG2E = math.log2(math.e)
VMEM_LIMIT = 56 * 1024 * 1024

VMEM_SPEC = pl.BlockSpec(memory_space=pltpu.VMEM)
SMEM_SPEC = pl.BlockSpec(memory_space=pltpu.SMEM)


def call_kernel(body, outs, operands, specs, scratch=(), flops=0, transcendentals=0):
    moved = sum(x.size * x.dtype.itemsize for x in operands)
    moved += sum(math.prod(o.shape) * o.dtype.itemsize for o in outs)
    return pl.pallas_call(
        body,
        out_shape=outs,
        in_specs=specs,
        out_specs=[VMEM_SPEC] * len(outs),
        scratch_shapes=list(scratch),
        compiler_params=pltpu.CompilerParams(vmem_limit_bytes=VMEM_LIMIT),
        cost_estimate=pl.CostEstimate(
            flops=flops, bytes_accessed=moved, transcendentals=transcendentals
        ),
    )(*operands)


def struct(shape, dtype):
    return jax.ShapeDtypeStruct(shape, dtype)


def row_scales(square_sum):
    return lax.rsqrt(square_sum + EPS)


def column_of(row):
    return jnp.broadcast_to(row, (TILE, TILE)).T


def weights_body(tile_count, chunks, piece_rows, own_pieces, *refs):
    piece_count = len(piece_rows)
    scale_ref, bias_ref, own_ref, other_ref = refs[:4]
    piece_refs = refs[4 : 4 + piece_count]
    rowb_ref, pos_ref, colb_ref, colid_ref = refs[4 + piece_count : 8 + piece_count]
    unit_ref, weight_ref, acc_own_ref, acc_other_ref, image_ref, acc_ref = refs[8 + piece_count :]
    rows = tile_count * TILE
    width = own_ref.shape[2]
    for half, source in enumerate((own_ref, other_ref)):
        for tile in range(tile_count):
            part = pl.ds(tile * TILE, TILE)
            parts = [source[c, part, :].astype(jnp.float32) for c in range(chunks)]
            total = sum(jnp.sum(x * x, axis=-1, keepdims=True) for x in parts)
            scales = row_scales(total)
            for c in range(chunks):
                unit_ref[pl.ds(half * rows + tile * TILE, TILE), pl.ds(c * width, width)] = (
                    parts[c] * scales
                ).astype(jnp.bfloat16)
    start = 0
    step = 64
    for piece, count in zip(piece_refs, piece_rows):
        for first in range(0, count, step):
            values = piece[pl.ds(first, step), :].astype(jnp.float32)
            scales = row_scales(jnp.sum(values * values, axis=-1, keepdims=True))
            image_ref[pl.ds(start + first, step), :] = (values * scales).astype(jnp.bfloat16)
        start += count
    scale = scale_ref[0]
    slope = -scale * LOG2E
    offset = -bias_ref[0] * LOG2E
    group = tile_count * TILE
    groups = start // group
    for q in range(groups):
        columns = pl.ds(q * group, group)
        images = image_ref[columns, :]
        products = lax.dot_general(
            unit_ref[...], images, (((1,), (1,)), ((), ())), preferred_element_type=jnp.float32
        )
        powers = products * slope + offset
        for a in range(2 * tile_count):
            row_bucket = column_of(rowb_ref[pl.ds(a, 1), :])
            for j in range(tile_count):
                lanes = pl.ds(q * group + j * TILE, TILE)
                power = powers[a * TILE : (a + 1) * TILE, j * TILE : (j + 1) * TILE]
                kept = row_bucket == colb_ref[pl.ds(a, 1), lanes]
                if a < tile_count and q in own_pieces:
                    matched = column_of(pos_ref[pl.ds(a, 1), :]) == colid_ref[:, lanes]
                    power = jnp.where(matched, -power, power)
                    factor = jnp.where(matched, -scale, jnp.where(kept, scale, 0.0))
                else:
                    factor = jnp.where(kept, scale, 0.0)
                weight_ref[pl.ds(a * TILE, TILE), lanes] = (
                    factor / (1.0 + jnp.exp2(power))
                ).astype(jnp.bfloat16)
        update = jnp.dot(weight_ref[:, columns], images, preferred_element_type=jnp.float32)
        if q == 0:
            acc_ref[...] = update
        else:
            acc_ref[...] += update
    acc_own_ref[...] = acc_ref[:rows, :]
    acc_other_ref[...] = acc_ref[rows:, :].astype(jnp.bfloat16)


def image_sum(weight_ref, unit_ref, columns):
    return lax.dot_general(
        weight_ref[:, columns],
        unit_ref[...],
        (((0,), (0,)), ((), ())),
        preferred_element_type=jnp.float32,
    )


def far_body(column, rows, weight_ref, unit_ref, low_ref, high_ref):
    total = image_sum(weight_ref, unit_ref, pl.ds(column, rows)).astype(jnp.bfloat16)
    low_ref[...] = total[: rows // 2, :]
    high_ref[...] = total[rows // 2 :, :]


def near_body(
    rows, weight_ref, unit_ref, x_high_ref, y_low_ref, x_low_ref, y_high_ref, own_ref
):
    half = rows // 2
    total = image_sum(weight_ref, unit_ref, pl.ds(rows, rows))
    x_low_ref[...] = total[:half, :]
    x_high_ref[...] = total[half:, :].astype(jnp.bfloat16)
    total = image_sum(weight_ref, unit_ref, pl.ds(2 * rows, rows))
    y_low_ref[...] = total[:half, :].astype(jnp.bfloat16)
    y_high_ref[...] = total[half:, :]
    own_ref[...] = image_sum(weight_ref, unit_ref, pl.ds(0, rows))


def relay_body(left_ref, left_in_ref, right_ref, right_in_ref, left_out_ref, right_out_ref):
    left_out_ref[...] = (left_ref[...] + left_in_ref[...].astype(jnp.float32)).astype(jnp.bfloat16)
    right_out_ref[...] = (right_ref[...] + right_in_ref[...].astype(jnp.float32)).astype(
        jnp.bfloat16
    )


def spread_body(rows, weight_ref, unit_ref, out_ref):
    for first in range(0, weight_ref.shape[1], rows):
        out_ref[pl.ds(first, rows), :] = image_sum(
            weight_ref, unit_ref, pl.ds(first, rows)
        ).astype(jnp.bfloat16)


def text_grad_body(tile_count, chunks, raw_ref, acc_ref, add_ref, out_ref):
    width = raw_ref.shape[2]
    for tile in range(tile_count):
        part = pl.ds(tile * TILE, TILE)
        raws = [raw_ref[c, part, :].astype(jnp.float32) for c in range(chunks)]
        scales = row_scales(sum(jnp.sum(x * x, axis=-1, keepdims=True) for x in raws))
        accs = [
            acc_ref[part, pl.ds(c * width, width)]
            + add_ref[part, pl.ds(c * width, width)].astype(jnp.float32)
            for c in range(chunks)
        ]
        units = [x * scales for x in raws]
        inner = sum(jnp.sum(u * a, axis=-1, keepdims=True) for u, a in zip(units, accs))
        for c in range(chunks):
            out_ref[c, part, :] = (scales * (accs[c] - units[c] * inner)).astype(jnp.bfloat16)


def image_grad_body(low_count, high_count, raw_ref, own_ref, *refs):
    low_refs = refs[:low_count]
    high_refs = refs[low_count : low_count + high_count]
    out_ref = refs[-1]
    half = low_refs[0].shape[0]
    step = 64
    for base, adds in ((0, low_refs), (half, high_refs)):
        if not adds:
            continue
        for first in range(0, half, step):
            part = pl.ds(base + first, step)
            raw = raw_ref[part, :].astype(jnp.float32)
            scales = row_scales(jnp.sum(raw * raw, axis=-1, keepdims=True))
            unit = raw * scales
            acc = own_ref[part, :].astype(jnp.float32)
            for ref in adds:
                acc = acc + ref[pl.ds(first, step), :].astype(jnp.float32)
            inner = jnp.sum(unit * acc, axis=-1, keepdims=True)
            out_ref[part, :] = (scales * (acc - unit * inner)).astype(jnp.bfloat16)


def swap(value, count, bit):
    return lax.ppermute(value, "blk", [(b, b ^ bit) for b in range(count)])


def per_device(text_emb, image_emb, logit_scale, logit_bias, bucket, positive, blocks):
    groups = lax.axis_size("tp")
    shards = lax.axis_size("blk")
    rows, embed = image_emb.shape
    tile_count = rows // TILE
    half = rows // 2
    width = text_emb.shape[1]
    chunks = groups
    here = lax.axis_index("blk")
    group = lax.axis_index("tp")
    square = shards == 4 * CORES

    text_own = lax.all_to_all(
        text_emb.reshape(groups, rows, width), "tp", split_axis=0, concat_axis=0, tiled=True
    )
    if square:
        low, high = image_emb[:half], image_emb[half:]
        y_low = swap(low, shards, 4)
        x_high = swap(high, shards, 2)
        x_low = swap(low, shards, 2)
        y_high = swap(high, shards, 4)
        far_low = swap(y_low, shards, 2)
        far_high = swap(x_high, shards, 4)
        pieces = [image_emb, x_low, x_high, y_low, y_high, far_low, far_high]
        sources = [here, here ^ 2, here ^ 4, here ^ 6]
        own_pieces = (0,)
    else:
        same_core = [[chip * CORES + core for chip in range(shards // CORES)] for core in range(CORES)]
        pieces = [
            lax.all_gather(image_emb, "blk", axis=0, tiled=True, axis_index_groups=same_core)
        ]
        sources = [chip * CORES + here % CORES for chip in range(shards // CORES)]
        own_pieces = tuple(range(shards // CORES))
    text_other = swap(text_own, shards, 1)
    piece_rows = [p.shape[0] for p in pieces]
    total_columns = sum(piece_rows)

    def device_rows(vector, shard):
        return lax.dynamic_slice_in_dim(vector, (shard * groups + group) * rows, rows, 0)

    def device_blocks(shard):
        return lax.dynamic_slice_in_dim(
            blocks, (shard * groups + group) * tile_count, tile_count, 0
        )

    text_shards = (here, here ^ 1)
    row_bucket = jnp.concatenate([device_rows(bucket, s) for s in text_shards]).reshape(-1, TILE)
    row_positive = jnp.concatenate([device_rows(positive, s) for s in text_shards]).reshape(
        -1, TILE
    )
    listed = jnp.concatenate([device_blocks(s) for s in text_shards])
    tile_range = jnp.arange(tile_count, dtype=jnp.int32)
    column_buckets = []
    for s in sources:
        entries = lax.dynamic_index_in_dim(listed, s, 1, keepdims=False)
        live = jnp.any(entries[:, None, :] == tile_range[None, :, None], axis=-1)
        tiles = device_rows(bucket, s).reshape(1, tile_count, TILE)
        column_buckets.append(
            jnp.where(live[:, :, None], tiles, -1).reshape(2 * tile_count, rows)
        )
    column_bucket = jnp.concatenate(column_buckets, axis=1)
    column_ids = jnp.concatenate(
        [(s * groups + group) * rows + jnp.arange(rows, dtype=jnp.int32) for s in sources]
    )[None, :]

    pair_flops = 2 * 2 * rows * total_columns * embed
    units, weights, acc_own, acc_other = call_kernel(
        functools.partial(weights_body, tile_count, chunks, piece_rows, own_pieces),
        [
            struct((2 * rows, embed), jnp.bfloat16),
            struct((2 * rows, total_columns), jnp.bfloat16),
            struct((rows, embed), jnp.float32),
            struct((rows, embed), jnp.bfloat16),
        ],
        [logit_scale, logit_bias, text_own, text_other]
        + pieces
        + [row_bucket, row_positive, column_bucket, column_ids],
        [SMEM_SPEC] * 2 + [VMEM_SPEC] * (6 + len(pieces)),
        scratch=[
            pltpu.VMEM((total_columns, embed), jnp.bfloat16),
            pltpu.VMEM((2 * rows, embed), jnp.float32),
        ],
        flops=2 * pair_flops,
        transcendentals=2 * 2 * rows * total_columns,
    )
    acc_in = swap(acc_other, shards, 1)

    def finish_text():
        grad = call_kernel(
            functools.partial(text_grad_body, tile_count, chunks),
            [struct((chunks, rows, width), jnp.bfloat16)],
            [text_own, acc_own, acc_in],
            [VMEM_SPEC] * 3,
        )[0]
        grad = lax.all_to_all(grad, "tp", split_axis=0, concat_axis=0, tiled=True)
        return grad.reshape(groups * rows, width)

    half_bf16 = struct((half, embed), jnp.bfloat16)
    half_f32 = struct((half, embed), jnp.float32)
    full_bf16 = struct((rows, embed), jnp.bfloat16)
    if square:
        to_far_low, to_far_high = call_kernel(
            functools.partial(far_body, 3 * rows, rows),
            [half_bf16, half_bf16],
            [weights, units],
            [VMEM_SPEC] * 2,
            flops=2 * 2 * rows * rows * embed,
        )
        relay_low = swap(to_far_low, shards, 4)
        relay_high = swap(to_far_high, shards, 2)
        text_grad = finish_text()
        to_x_high, to_y_low, near_x_low, near_y_high, own = call_kernel(
            functools.partial(near_body, rows),
            [half_bf16, half_bf16, half_f32, half_f32, struct((rows, embed), jnp.float32)],
            [weights, units],
            [VMEM_SPEC] * 2,
            flops=3 * 2 * 2 * rows * rows * embed,
        )
        from_x_high = swap(to_x_high, shards, 2)
        from_y_low = swap(to_y_low, shards, 4)
        to_x_low, to_y_high = call_kernel(
            relay_body,
            [half_bf16, half_bf16],
            [near_x_low, relay_low, near_y_high, relay_high],
            [VMEM_SPEC] * 4,
        )
        from_x_low = swap(to_x_low, shards, 2)
        from_y_high = swap(to_y_high, shards, 4)
        image_grad = call_kernel(
            functools.partial(image_grad_body, 2, 2),
            [full_bf16],
            [image_emb, own, from_x_low, from_y_low, from_x_high, from_y_high],
            [VMEM_SPEC] * 6,
        )[0]
    else:
        text_grad = finish_text()
        spread = call_kernel(
            functools.partial(spread_body, rows),
            [struct((total_columns, embed), jnp.bfloat16)],
            [weights, units],
            [VMEM_SPEC] * 2,
            flops=pair_flops,
        )[0]
        parts = lax.all_to_all(
            spread, "blk", split_axis=0, concat_axis=0, tiled=True, axis_index_groups=same_core
        )
        total = jnp.sum(
            parts.reshape(-1, rows, embed).astype(jnp.float32), axis=0
        ).reshape(2, half, embed)
        zero = jnp.zeros((half, embed), jnp.bfloat16)
        image_grad = call_kernel(
            functools.partial(image_grad_body, 1, 1),
            [full_bf16],
            [image_emb, total.reshape(rows, embed), zero, zero],
            [VMEM_SPEC] * 4,
        )[0]
    return (text_grad, image_grad)


def solution(mesh):
    in_specs = (P("blk", "tp"), P(("blk", "tp"), None), P(), P(), P(), P(), P())
    out_specs = (P("blk", "tp"), P(("blk", "tp"), None))
    return jax.shard_map(
        per_device, mesh=mesh, in_specs=in_specs, out_specs=out_specs, check_vma=False
    )
```

```python
import functools
import math

import jax
import jax.numpy as jnp
from jax import lax
from jax.experimental import pallas as pl
from jax.experimental.pallas import tpu as pltpu
from jax.sharding import PartitionSpec as P

TILE = 128
SLOTS = 3
CORES = 2
EPS = 1e-06
LOG2E = math.log2(math.e)
MIB = 1024 * 1024

VMEM_SPEC = pl.BlockSpec(memory_space=pltpu.VMEM)
SMEM_SPEC = pl.BlockSpec(memory_space=pltpu.SMEM)


def call_kernel(body, outs, operands, scalars=0, scratch=(), flops=0, transcendentals=0, limit=24):
    moved = sum(x.size * x.dtype.itemsize for x in operands)
    moved += sum(math.prod(o.shape) * o.dtype.itemsize for o in outs)
    return pl.pallas_call(
        body,
        out_shape=outs,
        in_specs=[SMEM_SPEC] * scalars + [VMEM_SPEC] * (len(operands) - scalars),
        out_specs=[VMEM_SPEC] * len(outs),
        scratch_shapes=list(scratch),
        compiler_params=pltpu.CompilerParams(vmem_limit_bytes=limit * MIB),
        cost_estimate=pl.CostEstimate(
            flops=flops, bytes_accessed=moved, transcendentals=transcendentals
        ),
    )(*operands)


def struct(shape, dtype):
    return jax.ShapeDtypeStruct(shape, dtype)


def row_scales(square_sum):
    return lax.rsqrt(square_sum + EPS)


def column_of(row):
    return jnp.broadcast_to(row, (TILE, TILE)).T


def dot_nt(left, right):
    return lax.dot_general(
        left, right, (((1,), (1,)), ((), ())), preferred_element_type=jnp.float32
    )


def dot_tn(left, right):
    return lax.dot_general(
        left, right, (((0,), (0,)), ((), ())), preferred_element_type=jnp.float32
    )


def feature_slice(place, k, width):
    return pl.ds(pl.multiple_of((place ^ k) * width, width), width)


def unit_text(place, chunk_refs, unit_ref, base):
    rows, width = chunk_refs[0].shape
    for first in range(0, rows, TILE):
        part = pl.ds(first, TILE)
        parts = [ref[part, :].astype(jnp.float32) for ref in chunk_refs]
        scales = row_scales(sum(jnp.sum(x * x, axis=-1, keepdims=True) for x in parts))
        for k, x in enumerate(parts):
            unit_ref[pl.ds(base + first, TILE), feature_slice(place, k, width)] = (
                x * scales
            ).astype(jnp.bfloat16)


def unit_images(piece_refs, image_ref):
    start = 0
    step = 64
    for ref in piece_refs:
        for first in range(0, ref.shape[0], step):
            values = ref[pl.ds(first, step), :].astype(jnp.float32)
            scales = row_scales(jnp.sum(values * values, axis=-1, keepdims=True))
            image_ref[pl.ds(start + first, step), :] = (values * scales).astype(jnp.bfloat16)
        start += ref.shape[0]


def pair_weights(scale, bias, products, meta_refs, column, own_rows, weight_ref):
    rowb_ref, pos_ref, colb_ref, colid_ref = meta_refs
    slope = -scale * LOG2E
    offset = -bias * LOG2E
    rows, columns = products.shape
    for a in range(rows // TILE):
        row_bucket = column_of(rowb_ref[pl.ds(a, 1), :])
        own = a * TILE < own_rows
        row_positive = column_of(pos_ref[pl.ds(a, 1), :]) if own else None
        for j in range(columns // TILE):
            lanes = pl.ds(column + j * TILE, TILE)
            power = (
                products[a * TILE : (a + 1) * TILE, j * TILE : (j + 1) * TILE] * slope + offset
            )
            factor = jnp.where(row_bucket == colb_ref[pl.ds(a, 1), lanes], scale, 0.0)
            if own:
                matched = row_positive == colid_ref[:, lanes]
                power = jnp.where(matched, -power, power)
                factor = jnp.where(matched, -scale, factor)
            below = 1.0 + jnp.exp2(power)
            inverse = pl.reciprocal(below, approx=True)
            inverse = inverse * (2.0 - below * inverse)
            weight_ref[pl.ds(a * TILE, TILE), lanes] = (factor * inverse).astype(jnp.bfloat16)


def near_body(chunks, *refs):
    scale_ref, bias_ref, place_ref = refs[:3]
    own_chunks, other_chunks = refs[3 : 3 + chunks], refs[3 + chunks : 3 + 2 * chunks]
    refs = refs[3 + 2 * chunks :]
    piece_refs, meta_refs = refs[:3], refs[3:7]
    x_high_ref, y_low_ref, x_low_ref, y_high_ref, unit_ref, acc_ref, own_weight_ref = refs[7:14]
    image_ref, weight_ref = refs[14:]
    rows = piece_refs[0].shape[0]
    half = rows // 2
    place = place_ref[0]
    scale, bias = scale_ref[0], bias_ref[0]
    unit_text(place, own_chunks, unit_ref, 0)
    unit_text(place, other_chunks, unit_ref, rows)
    unit_images(piece_refs, image_ref)
    order = (1, 2, 0)
    group = [pl.ds(q * rows, rows) for q in range(3)]
    products = dot_nt(unit_ref[...], image_ref[group[order[0]], :])
    for at, q in enumerate(order):
        now = products
        if at + 1 < len(order):
            products = dot_nt(unit_ref[...], image_ref[group[order[at + 1]], :])
        pair_weights(scale, bias, now, meta_refs, q * rows, rows if q == 0 else 0, weight_ref)
        if q == 0:
            own_weight_ref[...] = weight_ref[:, group[0]]
            continue
        total = dot_tn(weight_ref[:, group[q]], unit_ref[...])
        if q == 1:
            x_low_ref[...] = total[:half, :]
            x_high_ref[...] = total[half:, :].astype(jnp.bfloat16)
        else:
            y_low_ref[...] = total[:half, :].astype(jnp.bfloat16)
            y_high_ref[...] = total[half:, :]
    acc_ref[...] = jnp.dot(weight_ref[...], image_ref[...], preferred_element_type=jnp.float32)


def far_body(*refs):
    scale_ref, bias_ref = refs[:2]
    unit_ref, acc_ref = refs[2:4]
    piece_refs, meta_refs = refs[4:6], refs[6:10]
    low_ref, high_ref, acc_own_ref, acc_other_ref, image_ref, weight_ref = refs[10:]
    half = piece_refs[0].shape[0]
    rows = 2 * half
    unit_images(piece_refs, image_ref)
    products = dot_nt(unit_ref[...], image_ref[...])
    pair_weights(scale_ref[0], bias_ref[0], products, meta_refs, 0, 0, weight_ref)
    update = jnp.dot(weight_ref[...], image_ref[...], preferred_element_type=jnp.float32)
    acc_other_ref[...] = (acc_ref[rows:, :] + update[rows:, :]).astype(jnp.bfloat16)
    acc_own_ref[...] = acc_ref[:rows, :] + update[:rows, :]
    total = dot_tn(weight_ref[...], unit_ref[...]).astype(jnp.bfloat16)
    low_ref[...] = total[:half, :]
    high_ref[...] = total[half:, :]


def own_body(weight_ref, unit_ref, out_ref):
    out_ref[...] = dot_tn(weight_ref[...], unit_ref[...])


def all_body(chunks, *refs):
    scale_ref, bias_ref, place_ref = refs[:3]
    own_chunks, other_chunks = refs[3 : 3 + chunks], refs[3 + chunks : 3 + 2 * chunks]
    refs = refs[3 + 2 * chunks :]
    piece_ref, meta_refs = refs[0], refs[1:5]
    spread_ref, acc_own_ref, acc_other_ref, unit_ref, image_ref, weight_ref, acc_ref = refs[5:]
    rows = own_chunks[0].shape[0]
    place = place_ref[0]
    unit_text(place, own_chunks, unit_ref, 0)
    unit_text(place, other_chunks, unit_ref, rows)
    unit_images([piece_ref], image_ref)
    for first in range(0, piece_ref.shape[0], rows):
        group = pl.ds(first, rows)
        products = dot_nt(unit_ref[...], image_ref[group, :])
        pair_weights(scale_ref[0], bias_ref[0], products, meta_refs, first, rows, weight_ref)
        weights = weight_ref[:, group]
        update = jnp.dot(weights, image_ref[group, :], preferred_element_type=jnp.float32)
        acc_ref[...] = update if first == 0 else acc_ref[...] + update
        spread_ref[group, :] = dot_tn(weights, unit_ref[...]).astype(jnp.bfloat16)
    acc_own_ref[...] = acc_ref[:rows, :]
    acc_other_ref[...] = acc_ref[rows:, :].astype(jnp.bfloat16)


def relay_body(left_ref, left_in_ref, right_ref, right_in_ref, left_out_ref, right_out_ref):
    left_out_ref[...] = (left_ref[...] + left_in_ref[...].astype(jnp.float32)).astype(jnp.bfloat16)
    right_out_ref[...] = (right_ref[...] + right_in_ref[...].astype(jnp.float32)).astype(
        jnp.bfloat16
    )


def text_grad_body(chunks, *refs):
    place_ref = refs[0]
    raw_refs = refs[1 : 1 + chunks]
    acc_ref, add_ref = refs[1 + chunks : 3 + chunks]
    out_refs = refs[3 + chunks :]
    place = place_ref[0]
    rows, width = raw_refs[0].shape
    for first in range(0, rows, TILE):
        part = pl.ds(first, TILE)
        raws = [ref[part, :].astype(jnp.float32) for ref in raw_refs]
        scales = row_scales(sum(jnp.sum(x * x, axis=-1, keepdims=True) for x in raws))
        accs = []
        for k in range(chunks):
            features = feature_slice(place, k, width)
            accs.append(acc_ref[part, features] + add_ref[part, features].astype(jnp.float32))
        units = [x * scales for x in raws]
        inner = sum(jnp.sum(u * a, axis=-1, keepdims=True) for u, a in zip(units, accs))
        for k in range(chunks):
            out_refs[k][part, :] = (scales * (accs[k] - units[k] * inner)).astype(jnp.bfloat16)


def finish_body(chunks, low_count, high_count, *refs):
    place_ref = refs[0]
    text_refs = refs[1 : 1 + chunks]
    raw_ref, own_ref = refs[1 + chunks : 3 + chunks]
    refs = refs[3 + chunks :]
    low_refs, high_refs = refs[:low_count], refs[low_count : low_count + high_count]
    text_out_ref, image_out_ref = refs[low_count + high_count :]
    place = place_ref[0]
    rows = raw_ref.shape[0]
    half = rows // 2
    step = 64
    for base, adds in ((0, low_refs), (half, high_refs)):
        for first in range(0, half, step):
            part = pl.ds(base + first, step)
            raw = raw_ref[part, :].astype(jnp.float32)
            scales = row_scales(jnp.sum(raw * raw, axis=-1, keepdims=True))
            unit = raw * scales
            acc = own_ref[part, :].astype(jnp.float32)
            for ref in adds:
                acc = acc + ref[pl.ds(first, step), :].astype(jnp.float32)
            inner = jnp.sum(unit * acc, axis=-1, keepdims=True)
            image_out_ref[part, :] = (scales * (acc - unit * inner)).astype(jnp.bfloat16)
    for k in range(chunks):
        text_out_ref[pl.ds(pl.multiple_of((place ^ k) * rows, rows), rows), :] = text_refs[k][...]


def swap(value, axis, bits):
    count = lax.axis_size(axis)
    return lax.ppermute(value, axis, [(i, i ^ bits) for i in range(count)])


def per_device(text_emb, image_emb, logit_scale, logit_bias, bucket, positive, blocks):
    groups = lax.axis_size("tp")
    shards = lax.axis_size("blk")
    rows, embed = image_emb.shape
    tile_count = rows // TILE
    half = rows // 2
    width = text_emb.shape[1]
    here = lax.axis_index("blk")
    group = lax.axis_index("tp")
    place = group.astype(jnp.int32).reshape(1)
    square = shards == 4 * CORES
    same_core = [[chip * CORES + core for chip in range(shards // CORES)] for core in range(CORES)]

    def text_rows(k):
        return lax.dynamic_slice_in_dim(text_emb, (group ^ k) * rows, rows, 0)

    if square:
        from_x = swap(image_emb, "blk", 2)
        from_y = swap(image_emb, "blk", 4)
        sources = [here, here ^ 2, here ^ 4, here ^ 6]
    else:
        gathered = lax.all_gather(
            image_emb, "blk", axis=0, tiled=True, axis_index_groups=same_core
        )
        sources = [chip * CORES + here % CORES for chip in range(shards // CORES)]
    text_own = [text_rows(0)] + [swap(text_rows(k), "tp", k) for k in range(1, groups)]
    text_other = [swap(chunk, "blk", 1) for chunk in text_own]

    def device_rows(vector, shard):
        return lax.dynamic_slice_in_dim(vector, (shard * groups + group) * rows, rows, 0)

    def device_blocks(shard):
        return lax.dynamic_slice_in_dim(
            blocks, (shard * groups + group) * tile_count, tile_count, 0
        )

    text_shards = (here, here ^ 1)
    row_bucket = jnp.concatenate([device_rows(bucket, s) for s in text_shards]).reshape(-1, TILE)
    row_positive = jnp.concatenate([device_rows(positive, s) for s in text_shards]).reshape(
        -1, TILE
    )
    listed = jnp.concatenate([device_blocks(s) for s in text_shards])
    tile_range = jnp.arange(tile_count, dtype=jnp.int32)

    def meta(shard_list):
        buckets = []
        for s in shard_list:
            entries = lax.dynamic_index_in_dim(listed, s, 1, keepdims=False)
            live = jnp.any(entries[:, None, :] == tile_range[None, :, None], axis=-1)
            tiles = device_rows(bucket, s).reshape(1, tile_count, TILE)
            buckets.append(jnp.where(live[:, :, None], tiles, -1).reshape(2 * tile_count, rows))
        ids = [
            (s * groups + group) * rows + jnp.arange(rows, dtype=jnp.int32) for s in shard_list
        ]
        return [
            row_bucket,
            row_positive,
            jnp.concatenate(buckets, axis=1),
            jnp.concatenate(ids)[None, :],
        ]

    def bf16(count, columns=embed):
        return struct((count, columns), jnp.bfloat16)

    def f32(count, columns=embed):
        return struct((count, columns), jnp.float32)

    both = 2 * rows
    unit_flops = 2 * both * rows * embed
    scalars = [logit_scale, logit_bias]

    def finish_text(acc_own, acc_other):
        parts = call_kernel(
            functools.partial(text_grad_body, groups),
            [bf16(rows, width)] * groups,
            [place] + text_own + [acc_own, swap(acc_other, "blk", 1)],
            scalars=1,
            limit=16,
        )
        return [parts[0]] + [swap(parts[k], "tp", k) for k in range(1, groups)]

    def finish(text_parts, own, lows, highs):
        return call_kernel(
            functools.partial(finish_body, groups, len(lows), len(highs)),
            [bf16(groups * rows, width), bf16(rows)],
            [place] + text_parts + [image_emb, own] + lows + highs,
            scalars=1,
            limit=16,
        )

    if not square:
        spread, acc_own, acc_other = call_kernel(
            functools.partial(all_body, groups),
            [bf16(gathered.shape[0]), f32(rows), bf16(rows)],
            scalars + [place] + text_own + text_other + [gathered] + meta(sources),
            scalars=3,
            scratch=[
                pltpu.VMEM((both, embed), jnp.bfloat16),
                pltpu.VMEM(gathered.shape, jnp.bfloat16),
                pltpu.VMEM((both, gathered.shape[0]), jnp.bfloat16),
                pltpu.VMEM((both, embed), jnp.float32),
            ],
            limit=56,
        )
        text_parts = finish_text(acc_own, acc_other)
        parts = lax.all_to_all(
            spread, "blk", split_axis=0, concat_axis=0, tiled=True, axis_index_groups=same_core
        )
        total = jnp.sum(parts.reshape(-1, rows, embed).astype(jnp.float32), axis=0)
        return tuple(finish(text_parts, total, [], []))

    to_x_high, to_y_low, near_x_low, near_y_high, units, acc, own_weights = call_kernel(
        functools.partial(near_body, groups),
        [bf16(half), bf16(half), f32(half), f32(half), bf16(both), f32(both), bf16(both, rows)],
        scalars + [place] + text_own + text_other + [image_emb, from_x, from_y]
        + meta(sources[:3]),
        scalars=3,
        scratch=[
            pltpu.VMEM((3 * rows, embed), jnp.bfloat16),
            pltpu.VMEM((both, 3 * rows), jnp.bfloat16),
        ],
        flops=8 * unit_flops,
        transcendentals=2 * both * 3 * rows,
        limit=32,
    )
    from_x_high = swap(to_x_high, "blk", 2)
    from_y_low = swap(to_y_low, "blk", 4)
    far_low = swap(from_y[:half], "blk", 2)
    far_high = swap(from_x[half:], "blk", 4)
    to_far_low, to_far_high, acc_own, acc_other = call_kernel(
        far_body,
        [bf16(half), bf16(half), f32(rows), bf16(rows)],
        scalars + [units, acc, far_low, far_high] + meta(sources[3:]),
        scalars=2,
        scratch=[
            pltpu.VMEM((rows, embed), jnp.bfloat16),
            pltpu.VMEM((both, rows), jnp.bfloat16),
        ],
        flops=3 * unit_flops,
        transcendentals=2 * both * rows,
        limit=24,
    )
    relay_low = swap(to_far_low, "blk", 4)
    relay_high = swap(to_far_high, "blk", 2)
    text_parts = finish_text(acc_own, acc_other)
    own = call_kernel(own_body, [f32(rows)], [own_weights, units], flops=unit_flops, limit=16)[0]
    to_x_low, to_y_high = call_kernel(
        relay_body,
        [bf16(half), bf16(half)],
        [near_x_low, relay_low, near_y_high, relay_high],
        limit=16,
    )
    from_x_low = swap(to_x_low, "blk", 2)
    from_y_high = swap(to_y_high, "blk", 4)
    return tuple(
        finish(text_parts, own, [from_x_low, from_y_low], [from_x_high, from_y_high])
    )


def solution(mesh):
    in_specs = (P("blk", "tp"), P(("blk", "tp"), None), P(), P(), P(), P(), P())
    out_specs = (P("blk", "tp"), P(("blk", "tp"), None))
    return jax.shard_map(
        per_device, mesh=mesh, in_specs=in_specs, out_specs=out_specs, check_vma=False
    )
```

```python
import functools
import math

import jax
import jax.numpy as jnp
from jax import lax
from jax.experimental import pallas as pl
from jax.experimental.pallas import tpu as pltpu
from jax.sharding import PartitionSpec as P

TILE = 128
SLOTS = 3
WAIT_FLOPS = 20_000_000_000
TEXT_PIECES = 2
LAST_PIECES = 1
CORES = 2
EPS = 1e-06
LOG2E = math.log2(math.e)
MIB = 1024 * 1024

VMEM_SPEC = pl.BlockSpec(memory_space=pltpu.VMEM)
SMEM_SPEC = pl.BlockSpec(memory_space=pltpu.SMEM)


def call_kernel(
    body, outs, operands, scalars=0, anywhere=(), scratch=(), flops=0, transcendentals=0, limit=24
):
    moved = sum(x.size * x.dtype.itemsize for x in operands)
    moved += sum(math.prod(o.shape) * o.dtype.itemsize for o in outs)
    specs = [SMEM_SPEC] * scalars + [VMEM_SPEC] * (len(operands) - scalars)
    for at in anywhere:
        specs[at] = pl.BlockSpec(memory_space=pl.ANY)
    return pl.pallas_call(
        body,
        out_shape=outs,
        in_specs=specs,
        out_specs=[VMEM_SPEC] * len(outs),
        scratch_shapes=list(scratch),
        compiler_params=pltpu.CompilerParams(vmem_limit_bytes=limit * MIB),
        cost_estimate=pl.CostEstimate(
            flops=flops, bytes_accessed=moved, transcendentals=transcendentals
        ),
    )(*operands)


def struct(shape, dtype):
    return jax.ShapeDtypeStruct(shape, dtype)


def row_scales(square_sum):
    return lax.rsqrt(square_sum + EPS)


def column_of(row):
    return jnp.broadcast_to(row, (TILE, TILE)).T


def dot_nt(left, right):
    return lax.dot_general(
        left, right, (((1,), (1,)), ((), ())), preferred_element_type=jnp.float32
    )


def dot_tn(left, right):
    return lax.dot_general(
        left, right, (((0,), (0,)), ((), ())), preferred_element_type=jnp.float32
    )


def feature_slice(place, k, width):
    return pl.ds(pl.multiple_of((place ^ k) * width, width), width)


def pick_body(where_ref, text_ref, *refs):
    out_refs, sems = refs[:-1], refs[-1]
    place = where_ref[1]
    rows = out_refs[0].shape[0]
    copies = []
    for k in list(range(1, len(out_refs))) + [0]:
        block = pl.ds(pl.multiple_of((place ^ k) * rows, rows), rows)
        copies.append(pltpu.make_async_copy(text_ref.at[block, :], out_refs[k], sems.at[k]))
    for copy in copies:
        copy.start()
    for copy in copies:
        copy.wait()


def unit_text_body(chunks, *refs):
    where_ref, chunk_refs, unit_ref = refs[0], refs[1 : 1 + chunks], refs[1 + chunks]
    piece_refs = refs[2 + chunks :]
    place = where_ref[1]
    rows, width = chunk_refs[0].shape
    for first in range(0, rows, TILE):
        part = pl.ds(first, TILE)
        parts = [ref[part, :].astype(jnp.float32) for ref in chunk_refs]
        scales = row_scales(sum(jnp.sum(x * x, axis=-1, keepdims=True) for x in parts))
        for k, x in enumerate(parts):
            unit_ref[part, feature_slice(place, k, width)] = (x * scales).astype(jnp.bfloat16)
    split_rows(unit_ref, piece_refs)


def split_rows(whole_ref, piece_refs):
    for at, ref in enumerate(piece_refs):
        ref[...] = whole_ref[pl.ds(at * ref.shape[0], ref.shape[0]), :]


def join_rows(piece_refs, whole_ref):
    for at, ref in enumerate(piece_refs):
        whole_ref[pl.ds(at * ref.shape[0], ref.shape[0]), :] = ref[...]


def unit_images(piece_refs, image_ref):
    start = 0
    step = 64
    for ref in piece_refs:
        for first in range(0, ref.shape[0], step):
            values = ref[pl.ds(first, step), :].astype(jnp.float32)
            scales = row_scales(jnp.sum(values * values, axis=-1, keepdims=True))
            image_ref[pl.ds(start + first, step), :] = (values * scales).astype(jnp.bfloat16)
        start += ref.shape[0]


def unit_images_body(*refs):
    unit_images(refs[:-1], refs[-1])


def neighbour_bits(shard):
    core = shard % CORES
    return 2 << core, 4 >> core


class Pairs:
    count = 6

    def __init__(self, refs, groups, tiles):
        self.scale_ref, self.bias_ref, self.where_ref, self.blocks_ref = refs[:4]
        self.bucket_ref, self.positive_ref = refs[4:6]
        self.groups, self.tiles = groups, tiles
        self.here, self.place = self.where_ref[0], self.where_ref[1]
        self.first_bit, self.second_bit = neighbour_bits(self.here)
        self.scale = self.scale_ref[0]
        self.slope = -self.scale * LOG2E
        self.offset = -self.bias_ref[0] * LOG2E

    def first_tile(self, shard):
        return (shard * self.groups + self.place) * self.tiles

    def weigh(self, products, text_shard, image_shard, weight_ref, top, left, own):
        text_tile = self.first_tile(text_shard)
        image_tile = self.first_tile(image_shard)
        for a in range(self.tiles):
            tile = text_tile + a
            row_bucket = column_of(self.bucket_ref[pl.ds(tile, 1), :])
            entries = [self.blocks_ref[slot, image_shard, tile] for slot in range(SLOTS)]
            for j in range(self.tiles):
                listed = sum(jnp.where(entry == j, 1.0, 0.0) for entry in entries)
                amount = self.scale * listed
                column_bucket = self.bucket_ref[pl.ds(image_tile + j, 1), :]
                power = (
                    products[a * TILE : (a + 1) * TILE, j * TILE : (j + 1) * TILE] * self.slope
                    + self.offset
                )
                factor = jnp.where(row_bucket == column_bucket, amount, 0.0)
                if own == "search" or (own == "diagonal" and a == j):
                    ids = lax.broadcasted_iota(jnp.int32, (1, TILE), 1) + (image_tile + j) * TILE
                    matched = column_of(self.positive_ref[pl.ds(tile, 1), :]) == ids
                    power = jnp.where(matched, -power, power)
                    factor = jnp.where(matched, -amount, factor)
                below = 1.0 + jnp.exp2(power)
                inverse = pl.reciprocal(below, approx=True)
                inverse = inverse * (2.0 - below * inverse)
                weight_ref[pl.ds(top + a * TILE, TILE), pl.ds(left + j * TILE, TILE)] = (
                    factor * inverse
                ).astype(jnp.bfloat16)


def near_pairs(pairs, text_shard, own, unit_ref, image_ref, weight_ref, acc_ref, own_weight_ref):
    rows = unit_ref.shape[0]
    order = (1, 2, 0)
    shards = (pairs.here, pairs.here ^ pairs.first_bit, pairs.here ^ pairs.second_bit)
    group = [pl.ds(q * rows, rows) for q in range(3)]
    totals = []
    products = dot_nt(unit_ref[...], image_ref[group[order[0]], :])
    for at, q in enumerate(order):
        now = products
        if at + 1 < len(order):
            products = dot_nt(unit_ref[...], image_ref[group[order[at + 1]], :])
        pairs.weigh(now, text_shard, shards[q], weight_ref, 0, q * rows, own if q == 0 else None)
        if q == 0:
            own_weight_ref[...] = weight_ref[:, group[0]]
        else:
            totals.append(dot_tn(weight_ref[:, group[q]], unit_ref[...]))
    acc_ref[...] = jnp.dot(weight_ref[...], image_ref[...], preferred_element_type=jnp.float32)
    return totals


def near_own_body(groups, tiles, *refs):
    pairs = Pairs(refs, groups, tiles)
    unit_ref, image_ref, first_ref, second_ref, acc_ref, own_weight_ref, weight_ref = refs[
        Pairs.count :
    ]
    totals = near_pairs(
        pairs, pairs.here, "diagonal", unit_ref, image_ref, weight_ref, acc_ref, own_weight_ref
    )
    first_ref[...], second_ref[...] = totals


def near_other_body(groups, tiles, *refs):
    pairs = Pairs(refs, groups, tiles)
    piece_refs = refs[Pairs.count : Pairs.count + TEXT_PIECES]
    refs = refs[Pairs.count + TEXT_PIECES :]
    image_ref, first_in_ref, second_in_ref = refs[:3]
    unit_ref, first_ref, second_ref, acc_ref, own_weight_ref, weight_ref = refs[3:]
    join_rows(piece_refs, unit_ref)
    first, second = near_pairs(
        pairs, pairs.here ^ 1, None, unit_ref, image_ref, weight_ref, acc_ref, own_weight_ref
    )
    first_ref[...] = (first + first_in_ref[...]).astype(jnp.bfloat16)
    second_ref[...] = second + second_in_ref[...]


def far_body(groups, tiles, *refs):
    pairs = Pairs(refs, groups, tiles)
    own_ref, other_ref, acc_own_in_ref, acc_other_in_ref = refs[Pairs.count : Pairs.count + 4]
    piece_ref = refs[Pairs.count + 4]
    acc_other_ref, acc_own_ref, far_ref, image_ref, weight_ref = refs[Pairs.count + 5 :]
    shard = pairs.here ^ 6
    unit_images([piece_ref], image_ref)
    other_products = dot_nt(other_ref[...], image_ref[...])
    own_products = dot_nt(own_ref[...], image_ref[...])
    pairs.weigh(other_products, pairs.here ^ 1, shard, weight_ref, 0, 0, None)
    weights = weight_ref[...]
    acc_other_ref[...] = (
        acc_other_in_ref[...]
        + jnp.dot(weights, image_ref[...], preferred_element_type=jnp.float32)
    ).astype(jnp.bfloat16)
    total = dot_tn(weights, other_ref[...])
    pairs.weigh(own_products, pairs.here, shard, weight_ref, 0, 0, None)
    weights = weight_ref[...]
    acc_own_ref[...] = acc_own_in_ref[...] + jnp.dot(
        weights, image_ref[...], preferred_element_type=jnp.float32
    )
    far_ref[...] = (total + dot_tn(weights, own_ref[...])).astype(jnp.bfloat16)


def own_sum_body(own_weight_ref, own_ref, other_weight_ref, other_ref, out_ref):
    out_ref[...] = dot_tn(own_weight_ref[...], own_ref[...]) + dot_tn(
        other_weight_ref[...], other_ref[...]
    )


def widen_body(in_ref, out_ref):
    out_ref[...] = in_ref[...].astype(jnp.float32)


def all_body(groups, tiles, chips, *refs):
    pairs = Pairs(refs, groups, tiles)
    own_ref, other_ref, piece_ref = refs[Pairs.count : Pairs.count + 3]
    spread_ref, acc_own_ref, acc_other_ref, image_ref, weight_ref = refs[Pairs.count + 3 :]
    rows = own_ref.shape[0]
    unit_images([piece_ref], image_ref)
    for text_ref, shard, top, own in (
        (own_ref, pairs.here, 0, "search"),
        (other_ref, pairs.here ^ 1, rows, None),
    ):
        for chip in range(chips):
            products = dot_nt(text_ref[...], image_ref[pl.ds(chip * rows, rows), :])
            image_shard = chip * CORES + pairs.here % CORES
            pairs.weigh(products, shard, image_shard, weight_ref, top, chip * rows, own)
        acc = jnp.dot(
            weight_ref[pl.ds(top, rows), :], image_ref[...], preferred_element_type=jnp.float32
        )
        if top == 0:
            acc_own_ref[...] = acc
        else:
            acc_other_ref[...] = acc.astype(jnp.bfloat16)
    for chip in range(chips):
        columns = pl.ds(chip * rows, rows)
        total = dot_tn(weight_ref[pl.ds(0, rows), columns], own_ref[...])
        total += dot_tn(weight_ref[pl.ds(rows, rows), columns], other_ref[...])
        spread_ref[columns, :] = total.astype(jnp.bfloat16)


def relay_body(sum_ref, in_ref, *out_refs):
    for at, ref in enumerate(out_refs):
        part = pl.ds(at * ref.shape[0], ref.shape[0])
        ref[...] = (sum_ref[part, :] + in_ref[part, :].astype(jnp.float32)).astype(jnp.bfloat16)


def text_grad_body(chunks, *refs):
    where_ref = refs[0]
    raw_refs = refs[1 : 1 + chunks]
    acc_ref, add_ref = refs[1 + chunks : 3 + chunks]
    out_refs = refs[3 + chunks :]
    place = where_ref[1]
    rows, width = raw_refs[0].shape
    for first in range(0, rows, TILE):
        part = pl.ds(first, TILE)
        raws = [ref[part, :].astype(jnp.float32) for ref in raw_refs]
        scales = row_scales(sum(jnp.sum(x * x, axis=-1, keepdims=True) for x in raws))
        accs = []
        for k in range(chunks):
            features = feature_slice(place, k, width)
            accs.append(acc_ref[part, features] + add_ref[part, features].astype(jnp.float32))
        units = [x * scales for x in raws]
        inner = sum(jnp.sum(u * a, axis=-1, keepdims=True) for u, a in zip(units, accs))
        for k in range(chunks):
            out_refs[k][part, :] = (scales * (accs[k] - units[k] * inner)).astype(jnp.bfloat16)


def place_text_body(chunks, *refs):
    where_ref, part_refs, out_ref = refs[0], refs[1 : 1 + chunks], refs[1 + chunks]
    place = where_ref[1]
    rows = part_refs[0].shape[0]
    for k in range(chunks):
        block = pl.ds(pl.multiple_of((place ^ k) * rows, rows), rows)
        out_ref[block, :] = part_refs[k][...]


def image_grad_body(sum_count, raw_ref, *refs):
    sum_refs, piece_refs, out_ref = refs[:sum_count], refs[sum_count:-1], refs[-1]
    step = 64
    for first in range(0, raw_ref.shape[0], step):
        part = pl.ds(first, step)
        raw = raw_ref[part, :].astype(jnp.float32)
        scales = row_scales(jnp.sum(raw * raw, axis=-1, keepdims=True))
        unit = raw * scales
        acc = sum(ref[part, :].astype(jnp.float32) for ref in sum_refs)
        if piece_refs:
            size = piece_refs[0].shape[0]
            acc += piece_refs[first // size][pl.ds(first % size, step), :].astype(jnp.float32)
        inner = jnp.sum(unit * acc, axis=-1, keepdims=True)
        out_ref[part, :] = (scales * (acc - unit * inner)).astype(jnp.bfloat16)


def swap(value, axis, bits):
    count = lax.axis_size(axis)
    return lax.ppermute(value, axis, [(i, i ^ bits) for i in range(count)])


def swap_near(value, which):
    count = lax.axis_size("blk")
    return lax.ppermute(value, "blk", [(i, i ^ neighbour_bits(i)[which]) for i in range(count)])


def per_device(text_emb, image_emb, logit_scale, logit_bias, bucket, positive, blocks):
    groups = lax.axis_size("tp")
    shards = lax.axis_size("blk")
    rows, embed = image_emb.shape
    tiles = rows // TILE
    width = text_emb.shape[1]
    where = jnp.stack([lax.axis_index("blk"), lax.axis_index("tp")]).astype(jnp.int32)
    square = shards == 4 * CORES

    def bf16(count, columns=embed):
        return struct((count, columns), jnp.bfloat16)

    def f32(count, columns=embed):
        return struct((count, columns), jnp.float32)

    if square:
        from_second = swap_near(image_emb, 1)
        from_first = swap_near(image_emb, 0)
    else:
        chips = shards // CORES
        same_core = [[chip * CORES + core for chip in range(chips)] for core in range(CORES)]
        gathered = lax.all_gather(
            image_emb, "blk", axis=0, tiled=True, axis_index_groups=same_core
        )
    picked = call_kernel(
        pick_body,
        [bf16(rows, width)] * groups,
        [where, text_emb],
        scalars=1,
        anywhere=(1,),
        scratch=[pltpu.SemaphoreType.DMA((groups,))],
        limit=60,
    )
    text_raw = [picked[0]] + [swap(picked[k], "tp", k) for k in range(1, groups)]
    if square:
        from_far = swap_near(from_second, 0)
        images = call_kernel(
            unit_images_body, [bf16(3 * rows)], [image_emb, from_first, from_second], limit=8
        )[0]
        text_raw[-1], images = lax.optimization_barrier((text_raw[-1], images))
    text_own, *pieces = call_kernel(
        functools.partial(unit_text_body, groups),
        [bf16(rows)] + [bf16(rows // TEXT_PIECES)] * TEXT_PIECES,
        [where] + text_raw,
        scalars=1,
        limit=8,
    )
    text_other = [swap(piece, "blk", 1) for piece in pieces]

    pair_operands = [
        logit_scale,
        logit_bias,
        where,
        blocks.transpose(2, 1, 0),
        bucket.reshape(-1, TILE),
        positive.reshape(-1, TILE),
    ]
    unit_flops = 2 * rows * rows * embed

    def pair_kernel(body, outs, operands, columns, products, scratch, limit, extra=()):
        return call_kernel(
            functools.partial(body, groups, tiles, *extra),
            outs,
            pair_operands + operands,
            scalars=4,
            scratch=scratch,
            flops=products * unit_flops,
            transcendentals=2 * rows * columns,
            limit=limit,
        )

    def finish_text(acc_own, acc_other):
        parts = call_kernel(
            functools.partial(text_grad_body, groups),
            [bf16(rows, width)] * groups,
            [where] + text_raw + [acc_own, swap(acc_other, "blk", 1)],
            scalars=1,
            limit=16,
        )
        return [parts[0]] + [swap(parts[k], "tp", k) for k in range(1, groups)]

    def place_text(text_parts):
        return call_kernel(
            functools.partial(place_text_body, groups),
            [bf16(groups * rows, width)],
            [where] + text_parts,
            scalars=1,
            flops=WAIT_FLOPS,
            limit=8,
        )[0]

    def finish_image(sums, pieces):
        return call_kernel(
            functools.partial(image_grad_body, len(sums)),
            [bf16(rows)],
            [image_emb] + sums + pieces,
            limit=8,
        )[0]

    if not square:
        columns = gathered.shape[0]
        spread, acc_own, acc_other = pair_kernel(
            all_body,
            [bf16(columns), f32(rows), bf16(rows)],
            [text_own, jnp.concatenate(text_other), gathered],
            2 * columns,
            6 * chips,
            [pltpu.VMEM((columns, embed), jnp.bfloat16), pltpu.VMEM((2 * rows, columns), jnp.bfloat16)],
            56,
            (chips,),
        )
        text_parts = finish_text(acc_own, acc_other)
        parts = lax.all_to_all(
            spread, "blk", split_axis=0, concat_axis=0, tiled=True, axis_index_groups=same_core
        )
        total = jnp.sum(parts.reshape(-1, rows, embed).astype(jnp.float32), axis=0)
        return (place_text(text_parts), finish_image([total], []))

    near_scratch = [pltpu.VMEM((rows, 3 * rows), jnp.bfloat16)]
    first_sum, second_sum, acc_own, own_weights = pair_kernel(
        near_own_body,
        [f32(rows), f32(rows), f32(rows), bf16(rows, rows)],
        [text_own, images],
        3 * rows,
        8,
        near_scratch,
        24,
    )
    text_other, first_sum, second_sum, acc_other, other_weights = pair_kernel(
        near_other_body,
        [bf16(rows), bf16(rows), f32(rows), f32(rows), bf16(rows, rows)],
        text_other + [images, first_sum, second_sum],
        3 * rows,
        8,
        near_scratch,
        24,
    )
    image_add = swap_near(first_sum, 0)
    acc_other, acc_own, far_sum = pair_kernel(
        far_body,
        [bf16(rows), f32(rows), bf16(rows)],
        [text_own, text_other, acc_own, acc_other, from_far],
        2 * rows,
        6,
        [pltpu.VMEM((rows, embed), jnp.bfloat16), pltpu.VMEM((rows, rows), jnp.bfloat16)],
        24,
    )
    image_add = call_kernel(widen_body, [f32(rows)], [image_add], limit=8)[0]
    acc_own, image_add = lax.optimization_barrier((acc_own, image_add))
    text_parts = finish_text(acc_own, acc_other)
    own_weights, text_parts[0] = lax.optimization_barrier((own_weights, text_parts[0]))
    base = call_kernel(
        own_sum_body,
        [f32(rows)],
        [own_weights, text_own, other_weights, text_other],
        flops=2 * unit_flops,
        limit=8,
    )[0]
    base, second_sum = lax.optimization_barrier((base, second_sum))
    far_in = swap_near(far_sum, 0)
    relayed = call_kernel(
        relay_body, [bf16(rows // LAST_PIECES)] * LAST_PIECES, [second_sum, far_in], limit=8
    )
    image_last = [swap_near(piece, 1) for piece in relayed]
    text_grad = place_text(text_parts)
    base, _ = lax.optimization_barrier((base, text_grad))
    return (text_grad, finish_image([base, image_add], image_last))


def solution(mesh):
    in_specs = (P("blk", "tp"), P(("blk", "tp"), None), P(), P(), P(), P(), P())
    out_specs = (P("blk", "tp"), P(("blk", "tp"), None))
    return jax.shard_map(
        per_device, mesh=mesh, in_specs=in_specs, out_specs=out_specs, check_vma=False
    )
```

```python
import functools
import math

import jax
import jax.numpy as jnp
from jax import lax
from jax.experimental import pallas as pl
from jax.experimental.pallas import tpu as pltpu
from jax.sharding import PartitionSpec as P

TILE = 128
SLOTS = 3
WAIT_FLOPS = 20_000_000_000
TEXT_PIECES = 2
ACC_PIECES = 3
PICK_PARTS = 4
CORES = 2
EPS = 1e-06
LOG2E = math.log2(math.e)
MIB = 1024 * 1024

VMEM_SPEC = pl.BlockSpec(memory_space=pltpu.VMEM)
ANY_SPEC = pl.BlockSpec(memory_space=pl.ANY)
SMEM_SPEC = pl.BlockSpec(memory_space=pltpu.SMEM)


def call_kernel(
    body,
    outs,
    operands,
    scalars=0,
    anywhere=(),
    outs_anywhere=False,
    scratch=(),
    flops=0,
    limit=24,
):
    moved = sum(x.size * x.dtype.itemsize for x in operands)
    moved += sum(math.prod(o.shape) * o.dtype.itemsize for o in outs)
    specs = [SMEM_SPEC] * scalars + [VMEM_SPEC] * (len(operands) - scalars)
    for at in anywhere:
        specs[at] = ANY_SPEC
    return list(
        pl.pallas_call(
            body,
            out_shape=outs,
            in_specs=specs,
            out_specs=[ANY_SPEC if outs_anywhere else VMEM_SPEC] * len(outs),
            scratch_shapes=list(scratch),
            compiler_params=pltpu.CompilerParams(vmem_limit_bytes=limit * MIB),
            cost_estimate=pl.CostEstimate(flops=flops, bytes_accessed=moved, transcendentals=0),
        )(*operands)
    )


def struct(shape, dtype):
    return jax.ShapeDtypeStruct(shape, dtype)


def row_scales(square_sum):
    return lax.rsqrt(square_sum + EPS)


def column_of(row):
    return jnp.broadcast_to(row, (TILE, TILE)).T


def dot_nt(left, right):
    return lax.dot_general(
        left, right, (((1,), (1,)), ((), ())), preferred_element_type=jnp.float32
    )


def dot_tn(left, right):
    return lax.dot_general(
        left, right, (((0,), (0,)), ((), ())), preferred_element_type=jnp.float32
    )


def feature_slice(place, k, width):
    return pl.ds(pl.multiple_of((place ^ k) * width, width), width)


def pick_body(text_ref, *refs):
    out_refs, sems = refs[:-1], refs[-1]
    place = lax.axis_index("tp")
    rows = out_refs[0].shape[0]
    step = rows // PICK_PARTS
    copies = []
    for k, out_ref in enumerate(out_refs):
        for part in range(PICK_PARTS):
            start = pl.multiple_of((place ^ (k + 1)) * rows + part * step, step)
            copies.append(
                pltpu.make_async_copy(
                    text_ref.at[pl.ds(start, step), :],
                    out_ref.at[pl.ds(part * step, step), :],
                    sems.at[k * PICK_PARTS + part],
                )
            )
    for copy in copies:
        copy.start()
    for copy in copies:
        copy.wait()


def unit_text_body(chunks, *refs):
    chunk_refs, unit_ref, piece_refs = refs[:chunks], refs[chunks], refs[chunks + 1 :]
    place = lax.axis_index("tp")
    rows, width = chunk_refs[0].shape
    for first in range(0, rows, TILE):
        part = pl.ds(first, TILE)
        parts = [ref[part, :].astype(jnp.float32) for ref in chunk_refs]
        scales = row_scales(sum(jnp.sum(x * x, axis=-1, keepdims=True) for x in parts))
        for k, x in enumerate(parts):
            unit_ref[part, feature_slice(place, k, width)] = (x * scales).astype(jnp.bfloat16)
    split_rows(unit_ref, piece_refs)


def split_rows(whole_ref, piece_refs):
    for at, ref in enumerate(piece_refs):
        ref[...] = whole_ref[pl.ds(at * ref.shape[0], ref.shape[0]), :]


def join_rows(piece_refs, whole_ref):
    for at, ref in enumerate(piece_refs):
        whole_ref[pl.ds(at * ref.shape[0], ref.shape[0]), :] = ref[...]


def unit_images(piece_refs, image_ref):
    start = 0
    step = 64
    for ref in piece_refs:
        for first in range(0, ref.shape[0], step):
            values = ref[pl.ds(first, step), :].astype(jnp.float32)
            scales = row_scales(jnp.sum(values * values, axis=-1, keepdims=True))
            image_ref[pl.ds(start + first, step), :] = (values * scales).astype(jnp.bfloat16)
        start += ref.shape[0]


def unit_images_body(own_ref, first_ref, second_ref, own_out_ref, near_out_ref):
    unit_images([own_ref], own_out_ref)
    unit_images([first_ref, second_ref], near_out_ref)


def neighbour_bits(shard):
    core = shard % CORES
    return 2 << core, 4 >> core


def list_body(groups, tiles, chips, *refs):
    scale_ref, bias_ref, blocks_ref, bucket_ref, positive_ref = refs[:5]
    line_ref, amount_ref, column_ref, row_ref, match_ref, own_ref = refs[5:]
    here, place = lax.axis_index("blk"), lax.axis_index("tp")
    scale = scale_ref[0]
    line_ref[pl.ds(0, 1), :] = jnp.full((1, TILE), -scale * LOG2E, jnp.float32)
    line_ref[pl.ds(1, 1), :] = jnp.full((1, TILE), -bias_ref[0] * LOG2E, jnp.float32)
    if chips == 4:
        first, second = neighbour_bits(here)
        shards = [here, here ^ first, here ^ second, here ^ 6]
    else:
        shards = [chip * CORES + here % CORES for chip in range(chips)]
    count = len(shards) * tiles

    def first_tile(shard):
        return (shard * groups + place) * tiles

    for n, shard in enumerate(shards):
        own_ref[pl.ds(n, 1), :] = jnp.full((1, TILE), jnp.where(shard == here, 1.0, 0.0))
        for j in range(tiles):
            column_ref[pl.ds(n * tiles + j, 1), :] = bucket_ref[pl.ds(first_tile(shard) + j, 1), :]
    for at in range(CORES * tiles):
        tile = first_tile(here ^ (at // tiles)) + at % tiles
        row_ref[pl.ds(at * TILE, TILE), :] = column_of(bucket_ref[pl.ds(tile, 1), :])
        if at < tiles:
            ids = lax.broadcasted_iota(jnp.int32, (1, TILE), 1) + tile * TILE
            matched = column_of(positive_ref[pl.ds(tile, 1), :]) == ids
            match_ref[pl.ds(at * TILE, TILE), :] = jnp.where(matched, 1.0, 0.0)
        for n, shard in enumerate(shards):
            entries = [blocks_ref[slot, shard, tile] for slot in range(SLOTS)]
            for j in range(tiles):
                listed = sum(jnp.where(entry == j, 1.0, 0.0) for entry in entries)
                amount_ref[pl.ds(at * count + n * tiles + j, 1), :] = jnp.full(
                    (1, TILE), scale * listed, jnp.float32
                )


class Pairs:
    count = 6

    def __init__(self, refs, tiles):
        self.line_ref, self.amount_ref, self.column_ref = refs[:3]
        self.row_ref, self.match_ref, self.own_ref = refs[3:6]
        self.tiles = tiles

    def weigh(self, products, half, group, weight_ref, top, left, own=None):
        tiles = self.tiles
        slope, offset = self.line_ref[pl.ds(0, 1), :], self.line_ref[pl.ds(1, 1), :]
        count = self.column_ref.shape[0]
        for a in range(tiles):
            at = half * tiles + a
            row_bucket = self.row_ref[pl.ds(at * TILE, TILE), :]
            for j in range(tiles):
                n = group * tiles + j
                amount = self.amount_ref[pl.ds(at * count + n, 1), :]
                power = (
                    products[a * TILE : (a + 1) * TILE, j * TILE : (j + 1) * TILE] * slope + offset
                )
                factor = jnp.where(row_bucket == self.column_ref[pl.ds(n, 1), :], amount, 0.0)
                if own and a == j:
                    match = self.match_ref[pl.ds(a * TILE, TILE), :]
                    if own == "search":
                        match = match * self.own_ref[pl.ds(group, 1), :]
                    power = jnp.where(match > 0.0, -power, power)
                    factor = jnp.where(match > 0.0, -amount, factor)
                below = 1.0 + jnp.exp2(power)
                inverse = pl.reciprocal(below, approx=True)
                inverse = inverse * (2.0 - below * inverse)
                weight_ref[pl.ds(top + a * TILE, TILE), pl.ds(left + j * TILE, TILE)] = (
                    factor * inverse
                ).astype(jnp.bfloat16)


def near_weights(pairs, half, unit, own_image_ref, near_image_ref, own_weight_ref, weight_ref):
    rows = own_image_ref.shape[0]
    top = half * rows if weight_ref.shape[0] > rows else 0
    first = dot_nt(unit, near_image_ref[pl.ds(0, rows), :])
    second = dot_nt(unit, near_image_ref[pl.ds(rows, rows), :])
    pairs.weigh(first, half, 1, weight_ref, top, 0)
    own = dot_nt(unit, own_image_ref[...])
    pairs.weigh(second, half, 2, weight_ref, top, rows)
    pairs.weigh(own, half, 0, own_weight_ref, top, 0, None if half else "diagonal")


def near_own_body(tiles, *refs):
    pairs = Pairs(refs, tiles)
    unit_ref, own_image_ref, near_image_ref, own_weight_ref, weight_ref = refs[Pairs.count :]
    near_weights(
        pairs, 0, unit_ref[...], own_image_ref, near_image_ref, own_weight_ref, weight_ref
    )


def near_other_body(tiles, *refs):
    pairs = Pairs(refs, tiles)
    own_unit_ref, own_image_ref, near_image_ref, own_weight_in_ref, weight_in_ref = refs[
        Pairs.count : Pairs.count + 5
    ]
    piece_refs = refs[Pairs.count + 5 : Pairs.count + 5 + TEXT_PIECES]
    unit_ref, own_weight_ref, weight_ref, first_ref, second_ref = refs[
        Pairs.count + 5 + TEXT_PIECES :
    ]
    rows = own_unit_ref.shape[0]
    unit_ref[:rows, :] = own_unit_ref[...]
    own_weight_ref[:rows, :] = own_weight_in_ref[...]
    weight_ref[:rows, :] = weight_in_ref[...]
    for at, ref in enumerate(piece_refs):
        unit_ref[pl.ds(rows + at * ref.shape[0], ref.shape[0]), :] = ref[...]
    near_weights(
        pairs, 1, unit_ref[rows:, :], own_image_ref, near_image_ref, own_weight_ref, weight_ref
    )
    first_ref[...] = dot_tn(weight_ref[:, :rows], unit_ref[...]).astype(jnp.bfloat16)
    second_ref[...] = dot_tn(weight_ref[:, rows:], unit_ref[...])


def far_body(tiles, *refs):
    pairs = Pairs(refs, tiles)
    unit_ref, own_image_ref, near_image_ref, own_weight_ref, near_weight_ref, raw_ref = refs[
        Pairs.count : Pairs.count + 6
    ]
    outs = refs[Pairs.count + 6 :]
    acc_ref, acc_piece_refs = outs[0], outs[1 : 1 + ACC_PIECES]
    weight_ref, image_ref = outs[1 + ACC_PIECES :]
    rows = raw_ref.shape[0]
    unit_images([raw_ref], image_ref.at[pl.ds(rows, rows), :])
    image_ref[:rows, :] = own_image_ref[...]
    products = dot_nt(unit_ref[...], image_ref[rows:, :])
    weight_ref[:, :rows] = own_weight_ref[...]
    for half in range(CORES):
        part = products[half * rows : (half + 1) * rows, :]
        pairs.weigh(part, half, 3, weight_ref, half * rows, rows)
    acc = jnp.dot(near_weight_ref[...], near_image_ref[...], preferred_element_type=jnp.float32)
    acc += jnp.dot(weight_ref[...], image_ref[...], preferred_element_type=jnp.float32)
    size = rows // ACC_PIECES
    for at, ref in enumerate(acc_piece_refs):
        ref[...] = acc[rows + at * size : rows + (at + 1) * size, :].astype(jnp.bfloat16)
    acc_ref[...] = acc[:rows, :]


def far_sum_body(weight_ref, unit_ref, own_ref, far_ref):
    rows = own_ref.shape[0]
    far_ref[...] = dot_tn(weight_ref[:, rows:], unit_ref[...]).astype(jnp.bfloat16)
    own_ref[...] = dot_tn(weight_ref[:, :rows], unit_ref[...])


def add_body(left_ref, right_ref, out_ref):
    out_ref[...] = left_ref[...] + right_ref[...].astype(jnp.float32)


def all_body(tiles, chips, *refs):
    pairs = Pairs(refs, tiles)
    own_ref, other_ref, piece_ref = refs[Pairs.count : Pairs.count + 3]
    outs = refs[Pairs.count + 3 :]
    spread_ref, acc_ref, acc_piece_refs = outs[0], outs[1], outs[2 : 2 + ACC_PIECES]
    image_ref, weight_ref = outs[2 + ACC_PIECES :]
    rows = own_ref.shape[0]
    unit_images([piece_ref], image_ref)
    for half, text_ref in enumerate((own_ref, other_ref)):
        for chip in range(chips):
            products = dot_nt(text_ref[...], image_ref[pl.ds(chip * rows, rows), :])
            pairs.weigh(
                products, half, chip, weight_ref, half * rows, chip * rows, None if half else "search"
            )
        acc = jnp.dot(
            weight_ref[pl.ds(half * rows, rows), :],
            image_ref[...],
            preferred_element_type=jnp.float32,
        )
        if half == 0:
            acc_ref[...] = acc
            continue
        size = rows // ACC_PIECES
        for at, ref in enumerate(acc_piece_refs):
            ref[...] = acc[at * size : (at + 1) * size, :].astype(jnp.bfloat16)
    for chip in range(chips):
        columns = pl.ds(chip * rows, rows)
        total = dot_tn(weight_ref[pl.ds(0, rows), columns], own_ref[...])
        total += dot_tn(weight_ref[pl.ds(rows, rows), columns], other_ref[...])
        spread_ref[columns, :] = total.astype(jnp.bfloat16)


def relay_body(sum_ref, in_ref, out_ref):
    out_ref[...] = (sum_ref[...] + in_ref[...].astype(jnp.float32)).astype(jnp.bfloat16)


def text_grad_body(chunks, *refs):
    raw_refs, acc_ref, add_refs = refs[:chunks], refs[chunks], refs[chunks + 1 : -chunks]
    out_refs = refs[-chunks:]
    place = lax.axis_index("tp")
    rows, width = raw_refs[0].shape
    size = add_refs[0].shape[0]
    for first in range(0, rows, TILE):
        part = pl.ds(first, TILE)
        raws = [ref[part, :].astype(jnp.float32) for ref in raw_refs]
        scales = row_scales(sum(jnp.sum(x * x, axis=-1, keepdims=True) for x in raws))
        accs = []
        for k in range(chunks):
            features = feature_slice(place, k, width)
            added = add_refs[first // size][pl.ds(first % size, TILE), features]
            accs.append(acc_ref[part, features] + added.astype(jnp.float32))
        units = [x * scales for x in raws]
        inner = sum(jnp.sum(u * a, axis=-1, keepdims=True) for u, a in zip(units, accs))
        for k in range(chunks):
            out_refs[k][part, :] = (scales * (accs[k] - units[k] * inner)).astype(jnp.bfloat16)


def place_text_body(chunks, *refs):
    part_refs, out_ref, sems = refs[:chunks], refs[chunks], refs[chunks + 1]
    place = lax.axis_index("tp")
    rows = part_refs[0].shape[0]
    copies = []
    for k in range(chunks):
        block = pl.ds(pl.multiple_of((place ^ k) * rows, rows), rows)
        copies.append(pltpu.make_async_copy(part_refs[k], out_ref.at[block, :], sems.at[k]))
    for copy in copies:
        copy.start()
    for copy in copies:
        copy.wait()


def image_grad_body(sum_count, raw_ref, *refs):
    sum_refs, out_ref = refs[:sum_count], refs[-1]
    step = 64
    for first in range(0, raw_ref.shape[0], step):
        part = pl.ds(first, step)
        raw = raw_ref[part, :].astype(jnp.float32)
        scales = row_scales(jnp.sum(raw * raw, axis=-1, keepdims=True))
        unit = raw * scales
        acc = sum(ref[part, :].astype(jnp.float32) for ref in sum_refs)
        inner = jnp.sum(unit * acc, axis=-1, keepdims=True)
        out_ref[part, :] = (scales * (acc - unit * inner)).astype(jnp.bfloat16)


def swap(value, axis, bits):
    count = lax.axis_size(axis)
    return lax.ppermute(value, axis, [(i, i ^ bits) for i in range(count)])


def swap_near(value, which):
    count = lax.axis_size("blk")
    return lax.ppermute(value, "blk", [(i, i ^ neighbour_bits(i)[which]) for i in range(count)])


def per_device(text_emb, image_emb, logit_scale, logit_bias, bucket, positive, blocks):
    groups = lax.axis_size("tp")
    shards = lax.axis_size("blk")
    chips = shards // CORES
    rows, embed = image_emb.shape
    tiles = rows // TILE
    width = text_emb.shape[1]
    square = chips == 4

    def bf16(count, columns=embed):
        return struct((count, columns), jnp.bfloat16)

    def f32(count, columns=embed):
        return struct((count, columns), jnp.float32)

    def i32(count, columns):
        return struct((count, columns), jnp.int32)

    picked = call_kernel(
        pick_body,
        [bf16(rows, width)] * (groups - 1),
        [text_emb],
        anywhere=(0,),
        outs_anywhere=True,
        scratch=[pltpu.SemaphoreType.DMA(((groups - 1) * PICK_PARTS,))],
        limit=60,
    )
    own_chunk = lax.dynamic_slice_in_dim(text_emb, lax.axis_index("tp") * rows, rows, 0)
    text_raw = [own_chunk] + [swap(picked[k - 1], "tp", k) for k in range(1, groups)]
    if square:
        from_second = swap_near(image_emb, 1)
        from_first = swap_near(image_emb, 0)
        from_far = swap_near(from_second, 0)
        own_images, near_images = call_kernel(
            unit_images_body,
            [bf16(rows), bf16(2 * rows)],
            [image_emb, from_first, from_second],
            limit=8,
        )
    else:
        same_core = [[chip * CORES + core for chip in range(chips)] for core in range(CORES)]
        gathered = lax.all_gather(
            image_emb, "blk", axis=0, tiled=True, axis_index_groups=same_core
        )
    lists = call_kernel(
        functools.partial(list_body, groups, tiles, chips),
        [
            f32(2, TILE),
            f32(CORES * tiles * chips * tiles, TILE),
            i32(chips * tiles, TILE),
            i32(CORES * rows, TILE),
            f32(rows, TILE),
            f32(chips, TILE),
        ],
        [
            logit_scale,
            logit_bias,
            blocks.transpose(2, 1, 0),
            bucket.reshape(-1, TILE),
            positive.reshape(-1, TILE),
        ],
        scalars=3,
        limit=8,
    )
    if square:
        text_raw[-1], own_images, *lists = lax.optimization_barrier(
            (text_raw[-1], own_images, *lists)
        )
    text_own, *pieces = call_kernel(
        functools.partial(unit_text_body, groups),
        [bf16(rows)] + [bf16(rows // TEXT_PIECES)] * TEXT_PIECES,
        text_raw,
        limit=8,
    )
    text_other = [swap(piece, "blk", 1) for piece in pieces]
    unit_flops = 2 * rows * rows * embed

    def finish_text(acc_own, acc_other):
        parts = call_kernel(
            functools.partial(text_grad_body, groups),
            [bf16(rows, width)] * groups,
            text_raw + [acc_own] + [swap(piece, "blk", 1) for piece in acc_other],
            limit=16,
        )
        return [parts[0]] + [swap(parts[k], "tp", k) for k in range(1, groups)]

    def place_text(text_parts):
        return call_kernel(
            functools.partial(place_text_body, groups),
            [bf16(groups * rows, width)],
            text_parts,
            outs_anywhere=True,
            scratch=[pltpu.SemaphoreType.DMA((groups,))],
            flops=WAIT_FLOPS,
            limit=8,
        )[0]

    def finish_image(sums):
        return call_kernel(
            functools.partial(image_grad_body, len(sums)),
            [bf16(rows)],
            [image_emb] + sums,
            limit=8,
        )[0]

    if not square:
        columns = gathered.shape[0]
        spread, acc_own, *acc_other = call_kernel(
            functools.partial(all_body, tiles, chips),
            [bf16(columns), f32(rows)] + [bf16(rows // ACC_PIECES)] * ACC_PIECES,
            lists + [text_own, jnp.concatenate(text_other), gathered],
            scratch=[
                pltpu.VMEM((columns, embed), jnp.bfloat16),
                pltpu.VMEM((2 * rows, columns), jnp.bfloat16),
            ],
            flops=6 * chips * unit_flops,
            limit=56,
        )
        text_parts = finish_text(acc_own, acc_other)
        parts = lax.all_to_all(
            spread, "blk", split_axis=0, concat_axis=0, tiled=True, axis_index_groups=same_core
        )
        total = jnp.sum(parts.reshape(-1, rows, embed).astype(jnp.float32), axis=0)
        return (place_text(text_parts), finish_image([total]))

    own_weights, near_weights_own = call_kernel(
        functools.partial(near_own_body, tiles),
        [bf16(rows, rows), bf16(rows, 2 * rows)],
        lists + [text_own, own_images, near_images],
        limit=16,
    )
    units, own_weights, near_weights_all, first_sum, second_sum = call_kernel(
        functools.partial(near_other_body, tiles),
        [
            bf16(2 * rows),
            bf16(2 * rows, rows),
            bf16(2 * rows, 2 * rows),
            bf16(rows),
            f32(rows),
        ],
        lists + [text_own, own_images, near_images, own_weights, near_weights_own] + text_other,
        limit=24,
    )
    image_add = swap_near(first_sum, 0)
    acc_own, *rest = call_kernel(
        functools.partial(far_body, tiles),
        [f32(rows)] + [bf16(rows // ACC_PIECES)] * ACC_PIECES + [bf16(2 * rows, 2 * rows)],
        lists + [units, own_images, near_images, own_weights, near_weights_all, from_far],
        scratch=[pltpu.VMEM((2 * rows, embed), jnp.bfloat16)],
        flops=10 * unit_flops,
        limit=32,
    )
    acc_other, far_weights = rest[:-1], rest[-1]
    own_sum, far_sum = call_kernel(
        far_sum_body,
        [f32(rows), bf16(rows)],
        [far_weights, units],
        flops=4 * unit_flops,
        limit=16,
    )
    text_parts = finish_text(acc_own, acc_other)
    own_sum, text_parts[0] = lax.optimization_barrier((own_sum, text_parts[0]))
    base = call_kernel(add_body, [f32(rows)], [own_sum, image_add], flops=WAIT_FLOPS, limit=8)[0]
    base, second_sum = lax.optimization_barrier((base, second_sum))
    relayed = call_kernel(
        relay_body, [bf16(rows)], [second_sum, swap_near(far_sum, 0)], limit=8
    )[0]
    image_last = swap_near(relayed, 1)
    text_grad = place_text(text_parts)
    base, _ = lax.optimization_barrier((base, text_grad))
    return (text_grad, finish_image([base, image_last]))


def solution(mesh):
    in_specs = (P("blk", "tp"), P(("blk", "tp"), None), P(), P(), P(), P(), P())
    out_specs = (P("blk", "tp"), P(("blk", "tp"), None))
    return jax.shard_map(
        per_device, mesh=mesh, in_specs=in_specs, out_specs=out_specs, check_vma=False
    )
```

```python
import functools
import math

import jax
import jax.numpy as jnp
from jax import lax
from jax.experimental import pallas as pl
from jax.experimental.pallas import tpu as pltpu
from jax.sharding import PartitionSpec as P

TILE = 128
SLOTS = 3
WAIT_FLOPS = 20_000_000_000
TEXT_PIECES = 2
ACC_PIECES = 3
CORES = 2
EPS = 1e-06
LOG2E = math.log2(math.e)
MIB = 1024 * 1024

VMEM_SPEC = pl.BlockSpec(memory_space=pltpu.VMEM)
ANY_SPEC = pl.BlockSpec(memory_space=pl.ANY)
SMEM_SPEC = pl.BlockSpec(memory_space=pltpu.SMEM)


def call_kernel(
    body,
    outs,
    operands,
    scalars=0,
    anywhere=(),
    outs_anywhere=False,
    scratch=(),
    flops=0,
    limit=24,
):
    moved = sum(x.size * x.dtype.itemsize for x in operands)
    moved += sum(math.prod(o.shape) * o.dtype.itemsize for o in outs)
    specs = [SMEM_SPEC] * scalars + [VMEM_SPEC] * (len(operands) - scalars)
    for at in anywhere:
        specs[at] = ANY_SPEC
    return list(
        pl.pallas_call(
            body,
            out_shape=outs,
            in_specs=specs,
            out_specs=[ANY_SPEC if outs_anywhere else VMEM_SPEC] * len(outs),
            scratch_shapes=list(scratch),
            compiler_params=pltpu.CompilerParams(vmem_limit_bytes=limit * MIB),
            cost_estimate=pl.CostEstimate(flops=flops, bytes_accessed=moved, transcendentals=0),
        )(*operands)
    )


def struct(shape, dtype):
    return jax.ShapeDtypeStruct(shape, dtype)


def row_scales(square_sum):
    return lax.rsqrt(square_sum + EPS)


def column_of(row):
    return jnp.broadcast_to(row, (TILE, TILE)).T


def dot_nt(left, right):
    return lax.dot_general(
        left, right, (((1,), (1,)), ((), ())), preferred_element_type=jnp.float32
    )


def dot_tn(left, right):
    return lax.dot_general(
        left, right, (((0,), (0,)), ((), ())), preferred_element_type=jnp.float32
    )


def feature_slice(place, k, width):
    return pl.ds(pl.multiple_of((place ^ k) * width, width), width)


def pick_body(text_ref, *out_refs):
    place = lax.axis_index("tp")
    rows = out_refs[0].shape[0]
    for k, out_ref in enumerate(out_refs):
        out_ref[...] = text_ref[pl.ds(pl.multiple_of((place ^ k) * rows, rows), rows), :]


def unit_text_body(chunks, *refs):
    chunk_refs, unit_ref, piece_refs = refs[:chunks], refs[chunks], refs[chunks + 1 :]
    place = lax.axis_index("tp")
    rows, width = chunk_refs[0].shape
    for first in range(0, rows, TILE):
        part = pl.ds(first, TILE)
        parts = [ref[part, :].astype(jnp.float32) for ref in chunk_refs]
        scales = row_scales(sum(jnp.sum(x * x, axis=-1, keepdims=True) for x in parts))
        for k, x in enumerate(parts):
            unit_ref[part, feature_slice(place, k, width)] = (x * scales).astype(jnp.bfloat16)
    split_rows(unit_ref, piece_refs)


def split_rows(whole_ref, piece_refs):
    for at, ref in enumerate(piece_refs):
        ref[...] = whole_ref[pl.ds(at * ref.shape[0], ref.shape[0]), :]


def join_rows(piece_refs, whole_ref):
    for at, ref in enumerate(piece_refs):
        whole_ref[pl.ds(at * ref.shape[0], ref.shape[0]), :] = ref[...]


def unit_images(piece_refs, image_ref):
    start = 0
    step = 64
    for ref in piece_refs:
        for first in range(0, ref.shape[0], step):
            values = ref[pl.ds(first, step), :].astype(jnp.float32)
            scales = row_scales(jnp.sum(values * values, axis=-1, keepdims=True))
            image_ref[pl.ds(start + first, step), :] = (values * scales).astype(jnp.bfloat16)
        start += ref.shape[0]


def unit_images_body(own_ref, first_ref, second_ref, own_out_ref, near_out_ref):
    unit_images([own_ref], own_out_ref)
    unit_images([first_ref, second_ref], near_out_ref)


def neighbour_bits(shard):
    core = shard % CORES
    return 2 << core, 4 >> core


def list_body(groups, tiles, chips, *refs):
    scale_ref, bias_ref, blocks_ref, bucket_ref, positive_ref = refs[:5]
    line_ref, amount_ref, column_ref, row_ref, match_ref, own_ref = refs[5:]
    here, place = lax.axis_index("blk"), lax.axis_index("tp")
    scale = scale_ref[0]
    line_ref[pl.ds(0, 1), :] = jnp.full((1, TILE), -scale * LOG2E, jnp.float32)
    line_ref[pl.ds(1, 1), :] = jnp.full((1, TILE), -bias_ref[0] * LOG2E, jnp.float32)
    if chips == 4:
        first, second = neighbour_bits(here)
        shards = [here, here ^ first, here ^ second, here ^ 6]
    else:
        shards = [chip * CORES + here % CORES for chip in range(chips)]
    count = len(shards) * tiles

    def first_tile(shard):
        return (shard * groups + place) * tiles

    for n, shard in enumerate(shards):
        own_ref[pl.ds(n, 1), :] = jnp.full((1, TILE), jnp.where(shard == here, 1.0, 0.0))
        for j in range(tiles):
            column_ref[pl.ds(n * tiles + j, 1), :] = bucket_ref[pl.ds(first_tile(shard) + j, 1), :]
    for at in range(CORES * tiles):
        tile = first_tile(here ^ (at // tiles)) + at % tiles
        row_ref[pl.ds(at * TILE, TILE), :] = column_of(bucket_ref[pl.ds(tile, 1), :])
        if at < tiles:
            ids = lax.broadcasted_iota(jnp.int32, (1, TILE), 1) + tile * TILE
            matched = column_of(positive_ref[pl.ds(tile, 1), :]) == ids
            match_ref[pl.ds(at * TILE, TILE), :] = jnp.where(matched, 1.0, 0.0)
        for n, shard in enumerate(shards):
            entries = [blocks_ref[slot, shard, tile] for slot in range(SLOTS)]
            for j in range(tiles):
                listed = sum(jnp.where(entry == j, 1.0, 0.0) for entry in entries)
                amount_ref[pl.ds(at * count + n * tiles + j, 1), :] = jnp.full(
                    (1, TILE), scale * listed, jnp.float32
                )


class Pairs:
    count = 6

    def __init__(self, refs, tiles):
        self.line_ref, self.amount_ref, self.column_ref = refs[:3]
        self.row_ref, self.match_ref, self.own_ref = refs[3:6]
        self.tiles = tiles

    def weigh(self, products, half, group, weight_ref, top, left, own=None):
        tiles = self.tiles
        slope, offset = self.line_ref[pl.ds(0, 1), :], self.line_ref[pl.ds(1, 1), :]
        count = self.column_ref.shape[0]
        for a in range(tiles):
            at = half * tiles + a
            row_bucket = self.row_ref[pl.ds(at * TILE, TILE), :]
            for j in range(tiles):
                n = group * tiles + j
                amount = self.amount_ref[pl.ds(at * count + n, 1), :]
                power = (
                    products[a * TILE : (a + 1) * TILE, j * TILE : (j + 1) * TILE] * slope + offset
                )
                factor = jnp.where(row_bucket == self.column_ref[pl.ds(n, 1), :], amount, 0.0)
                if own and a == j:
                    match = self.match_ref[pl.ds(a * TILE, TILE), :]
                    if own == "search":
                        match = match * self.own_ref[pl.ds(group, 1), :]
                    power = jnp.where(match > 0.0, -power, power)
                    factor = jnp.where(match > 0.0, -amount, factor)
                below = 1.0 + jnp.exp2(power)
                inverse = pl.reciprocal(below, approx=True)
                inverse = inverse * (2.0 - below * inverse)
                weight_ref[pl.ds(top + a * TILE, TILE), pl.ds(left + j * TILE, TILE)] = (
                    factor * inverse
                ).astype(jnp.bfloat16)


def near_own_body(tiles, *refs):
    pairs = Pairs(refs, tiles)
    unit_ref, own_image_ref, near_image_ref, own_weight_ref, weight_ref = refs[Pairs.count :]
    rows = unit_ref.shape[0]
    first = dot_nt(unit_ref[...], near_image_ref[pl.ds(0, rows), :])
    second = dot_nt(unit_ref[...], near_image_ref[pl.ds(rows, rows), :])
    pairs.weigh(first, 0, 1, weight_ref, 0, 0)
    own = dot_nt(unit_ref[...], own_image_ref[...])
    pairs.weigh(second, 0, 2, weight_ref, 0, rows)
    pairs.weigh(own, 0, 0, own_weight_ref, 0, 0, "diagonal")


def first_sum_body(tiles, *refs):
    pairs = Pairs(refs, tiles)
    own_unit_ref, near_image_ref, weight_in_ref = refs[Pairs.count : Pairs.count + 3]
    piece_refs = refs[Pairs.count + 3 : Pairs.count + 3 + TEXT_PIECES]
    unit_ref, weight_ref, sum_ref = refs[Pairs.count + 3 + TEXT_PIECES :]
    rows = own_unit_ref.shape[0]
    for at, ref in enumerate(piece_refs):
        unit_ref[pl.ds(rows + at * ref.shape[0], ref.shape[0]), :] = ref[...]
    unit_ref[:rows, :] = own_unit_ref[...]
    weight_ref[:rows, :] = weight_in_ref[:, :rows]
    products = dot_nt(unit_ref[rows:, :], near_image_ref[pl.ds(0, rows), :])
    pairs.weigh(products, 1, 1, weight_ref, rows, 0)
    sum_ref[...] = dot_tn(weight_ref[...], unit_ref[...]).astype(jnp.bfloat16)


def second_sum_body(tiles, *refs):
    pairs = Pairs(refs, tiles)
    unit_ref, own_image_ref, near_image_ref, own_weight_in_ref, weight_in_ref, first_ref = refs[
        Pairs.count : Pairs.count + 6
    ]
    own_weight_ref, weight_ref, sum_ref = refs[Pairs.count + 6 :]
    rows = own_image_ref.shape[0]
    second = dot_nt(unit_ref[rows:, :], near_image_ref[pl.ds(rows, rows), :])
    own = dot_nt(unit_ref[rows:, :], own_image_ref[...])
    own_weight_ref[:rows, :] = own_weight_in_ref[...]
    weight_ref[:, :rows] = first_ref[...]
    weight_ref[:rows, rows:] = weight_in_ref[:, rows:]
    pairs.weigh(second, 1, 2, weight_ref, rows, rows)
    sum_ref[...] = dot_tn(weight_ref[:, rows:], unit_ref[...])
    pairs.weigh(own, 1, 0, own_weight_ref, rows, 0)


def far_sum_body(tiles, *refs):
    pairs = Pairs(refs, tiles)
    unit_ref, own_image_ref, own_weight_ref, raw_ref = refs[Pairs.count : Pairs.count + 4]
    sum_ref, weight_ref, image_ref = refs[Pairs.count + 4 :]
    rows = raw_ref.shape[0]
    unit_images([raw_ref], image_ref.at[pl.ds(rows, rows), :])
    products = dot_nt(unit_ref[...], image_ref[rows:, :])
    for half in range(CORES):
        part = products[half * rows : (half + 1) * rows, :]
        pairs.weigh(part, half, 3, weight_ref, half * rows, rows)
    sum_ref[...] = dot_tn(weight_ref[:, rows:], unit_ref[...]).astype(jnp.bfloat16)
    image_ref[:rows, :] = own_image_ref[...]
    weight_ref[:, :rows] = own_weight_ref[...]


def text_sum_body(near_weight_ref, near_image_ref, weight_ref, image_ref, acc_ref, *piece_refs):
    rows = acc_ref.shape[0]
    size = rows // ACC_PIECES
    for part in (slice(rows, 2 * rows), slice(0, rows)):
        acc = jnp.dot(
            near_weight_ref[part, :], near_image_ref[...], preferred_element_type=jnp.float32
        ) + jnp.dot(weight_ref[part, :], image_ref[...], preferred_element_type=jnp.float32)
        if part.start == 0:
            acc_ref[...] = acc
            continue
        for at, ref in enumerate(piece_refs):
            ref[...] = acc[at * size : (at + 1) * size, :].astype(jnp.bfloat16)


def own_sum_body(weight_ref, unit_ref, add_ref, out_ref):
    rows = out_ref.shape[0]
    out_ref[...] = dot_tn(weight_ref[:, :rows], unit_ref[...]) + add_ref[...].astype(jnp.float32)


def all_body(tiles, chips, *refs):
    pairs = Pairs(refs, tiles)
    own_ref, other_ref, piece_ref = refs[Pairs.count : Pairs.count + 3]
    outs = refs[Pairs.count + 3 :]
    spread_ref, acc_ref, acc_piece_refs = outs[0], outs[1], outs[2 : 2 + ACC_PIECES]
    image_ref, weight_ref = outs[2 + ACC_PIECES :]
    rows = own_ref.shape[0]
    unit_images([piece_ref], image_ref)
    for half, text_ref in enumerate((own_ref, other_ref)):
        for chip in range(chips):
            products = dot_nt(text_ref[...], image_ref[pl.ds(chip * rows, rows), :])
            pairs.weigh(
                products, half, chip, weight_ref, half * rows, chip * rows, None if half else "search"
            )
        acc = jnp.dot(
            weight_ref[pl.ds(half * rows, rows), :],
            image_ref[...],
            preferred_element_type=jnp.float32,
        )
        if half == 0:
            acc_ref[...] = acc
            continue
        size = rows // ACC_PIECES
        for at, ref in enumerate(acc_piece_refs):
            ref[...] = acc[at * size : (at + 1) * size, :].astype(jnp.bfloat16)
    for chip in range(chips):
        columns = pl.ds(chip * rows, rows)
        total = dot_tn(weight_ref[pl.ds(0, rows), columns], own_ref[...])
        total += dot_tn(weight_ref[pl.ds(rows, rows), columns], other_ref[...])
        spread_ref[columns, :] = total.astype(jnp.bfloat16)


def relay_body(sum_ref, in_ref, out_ref):
    out_ref[...] = (sum_ref[...] + in_ref[...].astype(jnp.float32)).astype(jnp.bfloat16)


def text_grad_body(chunks, *refs):
    raw_refs, acc_ref, add_refs = refs[:chunks], refs[chunks], refs[chunks + 1 : -chunks]
    out_refs = refs[-chunks:]
    place = lax.axis_index("tp")
    rows, width = raw_refs[0].shape
    size = add_refs[0].shape[0]
    for first in range(0, rows, TILE):
        part = pl.ds(first, TILE)
        raws = [ref[part, :].astype(jnp.float32) for ref in raw_refs]
        scales = row_scales(sum(jnp.sum(x * x, axis=-1, keepdims=True) for x in raws))
        accs = []
        for k in range(chunks):
            features = feature_slice(place, k, width)
            added = add_refs[first // size][pl.ds(first % size, TILE), features]
            accs.append(acc_ref[part, features] + added.astype(jnp.float32))
        units = [x * scales for x in raws]
        inner = sum(jnp.sum(u * a, axis=-1, keepdims=True) for u, a in zip(units, accs))
        for k in range(chunks):
            out_refs[k][part, :] = (scales * (accs[k] - units[k] * inner)).astype(jnp.bfloat16)


def place_text_body(chunks, *refs):
    part_refs, out_ref, sems = refs[:chunks], refs[chunks], refs[chunks + 1]
    place = lax.axis_index("tp")
    rows = part_refs[0].shape[0]
    copies = []
    for k in range(chunks):
        block = pl.ds(pl.multiple_of((place ^ k) * rows, rows), rows)
        copies.append(pltpu.make_async_copy(part_refs[k], out_ref.at[block, :], sems.at[k]))
    for copy in copies:
        copy.start()
    for copy in copies:
        copy.wait()


def image_grad_body(sum_count, raw_ref, *refs):
    sum_refs, (out_ref, grad_ref, sems) = refs[:sum_count], refs[sum_count:]
    copies = []
    for block in range(raw_ref.shape[0] // TILE):
        for first in range(block * TILE, (block + 1) * TILE, TILE // 2):
            part = pl.ds(first, TILE // 2)
            raw = raw_ref[part, :].astype(jnp.float32)
            scales = row_scales(jnp.sum(raw * raw, axis=-1, keepdims=True))
            unit = raw * scales
            acc = sum(ref[part, :].astype(jnp.float32) for ref in sum_refs)
            inner = jnp.sum(unit * acc, axis=-1, keepdims=True)
            grad_ref[part, :] = (scales * (acc - unit * inner)).astype(jnp.bfloat16)
        part = pl.ds(block * TILE, TILE)
        copies.append(
            pltpu.make_async_copy(grad_ref.at[part, :], out_ref.at[part, :], sems.at[block])
        )
        copies[-1].start()
    for copy in copies:
        copy.wait()


def swap(value, axis, bits):
    count = lax.axis_size(axis)
    return lax.ppermute(value, axis, [(i, i ^ bits) for i in range(count)])


def swap_near(value, which):
    count = lax.axis_size("blk")
    return lax.ppermute(value, "blk", [(i, i ^ neighbour_bits(i)[which]) for i in range(count)])


def per_device(text_emb, image_emb, logit_scale, logit_bias, bucket, positive, blocks):
    groups = lax.axis_size("tp")
    shards = lax.axis_size("blk")
    chips = shards // CORES
    rows, embed = image_emb.shape
    tiles = rows // TILE
    width = text_emb.shape[1]
    square = chips == 4

    def bf16(count, columns=embed):
        return struct((count, columns), jnp.bfloat16)

    def f32(count, columns=embed):
        return struct((count, columns), jnp.float32)

    def i32(count, columns):
        return struct((count, columns), jnp.int32)

    picked = call_kernel(pick_body, [bf16(rows, width)] * groups, [text_emb], limit=8)
    picked[-1], image_sent = lax.optimization_barrier((picked[-1], image_emb))
    text_raw = [picked[0]] + [swap(picked[k], "tp", k) for k in range(1, groups)]
    if square:
        from_second = swap_near(image_sent, 1)
        from_first = swap_near(image_sent, 0)
        from_far = swap_near(from_second, 0)
        own_images, near_images = call_kernel(
            unit_images_body,
            [bf16(rows), bf16(2 * rows)],
            [image_emb, from_first, from_second],
            limit=8,
        )
    else:
        same_core = [[chip * CORES + core for chip in range(chips)] for core in range(CORES)]
        gathered = lax.all_gather(
            image_emb, "blk", axis=0, tiled=True, axis_index_groups=same_core
        )
    lists = call_kernel(
        functools.partial(list_body, groups, tiles, chips),
        [
            f32(2, TILE),
            f32(CORES * tiles * chips * tiles, TILE),
            i32(chips * tiles, TILE),
            i32(CORES * rows, TILE),
            f32(rows, TILE),
            f32(chips, TILE),
        ],
        [
            logit_scale,
            logit_bias,
            blocks.transpose(2, 1, 0),
            bucket.reshape(-1, TILE),
            positive.reshape(-1, TILE),
        ],
        scalars=3,
        flops=WAIT_FLOPS // 2,
        limit=8,
    )
    if square:
        text_raw[-1], own_images, *lists = lax.optimization_barrier(
            (text_raw[-1], own_images, *lists)
        )
    text_own, *pieces = call_kernel(
        functools.partial(unit_text_body, groups),
        [bf16(rows)] + [bf16(rows // TEXT_PIECES)] * TEXT_PIECES,
        text_raw,
        limit=8,
    )
    text_other = [swap(piece, "blk", 1) for piece in pieces]
    unit_flops = 2 * rows * rows * embed

    def finish_text(acc_own, acc_other):
        parts = call_kernel(
            functools.partial(text_grad_body, groups),
            [bf16(rows, width)] * groups,
            text_raw + [acc_own] + [swap(piece, "blk", 1) for piece in acc_other],
            limit=16,
        )
        return [parts[0]] + [swap(parts[k], "tp", k) for k in range(1, groups)]

    def place_text(text_parts):
        return call_kernel(
            functools.partial(place_text_body, groups),
            [bf16(groups * rows, width)],
            text_parts,
            outs_anywhere=True,
            scratch=[pltpu.SemaphoreType.DMA((groups,))],
            flops=WAIT_FLOPS,
            limit=8,
        )[0]

    def finish_image(sums):
        return call_kernel(
            functools.partial(image_grad_body, len(sums)),
            [bf16(rows)],
            [image_emb] + sums,
            outs_anywhere=True,
            scratch=[pltpu.VMEM((rows, embed), jnp.bfloat16), pltpu.SemaphoreType.DMA((tiles,))],
            limit=8,
        )[0]

    if not square:
        columns = gathered.shape[0]
        spread, acc_own, *acc_other = call_kernel(
            functools.partial(all_body, tiles, chips),
            [bf16(columns), f32(rows)] + [bf16(rows // ACC_PIECES)] * ACC_PIECES,
            lists + [text_own, jnp.concatenate(text_other), gathered],
            scratch=[
                pltpu.VMEM((columns, embed), jnp.bfloat16),
                pltpu.VMEM((2 * rows, columns), jnp.bfloat16),
            ],
            flops=6 * chips * unit_flops,
            limit=56,
        )
        text_parts = finish_text(acc_own, acc_other)
        parts = lax.all_to_all(
            spread, "blk", split_axis=0, concat_axis=0, tiled=True, axis_index_groups=same_core
        )
        total = jnp.sum(parts.reshape(-1, rows, embed).astype(jnp.float32), axis=0)
        return (place_text(text_parts), finish_image([total]))

    own_weights, near_weights = call_kernel(
        functools.partial(near_own_body, tiles),
        [bf16(rows, rows), bf16(rows, 2 * rows)],
        lists + [text_own, own_images, near_images],
        limit=16,
    )
    units, first_weights, first_sum = call_kernel(
        functools.partial(first_sum_body, tiles),
        [bf16(2 * rows), bf16(2 * rows, rows), bf16(rows)],
        lists + [text_own, near_images, near_weights] + text_other,
        limit=16,
    )
    image_add = swap_near(first_sum, 0)
    own_weights, near_weights, second_sum = call_kernel(
        functools.partial(second_sum_body, tiles),
        [bf16(2 * rows, rows), bf16(2 * rows, 2 * rows), f32(rows)],
        lists + [units, own_images, near_images, own_weights, near_weights, first_weights],
        limit=16,
    )
    own_weights, from_far = lax.optimization_barrier((own_weights, from_far))
    far_sum, far_weights, far_images = call_kernel(
        functools.partial(far_sum_body, tiles),
        [bf16(rows), bf16(2 * rows, 2 * rows), bf16(2 * rows)],
        lists + [units, own_images, own_weights, from_far],
        limit=16,
    )
    acc_own, *acc_other = call_kernel(
        text_sum_body,
        [f32(rows)] + [bf16(rows // ACC_PIECES)] * ACC_PIECES,
        [near_weights, near_images, far_weights, far_images],
        limit=24,
    )
    text_parts = finish_text(acc_own, acc_other)
    far_weights, text_parts[0] = lax.optimization_barrier((far_weights, text_parts[0]))
    base = call_kernel(
        own_sum_body, [f32(rows)], [far_weights, units, image_add], limit=16
    )[0]
    base, second_sum = lax.optimization_barrier((base, second_sum))
    relayed = call_kernel(
        relay_body, [bf16(rows)], [second_sum, swap_near(far_sum, 0)], limit=8
    )[0]
    image_last = swap_near(relayed, 1)
    text_grad = place_text(text_parts)
    base, _ = lax.optimization_barrier((base, text_grad))
    return (text_grad, finish_image([base, image_last]))


def solution(mesh):
    in_specs = (P("blk", "tp"), P(("blk", "tp"), None), P(), P(), P(), P(), P())
    out_specs = (P("blk", "tp"), P(("blk", "tp"), None))
    return jax.shard_map(
        per_device, mesh=mesh, in_specs=in_specs, out_specs=out_specs, check_vma=False
    )
```

```python
import functools
import math

import jax
import jax.numpy as jnp
from jax import lax
from jax.experimental import pallas as pl
from jax.experimental.pallas import tpu as pltpu
from jax.sharding import PartitionSpec as P

TILE = 128
SLOTS = 3
WAIT_FLOPS = 20_000_000_000
TEXT_PIECES = 2
ACC_PIECES = 3
CORES = 2
EPS = 1e-06
LOG2E = math.log2(math.e)
MIB = 1024 * 1024

VMEM_SPEC = pl.BlockSpec(memory_space=pltpu.VMEM)
ANY_SPEC = pl.BlockSpec(memory_space=pl.ANY)
SMEM_SPEC = pl.BlockSpec(memory_space=pltpu.SMEM)


def call_kernel(
    body,
    outs,
    operands,
    scalars=0,
    anywhere=(),
    outs_anywhere=False,
    scratch=(),
    flops=0,
    limit=24,
):
    moved = sum(x.size * x.dtype.itemsize for x in operands)
    moved += sum(math.prod(o.shape) * o.dtype.itemsize for o in outs)
    specs = [SMEM_SPEC] * scalars + [VMEM_SPEC] * (len(operands) - scalars)
    for at in anywhere:
        specs[at] = ANY_SPEC
    return list(
        pl.pallas_call(
            body,
            out_shape=outs,
            in_specs=specs,
            out_specs=[ANY_SPEC if outs_anywhere else VMEM_SPEC] * len(outs),
            scratch_shapes=list(scratch),
            compiler_params=pltpu.CompilerParams(vmem_limit_bytes=limit * MIB),
            cost_estimate=pl.CostEstimate(flops=flops, bytes_accessed=moved, transcendentals=0),
        )(*operands)
    )


def struct(shape, dtype):
    return jax.ShapeDtypeStruct(shape, dtype)


def row_scales(square_sum):
    return lax.rsqrt(square_sum + EPS)


def column_of(row):
    return jnp.broadcast_to(row, (TILE, TILE)).T


def dot_nt(left, right):
    return lax.dot_general(
        left, right, (((1,), (1,)), ((), ())), preferred_element_type=jnp.float32
    )


def dot_tn(left, right):
    return lax.dot_general(
        left, right, (((0,), (0,)), ((), ())), preferred_element_type=jnp.float32
    )


def feature_slice(place, k, width):
    return pl.ds(pl.multiple_of((place ^ k) * width, width), width)


def pick_body(text_ref, *out_refs):
    place = lax.axis_index("tp")
    rows = out_refs[0].shape[0]
    for k, out_ref in enumerate(out_refs):
        out_ref[...] = text_ref[pl.ds(pl.multiple_of((place ^ k) * rows, rows), rows), :]


def unit_text_body(chunks, *refs):
    chunk_refs, unit_ref, piece_refs = refs[:chunks], refs[chunks], refs[chunks + 1 :]
    place = lax.axis_index("tp")
    rows, width = chunk_refs[0].shape
    for first in range(0, rows, TILE):
        part = pl.ds(first, TILE)
        parts = [ref[part, :].astype(jnp.float32) for ref in chunk_refs]
        scales = row_scales(sum(jnp.sum(x * x, axis=-1, keepdims=True) for x in parts))
        for k, x in enumerate(parts):
            unit_ref[part, feature_slice(place, k, width)] = (x * scales).astype(jnp.bfloat16)
    split_rows(unit_ref, piece_refs)


def split_rows(whole_ref, piece_refs):
    for at, ref in enumerate(piece_refs):
        ref[...] = whole_ref[pl.ds(at * ref.shape[0], ref.shape[0]), :]


def join_rows(piece_refs, whole_ref):
    for at, ref in enumerate(piece_refs):
        whole_ref[pl.ds(at * ref.shape[0], ref.shape[0]), :] = ref[...]


def unit_images(piece_refs, image_ref):
    start = 0
    step = 64
    for ref in piece_refs:
        for first in range(0, ref.shape[0], step):
            values = ref[pl.ds(first, step), :].astype(jnp.float32)
            scales = row_scales(jnp.sum(values * values, axis=-1, keepdims=True))
            image_ref[pl.ds(start + first, step), :] = (values * scales).astype(jnp.bfloat16)
        start += ref.shape[0]


def unit_images_body(own_ref, first_ref, second_ref, own_out_ref, near_out_ref):
    unit_images([own_ref], own_out_ref)
    unit_images([first_ref, second_ref], near_out_ref)


def neighbour_bits(shard):
    core = shard % CORES
    return 2 << core, 4 >> core


def list_body(groups, tiles, chips, *refs):
    scale_ref, bias_ref, blocks_ref, bucket_ref, positive_ref = refs[:5]
    line_ref, amount_ref, column_ref, row_ref, match_ref, own_ref = refs[5:]
    here, place = lax.axis_index("blk"), lax.axis_index("tp")
    scale = scale_ref[0]
    line_ref[pl.ds(0, 1), :] = jnp.full((1, TILE), -scale * LOG2E, jnp.float32)
    line_ref[pl.ds(1, 1), :] = jnp.full((1, TILE), -bias_ref[0] * LOG2E, jnp.float32)
    if chips == 4:
        first, second = neighbour_bits(here)
        shards = [here, here ^ first, here ^ second, here ^ 6]
    else:
        shards = [chip * CORES + here % CORES for chip in range(chips)]
    count = len(shards) * tiles

    def first_tile(shard):
        return (shard * groups + place) * tiles

    for n, shard in enumerate(shards):
        own_ref[pl.ds(n, 1), :] = jnp.full((1, TILE), jnp.where(shard == here, 1.0, 0.0))
        for j in range(tiles):
            column_ref[pl.ds(n * tiles + j, 1), :] = bucket_ref[pl.ds(first_tile(shard) + j, 1), :]
    for at in range(CORES * tiles):
        tile = first_tile(here ^ (at // tiles)) + at % tiles
        row_ref[pl.ds(at * TILE, TILE), :] = column_of(bucket_ref[pl.ds(tile, 1), :])
        if at < tiles:
            ids = lax.broadcasted_iota(jnp.int32, (1, TILE), 1) + tile * TILE
            matched = column_of(positive_ref[pl.ds(tile, 1), :]) == ids
            match_ref[pl.ds(at * TILE, TILE), :] = jnp.where(matched, 1.0, 0.0)
        for n, shard in enumerate(shards):
            entries = [blocks_ref[slot, shard, tile] for slot in range(SLOTS)]
            for j in range(tiles):
                listed = sum(jnp.where(entry == j, 1.0, 0.0) for entry in entries)
                amount_ref[pl.ds(at * count + n * tiles + j, 1), :] = jnp.full(
                    (1, TILE), scale * listed, jnp.float32
                )


class Pairs:
    count = 6

    def __init__(self, refs, tiles):
        self.line_ref, self.amount_ref, self.column_ref = refs[:3]
        self.row_ref, self.match_ref, self.own_ref = refs[3:6]
        self.tiles = tiles

    def weigh(self, products, half, group, weight_ref, top, left, own=None):
        tiles = self.tiles
        slope, offset = self.line_ref[pl.ds(0, 1), :], self.line_ref[pl.ds(1, 1), :]
        count = self.column_ref.shape[0]
        for a in range(tiles):
            at = half * tiles + a
            row_bucket = self.row_ref[pl.ds(at * TILE, TILE), :]
            for j in range(tiles):
                n = group * tiles + j
                amount = self.amount_ref[pl.ds(at * count + n, 1), :]
                power = (
                    products[a * TILE : (a + 1) * TILE, j * TILE : (j + 1) * TILE] * slope + offset
                )
                factor = jnp.where(row_bucket == self.column_ref[pl.ds(n, 1), :], amount, 0.0)
                if own and a == j:
                    match = self.match_ref[pl.ds(a * TILE, TILE), :]
                    if own == "search":
                        match = match * self.own_ref[pl.ds(group, 1), :]
                    power = jnp.where(match > 0.0, -power, power)
                    factor = jnp.where(match > 0.0, -amount, factor)
                below = 1.0 + jnp.exp2(power)
                inverse = pl.reciprocal(below, approx=True)
                inverse = inverse * (2.0 - below * inverse)
                weight_ref[pl.ds(top + a * TILE, TILE), pl.ds(left + j * TILE, TILE)] = (
                    factor * inverse
                ).astype(jnp.bfloat16)


def near_own_body(tiles, *refs):
    pairs = Pairs(refs, tiles)
    unit_ref, own_image_ref, near_image_ref, own_weight_ref, weight_ref = refs[Pairs.count :]
    rows = unit_ref.shape[0]
    first = dot_nt(unit_ref[...], near_image_ref[pl.ds(0, rows), :])
    second = dot_nt(unit_ref[...], near_image_ref[pl.ds(rows, rows), :])
    pairs.weigh(first, 0, 1, weight_ref, 0, 0)
    own = dot_nt(unit_ref[...], own_image_ref[...])
    pairs.weigh(second, 0, 2, weight_ref, 0, rows)
    pairs.weigh(own, 0, 0, own_weight_ref, 0, 0, "diagonal")


def first_sum_body(tiles, *refs):
    pairs = Pairs(refs, tiles)
    own_unit_ref, near_image_ref, weight_in_ref = refs[Pairs.count : Pairs.count + 3]
    piece_refs = refs[Pairs.count + 3 : Pairs.count + 3 + TEXT_PIECES]
    unit_ref, weight_ref, sum_ref = refs[Pairs.count + 3 + TEXT_PIECES :]
    rows = own_unit_ref.shape[0]
    for at, ref in enumerate(piece_refs):
        unit_ref[pl.ds(rows + at * ref.shape[0], ref.shape[0]), :] = ref[...]
    unit_ref[:rows, :] = own_unit_ref[...]
    weight_ref[:rows, :] = weight_in_ref[:, :rows]
    products = dot_nt(unit_ref[rows:, :], near_image_ref[pl.ds(0, rows), :])
    pairs.weigh(products, 1, 1, weight_ref, rows, 0)
    sum_ref[...] = dot_tn(weight_ref[...], unit_ref[...]).astype(jnp.bfloat16)


def second_sum_body(tiles, *refs):
    pairs = Pairs(refs, tiles)
    unit_ref, own_image_ref, near_image_ref, own_weight_in_ref, weight_in_ref, first_ref = refs[
        Pairs.count : Pairs.count + 6
    ]
    own_weight_ref, weight_ref, sum_ref = refs[Pairs.count + 6 :]
    rows = own_image_ref.shape[0]
    second = dot_nt(unit_ref[rows:, :], near_image_ref[pl.ds(rows, rows), :])
    own = dot_nt(unit_ref[rows:, :], own_image_ref[...])
    own_weight_ref[:rows, :] = own_weight_in_ref[...]
    weight_ref[:, :rows] = first_ref[...]
    weight_ref[:rows, rows:] = weight_in_ref[:, rows:]
    pairs.weigh(second, 1, 2, weight_ref, rows, rows)
    sum_ref[...] = dot_tn(weight_ref[:, rows:], unit_ref[...])
    pairs.weigh(own, 1, 0, own_weight_ref, rows, 0)


def far_sum_body(tiles, *refs):
    pairs = Pairs(refs, tiles)
    unit_ref, own_image_ref, own_weight_ref, raw_ref = refs[Pairs.count : Pairs.count + 4]
    sum_ref, weight_ref, image_ref = refs[Pairs.count + 4 :]
    rows = raw_ref.shape[0]
    unit_images([raw_ref], image_ref.at[pl.ds(rows, rows), :])
    products = dot_nt(unit_ref[...], image_ref[rows:, :])
    for half in range(CORES):
        part = products[half * rows : (half + 1) * rows, :]
        pairs.weigh(part, half, 3, weight_ref, half * rows, rows)
    sum_ref[...] = dot_tn(weight_ref[:, rows:], unit_ref[...]).astype(jnp.bfloat16)
    image_ref[:rows, :] = own_image_ref[...]
    weight_ref[:, :rows] = own_weight_ref[...]


def text_sum_body(near_weight_ref, near_image_ref, weight_ref, image_ref, acc_ref, *piece_refs):
    rows = acc_ref.shape[0]
    size = rows // ACC_PIECES
    for part in (slice(rows, 2 * rows), slice(0, rows)):
        acc = jnp.dot(
            near_weight_ref[part, :], near_image_ref[...], preferred_element_type=jnp.float32
        ) + jnp.dot(weight_ref[part, :], image_ref[...], preferred_element_type=jnp.float32)
        if part.start == 0:
            acc_ref[...] = acc
            continue
        for at, ref in enumerate(piece_refs):
            ref[...] = acc[at * size : (at + 1) * size, :].astype(jnp.bfloat16)


def own_sum_body(weight_ref, unit_ref, add_ref, out_ref):
    rows = out_ref.shape[0]
    out_ref[...] = dot_tn(weight_ref[:, :rows], unit_ref[...]) + add_ref[...].astype(jnp.float32)


def all_body(tiles, chips, *refs):
    pairs = Pairs(refs, tiles)
    own_ref, other_ref, piece_ref = refs[Pairs.count : Pairs.count + 3]
    outs = refs[Pairs.count + 3 :]
    spread_ref, acc_ref, acc_piece_refs = outs[0], outs[1], outs[2 : 2 + ACC_PIECES]
    image_ref, weight_ref = outs[2 + ACC_PIECES :]
    rows = own_ref.shape[0]
    unit_images([piece_ref], image_ref)
    for half, text_ref in enumerate((own_ref, other_ref)):
        for chip in range(chips):
            products = dot_nt(text_ref[...], image_ref[pl.ds(chip * rows, rows), :])
            pairs.weigh(
                products, half, chip, weight_ref, half * rows, chip * rows, None if half else "search"
            )
        acc = jnp.dot(
            weight_ref[pl.ds(half * rows, rows), :],
            image_ref[...],
            preferred_element_type=jnp.float32,
        )
        if half == 0:
            acc_ref[...] = acc
            continue
        size = rows // ACC_PIECES
        for at, ref in enumerate(acc_piece_refs):
            ref[...] = acc[at * size : (at + 1) * size, :].astype(jnp.bfloat16)
    for chip in range(chips):
        columns = pl.ds(chip * rows, rows)
        total = dot_tn(weight_ref[pl.ds(0, rows), columns], own_ref[...])
        total += dot_tn(weight_ref[pl.ds(rows, rows), columns], other_ref[...])
        spread_ref[columns, :] = total.astype(jnp.bfloat16)


def relay_body(sum_ref, in_ref, out_ref):
    out_ref[...] = (sum_ref[...] + in_ref[...].astype(jnp.float32)).astype(jnp.bfloat16)


def text_grad_body(chunks, *refs):
    raw_refs, acc_ref, add_refs = refs[:chunks], refs[chunks], refs[chunks + 1 : -chunks]
    out_refs = refs[-chunks:]
    place = lax.axis_index("tp")
    rows, width = raw_refs[0].shape
    size = add_refs[0].shape[0]
    for first in range(0, rows, TILE):
        part = pl.ds(first, TILE)
        raws = [ref[part, :].astype(jnp.float32) for ref in raw_refs]
        scales = row_scales(sum(jnp.sum(x * x, axis=-1, keepdims=True) for x in raws))
        accs = []
        for k in range(chunks):
            features = feature_slice(place, k, width)
            added = add_refs[first // size][pl.ds(first % size, TILE), features]
            accs.append(acc_ref[part, features] + added.astype(jnp.float32))
        units = [x * scales for x in raws]
        inner = sum(jnp.sum(u * a, axis=-1, keepdims=True) for u, a in zip(units, accs))
        for k in range(chunks):
            out_refs[k][part, :] = (scales * (accs[k] - units[k] * inner)).astype(jnp.bfloat16)


def place_text_body(chunks, *refs):
    part_refs, out_ref, sems = refs[:chunks], refs[chunks], refs[chunks + 1]
    place = lax.axis_index("tp")
    rows = part_refs[0].shape[0]
    copies = []
    for k in range(chunks):
        block = pl.ds(pl.multiple_of((place ^ k) * rows, rows), rows)
        copies.append(pltpu.make_async_copy(part_refs[k], out_ref.at[block, :], sems.at[k]))
    for copy in copies:
        copy.start()
    for copy in copies:
        copy.wait()


def image_grad_body(sum_count, raw_ref, *refs):
    sum_refs, (out_ref, grad_ref, sems) = refs[:sum_count], refs[sum_count:]
    copies = []
    for block in range(raw_ref.shape[0] // TILE):
        for first in range(block * TILE, (block + 1) * TILE, TILE // 2):
            part = pl.ds(first, TILE // 2)
            raw = raw_ref[part, :].astype(jnp.float32)
            scales = row_scales(jnp.sum(raw * raw, axis=-1, keepdims=True))
            unit = raw * scales
            acc = sum(ref[part, :].astype(jnp.float32) for ref in sum_refs)
            inner = jnp.sum(unit * acc, axis=-1, keepdims=True)
            grad_ref[part, :] = (scales * (acc - unit * inner)).astype(jnp.bfloat16)
        part = pl.ds(block * TILE, TILE)
        copies.append(
            pltpu.make_async_copy(grad_ref.at[part, :], out_ref.at[part, :], sems.at[block])
        )
        copies[-1].start()
    for copy in copies:
        copy.wait()


def swap(value, axis, bits):
    count = lax.axis_size(axis)
    return lax.ppermute(value, axis, [(i, i ^ bits) for i in range(count)])


def swap_near(value, which):
    count = lax.axis_size("blk")
    return lax.ppermute(value, "blk", [(i, i ^ neighbour_bits(i)[which]) for i in range(count)])


def per_device(text_emb, image_emb, logit_scale, logit_bias, bucket, positive, blocks):
    groups = lax.axis_size("tp")
    shards = lax.axis_size("blk")
    chips = shards // CORES
    rows, embed = image_emb.shape
    tiles = rows // TILE
    width = text_emb.shape[1]
    square = chips == 4

    def bf16(count, columns=embed):
        return struct((count, columns), jnp.bfloat16)

    def f32(count, columns=embed):
        return struct((count, columns), jnp.float32)

    def i32(count, columns):
        return struct((count, columns), jnp.int32)

    picked = call_kernel(pick_body, [bf16(rows, width)] * groups, [text_emb], limit=8)
    picked[-1], image_sent = lax.optimization_barrier((picked[-1], image_emb))
    text_raw = [picked[0]] + [swap(picked[k], "tp", k) for k in range(1, groups)]
    if square:
        from_second = swap_near(image_sent, 1)
        from_first = swap_near(image_sent, 0)
        from_far = swap_near(from_second, 0)
        blocks, from_second = lax.optimization_barrier((blocks, from_second))
    else:
        same_core = [[chip * CORES + core for chip in range(chips)] for core in range(CORES)]
        gathered = lax.all_gather(
            image_emb, "blk", axis=0, tiled=True, axis_index_groups=same_core
        )
    lists = call_kernel(
        functools.partial(list_body, groups, tiles, chips),
        [
            f32(2, TILE),
            f32(CORES * tiles * chips * tiles, TILE),
            i32(chips * tiles, TILE),
            i32(CORES * rows, TILE),
            f32(rows, TILE),
            f32(chips, TILE),
        ],
        [
            logit_scale,
            logit_bias,
            blocks.transpose(2, 1, 0),
            bucket.reshape(-1, TILE),
            positive.reshape(-1, TILE),
        ],
        scalars=3,
        flops=WAIT_FLOPS // 2,
        limit=8,
    )
    if square:
        text_raw[-1], *lists = lax.optimization_barrier((text_raw[-1], *lists))
    text_own, *pieces = call_kernel(
        functools.partial(unit_text_body, groups),
        [bf16(rows)] + [bf16(rows // TEXT_PIECES)] * TEXT_PIECES,
        text_raw,
        limit=8,
    )
    text_other = [swap(piece, "blk", 1) for piece in pieces]
    if square:
        from_first, text_own = lax.optimization_barrier((from_first, text_own))
        own_images, near_images = call_kernel(
            unit_images_body,
            [bf16(rows), bf16(2 * rows)],
            [image_emb, from_first, from_second],
            limit=8,
        )
    unit_flops = 2 * rows * rows * embed

    def finish_text(acc_own, acc_other):
        parts = call_kernel(
            functools.partial(text_grad_body, groups),
            [bf16(rows, width)] * groups,
            text_raw + [acc_own] + [swap(piece, "blk", 1) for piece in acc_other],
            limit=16,
        )
        return [parts[0]] + [swap(parts[k], "tp", k) for k in range(1, groups)]

    def place_text(text_parts):
        return call_kernel(
            functools.partial(place_text_body, groups),
            [bf16(groups * rows, width)],
            text_parts,
            outs_anywhere=True,
            scratch=[pltpu.SemaphoreType.DMA((groups,))],
            flops=WAIT_FLOPS,
            limit=8,
        )[0]

    def finish_image(sums):
        return call_kernel(
            functools.partial(image_grad_body, len(sums)),
            [bf16(rows)],
            [image_emb] + sums,
            outs_anywhere=True,
            scratch=[pltpu.VMEM((rows, embed), jnp.bfloat16), pltpu.SemaphoreType.DMA((tiles,))],
            limit=8,
        )[0]

    if not square:
        columns = gathered.shape[0]
        spread, acc_own, *acc_other = call_kernel(
            functools.partial(all_body, tiles, chips),
            [bf16(columns), f32(rows)] + [bf16(rows // ACC_PIECES)] * ACC_PIECES,
            lists + [text_own, jnp.concatenate(text_other), gathered],
            scratch=[
                pltpu.VMEM((columns, embed), jnp.bfloat16),
                pltpu.VMEM((2 * rows, columns), jnp.bfloat16),
            ],
            flops=6 * chips * unit_flops,
            limit=56,
        )
        text_parts = finish_text(acc_own, acc_other)
        parts = lax.all_to_all(
            spread, "blk", split_axis=0, concat_axis=0, tiled=True, axis_index_groups=same_core
        )
        total = jnp.sum(parts.reshape(-1, rows, embed).astype(jnp.float32), axis=0)
        return (place_text(text_parts), finish_image([total]))

    own_weights, near_weights = call_kernel(
        functools.partial(near_own_body, tiles),
        [bf16(rows, rows), bf16(rows, 2 * rows)],
        lists + [text_own, own_images, near_images],
        limit=16,
    )
    units, first_weights, first_sum = call_kernel(
        functools.partial(first_sum_body, tiles),
        [bf16(2 * rows), bf16(2 * rows, rows), bf16(rows)],
        lists + [text_own, near_images, near_weights] + text_other,
        limit=16,
    )
    image_add = swap_near(first_sum, 0)
    own_weights, near_weights, second_sum = call_kernel(
        functools.partial(second_sum_body, tiles),
        [bf16(2 * rows, rows), bf16(2 * rows, 2 * rows), f32(rows)],
        lists + [units, own_images, near_images, own_weights, near_weights, first_weights],
        limit=16,
    )
    own_weights, from_far = lax.optimization_barrier((own_weights, from_far))
    far_sum, far_weights, far_images = call_kernel(
        functools.partial(far_sum_body, tiles),
        [bf16(rows), bf16(2 * rows, 2 * rows), bf16(2 * rows)],
        lists + [units, own_images, own_weights, from_far],
        limit=16,
    )
    acc_own, *acc_other = call_kernel(
        text_sum_body,
        [f32(rows)] + [bf16(rows // ACC_PIECES)] * ACC_PIECES,
        [near_weights, near_images, far_weights, far_images],
        limit=24,
    )
    text_parts = finish_text(acc_own, acc_other)
    far_weights, text_parts[0] = lax.optimization_barrier((far_weights, text_parts[0]))
    base = call_kernel(
        own_sum_body, [f32(rows)], [far_weights, units, image_add], limit=16
    )[0]
    base, second_sum = lax.optimization_barrier((base, second_sum))
    relayed = call_kernel(
        relay_body, [bf16(rows)], [second_sum, swap_near(far_sum, 0)], limit=8
    )[0]
    image_last = swap_near(relayed, 1)
    text_grad = place_text(text_parts)
    base, _ = lax.optimization_barrier((base, text_grad))
    return (text_grad, finish_image([base, image_last]))


def solution(mesh):
    in_specs = (P("blk", "tp"), P(("blk", "tp"), None), P(), P(), P(), P(), P())
    out_specs = (P("blk", "tp"), P(("blk", "tp"), None))
    return jax.shard_map(
        per_device, mesh=mesh, in_specs=in_specs, out_specs=out_specs, check_vma=False
    )
```

```python
import functools
import math

import jax
import jax.numpy as jnp
from jax import lax
from jax.experimental import pallas as pl
from jax.experimental.pallas import tpu as pltpu
from jax.sharding import PartitionSpec as P

TILE = 128
SLOTS = 3
WAIT_FLOPS = 20_000_000_000
TEXT_PIECES = 2
ACC_PIECES = 3
CORES = 2
EPS = 1e-06
LOG2E = math.log2(math.e)
MIB = 1024 * 1024

VMEM_SPEC = pl.BlockSpec(memory_space=pltpu.VMEM)
ANY_SPEC = pl.BlockSpec(memory_space=pl.ANY)
SMEM_SPEC = pl.BlockSpec(memory_space=pltpu.SMEM)


def call_kernel(
    body,
    outs,
    operands,
    scalars=0,
    anywhere=(),
    outs_anywhere=False,
    scratch=(),
    flops=0,
    limit=24,
):
    moved = sum(x.size * x.dtype.itemsize for x in operands)
    moved += sum(math.prod(o.shape) * o.dtype.itemsize for o in outs)
    specs = [SMEM_SPEC] * scalars + [VMEM_SPEC] * (len(operands) - scalars)
    for at in anywhere:
        specs[at] = ANY_SPEC
    return list(
        pl.pallas_call(
            body,
            out_shape=outs,
            in_specs=specs,
            out_specs=[ANY_SPEC if outs_anywhere else VMEM_SPEC] * len(outs),
            scratch_shapes=list(scratch),
            compiler_params=pltpu.CompilerParams(vmem_limit_bytes=limit * MIB),
            cost_estimate=pl.CostEstimate(flops=flops, bytes_accessed=moved, transcendentals=0),
        )(*operands)
    )


def struct(shape, dtype):
    return jax.ShapeDtypeStruct(shape, dtype)


def row_scales(square_sum):
    return lax.rsqrt(square_sum + EPS)


def column_of(row):
    return jnp.broadcast_to(row, (TILE, TILE)).T


def dot_nt(left, right):
    return lax.dot_general(
        left, right, (((1,), (1,)), ((), ())), preferred_element_type=jnp.float32
    )


def dot_tn(left, right):
    return lax.dot_general(
        left, right, (((0,), (0,)), ((), ())), preferred_element_type=jnp.float32
    )


def feature_slice(place, k, width):
    return pl.ds(pl.multiple_of((place ^ k) * width, width), width)


def pick_body(text_ref, *out_refs):
    place = lax.axis_index("tp")
    rows = out_refs[0].shape[0]
    for k, out_ref in enumerate(out_refs):
        out_ref[...] = text_ref[pl.ds(pl.multiple_of((place ^ k) * rows, rows), rows), :]


def unit_text_body(chunks, *refs):
    chunk_refs, unit_ref, piece_refs = refs[:chunks], refs[chunks], refs[chunks + 1 :]
    place = lax.axis_index("tp")
    rows, width = chunk_refs[0].shape
    for first in range(0, rows, TILE):
        part = pl.ds(first, TILE)
        parts = [ref[part, :].astype(jnp.float32) for ref in chunk_refs]
        scales = row_scales(sum(jnp.sum(x * x, axis=-1, keepdims=True) for x in parts))
        for k, x in enumerate(parts):
            unit_ref[part, feature_slice(place, k, width)] = (x * scales).astype(jnp.bfloat16)
    split_rows(unit_ref, piece_refs)


def split_rows(whole_ref, piece_refs):
    for at, ref in enumerate(piece_refs):
        ref[...] = whole_ref[pl.ds(at * ref.shape[0], ref.shape[0]), :]


def join_rows(piece_refs, whole_ref):
    for at, ref in enumerate(piece_refs):
        whole_ref[pl.ds(at * ref.shape[0], ref.shape[0]), :] = ref[...]


def unit_images(piece_refs, image_ref):
    start = 0
    step = 64
    for ref in piece_refs:
        for first in range(0, ref.shape[0], step):
            values = ref[pl.ds(first, step), :].astype(jnp.float32)
            scales = row_scales(jnp.sum(values * values, axis=-1, keepdims=True))
            image_ref[pl.ds(start + first, step), :] = (values * scales).astype(jnp.bfloat16)
        start += ref.shape[0]


def unit_images_body(raw_ref, out_ref):
    unit_images([raw_ref], out_ref)


def near_images_body(first_ref, second_unit_ref, out_ref):
    rows = first_ref.shape[0]
    unit_images([first_ref], out_ref)
    out_ref[rows:, :] = second_unit_ref[...]


def neighbour_bits(shard):
    core = shard % CORES
    return 2 << core, 4 >> core


def list_body(groups, tiles, chips, *refs):
    scale_ref, bias_ref, blocks_ref, bucket_ref, positive_ref = refs[:5]
    line_ref, amount_ref, column_ref, row_ref, match_ref, own_ref = refs[5:]
    here, place = lax.axis_index("blk"), lax.axis_index("tp")
    scale = scale_ref[0]
    line_ref[pl.ds(0, 1), :] = jnp.full((1, TILE), -scale * LOG2E, jnp.float32)
    line_ref[pl.ds(1, 1), :] = jnp.full((1, TILE), -bias_ref[0] * LOG2E, jnp.float32)
    if chips == 4:
        first, second = neighbour_bits(here)
        shards = [here, here ^ first, here ^ second, here ^ 6]
    else:
        shards = [chip * CORES + here % CORES for chip in range(chips)]
    count = len(shards) * tiles

    def first_tile(shard):
        return (shard * groups + place) * tiles

    for n, shard in enumerate(shards):
        own_ref[pl.ds(n, 1), :] = jnp.full((1, TILE), jnp.where(shard == here, 1.0, 0.0))
        for j in range(tiles):
            column_ref[pl.ds(n * tiles + j, 1), :] = bucket_ref[pl.ds(first_tile(shard) + j, 1), :]
    for at in range(CORES * tiles):
        tile = first_tile(here ^ (at // tiles)) + at % tiles
        row_ref[pl.ds(at * TILE, TILE), :] = column_of(bucket_ref[pl.ds(tile, 1), :])
        if at < tiles:
            ids = lax.broadcasted_iota(jnp.int32, (1, TILE), 1) + tile * TILE
            matched = column_of(positive_ref[pl.ds(tile, 1), :]) == ids
            match_ref[pl.ds(at * TILE, TILE), :] = jnp.where(matched, 1.0, 0.0)
        for n, shard in enumerate(shards):
            entries = [blocks_ref[slot, shard, tile] for slot in range(SLOTS)]
            for j in range(tiles):
                listed = sum(jnp.where(entry == j, 1.0, 0.0) for entry in entries)
                amount_ref[pl.ds(at * count + n * tiles + j, 1), :] = jnp.full(
                    (1, TILE), scale * listed, jnp.float32
                )


class Pairs:
    count = 6

    def __init__(self, refs, tiles):
        self.line_ref, self.amount_ref, self.column_ref = refs[:3]
        self.row_ref, self.match_ref, self.own_ref = refs[3:6]
        self.tiles = tiles

    def weigh(self, products, half, group, weight_ref, top, left, own=None):
        tiles = self.tiles
        slope, offset = self.line_ref[pl.ds(0, 1), :], self.line_ref[pl.ds(1, 1), :]
        count = self.column_ref.shape[0]
        for a in range(tiles):
            at = half * tiles + a
            row_bucket = self.row_ref[pl.ds(at * TILE, TILE), :]
            for j in range(tiles):
                n = group * tiles + j
                amount = self.amount_ref[pl.ds(at * count + n, 1), :]
                power = (
                    products[a * TILE : (a + 1) * TILE, j * TILE : (j + 1) * TILE] * slope + offset
                )
                factor = jnp.where(row_bucket == self.column_ref[pl.ds(n, 1), :], amount, 0.0)
                if own and a == j:
                    match = self.match_ref[pl.ds(a * TILE, TILE), :]
                    if own == "search":
                        match = match * self.own_ref[pl.ds(group, 1), :]
                    power = jnp.where(match > 0.0, -power, power)
                    factor = jnp.where(match > 0.0, -amount, factor)
                below = 1.0 + jnp.exp2(power)
                inverse = pl.reciprocal(below, approx=True)
                inverse = inverse * (2.0 - below * inverse)
                weight_ref[pl.ds(top + a * TILE, TILE), pl.ds(left + j * TILE, TILE)] = (
                    factor * inverse
                ).astype(jnp.bfloat16)


def near_own_body(tiles, *refs):
    pairs = Pairs(refs, tiles)
    unit_ref, own_image_ref, near_image_ref, own_weight_ref, weight_ref = refs[Pairs.count :]
    rows = unit_ref.shape[0]
    first = dot_nt(unit_ref[...], near_image_ref[pl.ds(0, rows), :])
    second = dot_nt(unit_ref[...], near_image_ref[pl.ds(rows, rows), :])
    pairs.weigh(first, 0, 1, weight_ref, 0, 0)
    own = dot_nt(unit_ref[...], own_image_ref[...])
    pairs.weigh(second, 0, 2, weight_ref, 0, rows)
    pairs.weigh(own, 0, 0, own_weight_ref, 0, 0, "diagonal")


def first_sum_body(tiles, *refs):
    pairs = Pairs(refs, tiles)
    own_unit_ref, near_image_ref, weight_in_ref = refs[Pairs.count : Pairs.count + 3]
    piece_refs = refs[Pairs.count + 3 : Pairs.count + 3 + TEXT_PIECES]
    unit_ref, weight_ref, sum_ref = refs[Pairs.count + 3 + TEXT_PIECES :]
    rows = own_unit_ref.shape[0]
    for at, ref in enumerate(piece_refs):
        unit_ref[pl.ds(rows + at * ref.shape[0], ref.shape[0]), :] = ref[...]
    unit_ref[:rows, :] = own_unit_ref[...]
    weight_ref[:rows, :] = weight_in_ref[:, :rows]
    products = dot_nt(unit_ref[rows:, :], near_image_ref[pl.ds(0, rows), :])
    pairs.weigh(products, 1, 1, weight_ref, rows, 0)
    sum_ref[...] = dot_tn(weight_ref[...], unit_ref[...]).astype(jnp.bfloat16)


def second_sum_body(tiles, *refs):
    pairs = Pairs(refs, tiles)
    unit_ref, own_image_ref, near_image_ref, own_weight_in_ref, weight_in_ref, first_ref = refs[
        Pairs.count : Pairs.count + 6
    ]
    own_weight_ref, weight_ref, sum_ref = refs[Pairs.count + 6 :]
    rows = own_image_ref.shape[0]
    second = dot_nt(unit_ref[rows:, :], near_image_ref[pl.ds(rows, rows), :])
    own = dot_nt(unit_ref[rows:, :], own_image_ref[...])
    own_weight_ref[:rows, :] = own_weight_in_ref[...]
    weight_ref[:, :rows] = first_ref[...]
    weight_ref[:rows, rows:] = weight_in_ref[:, rows:]
    pairs.weigh(second, 1, 2, weight_ref, rows, rows)
    sum_ref[...] = dot_tn(weight_ref[:, rows:], unit_ref[...])
    pairs.weigh(own, 1, 0, own_weight_ref, rows, 0)


def far_sum_body(tiles, *refs):
    pairs = Pairs(refs, tiles)
    unit_ref, own_image_ref, own_weight_ref, raw_ref = refs[Pairs.count : Pairs.count + 4]
    sum_ref, weight_ref, image_ref = refs[Pairs.count + 4 :]
    rows = raw_ref.shape[0]
    unit_images([raw_ref], image_ref.at[pl.ds(rows, rows), :])
    products = dot_nt(unit_ref[...], image_ref[rows:, :])
    for half in range(CORES):
        part = products[half * rows : (half + 1) * rows, :]
        pairs.weigh(part, half, 3, weight_ref, half * rows, rows)
    sum_ref[...] = dot_tn(weight_ref[:, rows:], unit_ref[...]).astype(jnp.bfloat16)
    image_ref[:rows, :] = own_image_ref[...]
    weight_ref[:, :rows] = own_weight_ref[...]


def text_sum_body(near_weight_ref, near_image_ref, weight_ref, image_ref, acc_ref, *piece_refs):
    rows = acc_ref.shape[0]
    size = rows // ACC_PIECES
    for part in (slice(rows, 2 * rows), slice(0, rows)):
        acc = jnp.dot(
            near_weight_ref[part, :], near_image_ref[...], preferred_element_type=jnp.float32
        ) + jnp.dot(weight_ref[part, :], image_ref[...], preferred_element_type=jnp.float32)
        if part.start == 0:
            acc_ref[...] = acc
            continue
        for at, ref in enumerate(piece_refs):
            ref[...] = acc[at * size : (at + 1) * size, :].astype(jnp.bfloat16)


def own_sum_body(weight_ref, unit_ref, add_ref, out_ref):
    rows = out_ref.shape[0]
    out_ref[...] = dot_tn(weight_ref[:, :rows], unit_ref[...]) + add_ref[...].astype(jnp.float32)


def all_body(tiles, chips, *refs):
    pairs = Pairs(refs, tiles)
    own_ref, other_ref, piece_ref = refs[Pairs.count : Pairs.count + 3]
    outs = refs[Pairs.count + 3 :]
    spread_ref, acc_ref, acc_piece_refs = outs[0], outs[1], outs[2 : 2 + ACC_PIECES]
    image_ref, weight_ref = outs[2 + ACC_PIECES :]
    rows = own_ref.shape[0]
    unit_images([piece_ref], image_ref)
    for half, text_ref in enumerate((own_ref, other_ref)):
        for chip in range(chips):
            products = dot_nt(text_ref[...], image_ref[pl.ds(chip * rows, rows), :])
            pairs.weigh(
                products, half, chip, weight_ref, half * rows, chip * rows, None if half else "search"
            )
        acc = jnp.dot(
            weight_ref[pl.ds(half * rows, rows), :],
            image_ref[...],
            preferred_element_type=jnp.float32,
        )
        if half == 0:
            acc_ref[...] = acc
            continue
        size = rows // ACC_PIECES
        for at, ref in enumerate(acc_piece_refs):
            ref[...] = acc[at * size : (at + 1) * size, :].astype(jnp.bfloat16)
    for chip in range(chips):
        columns = pl.ds(chip * rows, rows)
        total = dot_tn(weight_ref[pl.ds(0, rows), columns], own_ref[...])
        total += dot_tn(weight_ref[pl.ds(rows, rows), columns], other_ref[...])
        spread_ref[columns, :] = total.astype(jnp.bfloat16)


def relay_body(sum_ref, in_ref, out_ref):
    out_ref[...] = (sum_ref[...] + in_ref[...].astype(jnp.float32)).astype(jnp.bfloat16)


def text_grad_body(chunks, *refs):
    raw_refs, acc_ref, add_refs = refs[:chunks], refs[chunks], refs[chunks + 1 : -chunks]
    out_refs = refs[-chunks:]
    place = lax.axis_index("tp")
    rows, width = raw_refs[0].shape
    size = add_refs[0].shape[0]
    for first in range(0, rows, TILE):
        part = pl.ds(first, TILE)
        raws = [ref[part, :].astype(jnp.float32) for ref in raw_refs]
        scales = row_scales(sum(jnp.sum(x * x, axis=-1, keepdims=True) for x in raws))
        accs = []
        for k in range(chunks):
            features = feature_slice(place, k, width)
            added = add_refs[first // size][pl.ds(first % size, TILE), features]
            accs.append(acc_ref[part, features] + added.astype(jnp.float32))
        units = [x * scales for x in raws]
        inner = sum(jnp.sum(u * a, axis=-1, keepdims=True) for u, a in zip(units, accs))
        for k in range(chunks):
            out_refs[k][part, :] = (scales * (accs[k] - units[k] * inner)).astype(jnp.bfloat16)


def place_text_body(chunks, *refs):
    part_refs, out_ref, sems = refs[:chunks], refs[chunks], refs[chunks + 1]
    place = lax.axis_index("tp")
    rows = part_refs[0].shape[0]
    copies = []
    for k in range(chunks):
        block = pl.ds(pl.multiple_of((place ^ k) * rows, rows), rows)
        copies.append(pltpu.make_async_copy(part_refs[k], out_ref.at[block, :], sems.at[k]))
    for copy in copies:
        copy.start()
    for copy in copies:
        copy.wait()


def image_grad_body(sum_count, raw_ref, *refs):
    sum_refs, (out_ref, grad_ref, sems) = refs[:sum_count], refs[sum_count:]
    copies = []
    for block in range(raw_ref.shape[0] // TILE):
        for first in range(block * TILE, (block + 1) * TILE, TILE // 2):
            part = pl.ds(first, TILE // 2)
            raw = raw_ref[part, :].astype(jnp.float32)
            scales = row_scales(jnp.sum(raw * raw, axis=-1, keepdims=True))
            unit = raw * scales
            acc = sum(ref[part, :].astype(jnp.float32) for ref in sum_refs)
            inner = jnp.sum(unit * acc, axis=-1, keepdims=True)
            grad_ref[part, :] = (scales * (acc - unit * inner)).astype(jnp.bfloat16)
        part = pl.ds(block * TILE, TILE)
        copies.append(
            pltpu.make_async_copy(grad_ref.at[part, :], out_ref.at[part, :], sems.at[block])
        )
        copies[-1].start()
    for copy in copies:
        copy.wait()


def swap(value, axis, bits):
    count = lax.axis_size(axis)
    return lax.ppermute(value, axis, [(i, i ^ bits) for i in range(count)])


def swap_near(value, which):
    count = lax.axis_size("blk")
    return lax.ppermute(value, "blk", [(i, i ^ neighbour_bits(i)[which]) for i in range(count)])


def per_device(text_emb, image_emb, logit_scale, logit_bias, bucket, positive, blocks):
    groups = lax.axis_size("tp")
    shards = lax.axis_size("blk")
    chips = shards // CORES
    rows, embed = image_emb.shape
    tiles = rows // TILE
    width = text_emb.shape[1]
    square = chips == 4

    def bf16(count, columns=embed):
        return struct((count, columns), jnp.bfloat16)

    def f32(count, columns=embed):
        return struct((count, columns), jnp.float32)

    def i32(count, columns):
        return struct((count, columns), jnp.int32)

    picked = call_kernel(pick_body, [bf16(rows, width)] * groups, [text_emb], limit=8)
    picked[-1], image_sent = lax.optimization_barrier((picked[-1], image_emb))
    text_raw = [picked[0]] + [swap(picked[k], "tp", k) for k in range(1, groups)]
    if square:
        from_second = swap_near(image_sent, 1)
        from_first = swap_near(image_sent, 0)
    else:
        same_core = [[chip * CORES + core for chip in range(chips)] for core in range(CORES)]
        gathered = lax.all_gather(
            image_emb, "blk", axis=0, tiled=True, axis_index_groups=same_core
        )
    lists = call_kernel(
        functools.partial(list_body, groups, tiles, chips),
        [
            f32(2, TILE),
            f32(CORES * tiles * chips * tiles, TILE),
            i32(chips * tiles, TILE),
            i32(CORES * rows, TILE),
            f32(rows, TILE),
            f32(chips, TILE),
        ],
        [
            logit_scale,
            logit_bias,
            blocks.transpose(2, 1, 0),
            bucket.reshape(-1, TILE),
            positive.reshape(-1, TILE),
        ],
        scalars=3,
        limit=8,
    )
    if square:
        own_images = call_kernel(unit_images_body, [bf16(rows)], [image_emb], limit=8)[0]
        from_second, own_images, *lists = lax.optimization_barrier(
            (from_second, own_images, *lists)
        )
        from_far = swap_near(from_second, 0)
        second_images = call_kernel(
            unit_images_body, [bf16(rows)], [from_second], flops=WAIT_FLOPS // 2, limit=8
        )[0]
        text_raw[-1], second_images = lax.optimization_barrier((text_raw[-1], second_images))
    text_own, *pieces = call_kernel(
        functools.partial(unit_text_body, groups),
        [bf16(rows)] + [bf16(rows // TEXT_PIECES)] * TEXT_PIECES,
        text_raw,
        limit=8,
    )
    text_other = [swap(piece, "blk", 1) for piece in pieces]
    if square:
        from_first, text_own = lax.optimization_barrier((from_first, text_own))
        near_images = call_kernel(
            near_images_body, [bf16(2 * rows)], [from_first, second_images], limit=8
        )[0]
    unit_flops = 2 * rows * rows * embed

    def finish_text(acc_own, acc_other):
        parts = call_kernel(
            functools.partial(text_grad_body, groups),
            [bf16(rows, width)] * groups,
            text_raw + [acc_own] + [swap(piece, "blk", 1) for piece in acc_other],
            limit=16,
        )
        return [parts[0]] + [swap(parts[k], "tp", k) for k in range(1, groups)]

    def place_text(text_parts):
        return call_kernel(
            functools.partial(place_text_body, groups),
            [bf16(groups * rows, width)],
            text_parts,
            outs_anywhere=True,
            scratch=[pltpu.SemaphoreType.DMA((groups,))],
            flops=WAIT_FLOPS,
            limit=8,
        )[0]

    def finish_image(sums):
        return call_kernel(
            functools.partial(image_grad_body, len(sums)),
            [bf16(rows)],
            [image_emb] + sums,
            outs_anywhere=True,
            scratch=[pltpu.VMEM((rows, embed), jnp.bfloat16), pltpu.SemaphoreType.DMA((tiles,))],
            limit=8,
        )[0]

    if not square:
        columns = gathered.shape[0]
        spread, acc_own, *acc_other = call_kernel(
            functools.partial(all_body, tiles, chips),
            [bf16(columns), f32(rows)] + [bf16(rows // ACC_PIECES)] * ACC_PIECES,
            lists + [text_own, jnp.concatenate(text_other), gathered],
            scratch=[
                pltpu.VMEM((columns, embed), jnp.bfloat16),
                pltpu.VMEM((2 * rows, columns), jnp.bfloat16),
            ],
            flops=6 * chips * unit_flops,
            limit=56,
        )
        text_parts = finish_text(acc_own, acc_other)
        parts = lax.all_to_all(
            spread, "blk", split_axis=0, concat_axis=0, tiled=True, axis_index_groups=same_core
        )
        total = jnp.sum(parts.reshape(-1, rows, embed).astype(jnp.float32), axis=0)
        return (place_text(text_parts), finish_image([total]))

    own_weights, near_weights = call_kernel(
        functools.partial(near_own_body, tiles),
        [bf16(rows, rows), bf16(rows, 2 * rows)],
        lists + [text_own, own_images, near_images],
        limit=16,
    )
    units, first_weights, first_sum = call_kernel(
        functools.partial(first_sum_body, tiles),
        [bf16(2 * rows), bf16(2 * rows, rows), bf16(rows)],
        lists + [text_own, near_images, near_weights] + text_other,
        limit=16,
    )
    image_add = swap_near(first_sum, 0)
    own_weights, near_weights, second_sum = call_kernel(
        functools.partial(second_sum_body, tiles),
        [bf16(2 * rows, rows), bf16(2 * rows, 2 * rows), f32(rows)],
        lists + [units, own_images, near_images, own_weights, near_weights, first_weights],
        limit=16,
    )
    own_weights, from_far = lax.optimization_barrier((own_weights, from_far))
    far_sum, far_weights, far_images = call_kernel(
        functools.partial(far_sum_body, tiles),
        [bf16(rows), bf16(2 * rows, 2 * rows), bf16(2 * rows)],
        lists + [units, own_images, own_weights, from_far],
        limit=16,
    )
    acc_own, *acc_other = call_kernel(
        text_sum_body,
        [f32(rows)] + [bf16(rows // ACC_PIECES)] * ACC_PIECES,
        [near_weights, near_images, far_weights, far_images],
        limit=24,
    )
    text_parts = finish_text(acc_own, acc_other)
    far_weights, text_parts[0] = lax.optimization_barrier((far_weights, text_parts[0]))
    base = call_kernel(
        own_sum_body, [f32(rows)], [far_weights, units, image_add], limit=16
    )[0]
    base, second_sum = lax.optimization_barrier((base, second_sum))
    relayed = call_kernel(
        relay_body, [bf16(rows)], [second_sum, swap_near(far_sum, 0)], limit=8
    )[0]
    image_last = swap_near(relayed, 1)
    text_grad = place_text(text_parts)
    base, _ = lax.optimization_barrier((base, text_grad))
    return (text_grad, finish_image([base, image_last]))


def solution(mesh):
    in_specs = (P("blk", "tp"), P(("blk", "tp"), None), P(), P(), P(), P(), P())
    out_specs = (P("blk", "tp"), P(("blk", "tp"), None))
    return jax.shard_map(
        per_device, mesh=mesh, in_specs=in_specs, out_specs=out_specs, check_vma=False
    )
```

```python
import functools
import math

import jax
import jax.numpy as jnp
from jax import lax
from jax.experimental import pallas as pl
from jax.experimental.pallas import tpu as pltpu
from jax.sharding import PartitionSpec as P

TILE = 128
SLOTS = 3
WAIT_FLOPS = 20_000_000_000
TEXT_PIECES = 2
ACC_PIECES = 3
CORES = 2
EPS = 1e-06
LOG2E = math.log2(math.e)
MIB = 1024 * 1024

VMEM_SPEC = pl.BlockSpec(memory_space=pltpu.VMEM)
ANY_SPEC = pl.BlockSpec(memory_space=pl.ANY)
SMEM_SPEC = pl.BlockSpec(memory_space=pltpu.SMEM)


def call_kernel(
    body,
    outs,
    operands,
    scalars=0,
    anywhere=(),
    outs_anywhere=False,
    scratch=(),
    flops=0,
    limit=24,
):
    moved = sum(x.size * x.dtype.itemsize for x in operands)
    moved += sum(math.prod(o.shape) * o.dtype.itemsize for o in outs)
    specs = [SMEM_SPEC] * scalars + [VMEM_SPEC] * (len(operands) - scalars)
    for at in anywhere:
        specs[at] = ANY_SPEC
    return list(
        pl.pallas_call(
            body,
            out_shape=outs,
            in_specs=specs,
            out_specs=[ANY_SPEC if outs_anywhere else VMEM_SPEC] * len(outs),
            scratch_shapes=list(scratch),
            compiler_params=pltpu.CompilerParams(vmem_limit_bytes=limit * MIB),
            cost_estimate=pl.CostEstimate(flops=flops, bytes_accessed=moved, transcendentals=0),
        )(*operands)
    )


def struct(shape, dtype):
    return jax.ShapeDtypeStruct(shape, dtype)


def row_scales(square_sum):
    return lax.rsqrt(square_sum + EPS)


def column_of(row):
    return jnp.broadcast_to(row, (TILE, TILE)).T


def dot_nt(left, right):
    return lax.dot_general(
        left, right, (((1,), (1,)), ((), ())), preferred_element_type=jnp.float32
    )


def dot_tn(left, right):
    return lax.dot_general(
        left, right, (((0,), (0,)), ((), ())), preferred_element_type=jnp.float32
    )


def feature_slice(place, k, width):
    return pl.ds(pl.multiple_of((place ^ k) * width, width), width)


def pick_body(text_ref, *out_refs):
    place = lax.axis_index("tp")
    rows = out_refs[0].shape[0]
    for k, out_ref in enumerate(out_refs):
        out_ref[...] = text_ref[pl.ds(pl.multiple_of((place ^ k) * rows, rows), rows), :]


def unit_text_body(chunks, *refs):
    chunk_refs, unit_ref, piece_refs = refs[:chunks], refs[chunks], refs[chunks + 1 :]
    place = lax.axis_index("tp")
    rows, width = chunk_refs[0].shape
    for first in range(0, rows, TILE):
        part = pl.ds(first, TILE)
        parts = [ref[part, :].astype(jnp.float32) for ref in chunk_refs]
        scales = row_scales(sum(jnp.sum(x * x, axis=-1, keepdims=True) for x in parts))
        for k, x in enumerate(parts):
            unit_ref[part, feature_slice(place, k, width)] = (x * scales).astype(jnp.bfloat16)
    split_rows(unit_ref, piece_refs)


def split_rows(whole_ref, piece_refs):
    for at, ref in enumerate(piece_refs):
        ref[...] = whole_ref[pl.ds(at * ref.shape[0], ref.shape[0]), :]


def join_rows(piece_refs, whole_ref):
    for at, ref in enumerate(piece_refs):
        whole_ref[pl.ds(at * ref.shape[0], ref.shape[0]), :] = ref[...]


def unit_images(piece_refs, image_ref):
    start = 0
    step = 64
    for ref in piece_refs:
        for first in range(0, ref.shape[0], step):
            values = ref[pl.ds(first, step), :].astype(jnp.float32)
            scales = row_scales(jnp.sum(values * values, axis=-1, keepdims=True))
            image_ref[pl.ds(start + first, step), :] = (values * scales).astype(jnp.bfloat16)
        start += ref.shape[0]


def unit_images_body(raw_ref, out_ref):
    unit_images([raw_ref], out_ref)


def own_images_body(raw_ref, out_ref, raw_out_ref):
    unit_images([raw_ref], out_ref)
    raw_out_ref[...] = raw_ref[...]


def near_images_body(first_ref, second_unit_ref, out_ref):
    rows = first_ref.shape[0]
    unit_images([first_ref], out_ref)
    out_ref[rows:, :] = second_unit_ref[...]


def neighbour_bits(shard):
    core = shard % CORES
    return 2 << core, 4 >> core


def list_body(groups, tiles, chips, *refs):
    scale_ref, bias_ref, blocks_ref, bucket_ref, positive_ref = refs[:5]
    line_ref, amount_ref, column_ref, row_ref, match_ref, own_ref = refs[5:]
    here, place = lax.axis_index("blk"), lax.axis_index("tp")
    scale = scale_ref[0]
    line_ref[pl.ds(0, 1), :] = jnp.full((1, TILE), -scale * LOG2E, jnp.float32)
    line_ref[pl.ds(1, 1), :] = jnp.full((1, TILE), -bias_ref[0] * LOG2E, jnp.float32)
    if chips == 4:
        first, second = neighbour_bits(here)
        shards = [here, here ^ first, here ^ second, here ^ 6]
    else:
        shards = [chip * CORES + here % CORES for chip in range(chips)]
    count = len(shards) * tiles

    def first_tile(shard):
        return (shard * groups + place) * tiles

    for n, shard in enumerate(shards):
        own_ref[pl.ds(n, 1), :] = jnp.full((1, TILE), jnp.where(shard == here, 1.0, 0.0))
        for j in range(tiles):
            column_ref[pl.ds(n * tiles + j, 1), :] = bucket_ref[pl.ds(first_tile(shard) + j, 1), :]
    for at in range(CORES * tiles):
        tile = first_tile(here ^ (at // tiles)) + at % tiles
        row_ref[pl.ds(at * TILE, TILE), :] = column_of(bucket_ref[pl.ds(tile, 1), :])
        if at < tiles:
            ids = lax.broadcasted_iota(jnp.int32, (1, TILE), 1) + tile * TILE
            matched = column_of(positive_ref[pl.ds(tile, 1), :]) == ids
            match_ref[pl.ds(at * TILE, TILE), :] = jnp.where(matched, 1.0, 0.0)
        for n, shard in enumerate(shards):
            entries = [blocks_ref[slot, shard, tile] for slot in range(SLOTS)]
            for j in range(tiles):
                listed = sum(jnp.where(entry == j, 1.0, 0.0) for entry in entries)
                amount_ref[pl.ds(at * count + n * tiles + j, 1), :] = jnp.full(
                    (1, TILE), scale * listed, jnp.float32
                )


class Pairs:
    count = 6

    def __init__(self, refs, tiles):
        self.line_ref, self.amount_ref, self.column_ref = refs[:3]
        self.row_ref, self.match_ref, self.own_ref = refs[3:6]
        self.tiles = tiles

    def weigh(self, products, half, group, weight_ref, top, left, own=None):
        tiles = self.tiles
        slope, offset = self.line_ref[pl.ds(0, 1), :], self.line_ref[pl.ds(1, 1), :]
        count = self.column_ref.shape[0]
        for a in range(tiles):
            at = half * tiles + a
            row_bucket = self.row_ref[pl.ds(at * TILE, TILE), :]
            for j in range(tiles):
                n = group * tiles + j
                amount = self.amount_ref[pl.ds(at * count + n, 1), :]
                power = (
                    products[a * TILE : (a + 1) * TILE, j * TILE : (j + 1) * TILE] * slope + offset
                )
                factor = jnp.where(row_bucket == self.column_ref[pl.ds(n, 1), :], amount, 0.0)
                if own and a == j:
                    match = self.match_ref[pl.ds(a * TILE, TILE), :]
                    if own == "search":
                        match = match * self.own_ref[pl.ds(group, 1), :]
                    power = jnp.where(match > 0.0, -power, power)
                    factor = jnp.where(match > 0.0, -amount, factor)
                below = 1.0 + jnp.exp2(power)
                inverse = pl.reciprocal(below, approx=True)
                inverse = inverse * (2.0 - below * inverse)
                weight_ref[pl.ds(top + a * TILE, TILE), pl.ds(left + j * TILE, TILE)] = (
                    factor * inverse
                ).astype(jnp.bfloat16)


def near_own_body(tiles, *refs):
    pairs = Pairs(refs, tiles)
    unit_ref, own_image_ref, near_image_ref, own_weight_ref, weight_ref = refs[Pairs.count :]
    rows = unit_ref.shape[0]
    first = dot_nt(unit_ref[...], near_image_ref[pl.ds(0, rows), :])
    second = dot_nt(unit_ref[...], near_image_ref[pl.ds(rows, rows), :])
    pairs.weigh(first, 0, 1, weight_ref, 0, 0)
    own = dot_nt(unit_ref[...], own_image_ref[...])
    pairs.weigh(second, 0, 2, weight_ref, 0, rows)
    pairs.weigh(own, 0, 0, own_weight_ref, 0, 0, "diagonal")


def first_sum_body(tiles, *refs):
    pairs = Pairs(refs, tiles)
    own_unit_ref, near_image_ref, weight_in_ref = refs[Pairs.count : Pairs.count + 3]
    piece_refs = refs[Pairs.count + 3 : Pairs.count + 3 + TEXT_PIECES]
    unit_ref, weight_ref, sum_ref = refs[Pairs.count + 3 + TEXT_PIECES :]
    rows = own_unit_ref.shape[0]
    for at, ref in enumerate(piece_refs):
        unit_ref[pl.ds(rows + at * ref.shape[0], ref.shape[0]), :] = ref[...]
    unit_ref[:rows, :] = own_unit_ref[...]
    weight_ref[:rows, :] = weight_in_ref[:, :rows]
    products = dot_nt(unit_ref[rows:, :], near_image_ref[pl.ds(0, rows), :])
    pairs.weigh(products, 1, 1, weight_ref, rows, 0)
    sum_ref[...] = dot_tn(weight_ref[...], unit_ref[...]).astype(jnp.bfloat16)


def second_sum_body(tiles, *refs):
    pairs = Pairs(refs, tiles)
    unit_ref, own_image_ref, near_image_ref, own_weight_in_ref, weight_in_ref, first_ref = refs[
        Pairs.count : Pairs.count + 6
    ]
    own_weight_ref, acc_ref, sum_ref, weight_ref = refs[Pairs.count + 6 :]
    rows = own_image_ref.shape[0]
    second = dot_nt(unit_ref[rows:, :], near_image_ref[pl.ds(rows, rows), :])
    own = dot_nt(unit_ref[rows:, :], own_image_ref[...])
    own_weight_ref[:rows, :] = own_weight_in_ref[...]
    weight_ref[:, :rows] = first_ref[...]
    weight_ref[:rows, rows:] = weight_in_ref[:, rows:]
    pairs.weigh(second, 1, 2, weight_ref, rows, rows)
    sum_ref[...] = dot_tn(weight_ref[:, rows:], unit_ref[...])
    pairs.weigh(own, 1, 0, own_weight_ref, rows, 0)
    acc_ref[...] = jnp.dot(
        weight_ref[...], near_image_ref[...], preferred_element_type=jnp.float32
    )


def far_sum_body(tiles, *refs):
    pairs = Pairs(refs, tiles)
    unit_ref, own_image_ref, own_weight_ref, raw_ref = refs[Pairs.count : Pairs.count + 4]
    sum_ref, weight_ref, image_ref = refs[Pairs.count + 4 :]
    rows = raw_ref.shape[0]
    unit_images([raw_ref], image_ref.at[pl.ds(rows, rows), :])
    products = dot_nt(unit_ref[...], image_ref[rows:, :])
    for half in range(CORES):
        part = products[half * rows : (half + 1) * rows, :]
        pairs.weigh(part, half, 3, weight_ref, half * rows, rows)
    sum_ref[...] = dot_tn(weight_ref[:, rows:], unit_ref[...]).astype(jnp.bfloat16)
    image_ref[:rows, :] = own_image_ref[...]
    weight_ref[:, :rows] = own_weight_ref[...]


def text_sum_body(half, weight_ref, image_ref, acc_ref, *out_refs):
    rows = weight_ref.shape[0] // CORES
    size = out_refs[0].shape[0]
    part = pl.ds(half * rows, rows)
    acc = acc_ref[part, :] + jnp.dot(
        weight_ref[part, :], image_ref[...], preferred_element_type=jnp.float32
    )
    for at, ref in enumerate(out_refs):
        ref[...] = acc[at * size : (at + 1) * size, :].astype(ref.dtype)


def own_sum_body(weight_ref, unit_ref, add_ref, out_ref):
    rows = out_ref.shape[0]
    out_ref[...] = dot_tn(weight_ref[:, :rows], unit_ref[...]) + add_ref[...].astype(jnp.float32)


def all_body(tiles, chips, *refs):
    pairs = Pairs(refs, tiles)
    own_ref, other_ref, piece_ref = refs[Pairs.count : Pairs.count + 3]
    outs = refs[Pairs.count + 3 :]
    spread_ref, acc_ref, acc_piece_refs = outs[0], outs[1], outs[2 : 2 + ACC_PIECES]
    image_ref, weight_ref = outs[2 + ACC_PIECES :]
    rows = own_ref.shape[0]
    unit_images([piece_ref], image_ref)
    for half, text_ref in enumerate((own_ref, other_ref)):
        for chip in range(chips):
            products = dot_nt(text_ref[...], image_ref[pl.ds(chip * rows, rows), :])
            pairs.weigh(
                products, half, chip, weight_ref, half * rows, chip * rows, None if half else "search"
            )
        acc = jnp.dot(
            weight_ref[pl.ds(half * rows, rows), :],
            image_ref[...],
            preferred_element_type=jnp.float32,
        )
        if half == 0:
            acc_ref[...] = acc
            continue
        size = rows // ACC_PIECES
        for at, ref in enumerate(acc_piece_refs):
            ref[...] = acc[at * size : (at + 1) * size, :].astype(jnp.bfloat16)
    for chip in range(chips):
        columns = pl.ds(chip * rows, rows)
        total = dot_tn(weight_ref[pl.ds(0, rows), columns], own_ref[...])
        total += dot_tn(weight_ref[pl.ds(rows, rows), columns], other_ref[...])
        spread_ref[columns, :] = total.astype(jnp.bfloat16)


def relay_body(sum_ref, in_ref, out_ref):
    out_ref[...] = (sum_ref[...] + in_ref[...].astype(jnp.float32)).astype(jnp.bfloat16)


def text_grad_body(chunks, *refs):
    raw_refs, acc_ref, add_refs = refs[:chunks], refs[chunks], refs[chunks + 1 : -chunks]
    out_refs = refs[-chunks:]
    place = lax.axis_index("tp")
    rows, width = raw_refs[0].shape
    size = add_refs[0].shape[0]
    for first in range(0, rows, TILE):
        part = pl.ds(first, TILE)
        raws = [ref[part, :].astype(jnp.float32) for ref in raw_refs]
        scales = row_scales(sum(jnp.sum(x * x, axis=-1, keepdims=True) for x in raws))
        accs = []
        for k in range(chunks):
            features = feature_slice(place, k, width)
            added = add_refs[first // size][pl.ds(first % size, TILE), features]
            accs.append(acc_ref[part, features] + added.astype(jnp.float32))
        units = [x * scales for x in raws]
        inner = sum(jnp.sum(u * a, axis=-1, keepdims=True) for u, a in zip(units, accs))
        for k in range(chunks):
            out_refs[k][part, :] = (scales * (accs[k] - units[k] * inner)).astype(jnp.bfloat16)


def place_text_body(chunks, *refs):
    part_refs, out_ref, sems = refs[:chunks], refs[chunks], refs[chunks + 1]
    place = lax.axis_index("tp")
    rows = part_refs[0].shape[0]
    copies = []
    for k in range(chunks):
        block = pl.ds(pl.multiple_of((place ^ k) * rows, rows), rows)
        copies.append(pltpu.make_async_copy(part_refs[k], out_ref.at[block, :], sems.at[k]))
    for copy in copies:
        copy.start()
    for copy in copies:
        copy.wait()


def image_grad_body(sum_count, raw_ref, *refs):
    sum_refs, (out_ref, grad_ref, sems) = refs[:sum_count], refs[sum_count:]
    copies = []
    for block in range(raw_ref.shape[0] // TILE):
        for first in range(block * TILE, (block + 1) * TILE, TILE // 2):
            part = pl.ds(first, TILE // 2)
            raw = raw_ref[part, :].astype(jnp.float32)
            scales = row_scales(jnp.sum(raw * raw, axis=-1, keepdims=True))
            unit = raw * scales
            acc = sum(ref[part, :].astype(jnp.float32) for ref in sum_refs)
            inner = jnp.sum(unit * acc, axis=-1, keepdims=True)
            grad_ref[part, :] = (scales * (acc - unit * inner)).astype(jnp.bfloat16)
        part = pl.ds(block * TILE, TILE)
        copies.append(
            pltpu.make_async_copy(grad_ref.at[part, :], out_ref.at[part, :], sems.at[block])
        )
        copies[-1].start()
    for copy in copies:
        copy.wait()


def swap(value, axis, bits):
    count = lax.axis_size(axis)
    return lax.ppermute(value, axis, [(i, i ^ bits) for i in range(count)])


def swap_near(value, which):
    count = lax.axis_size("blk")
    return lax.ppermute(value, "blk", [(i, i ^ neighbour_bits(i)[which]) for i in range(count)])


def per_device(text_emb, image_emb, logit_scale, logit_bias, bucket, positive, blocks):
    groups = lax.axis_size("tp")
    shards = lax.axis_size("blk")
    chips = shards // CORES
    rows, embed = image_emb.shape
    tiles = rows // TILE
    width = text_emb.shape[1]
    square = chips == 4

    def bf16(count, columns=embed):
        return struct((count, columns), jnp.bfloat16)

    def f32(count, columns=embed):
        return struct((count, columns), jnp.float32)

    def i32(count, columns):
        return struct((count, columns), jnp.int32)

    picked = call_kernel(pick_body, [bf16(rows, width)] * groups, [text_emb], limit=8)
    picked[-1], image_sent = lax.optimization_barrier((picked[-1], image_emb))
    text_raw = [picked[0]] + [swap(picked[k], "tp", k) for k in range(1, groups)]
    if square:
        from_second = swap_near(image_sent, 1)
    else:
        same_core = [[chip * CORES + core for chip in range(chips)] for core in range(CORES)]
        gathered = lax.all_gather(
            image_emb, "blk", axis=0, tiled=True, axis_index_groups=same_core
        )
    lists = call_kernel(
        functools.partial(list_body, groups, tiles, chips),
        [
            f32(2, TILE),
            f32(CORES * tiles * chips * tiles, TILE),
            i32(chips * tiles, TILE),
            i32(CORES * rows, TILE),
            f32(rows, TILE),
            f32(chips, TILE),
        ],
        [
            logit_scale,
            logit_bias,
            blocks.transpose(2, 1, 0),
            bucket.reshape(-1, TILE),
            positive.reshape(-1, TILE),
        ],
        scalars=3,
        limit=8,
    )
    if square:
        own_images, image_emb = call_kernel(
            own_images_body, [bf16(rows)] * 2, [image_emb], limit=8
        )
        image_sent, own_images = lax.optimization_barrier((image_sent, own_images))
        from_first = swap_near(image_sent, 0)
        from_second, own_images, *lists = lax.optimization_barrier(
            (from_second, own_images, *lists)
        )
        from_far = swap_near(from_second, 0)
        second_images = call_kernel(
            unit_images_body, [bf16(rows)], [from_second], flops=WAIT_FLOPS // 2, limit=8
        )[0]
        text_raw[-1], second_images = lax.optimization_barrier((text_raw[-1], second_images))
    text_own, *pieces = call_kernel(
        functools.partial(unit_text_body, groups),
        [bf16(rows)] + [bf16(rows // TEXT_PIECES)] * TEXT_PIECES,
        text_raw,
        limit=8,
    )
    text_other = [swap(piece, "blk", 1) for piece in pieces]
    if square:
        from_first, text_own = lax.optimization_barrier((from_first, text_own))
        near_images = call_kernel(
            near_images_body, [bf16(2 * rows)], [from_first, second_images], limit=8
        )[0]
    unit_flops = 2 * rows * rows * embed

    def finish_text(acc_own, acc_other):
        parts = call_kernel(
            functools.partial(text_grad_body, groups),
            [bf16(rows, width)] * groups,
            text_raw + [acc_own] + [swap(piece, "blk", 1) for piece in acc_other],
            limit=16,
        )
        return [parts[0]] + [swap(parts[k], "tp", k) for k in range(1, groups)]

    def place_text(text_parts):
        return call_kernel(
            functools.partial(place_text_body, groups),
            [bf16(groups * rows, width)],
            text_parts,
            outs_anywhere=True,
            scratch=[pltpu.SemaphoreType.DMA((groups,))],
            flops=WAIT_FLOPS,
            limit=8,
        )[0]

    def finish_image(sums):
        return call_kernel(
            functools.partial(image_grad_body, len(sums)),
            [bf16(rows)],
            [image_emb] + sums,
            outs_anywhere=True,
            scratch=[pltpu.VMEM((rows, embed), jnp.bfloat16), pltpu.SemaphoreType.DMA((tiles,))],
            limit=8,
        )[0]

    if not square:
        columns = gathered.shape[0]
        spread, acc_own, *acc_other = call_kernel(
            functools.partial(all_body, tiles, chips),
            [bf16(columns), f32(rows)] + [bf16(rows // ACC_PIECES)] * ACC_PIECES,
            lists + [text_own, jnp.concatenate(text_other), gathered],
            scratch=[
                pltpu.VMEM((columns, embed), jnp.bfloat16),
                pltpu.VMEM((2 * rows, columns), jnp.bfloat16),
            ],
            flops=6 * chips * unit_flops,
            limit=56,
        )
        text_parts = finish_text(acc_own, acc_other)
        parts = lax.all_to_all(
            spread, "blk", split_axis=0, concat_axis=0, tiled=True, axis_index_groups=same_core
        )
        total = jnp.sum(parts.reshape(-1, rows, embed).astype(jnp.float32), axis=0)
        return (place_text(text_parts), finish_image([total]))

    own_weights, near_weights = call_kernel(
        functools.partial(near_own_body, tiles),
        [bf16(rows, rows), bf16(rows, 2 * rows)],
        lists + [text_own, own_images, near_images],
        limit=16,
    )
    units, first_weights, first_sum = call_kernel(
        functools.partial(first_sum_body, tiles),
        [bf16(2 * rows), bf16(2 * rows, rows), bf16(rows)],
        lists + [text_own, near_images, near_weights] + text_other,
        limit=16,
    )
    image_add = swap_near(first_sum, 0)
    own_weights, acc, second_sum = call_kernel(
        functools.partial(second_sum_body, tiles),
        [bf16(2 * rows, rows), f32(2 * rows), f32(rows)],
        lists + [units, own_images, near_images, own_weights, near_weights, first_weights],
        scratch=[pltpu.VMEM((2 * rows, 2 * rows), jnp.bfloat16)],
        limit=24,
    )
    own_weights, from_far = lax.optimization_barrier((own_weights, from_far))
    far_sum, far_weights, far_images = call_kernel(
        functools.partial(far_sum_body, tiles),
        [bf16(rows), bf16(2 * rows, 2 * rows), bf16(2 * rows)],
        lists + [units, own_images, own_weights, from_far],
        limit=16,
    )
    acc_other = call_kernel(
        functools.partial(text_sum_body, 1),
        [bf16(rows // ACC_PIECES)] * ACC_PIECES,
        [far_weights, far_images, acc],
        limit=16,
    )
    far_images, acc_other[0] = lax.optimization_barrier((far_images, acc_other[0]))
    acc_own = call_kernel(
        functools.partial(text_sum_body, 0),
        [f32(rows)],
        [far_weights, far_images, acc],
        limit=16,
    )[0]
    text_parts = finish_text(acc_own, acc_other)
    far_weights, text_parts[0] = lax.optimization_barrier((far_weights, text_parts[0]))
    base = call_kernel(
        own_sum_body, [f32(rows)], [far_weights, units, image_add], limit=16
    )[0]
    base, second_sum = lax.optimization_barrier((base, second_sum))
    relayed = call_kernel(
        relay_body, [bf16(rows)], [second_sum, swap_near(far_sum, 0)], limit=8
    )[0]
    image_last = swap_near(relayed, 1)
    text_grad = place_text(text_parts)
    base, _ = lax.optimization_barrier((base, text_grad))
    return (text_grad, finish_image([base, image_last]))


def solution(mesh):
    in_specs = (P("blk", "tp"), P(("blk", "tp"), None), P(), P(), P(), P(), P())
    out_specs = (P("blk", "tp"), P(("blk", "tp"), None))
    return jax.shard_map(
        per_device, mesh=mesh, in_specs=in_specs, out_specs=out_specs, check_vma=False
    )
```

```python
import functools
import math

import jax
import jax.numpy as jnp
from jax import lax
from jax.experimental import pallas as pl
from jax.experimental.pallas import tpu as pltpu
from jax.sharding import PartitionSpec as P

TILE = 128
SLOTS = 3
WAIT_FLOPS = 20_000_000_000
TEXT_PIECES = 3
ACC_PIECES = 3
LAST_PIECES = 2
CORES = 2
EPS = 1e-06
LOG2E = math.log2(math.e)
MIB = 1024 * 1024

VMEM_SPEC = pl.BlockSpec(memory_space=pltpu.VMEM)
ANY_SPEC = pl.BlockSpec(memory_space=pl.ANY)
SMEM_SPEC = pl.BlockSpec(memory_space=pltpu.SMEM)


def call_kernel(
    body,
    outs,
    operands,
    scalars=0,
    anywhere=(),
    outs_anywhere=False,
    scratch=(),
    flops=0,
    moved=None,
    limit=24,
):
    if moved is None:
        moved = sum(x.size * x.dtype.itemsize for x in operands)
        moved += sum(math.prod(o.shape) * o.dtype.itemsize for o in outs)
    specs = [SMEM_SPEC] * scalars + [VMEM_SPEC] * (len(operands) - scalars)
    for at in anywhere:
        specs[at] = ANY_SPEC
    return list(
        pl.pallas_call(
            body,
            out_shape=outs,
            in_specs=specs,
            out_specs=[ANY_SPEC if outs_anywhere else VMEM_SPEC] * len(outs),
            scratch_shapes=list(scratch),
            compiler_params=pltpu.CompilerParams(vmem_limit_bytes=limit * MIB),
            cost_estimate=pl.CostEstimate(flops=flops, bytes_accessed=moved, transcendentals=0),
        )(*operands)
    )


def struct(shape, dtype):
    return jax.ShapeDtypeStruct(shape, dtype)


def row_scales(square_sum):
    return lax.rsqrt(square_sum + EPS)


def column_of(row):
    return jnp.broadcast_to(row, (TILE, TILE)).T


def dot_nt(left, right):
    return lax.dot_general(
        left, right, (((1,), (1,)), ((), ())), preferred_element_type=jnp.float32
    )


def dot_tn(left, right):
    return lax.dot_general(
        left, right, (((0,), (0,)), ((), ())), preferred_element_type=jnp.float32
    )


def feature_slice(place, k, width):
    return pl.ds(pl.multiple_of((place ^ k) * width, width), width)


def pick_body(text_ref, *out_refs):
    place = lax.axis_index("tp")
    rows = out_refs[0].shape[0]
    for k, out_ref in enumerate(out_refs):
        out_ref[...] = text_ref[pl.ds(pl.multiple_of((place ^ k) * rows, rows), rows), :]


def unit_text_body(chunks, *refs):
    chunk_refs, (unit_ref, scale_ref) = refs[:chunks], refs[chunks : chunks + 2]
    piece_refs = refs[chunks + 2 :]
    place = lax.axis_index("tp")
    rows, width = chunk_refs[0].shape
    for first in range(0, rows, TILE):
        part = pl.ds(first, TILE)
        parts = [ref[part, :].astype(jnp.float32) for ref in chunk_refs]
        scales = row_scales(sum(jnp.sum(x * x, axis=-1, keepdims=True) for x in parts))
        scale_ref[part, :] = jnp.broadcast_to(scales, (TILE, TILE))
        for k, x in enumerate(parts):
            unit_ref[part, feature_slice(place, k, width)] = (x * scales).astype(jnp.bfloat16)
    split_rows(unit_ref, piece_refs)


def split_rows(whole_ref, piece_refs):
    for at, ref in enumerate(piece_refs):
        ref[...] = whole_ref[pl.ds(at * ref.shape[0], ref.shape[0]), :]


def join_rows(piece_refs, whole_ref):
    for at, ref in enumerate(piece_refs):
        whole_ref[pl.ds(at * ref.shape[0], ref.shape[0]), :] = ref[...]


def unit_images(ref, image_ref, scale_ref=None):
    step = 64
    for first in range(0, ref.shape[0], step):
        part = pl.ds(first, step)
        values = ref[part, :].astype(jnp.float32)
        scales = row_scales(jnp.sum(values * values, axis=-1, keepdims=True))
        image_ref[part, :] = (values * scales).astype(jnp.bfloat16)
        if scale_ref is not None:
            scale_ref[part, :] = jnp.broadcast_to(scales, (step, TILE))


def unit_images_body(raw_ref, out_ref):
    unit_images(raw_ref, out_ref)


def own_images_body(raw_ref, out_ref, raw_out_ref, scale_ref):
    unit_images(raw_ref, out_ref, scale_ref)
    raw_out_ref[...] = raw_ref[...]


def near_images_body(first_ref, second_unit_ref, out_ref):
    rows = first_ref.shape[0]
    unit_images(first_ref, out_ref)
    out_ref[rows:, :] = second_unit_ref[...]


def neighbour_bits(shard):
    core = shard % CORES
    return 2 << core, 4 >> core


def list_body(groups, tiles, chips, *refs):
    scale_ref, bias_ref, blocks_ref, bucket_ref, positive_ref = refs[:5]
    line_ref, amount_ref, column_ref, row_ref, match_ref, own_ref = refs[5:]
    here, place = lax.axis_index("blk"), lax.axis_index("tp")
    scale = scale_ref[0]
    line_ref[pl.ds(0, 1), :] = jnp.full((1, TILE), -scale * LOG2E, jnp.float32)
    line_ref[pl.ds(1, 1), :] = jnp.full((1, TILE), -bias_ref[0] * LOG2E, jnp.float32)
    if chips == 4:
        first, second = neighbour_bits(here)
        shards = [here, here ^ first, here ^ second, here ^ 6]
    else:
        shards = [chip * CORES + here % CORES for chip in range(chips)]
    count = len(shards) * tiles

    def first_tile(shard):
        return (shard * groups + place) * tiles

    for n, shard in enumerate(shards):
        own_ref[pl.ds(n, 1), :] = jnp.full((1, TILE), jnp.where(shard == here, 1.0, 0.0))
        for j in range(tiles):
            column_ref[pl.ds(n * tiles + j, 1), :] = bucket_ref[pl.ds(first_tile(shard) + j, 1), :]
    for at in range(CORES * tiles):
        tile = first_tile(here ^ (at // tiles)) + at % tiles
        row_ref[pl.ds(at * TILE, TILE), :] = column_of(bucket_ref[pl.ds(tile, 1), :])
        if at < tiles:
            ids = lax.broadcasted_iota(jnp.int32, (1, TILE), 1) + tile * TILE
            matched = column_of(positive_ref[pl.ds(tile, 1), :]) == ids
            match_ref[pl.ds(at * TILE, TILE), :] = jnp.where(matched, 1.0, 0.0)
        for n, shard in enumerate(shards):
            entries = [blocks_ref[slot, shard, tile] for slot in range(SLOTS)]
            for j in range(tiles):
                listed = sum(jnp.where(entry == j, 1.0, 0.0) for entry in entries)
                amount_ref[pl.ds(at * count + n * tiles + j, 1), :] = jnp.full(
                    (1, TILE), scale * listed, jnp.float32
                )


class Pairs:
    count = 6

    def __init__(self, refs, tiles):
        self.line_ref, self.amount_ref, self.column_ref = refs[:3]
        self.row_ref, self.match_ref, self.own_ref = refs[3:6]
        self.tiles = tiles

    def weigh(self, products, half, group, weight_ref, top, left, own=None):
        tiles = self.tiles
        slope, offset = self.line_ref[pl.ds(0, 1), :], self.line_ref[pl.ds(1, 1), :]
        count = self.column_ref.shape[0]
        for a in range(tiles):
            at = half * tiles + a
            row_bucket = self.row_ref[pl.ds(at * TILE, TILE), :]
            for j in range(tiles):
                n = group * tiles + j
                amount = self.amount_ref[pl.ds(at * count + n, 1), :]
                power = (
                    products[a * TILE : (a + 1) * TILE, j * TILE : (j + 1) * TILE] * slope + offset
                )
                factor = jnp.where(row_bucket == self.column_ref[pl.ds(n, 1), :], amount, 0.0)
                if own and a == j:
                    match = self.match_ref[pl.ds(a * TILE, TILE), :]
                    if own == "search":
                        match = match * self.own_ref[pl.ds(group, 1), :]
                    power = jnp.where(match > 0.0, -power, power)
                    factor = jnp.where(match > 0.0, -amount, factor)
                below = 1.0 + jnp.exp2(power)
                inverse = pl.reciprocal(below, approx=True)
                inverse = inverse * (2.0 - below * inverse)
                weight_ref[pl.ds(top + a * TILE, TILE), pl.ds(left + j * TILE, TILE)] = (
                    factor * inverse
                ).astype(jnp.bfloat16)


def near_own_body(tiles, *refs):
    pairs = Pairs(refs, tiles)
    unit_ref, own_image_ref, near_image_ref, own_weight_ref, weight_ref = refs[Pairs.count :]
    rows = unit_ref.shape[0]
    first = dot_nt(unit_ref[...], near_image_ref[pl.ds(0, rows), :])
    second = dot_nt(unit_ref[...], near_image_ref[pl.ds(rows, rows), :])
    pairs.weigh(first, 0, 1, weight_ref, 0, 0)
    own = dot_nt(unit_ref[...], own_image_ref[...])
    pairs.weigh(second, 0, 2, weight_ref, 0, rows)
    pairs.weigh(own, 0, 0, own_weight_ref, 0, 0, "diagonal")


def first_sum_body(tiles, *refs):
    pairs = Pairs(refs, tiles)
    own_unit_ref, near_image_ref, weight_in_ref = refs[Pairs.count : Pairs.count + 3]
    piece_refs = refs[Pairs.count + 3 : Pairs.count + 3 + TEXT_PIECES]
    unit_ref, weight_ref, sum_ref = refs[Pairs.count + 3 + TEXT_PIECES :]
    rows = own_unit_ref.shape[0]
    for at, ref in enumerate(piece_refs):
        unit_ref[pl.ds(rows + at * ref.shape[0], ref.shape[0]), :] = ref[...]
    unit_ref[:rows, :] = own_unit_ref[...]
    weight_ref[:rows, :] = weight_in_ref[:, :rows]
    products = dot_nt(unit_ref[rows:, :], near_image_ref[pl.ds(0, rows), :])
    pairs.weigh(products, 1, 1, weight_ref, rows, 0)
    sum_ref[...] = dot_tn(weight_ref[...], unit_ref[...]).astype(jnp.bfloat16)


def near_sum_body(tiles, *refs):
    pairs = Pairs(refs, tiles)
    unit_ref, own_image_ref, near_image_ref, own_weight_in_ref, weight_in_ref, first_ref = refs[
        Pairs.count : Pairs.count + 6
    ]
    own_weight_ref, acc_ref, weight_ref = refs[Pairs.count + 6 :]
    rows = own_image_ref.shape[0]
    second = dot_nt(unit_ref[rows:, :], near_image_ref[pl.ds(rows, rows), :])
    own = dot_nt(unit_ref[rows:, :], own_image_ref[...])
    own_weight_ref[:rows, :] = own_weight_in_ref[...]
    weight_ref[:, :rows] = first_ref[...]
    weight_ref[:rows, rows:] = weight_in_ref[:, rows:]
    pairs.weigh(second, 1, 2, weight_ref, rows, rows)
    pairs.weigh(own, 1, 0, own_weight_ref, rows, 0)
    acc_ref[...] = jnp.dot(
        weight_ref[...], near_image_ref[...], preferred_element_type=jnp.float32
    )


def far_weights_body(tiles, *refs):
    pairs = Pairs(refs, tiles)
    unit_ref, own_image_ref, own_weight_ref, raw_ref = refs[Pairs.count : Pairs.count + 4]
    weight_ref, image_ref = refs[Pairs.count + 4 :]
    rows = raw_ref.shape[0]
    unit_images(raw_ref, image_ref.at[pl.ds(rows, rows), :])
    products = dot_nt(unit_ref[...], image_ref[rows:, :])
    for half in range(CORES):
        part = products[half * rows : (half + 1) * rows, :]
        pairs.weigh(part, half, 3, weight_ref, half * rows, rows)
    image_ref[:rows, :] = own_image_ref[...]
    weight_ref[:, :rows] = own_weight_ref[...]


def far_sum_body(weight_ref, unit_ref, out_ref):
    rows = out_ref.shape[0]
    out_ref[...] = dot_tn(weight_ref[:, rows:], unit_ref[...]).astype(jnp.bfloat16)


def text_sum_body(half, weight_ref, image_ref, acc_ref, *out_refs):
    rows = weight_ref.shape[0] // CORES
    size = out_refs[0].shape[0]
    part = pl.ds(half * rows, rows)
    acc = acc_ref[part, :] + jnp.dot(
        weight_ref[part, :], image_ref[...], preferred_element_type=jnp.float32
    )
    for at, ref in enumerate(out_refs):
        ref[...] = acc[at * size : (at + 1) * size, :].astype(ref.dtype)


def own_sum_body(own_weight_ref, near_weight_ref, unit_ref, add_ref, own_ref, second_ref):
    rows = own_ref.shape[0]
    second_ref[...] = dot_tn(near_weight_ref[:, rows:], unit_ref[...])
    own_ref[...] = dot_tn(own_weight_ref[...], unit_ref[...]) + add_ref[...].astype(jnp.float32)


def all_body(tiles, chips, *refs):
    pairs = Pairs(refs, tiles)
    own_ref, other_ref, piece_ref = refs[Pairs.count : Pairs.count + 3]
    outs = refs[Pairs.count + 3 :]
    spread_ref, acc_ref, acc_piece_refs = outs[0], outs[1], outs[2 : 2 + ACC_PIECES]
    image_ref, weight_ref = outs[2 + ACC_PIECES :]
    rows = own_ref.shape[0]
    unit_images(piece_ref, image_ref)
    for half, text_ref in enumerate((own_ref, other_ref)):
        for chip in range(chips):
            products = dot_nt(text_ref[...], image_ref[pl.ds(chip * rows, rows), :])
            pairs.weigh(
                products, half, chip, weight_ref, half * rows, chip * rows, None if half else "search"
            )
        acc = jnp.dot(
            weight_ref[pl.ds(half * rows, rows), :],
            image_ref[...],
            preferred_element_type=jnp.float32,
        )
        if half == 0:
            acc_ref[...] = acc
            continue
        size = rows // ACC_PIECES
        for at, ref in enumerate(acc_piece_refs):
            ref[...] = acc[at * size : (at + 1) * size, :].astype(jnp.bfloat16)
    for chip in range(chips):
        columns = pl.ds(chip * rows, rows)
        total = dot_tn(weight_ref[pl.ds(0, rows), columns], own_ref[...])
        total += dot_tn(weight_ref[pl.ds(rows, rows), columns], other_ref[...])
        spread_ref[columns, :] = total.astype(jnp.bfloat16)


def relay_body(sum_ref, in_ref, *out_refs):
    for at, ref in enumerate(out_refs):
        part = pl.ds(at * ref.shape[0], ref.shape[0])
        ref[...] = (sum_ref[part, :] + in_ref[part, :].astype(jnp.float32)).astype(jnp.bfloat16)


def text_grad_body(chunks, *refs):
    scale_ref, raw_refs, acc_ref = refs[0], refs[1 : 1 + chunks], refs[1 + chunks]
    add_refs, out_refs = refs[2 + chunks : -chunks], refs[-chunks:]
    place = lax.axis_index("tp")
    rows, width = raw_refs[0].shape
    size = add_refs[0].shape[0]
    for first in range(0, rows, TILE // 2):
        part = pl.ds(first, TILE // 2)
        scales = scale_ref[part, :1]
        raws = [ref[part, :].astype(jnp.float32) for ref in raw_refs]
        accs = []
        for k in range(chunks):
            features = feature_slice(place, k, width)
            added = add_refs[first // size][pl.ds(first % size, TILE // 2), features]
            accs.append(acc_ref[part, features] + added.astype(jnp.float32))
        inner = sum(jnp.sum(x * a, axis=-1, keepdims=True) for x, a in zip(raws, accs))
        inner = inner * scales * scales
        for k in range(chunks):
            out_refs[k][part, :] = (scales * (accs[k] - raws[k] * inner)).astype(jnp.bfloat16)


def place_text_body(chunks, *refs):
    part_refs, out_ref, sems = refs[:chunks], refs[chunks], refs[chunks + 1]
    place = lax.axis_index("tp")
    rows = part_refs[0].shape[0]
    copies = []
    for k in range(chunks):
        block = pl.ds(pl.multiple_of((place ^ k) * rows, rows), rows)
        copies.append(pltpu.make_async_copy(part_refs[k], out_ref.at[block, :], sems.at[k]))
    for copy in copies:
        copy.start()
    for copy in copies:
        copy.wait()


def image_grad_body(piece_count, raw_ref, scale_ref, sum_ref, *refs):
    piece_refs, (out_ref, grad_ref, sems) = refs[:piece_count], refs[piece_count:]
    copies = []
    for block in range(raw_ref.shape[0] // TILE):
        for first in range(block * TILE, (block + 1) * TILE, TILE // 2):
            part = pl.ds(first, TILE // 2)
            raw = raw_ref[part, :].astype(jnp.float32)
            scales = scale_ref[part, :1]
            acc = sum_ref[part, :]
            if piece_refs:
                size = piece_refs[0].shape[0]
                piece = piece_refs[first // size][pl.ds(first % size, TILE // 2), :]
                acc = acc + piece.astype(jnp.float32)
            inner = jnp.sum(raw * acc, axis=-1, keepdims=True) * scales * scales
            grad_ref[part, :] = (scales * (acc - raw * inner)).astype(jnp.bfloat16)
        part = pl.ds(block * TILE, TILE)
        copies.append(
            pltpu.make_async_copy(grad_ref.at[part, :], out_ref.at[part, :], sems.at[block])
        )
        copies[-1].start()
    for copy in copies:
        copy.wait()


def swap(value, axis, bits):
    count = lax.axis_size(axis)
    return lax.ppermute(value, axis, [(i, i ^ bits) for i in range(count)])


def swap_near(value, which):
    count = lax.axis_size("blk")
    return lax.ppermute(value, "blk", [(i, i ^ neighbour_bits(i)[which]) for i in range(count)])


def per_device(text_emb, image_emb, logit_scale, logit_bias, bucket, positive, blocks):
    groups = lax.axis_size("tp")
    shards = lax.axis_size("blk")
    chips = shards // CORES
    rows, embed = image_emb.shape
    tiles = rows // TILE
    width = text_emb.shape[1]
    square = chips == 4

    def bf16(count, columns=embed):
        return struct((count, columns), jnp.bfloat16)

    def f32(count, columns=embed):
        return struct((count, columns), jnp.float32)

    def i32(count, columns):
        return struct((count, columns), jnp.int32)

    picked = call_kernel(pick_body, [bf16(rows, width)] * groups, [text_emb], limit=8)
    text_raw = [picked[0]] + [swap(picked[k], "tp", k) for k in range(1, groups)]
    if square:
        from_second = swap_near(image_emb, 1)
    else:
        same_core = [[chip * CORES + core for chip in range(chips)] for core in range(CORES)]
        gathered = lax.all_gather(
            image_emb, "blk", axis=0, tiled=True, axis_index_groups=same_core
        )
        _, image_raw, image_scales = call_kernel(
            own_images_body, [bf16(rows), bf16(rows), f32(rows, TILE)], [image_emb], limit=8
        )
    lists = call_kernel(
        functools.partial(list_body, groups, tiles, chips),
        [
            f32(2, TILE),
            f32(CORES * tiles * chips * tiles, TILE),
            i32(chips * tiles, TILE),
            i32(CORES * rows, TILE),
            f32(rows, TILE),
            f32(chips, TILE),
        ],
        [
            logit_scale,
            logit_bias,
            blocks.transpose(2, 1, 0),
            bucket.reshape(-1, TILE),
            positive.reshape(-1, TILE),
        ],
        scalars=3,
        limit=8,
    )
    if square:
        own_images, image_raw, image_scales = call_kernel(
            own_images_body, [bf16(rows), bf16(rows), f32(rows, TILE)], [image_emb], limit=8
        )
        image_sent, own_images = lax.optimization_barrier((image_emb, own_images))
        from_first = swap_near(image_sent, 0)
        from_second, own_images, *lists = lax.optimization_barrier(
            (from_second, own_images, *lists)
        )
        from_far = swap_near(from_second, 0)
        second_images = call_kernel(
            unit_images_body, [bf16(rows)], [from_second], flops=WAIT_FLOPS // 2, limit=8
        )[0]
        text_raw[-1], second_images = lax.optimization_barrier((text_raw[-1], second_images))
    text_own, text_scales, *pieces = call_kernel(
        functools.partial(unit_text_body, groups),
        [bf16(rows), f32(rows, TILE)] + [bf16(rows // TEXT_PIECES)] * TEXT_PIECES,
        text_raw,
        limit=8,
    )
    text_other = [swap(piece, "blk", 1) for piece in pieces]
    if square:
        from_first, text_own = lax.optimization_barrier((from_first, text_own))
        near_images = call_kernel(
            near_images_body, [bf16(2 * rows)], [from_first, second_images], limit=8
        )[0]
    unit_flops = 2 * rows * rows * embed

    def finish_text(acc_own, acc_other):
        parts = call_kernel(
            functools.partial(text_grad_body, groups),
            [bf16(rows, width)] * groups,
            [text_scales] + text_raw + [acc_own] + [swap(piece, "blk", 1) for piece in acc_other],
            limit=16,
        )
        sent = [swap(parts[k], "tp", k) for k in reversed(range(1, groups))]
        return [parts[0]] + sent[::-1]

    def place_text(text_parts):
        return call_kernel(
            functools.partial(place_text_body, groups),
            [bf16(groups * rows, width)],
            text_parts,
            outs_anywhere=True,
            scratch=[pltpu.SemaphoreType.DMA((groups,))],
            flops=WAIT_FLOPS,
            limit=8,
        )[0]

    def finish_image(total, pieces):
        return call_kernel(
            functools.partial(image_grad_body, len(pieces)),
            [bf16(rows)],
            [image_raw, image_scales, total] + pieces,
            outs_anywhere=True,
            scratch=[pltpu.VMEM((rows, embed), jnp.bfloat16), pltpu.SemaphoreType.DMA((tiles,))],
            limit=8,
        )[0]

    if not square:
        columns = gathered.shape[0]
        spread, acc_own, *acc_other = call_kernel(
            functools.partial(all_body, tiles, chips),
            [bf16(columns), f32(rows)] + [bf16(rows // ACC_PIECES)] * ACC_PIECES,
            lists + [text_own, jnp.concatenate(text_other), gathered],
            scratch=[
                pltpu.VMEM((columns, embed), jnp.bfloat16),
                pltpu.VMEM((2 * rows, columns), jnp.bfloat16),
            ],
            flops=6 * chips * unit_flops,
            limit=56,
        )
        text_parts = finish_text(acc_own, acc_other)
        parts = lax.all_to_all(
            spread, "blk", split_axis=0, concat_axis=0, tiled=True, axis_index_groups=same_core
        )
        total = jnp.sum(parts.reshape(-1, rows, embed).astype(jnp.float32), axis=0)
        return (place_text(text_parts), finish_image(total, []))

    own_weights, near_weights = call_kernel(
        functools.partial(near_own_body, tiles),
        [bf16(rows, rows), bf16(rows, 2 * rows)],
        lists + [text_own, own_images, near_images],
        limit=16,
    )
    units, first_weights, first_sum = call_kernel(
        functools.partial(first_sum_body, tiles),
        [bf16(2 * rows), bf16(2 * rows, rows), bf16(rows)],
        lists + [text_own, near_images, near_weights] + text_other,
        limit=16,
    )
    image_add = swap_near(first_sum, 0)
    own_weights, acc, near_weights = call_kernel(
        functools.partial(near_sum_body, tiles),
        [bf16(2 * rows, rows), f32(2 * rows), bf16(2 * rows, 2 * rows)],
        lists + [units, own_images, near_images, own_weights, near_weights, first_weights],
        limit=24,
    )
    own_weights, from_far = lax.optimization_barrier((own_weights, from_far))
    far_weights, far_images = call_kernel(
        functools.partial(far_weights_body, tiles),
        [bf16(2 * rows, 2 * rows), bf16(2 * rows)],
        lists + [units, own_images, own_weights, from_far],
        limit=16,
    )
    acc_other = call_kernel(
        functools.partial(text_sum_body, 1),
        [bf16(rows // ACC_PIECES)] * ACC_PIECES,
        [far_weights, far_images, acc],
        limit=16,
    )
    far_images, acc_other[0] = lax.optimization_barrier((far_images, acc_other[0]))
    acc_own = call_kernel(
        functools.partial(text_sum_body, 0),
        [f32(rows)],
        [far_weights, far_images, acc],
        limit=16,
    )[0]
    far_weights, acc_own = lax.optimization_barrier((far_weights, acc_own))
    far_sum = call_kernel(far_sum_body, [bf16(rows)], [far_weights, units], limit=16)[0]
    acc_own, far_sum = lax.optimization_barrier((acc_own, far_sum))
    text_parts = finish_text(acc_own, acc_other)
    own_weights, text_parts[0] = lax.optimization_barrier((own_weights, text_parts[0]))
    base, second_sum = call_kernel(
        own_sum_body,
        [f32(rows), f32(rows)],
        [own_weights, near_weights, units, image_add],
        flops=WAIT_FLOPS,
        limit=16,
    )
    relayed = call_kernel(
        relay_body,
        [bf16(rows // LAST_PIECES)] * LAST_PIECES,
        [second_sum, swap_near(far_sum, 0)],
        limit=8,
    )
    image_last = [swap_near(piece, 1) for piece in relayed]
    text_grad = place_text(text_parts)
    base, _ = lax.optimization_barrier((base, text_grad))
    return (text_grad, finish_image(base, image_last))


def solution(mesh):
    in_specs = (P("blk", "tp"), P(("blk", "tp"), None), P(), P(), P(), P(), P())
    out_specs = (P("blk", "tp"), P(("blk", "tp"), None))
    return jax.shard_map(
        per_device, mesh=mesh, in_specs=in_specs, out_specs=out_specs, check_vma=False
    )
```

```python
import functools
import math

import jax
import jax.numpy as jnp
from jax import lax
from jax.experimental import pallas as pl
from jax.experimental.pallas import tpu as pltpu
from jax.sharding import PartitionSpec as P

TILE = 128
SLOTS = 3
WAIT_FLOPS = 20_000_000_000
TEXT_PIECES = 3
ACC_PIECES = 3
LAST_PIECES = 2
CORES = 2
EPS = 1e-06
LOG2E = math.log2(math.e)
MIB = 1024 * 1024

VMEM_SPEC = pl.BlockSpec(memory_space=pltpu.VMEM)
ANY_SPEC = pl.BlockSpec(memory_space=pl.ANY)
SMEM_SPEC = pl.BlockSpec(memory_space=pltpu.SMEM)


def call_kernel(
    body,
    outs,
    operands,
    scalars=0,
    anywhere=(),
    outs_anywhere=False,
    scratch=(),
    flops=0,
    moved=None,
    limit=24,
):
    if moved is None:
        moved = sum(x.size * x.dtype.itemsize for x in operands)
        moved += sum(math.prod(o.shape) * o.dtype.itemsize for o in outs)
    specs = [SMEM_SPEC] * scalars + [VMEM_SPEC] * (len(operands) - scalars)
    for at in anywhere:
        specs[at] = ANY_SPEC
    return list(
        pl.pallas_call(
            body,
            out_shape=outs,
            in_specs=specs,
            out_specs=[ANY_SPEC if outs_anywhere else VMEM_SPEC] * len(outs),
            scratch_shapes=list(scratch),
            compiler_params=pltpu.CompilerParams(vmem_limit_bytes=limit * MIB),
            cost_estimate=pl.CostEstimate(flops=flops, bytes_accessed=moved, transcendentals=0),
        )(*operands)
    )


def struct(shape, dtype):
    return jax.ShapeDtypeStruct(shape, dtype)


def row_scales(square_sum):
    return lax.rsqrt(square_sum + EPS)


def column_of(row):
    return jnp.broadcast_to(row, (TILE, TILE)).T


def dot_nt(left, right):
    return lax.dot_general(
        left, right, (((1,), (1,)), ((), ())), preferred_element_type=jnp.float32
    )


def dot_tn(left, right):
    return lax.dot_general(
        left, right, (((0,), (0,)), ((), ())), preferred_element_type=jnp.float32
    )


def peer_bits(k, chunks):
    return (chunks - k) % chunks


def feature_slice(peer, width):
    return pl.ds(pl.multiple_of(peer * width, width), width)


def pick_body(text_ref, *out_refs):
    place = lax.axis_index("tp")
    rows = out_refs[0].shape[0]
    for k, out_ref in enumerate(out_refs):
        peer = place ^ peer_bits(k, len(out_refs))
        out_ref[...] = text_ref[pl.ds(pl.multiple_of(peer * rows, rows), rows), :]


def unit_text_body(chunks, *refs):
    chunk_refs, (unit_ref, scale_ref) = refs[:chunks], refs[chunks : chunks + 2]
    piece_refs = refs[chunks + 2 :]
    place = lax.axis_index("tp")
    rows, width = chunk_refs[0].shape
    for first in range(0, rows, TILE):
        part = pl.ds(first, TILE)
        parts = [ref[part, :].astype(jnp.float32) for ref in chunk_refs]
        scales = row_scales(sum(jnp.sum(x * x, axis=-1, keepdims=True) for x in parts))
        scale_ref[part, :] = jnp.broadcast_to(scales, (TILE, TILE))
        for k, x in enumerate(parts):
            unit_ref[part, feature_slice(place ^ peer_bits(k, chunks), width)] = (x * scales).astype(jnp.bfloat16)
    split_rows(unit_ref, piece_refs)


def split_rows(whole_ref, piece_refs):
    for at, ref in enumerate(piece_refs):
        ref[...] = whole_ref[pl.ds(at * ref.shape[0], ref.shape[0]), :]


def join_rows(piece_refs, whole_ref):
    for at, ref in enumerate(piece_refs):
        whole_ref[pl.ds(at * ref.shape[0], ref.shape[0]), :] = ref[...]


def unit_images(ref, image_ref, scale_ref=None):
    step = 64
    for first in range(0, ref.shape[0], step):
        part = pl.ds(first, step)
        values = ref[part, :].astype(jnp.float32)
        scales = row_scales(jnp.sum(values * values, axis=-1, keepdims=True))
        image_ref[part, :] = (values * scales).astype(jnp.bfloat16)
        if scale_ref is not None:
            scale_ref[part, :] = jnp.broadcast_to(scales, (step, TILE))


def unit_images_body(raw_ref, out_ref):
    unit_images(raw_ref, out_ref)


def own_images_body(raw_ref, out_ref, raw_out_ref, scale_ref):
    unit_images(raw_ref, out_ref, scale_ref)
    raw_out_ref[...] = raw_ref[...]


def near_images_body(first_ref, second_unit_ref, out_ref):
    rows = first_ref.shape[0]
    unit_images(first_ref, out_ref)
    out_ref[rows:, :] = second_unit_ref[...]


def neighbour_bits(shard):
    core = shard % CORES
    return 2 << core, 4 >> core


def list_body(groups, tiles, chips, *refs):
    scale_ref, bias_ref, blocks_ref, bucket_ref, positive_ref = refs[:5]
    line_ref, amount_ref, column_ref, row_ref, match_ref, own_ref = refs[5:]
    here, place = lax.axis_index("blk"), lax.axis_index("tp")
    scale = scale_ref[0]
    line_ref[pl.ds(0, 1), :] = jnp.full((1, TILE), -scale * LOG2E, jnp.float32)
    line_ref[pl.ds(1, 1), :] = jnp.full((1, TILE), -bias_ref[0] * LOG2E, jnp.float32)
    if chips == 4:
        first, second = neighbour_bits(here)
        shards = [here, here ^ first, here ^ second, here ^ 6]
    else:
        shards = [chip * CORES + here % CORES for chip in range(chips)]
    count = len(shards) * tiles

    def first_tile(shard):
        return (shard * groups + place) * tiles

    for n, shard in enumerate(shards):
        own_ref[pl.ds(n, 1), :] = jnp.full((1, TILE), jnp.where(shard == here, 1.0, 0.0))
        for j in range(tiles):
            column_ref[pl.ds(n * tiles + j, 1), :] = bucket_ref[pl.ds(first_tile(shard) + j, 1), :]
    for at in range(CORES * tiles):
        tile = first_tile(here ^ (at // tiles)) + at % tiles
        row_ref[pl.ds(at * TILE, TILE), :] = column_of(bucket_ref[pl.ds(tile, 1), :])
        if at < tiles:
            ids = lax.broadcasted_iota(jnp.int32, (1, TILE), 1) + tile * TILE
            matched = column_of(positive_ref[pl.ds(tile, 1), :]) == ids
            match_ref[pl.ds(at * TILE, TILE), :] = jnp.where(matched, 1.0, 0.0)
        for n, shard in enumerate(shards):
            entries = [blocks_ref[slot, shard, tile] for slot in range(SLOTS)]
            for j in range(tiles):
                listed = sum(jnp.where(entry == j, 1.0, 0.0) for entry in entries)
                amount_ref[pl.ds(at * count + n * tiles + j, 1), :] = jnp.full(
                    (1, TILE), scale * listed, jnp.float32
                )


class Pairs:
    count = 6

    def __init__(self, refs, tiles):
        self.line_ref, self.amount_ref, self.column_ref = refs[:3]
        self.row_ref, self.match_ref, self.own_ref = refs[3:6]
        self.tiles = tiles

    def weigh(self, products, half, group, weight_ref, top, left, own=None):
        tiles = self.tiles
        slope, offset = self.line_ref[pl.ds(0, 1), :], self.line_ref[pl.ds(1, 1), :]
        count = self.column_ref.shape[0]
        for a in range(tiles):
            at = half * tiles + a
            row_bucket = self.row_ref[pl.ds(at * TILE, TILE), :]
            for j in range(tiles):
                n = group * tiles + j
                amount = self.amount_ref[pl.ds(at * count + n, 1), :]
                power = (
                    products[a * TILE : (a + 1) * TILE, j * TILE : (j + 1) * TILE] * slope + offset
                )
                factor = jnp.where(row_bucket == self.column_ref[pl.ds(n, 1), :], amount, 0.0)
                if own and a == j:
                    match = self.match_ref[pl.ds(a * TILE, TILE), :]
                    if own == "search":
                        match = match * self.own_ref[pl.ds(group, 1), :]
                    power = jnp.where(match > 0.0, -power, power)
                    factor = jnp.where(match > 0.0, -amount, factor)
                below = 1.0 + jnp.exp2(power)
                inverse = pl.reciprocal(below, approx=True)
                inverse = inverse * (2.0 - below * inverse)
                weight_ref[pl.ds(top + a * TILE, TILE), pl.ds(left + j * TILE, TILE)] = (
                    factor * inverse
                ).astype(jnp.bfloat16)


def near_own_body(tiles, *refs):
    pairs = Pairs(refs, tiles)
    unit_ref, own_image_ref, near_image_ref, own_weight_ref, weight_ref = refs[Pairs.count :]
    rows = unit_ref.shape[0]
    first = dot_nt(unit_ref[...], near_image_ref[pl.ds(0, rows), :])
    second = dot_nt(unit_ref[...], near_image_ref[pl.ds(rows, rows), :])
    pairs.weigh(first, 0, 1, weight_ref, 0, 0)
    own = dot_nt(unit_ref[...], own_image_ref[...])
    pairs.weigh(second, 0, 2, weight_ref, 0, rows)
    pairs.weigh(own, 0, 0, own_weight_ref, 0, 0, "diagonal")


def first_sum_body(tiles, *refs):
    pairs = Pairs(refs, tiles)
    own_unit_ref, near_image_ref, weight_in_ref = refs[Pairs.count : Pairs.count + 3]
    piece_refs = refs[Pairs.count + 3 : Pairs.count + 3 + TEXT_PIECES]
    unit_ref, weight_ref, sum_ref = refs[Pairs.count + 3 + TEXT_PIECES :]
    rows = own_unit_ref.shape[0]
    for at, ref in enumerate(piece_refs):
        unit_ref[pl.ds(rows + at * ref.shape[0], ref.shape[0]), :] = ref[...]
    unit_ref[:rows, :] = own_unit_ref[...]
    weight_ref[:rows, :] = weight_in_ref[:, :rows]
    products = dot_nt(unit_ref[rows:, :], near_image_ref[pl.ds(0, rows), :])
    pairs.weigh(products, 1, 1, weight_ref, rows, 0)
    sum_ref[...] = dot_tn(weight_ref[...], unit_ref[...]).astype(jnp.bfloat16)


def near_sum_body(tiles, *refs):
    pairs = Pairs(refs, tiles)
    unit_ref, own_image_ref, near_image_ref, own_weight_in_ref, weight_in_ref, first_ref = refs[
        Pairs.count : Pairs.count + 6
    ]
    own_weight_ref, acc_ref, weight_ref = refs[Pairs.count + 6 :]
    rows = own_image_ref.shape[0]
    second = dot_nt(unit_ref[rows:, :], near_image_ref[pl.ds(rows, rows), :])
    own = dot_nt(unit_ref[rows:, :], own_image_ref[...])
    own_weight_ref[:rows, :] = own_weight_in_ref[...]
    weight_ref[:, :rows] = first_ref[...]
    weight_ref[:rows, rows:] = weight_in_ref[:, rows:]
    pairs.weigh(second, 1, 2, weight_ref, rows, rows)
    pairs.weigh(own, 1, 0, own_weight_ref, rows, 0)
    acc_ref[...] = jnp.dot(
        weight_ref[...], near_image_ref[...], preferred_element_type=jnp.float32
    )


def far_weights_body(tiles, *refs):
    pairs = Pairs(refs, tiles)
    unit_ref, own_image_ref, own_weight_ref, raw_ref = refs[Pairs.count : Pairs.count + 4]
    weight_ref, image_ref = refs[Pairs.count + 4 :]
    rows = raw_ref.shape[0]
    unit_images(raw_ref, image_ref.at[pl.ds(rows, rows), :])
    products = dot_nt(unit_ref[...], image_ref[rows:, :])
    for half in range(CORES):
        part = products[half * rows : (half + 1) * rows, :]
        pairs.weigh(part, half, 3, weight_ref, half * rows, rows)
    image_ref[:rows, :] = own_image_ref[...]
    weight_ref[:, :rows] = own_weight_ref[...]


def far_sum_body(weight_ref, unit_ref, out_ref):
    rows = out_ref.shape[0]
    out_ref[...] = dot_tn(weight_ref[:, rows:], unit_ref[...]).astype(jnp.bfloat16)


def text_sum_body(half, weight_ref, image_ref, acc_ref, *out_refs):
    rows = weight_ref.shape[0] // CORES
    size = out_refs[0].shape[0]
    part = pl.ds(half * rows, rows)
    acc = acc_ref[part, :] + jnp.dot(
        weight_ref[part, :], image_ref[...], preferred_element_type=jnp.float32
    )
    for at, ref in enumerate(out_refs):
        ref[...] = acc[at * size : (at + 1) * size, :].astype(ref.dtype)


def own_sum_body(own_weight_ref, near_weight_ref, unit_ref, add_ref, own_ref, second_ref):
    rows = own_ref.shape[0]
    second_ref[...] = dot_tn(near_weight_ref[:, rows:], unit_ref[...])
    own_ref[...] = dot_tn(own_weight_ref[...], unit_ref[...]) + add_ref[...].astype(jnp.float32)


def all_body(tiles, chips, *refs):
    pairs = Pairs(refs, tiles)
    own_ref, other_ref, piece_ref = refs[Pairs.count : Pairs.count + 3]
    outs = refs[Pairs.count + 3 :]
    spread_ref, acc_ref, acc_piece_refs = outs[0], outs[1], outs[2 : 2 + ACC_PIECES]
    image_ref, weight_ref = outs[2 + ACC_PIECES :]
    rows = own_ref.shape[0]
    unit_images(piece_ref, image_ref)
    for half, text_ref in enumerate((own_ref, other_ref)):
        for chip in range(chips):
            products = dot_nt(text_ref[...], image_ref[pl.ds(chip * rows, rows), :])
            pairs.weigh(
                products, half, chip, weight_ref, half * rows, chip * rows, None if half else "search"
            )
        acc = jnp.dot(
            weight_ref[pl.ds(half * rows, rows), :],
            image_ref[...],
            preferred_element_type=jnp.float32,
        )
        if half == 0:
            acc_ref[...] = acc
            continue
        size = rows // ACC_PIECES
        for at, ref in enumerate(acc_piece_refs):
            ref[...] = acc[at * size : (at + 1) * size, :].astype(jnp.bfloat16)
    for chip in range(chips):
        columns = pl.ds(chip * rows, rows)
        total = dot_tn(weight_ref[pl.ds(0, rows), columns], own_ref[...])
        total += dot_tn(weight_ref[pl.ds(rows, rows), columns], other_ref[...])
        spread_ref[columns, :] = total.astype(jnp.bfloat16)


def relay_body(sum_ref, in_ref, *out_refs):
    for at, ref in enumerate(out_refs):
        part = pl.ds(at * ref.shape[0], ref.shape[0])
        ref[...] = (sum_ref[part, :] + in_ref[part, :].astype(jnp.float32)).astype(jnp.bfloat16)


def text_grad_body(chunks, *refs):
    scale_ref, raw_refs, acc_ref = refs[0], refs[1 : 1 + chunks], refs[1 + chunks]
    add_refs, out_refs = refs[2 + chunks : -chunks], refs[-chunks:]
    place = lax.axis_index("tp")
    rows, width = raw_refs[0].shape
    size = add_refs[0].shape[0]
    for first in range(0, rows, TILE // 2):
        part = pl.ds(first, TILE // 2)
        scales = scale_ref[part, :1]
        raws = [ref[part, :].astype(jnp.float32) for ref in raw_refs]
        accs = []
        for k in range(chunks):
            features = feature_slice(place ^ peer_bits(k, chunks), width)
            added = add_refs[first // size][pl.ds(first % size, TILE // 2), features]
            accs.append(acc_ref[part, features] + added.astype(jnp.float32))
        inner = sum(jnp.sum(x * a, axis=-1, keepdims=True) for x, a in zip(raws, accs))
        inner = inner * scales * scales
        for k in range(chunks):
            out_refs[k][part, :] = (scales * (accs[k] - raws[k] * inner)).astype(jnp.bfloat16)


def place_text_body(chunks, *refs):
    part_refs, out_ref, sems = refs[:chunks], refs[chunks], refs[chunks + 1]
    place = lax.axis_index("tp")
    rows = part_refs[0].shape[0]
    copies = []
    for k in range(chunks):
        peer = place ^ peer_bits(k, chunks)
        block = pl.ds(pl.multiple_of(peer * rows, rows), rows)
        copies.append(pltpu.make_async_copy(part_refs[k], out_ref.at[block, :], sems.at[k]))
    for copy in copies:
        copy.start()
    for copy in copies:
        copy.wait()


def image_grad_body(piece_count, raw_ref, scale_ref, sum_ref, *refs):
    piece_refs, (out_ref, grad_ref, sems) = refs[:piece_count], refs[piece_count:]
    copies = []
    for block in range(raw_ref.shape[0] // TILE):
        for first in range(block * TILE, (block + 1) * TILE, TILE // 2):
            part = pl.ds(first, TILE // 2)
            raw = raw_ref[part, :].astype(jnp.float32)
            scales = scale_ref[part, :1]
            acc = sum_ref[part, :]
            if piece_refs:
                size = piece_refs[0].shape[0]
                piece = piece_refs[first // size][pl.ds(first % size, TILE // 2), :]
                acc = acc + piece.astype(jnp.float32)
            inner = jnp.sum(raw * acc, axis=-1, keepdims=True) * scales * scales
            grad_ref[part, :] = (scales * (acc - raw * inner)).astype(jnp.bfloat16)
        part = pl.ds(block * TILE, TILE)
        copies.append(
            pltpu.make_async_copy(grad_ref.at[part, :], out_ref.at[part, :], sems.at[block])
        )
        copies[-1].start()
    for copy in copies:
        copy.wait()


def swap(value, axis, bits):
    count = lax.axis_size(axis)
    return lax.ppermute(value, axis, [(i, i ^ bits) for i in range(count)])


def swap_near(value, which):
    count = lax.axis_size("blk")
    return lax.ppermute(value, "blk", [(i, i ^ neighbour_bits(i)[which]) for i in range(count)])


def swap_chunks(chunks):
    count = len(chunks)
    return chunks[:1] + [swap(chunks[k], "tp", peer_bits(k, count)) for k in range(1, count)]


def per_device(text_emb, image_emb, logit_scale, logit_bias, bucket, positive, blocks):
    groups = lax.axis_size("tp")
    shards = lax.axis_size("blk")
    chips = shards // CORES
    rows, embed = image_emb.shape
    tiles = rows // TILE
    width = text_emb.shape[1]
    square = chips == 4

    def bf16(count, columns=embed):
        return struct((count, columns), jnp.bfloat16)

    def f32(count, columns=embed):
        return struct((count, columns), jnp.float32)

    def i32(count, columns):
        return struct((count, columns), jnp.int32)

    picked = call_kernel(pick_body, [bf16(rows, width)] * groups, [text_emb], limit=8)
    text_raw = swap_chunks(picked)
    if square:
        from_second = swap_near(image_emb, 1)
    else:
        same_core = [[chip * CORES + core for chip in range(chips)] for core in range(CORES)]
        gathered = lax.all_gather(
            image_emb, "blk", axis=0, tiled=True, axis_index_groups=same_core
        )
        _, image_raw, image_scales = call_kernel(
            own_images_body, [bf16(rows), bf16(rows), f32(rows, TILE)], [image_emb], limit=8
        )
    lists = call_kernel(
        functools.partial(list_body, groups, tiles, chips),
        [
            f32(2, TILE),
            f32(CORES * tiles * chips * tiles, TILE),
            i32(chips * tiles, TILE),
            i32(CORES * rows, TILE),
            f32(rows, TILE),
            f32(chips, TILE),
        ],
        [
            logit_scale,
            logit_bias,
            blocks.transpose(2, 1, 0),
            bucket.reshape(-1, TILE),
            positive.reshape(-1, TILE),
        ],
        scalars=3,
        limit=8,
    )
    if square:
        own_images, image_raw, image_scales = call_kernel(
            own_images_body, [bf16(rows), bf16(rows), f32(rows, TILE)], [image_emb], limit=8
        )
        image_sent, own_images = lax.optimization_barrier((image_emb, own_images))
        from_first = swap_near(image_sent, 0)
        from_second, own_images, *lists = lax.optimization_barrier(
            (from_second, own_images, *lists)
        )
        from_far = swap_near(from_second, 0)
        second_images = call_kernel(
            unit_images_body, [bf16(rows)], [from_second], flops=WAIT_FLOPS // 2, limit=8
        )[0]
        text_raw[-1], second_images = lax.optimization_barrier((text_raw[-1], second_images))
    text_own, text_scales, *pieces = call_kernel(
        functools.partial(unit_text_body, groups),
        [bf16(rows), f32(rows, TILE)] + [bf16(rows // TEXT_PIECES)] * TEXT_PIECES,
        text_raw,
        limit=8,
    )
    text_other = [swap(piece, "blk", 1) for piece in pieces]
    if square:
        from_first, text_own = lax.optimization_barrier((from_first, text_own))
        near_images = call_kernel(
            near_images_body, [bf16(2 * rows)], [from_first, second_images], limit=8
        )[0]
    unit_flops = 2 * rows * rows * embed

    def finish_text(acc_own, acc_other):
        parts = call_kernel(
            functools.partial(text_grad_body, groups),
            [bf16(rows, width)] * groups,
            [text_scales] + text_raw + [acc_own] + [swap(piece, "blk", 1) for piece in acc_other],
            limit=16,
        )
        return swap_chunks(parts)

    def place_text(text_parts):
        return call_kernel(
            functools.partial(place_text_body, groups),
            [bf16(groups * rows, width)],
            text_parts,
            outs_anywhere=True,
            scratch=[pltpu.SemaphoreType.DMA((groups,))],
            flops=WAIT_FLOPS,
            limit=8,
        )[0]

    def finish_image(total, pieces):
        return call_kernel(
            functools.partial(image_grad_body, len(pieces)),
            [bf16(rows)],
            [image_raw, image_scales, total] + pieces,
            outs_anywhere=True,
            scratch=[pltpu.VMEM((rows, embed), jnp.bfloat16), pltpu.SemaphoreType.DMA((tiles,))],
            limit=8,
        )[0]

    if not square:
        columns = gathered.shape[0]
        spread, acc_own, *acc_other = call_kernel(
            functools.partial(all_body, tiles, chips),
            [bf16(columns), f32(rows)] + [bf16(rows // ACC_PIECES)] * ACC_PIECES,
            lists + [text_own, jnp.concatenate(text_other), gathered],
            scratch=[
                pltpu.VMEM((columns, embed), jnp.bfloat16),
                pltpu.VMEM((2 * rows, columns), jnp.bfloat16),
            ],
            flops=6 * chips * unit_flops,
            limit=56,
        )
        text_parts = finish_text(acc_own, acc_other)
        parts = lax.all_to_all(
            spread, "blk", split_axis=0, concat_axis=0, tiled=True, axis_index_groups=same_core
        )
        total = jnp.sum(parts.reshape(-1, rows, embed).astype(jnp.float32), axis=0)
        return (place_text(text_parts), finish_image(total, []))

    own_weights, near_weights = call_kernel(
        functools.partial(near_own_body, tiles),
        [bf16(rows, rows), bf16(rows, 2 * rows)],
        lists + [text_own, own_images, near_images],
        limit=16,
    )
    units, first_weights, first_sum = call_kernel(
        functools.partial(first_sum_body, tiles),
        [bf16(2 * rows), bf16(2 * rows, rows), bf16(rows)],
        lists + [text_own, near_images, near_weights] + text_other,
        limit=16,
    )
    image_add = swap_near(first_sum, 0)
    own_weights, acc, near_weights = call_kernel(
        functools.partial(near_sum_body, tiles),
        [bf16(2 * rows, rows), f32(2 * rows), bf16(2 * rows, 2 * rows)],
        lists + [units, own_images, near_images, own_weights, near_weights, first_weights],
        limit=24,
    )
    own_weights, from_far = lax.optimization_barrier((own_weights, from_far))
    far_weights, far_images = call_kernel(
        functools.partial(far_weights_body, tiles),
        [bf16(2 * rows, 2 * rows), bf16(2 * rows)],
        lists + [units, own_images, own_weights, from_far],
        limit=16,
    )
    acc_other = call_kernel(
        functools.partial(text_sum_body, 1),
        [bf16(rows // ACC_PIECES)] * ACC_PIECES,
        [far_weights, far_images, acc],
        limit=16,
    )
    far_images, acc_other[0] = lax.optimization_barrier((far_images, acc_other[0]))
    acc_own = call_kernel(
        functools.partial(text_sum_body, 0),
        [f32(rows)],
        [far_weights, far_images, acc],
        limit=16,
    )[0]
    far_weights, acc_own = lax.optimization_barrier((far_weights, acc_own))
    far_sum = call_kernel(far_sum_body, [bf16(rows)], [far_weights, units], limit=16)[0]
    acc_own, far_sum = lax.optimization_barrier((acc_own, far_sum))
    text_parts = finish_text(acc_own, acc_other)
    own_weights, text_parts[0] = lax.optimization_barrier((own_weights, text_parts[0]))
    base, second_sum = call_kernel(
        own_sum_body,
        [f32(rows), f32(rows)],
        [own_weights, near_weights, units, image_add],
        flops=WAIT_FLOPS,
        limit=16,
    )
    relayed = call_kernel(
        relay_body,
        [bf16(rows // LAST_PIECES)] * LAST_PIECES,
        [second_sum, swap_near(far_sum, 0)],
        limit=8,
    )
    image_last = [swap_near(piece, 1) for piece in relayed]
    text_grad = place_text(text_parts)
    base, _ = lax.optimization_barrier((base, text_grad))
    return (text_grad, finish_image(base, image_last))


def solution(mesh):
    in_specs = (P("blk", "tp"), P(("blk", "tp"), None), P(), P(), P(), P(), P())
    out_specs = (P("blk", "tp"), P(("blk", "tp"), None))
    return jax.shard_map(
        per_device, mesh=mesh, in_specs=in_specs, out_specs=out_specs, check_vma=False
    )
```

```python
import functools
import math

import jax
import jax.numpy as jnp
from jax import lax
from jax.experimental import pallas as pl
from jax.experimental.pallas import tpu as pltpu
from jax.sharding import PartitionSpec as P

TILE = 128
SLOTS = 3
WAIT_FLOPS = 20_000_000_000
TEXT_PIECES = 3
ACC_PIECES = 2
CORES = 2
EPS = 1e-06
LOG2E = math.log2(math.e)
MIB = 1024 * 1024

VMEM_SPEC = pl.BlockSpec(memory_space=pltpu.VMEM)
ANY_SPEC = pl.BlockSpec(memory_space=pl.ANY)
SMEM_SPEC = pl.BlockSpec(memory_space=pltpu.SMEM)


def call_kernel(
    body,
    outs,
    operands,
    scalars=0,
    anywhere=(),
    outs_anywhere=False,
    scratch=(),
    flops=0,
    moved=None,
    limit=24,
):
    if moved is None:
        moved = sum(x.size * x.dtype.itemsize for x in operands)
        moved += sum(math.prod(o.shape) * o.dtype.itemsize for o in outs)
    specs = [SMEM_SPEC] * scalars + [VMEM_SPEC] * (len(operands) - scalars)
    for at in anywhere:
        specs[at] = ANY_SPEC
    return list(
        pl.pallas_call(
            body,
            out_shape=outs,
            in_specs=specs,
            out_specs=[ANY_SPEC if outs_anywhere else VMEM_SPEC] * len(outs),
            scratch_shapes=list(scratch),
            compiler_params=pltpu.CompilerParams(vmem_limit_bytes=limit * MIB),
            cost_estimate=pl.CostEstimate(flops=flops, bytes_accessed=moved, transcendentals=0),
        )(*operands)
    )


def struct(shape, dtype):
    return jax.ShapeDtypeStruct(shape, dtype)


def row_scales(square_sum):
    return lax.rsqrt(square_sum + EPS)


def column_of(row):
    return jnp.broadcast_to(row, (TILE, TILE)).T


def dot_nt(left, right):
    return lax.dot_general(
        left, right, (((1,), (1,)), ((), ())), preferred_element_type=jnp.float32
    )


def dot_tn(left, right):
    return lax.dot_general(
        left, right, (((0,), (0,)), ((), ())), preferred_element_type=jnp.float32
    )


def peer_bits(k, chunks):
    return (chunks - k) % chunks


def feature_slice(peer, width):
    return pl.ds(pl.multiple_of(peer * width, width), width)


def pick_body(text_ref, *out_refs):
    place = lax.axis_index("tp")
    rows = out_refs[0].shape[0]
    for k, out_ref in enumerate(out_refs):
        peer = place ^ peer_bits(k, len(out_refs))
        out_ref[...] = text_ref[pl.ds(pl.multiple_of(peer * rows, rows), rows), :]


def unit_text_body(chunks, *refs):
    chunk_refs, (unit_ref, scale_ref) = refs[:chunks], refs[chunks : chunks + 2]
    piece_refs = refs[chunks + 2 :]
    place = lax.axis_index("tp")
    rows, width = chunk_refs[0].shape
    for first in range(0, rows, TILE):
        part = pl.ds(first, TILE)
        parts = [ref[part, :].astype(jnp.float32) for ref in chunk_refs]
        scales = row_scales(sum(jnp.sum(x * x, axis=-1, keepdims=True) for x in parts))
        scale_ref[part, :] = jnp.broadcast_to(scales, (TILE, TILE))
        for k, x in enumerate(parts):
            unit_ref[part, feature_slice(place ^ peer_bits(k, chunks), width)] = (x * scales).astype(jnp.bfloat16)
    split_rows(unit_ref, piece_refs)


def split_rows(whole_ref, piece_refs):
    for at, ref in enumerate(piece_refs):
        ref[...] = whole_ref[pl.ds(at * ref.shape[0], ref.shape[0]), :]


def join_rows(piece_refs, whole_ref):
    for at, ref in enumerate(piece_refs):
        whole_ref[pl.ds(at * ref.shape[0], ref.shape[0]), :] = ref[...]


def unit_images(ref, image_ref, scale_ref=None):
    step = 64
    for first in range(0, ref.shape[0], step):
        part = pl.ds(first, step)
        values = ref[part, :].astype(jnp.float32)
        scales = row_scales(jnp.sum(values * values, axis=-1, keepdims=True))
        image_ref[part, :] = (values * scales).astype(jnp.bfloat16)
        if scale_ref is not None:
            scale_ref[part, :] = jnp.broadcast_to(scales, (step, TILE))


def unit_images_body(raw_ref, out_ref):
    unit_images(raw_ref, out_ref)


def own_images_body(raw_ref, out_ref, raw_out_ref, scale_ref):
    unit_images(raw_ref, out_ref, scale_ref)
    raw_out_ref[...] = raw_ref[...]


def near_images_body(first_ref, second_unit_ref, out_ref):
    rows = first_ref.shape[0]
    unit_images(first_ref, out_ref)
    out_ref[rows:, :] = second_unit_ref[...]


def neighbour_bits(shard):
    core = shard % CORES
    return 2 << core, 4 >> core


def list_body(groups, tiles, chips, *refs):
    scale_ref, bias_ref, blocks_ref, bucket_ref, positive_ref = refs[:5]
    line_ref, amount_ref, column_ref, row_ref, match_ref, own_ref = refs[5:]
    here, place = lax.axis_index("blk"), lax.axis_index("tp")
    scale = scale_ref[0]
    line_ref[pl.ds(0, 1), :] = jnp.full((1, TILE), -scale * LOG2E, jnp.float32)
    line_ref[pl.ds(1, 1), :] = jnp.full((1, TILE), -bias_ref[0] * LOG2E, jnp.float32)
    if chips == 4:
        first, second = neighbour_bits(here)
        shards = [here, here ^ first, here ^ second, here ^ 6]
    else:
        shards = [chip * CORES + here % CORES for chip in range(chips)]
    count = len(shards) * tiles

    def first_tile(shard):
        return (shard * groups + place) * tiles

    for n, shard in enumerate(shards):
        own_ref[pl.ds(n, 1), :] = jnp.full((1, TILE), jnp.where(shard == here, 1.0, 0.0))
        for j in range(tiles):
            column_ref[pl.ds(n * tiles + j, 1), :] = bucket_ref[pl.ds(first_tile(shard) + j, 1), :]
    for at in range(CORES * tiles):
        tile = first_tile(here ^ (at // tiles)) + at % tiles
        row_ref[pl.ds(at * TILE, TILE), :] = column_of(bucket_ref[pl.ds(tile, 1), :])
        if at < tiles:
            ids = lax.broadcasted_iota(jnp.int32, (1, TILE), 1) + tile * TILE
            matched = column_of(positive_ref[pl.ds(tile, 1), :]) == ids
            match_ref[pl.ds(at * TILE, TILE), :] = jnp.where(matched, 1.0, 0.0)
        for n, shard in enumerate(shards):
            entries = [blocks_ref[slot, shard, tile] for slot in range(SLOTS)]
            for j in range(tiles):
                listed = sum(jnp.where(entry == j, 1.0, 0.0) for entry in entries)
                amount_ref[pl.ds(at * count + n * tiles + j, 1), :] = jnp.full(
                    (1, TILE), scale * listed, jnp.float32
                )


class Pairs:
    count = 6

    def __init__(self, refs, tiles):
        self.line_ref, self.amount_ref, self.column_ref = refs[:3]
        self.row_ref, self.match_ref, self.own_ref = refs[3:6]
        self.tiles = tiles

    def weigh(self, products, half, group, weight_ref, top, left, own=None):
        tiles = self.tiles
        slope, offset = self.line_ref[pl.ds(0, 1), :], self.line_ref[pl.ds(1, 1), :]
        count = self.column_ref.shape[0]
        for a in range(tiles):
            at = half * tiles + a
            row_bucket = self.row_ref[pl.ds(at * TILE, TILE), :]
            for j in range(tiles):
                n = group * tiles + j
                amount = self.amount_ref[pl.ds(at * count + n, 1), :]
                power = (
                    products[a * TILE : (a + 1) * TILE, j * TILE : (j + 1) * TILE] * slope + offset
                )
                factor = jnp.where(row_bucket == self.column_ref[pl.ds(n, 1), :], amount, 0.0)
                if own and a == j:
                    match = self.match_ref[pl.ds(a * TILE, TILE), :]
                    if own == "search":
                        match = match * self.own_ref[pl.ds(group, 1), :]
                    power = jnp.where(match > 0.0, -power, power)
                    factor = jnp.where(match > 0.0, -amount, factor)
                below = 1.0 + jnp.exp2(power)
                inverse = pl.reciprocal(below, approx=True)
                inverse = inverse * (2.0 - below * inverse)
                weight_ref[pl.ds(top + a * TILE, TILE), pl.ds(left + j * TILE, TILE)] = (
                    factor * inverse
                ).astype(jnp.bfloat16)


def near_own_body(tiles, *refs):
    pairs = Pairs(refs, tiles)
    unit_ref, own_image_ref, near_image_ref, own_weight_ref, weight_ref = refs[Pairs.count :]
    rows = unit_ref.shape[0]
    first = dot_nt(unit_ref[...], near_image_ref[pl.ds(0, rows), :])
    second = dot_nt(unit_ref[...], near_image_ref[pl.ds(rows, rows), :])
    pairs.weigh(first, 0, 1, weight_ref, 0, 0)
    own = dot_nt(unit_ref[...], own_image_ref[...])
    pairs.weigh(second, 0, 2, weight_ref, 0, rows)
    pairs.weigh(own, 0, 0, own_weight_ref, 0, 0, "diagonal")


def first_sum_body(tiles, *refs):
    pairs = Pairs(refs, tiles)
    own_unit_ref, near_image_ref, weight_in_ref = refs[Pairs.count : Pairs.count + 3]
    piece_refs = refs[Pairs.count + 3 : Pairs.count + 3 + TEXT_PIECES]
    unit_ref, weight_ref, sum_ref = refs[Pairs.count + 3 + TEXT_PIECES :]
    rows = own_unit_ref.shape[0]
    for at, ref in enumerate(piece_refs):
        unit_ref[pl.ds(rows + at * ref.shape[0], ref.shape[0]), :] = ref[...]
    unit_ref[:rows, :] = own_unit_ref[...]
    weight_ref[:rows, :] = weight_in_ref[:, :rows]
    products = dot_nt(unit_ref[rows:, :], near_image_ref[pl.ds(0, rows), :])
    pairs.weigh(products, 1, 1, weight_ref, rows, 0)
    sum_ref[...] = dot_tn(weight_ref[...], unit_ref[...]).astype(jnp.bfloat16)


def near_sum_body(tiles, *refs):
    pairs = Pairs(refs, tiles)
    unit_ref, own_image_ref, near_image_ref, own_weight_in_ref, weight_in_ref, first_ref = refs[
        Pairs.count : Pairs.count + 6
    ]
    own_weight_ref, acc_ref, sum_ref, weight_ref = refs[Pairs.count + 6 :]
    rows = own_image_ref.shape[0]
    second = dot_nt(unit_ref[rows:, :], near_image_ref[pl.ds(rows, rows), :])
    own = dot_nt(unit_ref[rows:, :], own_image_ref[...])
    own_weight_ref[:rows, :] = own_weight_in_ref[...]
    weight_ref[:, :rows] = first_ref[...]
    weight_ref[:rows, rows:] = weight_in_ref[:, rows:]
    pairs.weigh(second, 1, 2, weight_ref, rows, rows)
    sum_ref[...] = dot_tn(weight_ref[:, rows:], unit_ref[...]).astype(jnp.bfloat16)
    pairs.weigh(own, 1, 0, own_weight_ref, rows, 0)
    acc_ref[...] = jnp.dot(
        weight_ref[...], near_image_ref[...], preferred_element_type=jnp.float32
    )


def far_weights_body(tiles, *refs):
    pairs = Pairs(refs, tiles)
    unit_ref, own_image_ref, own_weight_ref, raw_ref = refs[Pairs.count : Pairs.count + 4]
    weight_ref, image_ref = refs[Pairs.count + 4 :]
    rows = raw_ref.shape[0]
    unit_images(raw_ref, image_ref.at[pl.ds(rows, rows), :])
    products = dot_nt(unit_ref[...], image_ref[rows:, :])
    for half in range(CORES):
        part = products[half * rows : (half + 1) * rows, :]
        pairs.weigh(part, half, 3, weight_ref, half * rows, rows)
    image_ref[:rows, :] = own_image_ref[...]
    weight_ref[:, :rows] = own_weight_ref[...]


def far_sum_body(weight_ref, unit_ref, out_ref):
    rows = out_ref.shape[0]
    out_ref[...] = dot_tn(weight_ref[:, rows:], unit_ref[...]).astype(jnp.bfloat16)


def text_sum_body(half, weight_ref, image_ref, acc_ref, *out_refs):
    rows = weight_ref.shape[0] // CORES
    size = out_refs[0].shape[0]
    part = pl.ds(half * rows, rows)
    acc = acc_ref[part, :] + jnp.dot(
        weight_ref[part, :], image_ref[...], preferred_element_type=jnp.float32
    )
    for at, ref in enumerate(out_refs):
        ref[...] = acc[at * size : (at + 1) * size, :].astype(ref.dtype)


def own_sum_body(weight_ref, unit_ref, first_ref, second_ref, out_ref):
    total = dot_tn(weight_ref[...], unit_ref[...])
    out_ref[...] = total + first_ref[...].astype(jnp.float32) + second_ref[...].astype(jnp.float32)


def all_body(tiles, chips, *refs):
    pairs = Pairs(refs, tiles)
    own_ref, other_ref, piece_ref = refs[Pairs.count : Pairs.count + 3]
    outs = refs[Pairs.count + 3 :]
    spread_ref, acc_ref, acc_piece_refs = outs[0], outs[1], outs[2 : 2 + ACC_PIECES]
    image_ref, weight_ref = outs[2 + ACC_PIECES :]
    rows = own_ref.shape[0]
    unit_images(piece_ref, image_ref)
    for half, text_ref in enumerate((own_ref, other_ref)):
        for chip in range(chips):
            products = dot_nt(text_ref[...], image_ref[pl.ds(chip * rows, rows), :])
            pairs.weigh(
                products, half, chip, weight_ref, half * rows, chip * rows, None if half else "search"
            )
        acc = jnp.dot(
            weight_ref[pl.ds(half * rows, rows), :],
            image_ref[...],
            preferred_element_type=jnp.float32,
        )
        if half == 0:
            acc_ref[...] = acc
            continue
        size = rows // ACC_PIECES
        for at, ref in enumerate(acc_piece_refs):
            ref[...] = acc[at * size : (at + 1) * size, :].astype(jnp.bfloat16)
    for chip in range(chips):
        columns = pl.ds(chip * rows, rows)
        total = dot_tn(weight_ref[pl.ds(0, rows), columns], own_ref[...])
        total += dot_tn(weight_ref[pl.ds(rows, rows), columns], other_ref[...])
        spread_ref[columns, :] = total.astype(jnp.bfloat16)


def text_grad_body(chunks, *refs):
    scale_ref, raw_refs, acc_ref = refs[0], refs[1 : 1 + chunks], refs[1 + chunks]
    add_refs, out_refs = refs[2 + chunks : -chunks], refs[-chunks:]
    place = lax.axis_index("tp")
    rows, width = raw_refs[0].shape
    size = add_refs[0].shape[0]
    for first in range(0, rows, TILE // 2):
        part = pl.ds(first, TILE // 2)
        scales = scale_ref[part, :1]
        raws = [ref[part, :].astype(jnp.float32) for ref in raw_refs]
        accs = []
        for k in range(chunks):
            features = feature_slice(place ^ peer_bits(k, chunks), width)
            added = add_refs[first // size][pl.ds(first % size, TILE // 2), features]
            accs.append(acc_ref[part, features] + added.astype(jnp.float32))
        inner = sum(jnp.sum(x * a, axis=-1, keepdims=True) for x, a in zip(raws, accs))
        inner = inner * scales * scales
        for k in range(chunks):
            out_refs[k][part, :] = (scales * (accs[k] - raws[k] * inner)).astype(jnp.bfloat16)


def place_text_body(chunks, *refs):
    part_refs, out_ref, sems = refs[:chunks], refs[chunks], refs[chunks + 1]
    place = lax.axis_index("tp")
    rows = part_refs[0].shape[0]
    copies = []
    for k in range(chunks):
        peer = place ^ peer_bits(k, chunks)
        block = pl.ds(pl.multiple_of(peer * rows, rows), rows)
        copies.append(pltpu.make_async_copy(part_refs[k], out_ref.at[block, :], sems.at[k]))
    for copy in copies:
        copy.start()
    for copy in copies:
        copy.wait()


def image_grad_body(raw_ref, scale_ref, sum_ref, *refs):
    add_refs, (out_ref, grad_ref, sems) = refs[:-3], refs[-3:]
    copies = []
    for block in range(raw_ref.shape[0] // TILE):
        for first in range(block * TILE, (block + 1) * TILE, TILE // 2):
            part = pl.ds(first, TILE // 2)
            raw = raw_ref[part, :].astype(jnp.float32)
            scales = scale_ref[part, :1]
            acc = sum_ref[part, :]
            for ref in add_refs:
                acc = acc + ref[part, :].astype(jnp.float32)
            inner = jnp.sum(raw * acc, axis=-1, keepdims=True) * scales * scales
            grad_ref[part, :] = (scales * (acc - raw * inner)).astype(jnp.bfloat16)
        part = pl.ds(block * TILE, TILE)
        copies.append(
            pltpu.make_async_copy(grad_ref.at[part, :], out_ref.at[part, :], sems.at[block])
        )
        copies[-1].start()
    for copy in copies:
        copy.wait()


def swap(value, axis, bits):
    count = lax.axis_size(axis)
    return lax.ppermute(value, axis, [(i, i ^ bits) for i in range(count)])


def swap_near(value, which):
    count = lax.axis_size("blk")
    return lax.ppermute(value, "blk", [(i, i ^ neighbour_bits(i)[which]) for i in range(count)])


def swap_chunks(chunks):
    count = len(chunks)
    return chunks[:1] + [swap(chunks[k], "tp", peer_bits(k, count)) for k in range(1, count)]


def per_device(text_emb, image_emb, logit_scale, logit_bias, bucket, positive, blocks):
    groups = lax.axis_size("tp")
    shards = lax.axis_size("blk")
    chips = shards // CORES
    rows, embed = image_emb.shape
    tiles = rows // TILE
    width = text_emb.shape[1]
    square = chips == 4

    def bf16(count, columns=embed):
        return struct((count, columns), jnp.bfloat16)

    def f32(count, columns=embed):
        return struct((count, columns), jnp.float32)

    def i32(count, columns):
        return struct((count, columns), jnp.int32)

    picked = call_kernel(pick_body, [bf16(rows, width)] * groups, [text_emb], limit=8)
    text_raw = swap_chunks(picked)
    if square:
        from_second = swap_near(image_emb, 1)
    else:
        same_core = [[chip * CORES + core for chip in range(chips)] for core in range(CORES)]
        gathered = lax.all_gather(
            image_emb, "blk", axis=0, tiled=True, axis_index_groups=same_core
        )
        _, image_raw, image_scales = call_kernel(
            own_images_body, [bf16(rows), bf16(rows), f32(rows, TILE)], [image_emb], limit=8
        )
    lists = call_kernel(
        functools.partial(list_body, groups, tiles, chips),
        [
            f32(2, TILE),
            f32(CORES * tiles * chips * tiles, TILE),
            i32(chips * tiles, TILE),
            i32(CORES * rows, TILE),
            f32(rows, TILE),
            f32(chips, TILE),
        ],
        [
            logit_scale,
            logit_bias,
            blocks.transpose(2, 1, 0),
            bucket.reshape(-1, TILE),
            positive.reshape(-1, TILE),
        ],
        scalars=3,
        limit=8,
    )
    if square:
        own_images, image_raw, image_scales = call_kernel(
            own_images_body, [bf16(rows), bf16(rows), f32(rows, TILE)], [image_emb], limit=8
        )
        image_sent, own_images = lax.optimization_barrier((image_emb, own_images))
        from_first = swap_near(image_sent, 0)
        from_second, own_images, *lists = lax.optimization_barrier(
            (from_second, own_images, *lists)
        )
        from_far = swap_near(from_second, 0)
        second_images = call_kernel(
            unit_images_body, [bf16(rows)], [from_second], flops=WAIT_FLOPS // 2, limit=8
        )[0]
        text_raw[-1], second_images = lax.optimization_barrier((text_raw[-1], second_images))
    text_own, text_scales, *pieces = call_kernel(
        functools.partial(unit_text_body, groups),
        [bf16(rows), f32(rows, TILE)] + [bf16(rows // TEXT_PIECES)] * TEXT_PIECES,
        text_raw,
        limit=8,
    )
    text_other = [swap(piece, "blk", 1) for piece in pieces]
    if square:
        from_first, text_own = lax.optimization_barrier((from_first, text_own))
        near_images = call_kernel(
            near_images_body, [bf16(2 * rows)], [from_first, second_images], limit=8
        )[0]
    unit_flops = 2 * rows * rows * embed

    def finish_text(acc_own, acc_other):
        parts = call_kernel(
            functools.partial(text_grad_body, groups),
            [bf16(rows, width)] * groups,
            [text_scales] + text_raw + [acc_own] + [swap(piece, "blk", 1) for piece in acc_other],
            limit=16,
        )
        return swap_chunks(parts)

    def place_text(text_parts):
        return call_kernel(
            functools.partial(place_text_body, groups),
            [bf16(groups * rows, width)],
            text_parts,
            outs_anywhere=True,
            scratch=[pltpu.SemaphoreType.DMA((groups,))],
            flops=WAIT_FLOPS,
            limit=8,
        )[0]

    def finish_image(total, adds):
        return call_kernel(
            image_grad_body,
            [bf16(rows)],
            [image_raw, image_scales, total] + adds,
            outs_anywhere=True,
            scratch=[pltpu.VMEM((rows, embed), jnp.bfloat16), pltpu.SemaphoreType.DMA((tiles,))],
            limit=8,
        )[0]

    if not square:
        columns = gathered.shape[0]
        spread, acc_own, *acc_other = call_kernel(
            functools.partial(all_body, tiles, chips),
            [bf16(columns), f32(rows)] + [bf16(rows // ACC_PIECES)] * ACC_PIECES,
            lists + [text_own, jnp.concatenate(text_other), gathered],
            scratch=[
                pltpu.VMEM((columns, embed), jnp.bfloat16),
                pltpu.VMEM((2 * rows, columns), jnp.bfloat16),
            ],
            flops=6 * chips * unit_flops,
            limit=56,
        )
        text_parts = finish_text(acc_own, acc_other)
        parts = lax.all_to_all(
            spread, "blk", split_axis=0, concat_axis=0, tiled=True, axis_index_groups=same_core
        )
        total = jnp.sum(parts.reshape(-1, rows, embed).astype(jnp.float32), axis=0)
        return (place_text(text_parts), finish_image(total, []))

    own_weights, near_weights = call_kernel(
        functools.partial(near_own_body, tiles),
        [bf16(rows, rows), bf16(rows, 2 * rows)],
        lists + [text_own, own_images, near_images],
        limit=16,
    )
    units, first_weights, first_sum = call_kernel(
        functools.partial(first_sum_body, tiles),
        [bf16(2 * rows), bf16(2 * rows, rows), bf16(rows)],
        lists + [text_own, near_images, near_weights] + text_other,
        limit=16,
    )
    image_add = swap_near(first_sum, 0)
    own_weights, acc, second_sum = call_kernel(
        functools.partial(near_sum_body, tiles),
        [bf16(2 * rows, rows), f32(2 * rows), bf16(rows)],
        lists + [units, own_images, near_images, own_weights, near_weights, first_weights],
        scratch=[pltpu.VMEM((2 * rows, 2 * rows), jnp.bfloat16)],
        limit=24,
    )
    second_add = swap_near(second_sum, 1)
    own_weights, from_far = lax.optimization_barrier((own_weights, from_far))
    far_weights, far_images = call_kernel(
        functools.partial(far_weights_body, tiles),
        [bf16(2 * rows, 2 * rows), bf16(2 * rows)],
        lists + [units, own_images, own_weights, from_far],
        limit=16,
    )
    acc_other = call_kernel(
        functools.partial(text_sum_body, 1),
        [bf16(rows // ACC_PIECES)] * ACC_PIECES,
        [far_weights, far_images, acc],
        limit=16,
    )
    far_images, acc_other[0] = lax.optimization_barrier((far_images, acc_other[0]))
    acc_own = call_kernel(
        functools.partial(text_sum_body, 0),
        [f32(rows)],
        [far_weights, far_images, acc],
        limit=16,
    )[0]
    far_weights, acc_own = lax.optimization_barrier((far_weights, acc_own))
    far_sum = call_kernel(far_sum_body, [bf16(rows)], [far_weights, units], limit=16)[0]
    acc_own, far_sum = lax.optimization_barrier((acc_own, far_sum))
    text_parts = finish_text(acc_own, acc_other)
    far_add = swap(far_sum, "blk", 6)
    own_weights, text_parts[0] = lax.optimization_barrier((own_weights, text_parts[0]))
    base = call_kernel(
        own_sum_body,
        [f32(rows)],
        [own_weights, units, image_add, second_add],
        flops=WAIT_FLOPS,
        limit=16,
    )[0]
    text_grad = place_text(text_parts)
    base, _ = lax.optimization_barrier((base, text_grad))
    return (text_grad, finish_image(base, [far_add]))


def solution(mesh):
    in_specs = (P("blk", "tp"), P(("blk", "tp"), None), P(), P(), P(), P(), P())
    out_specs = (P("blk", "tp"), P(("blk", "tp"), None))
    return jax.shard_map(
        per_device, mesh=mesh, in_specs=in_specs, out_specs=out_specs, check_vma=False
    )
```

```python
import functools
import math

import jax
import jax.numpy as jnp
from jax import lax
from jax.experimental import pallas as pl
from jax.experimental.pallas import tpu as pltpu
from jax.sharding import PartitionSpec as P

TILE = 128
SLOTS = 3
WAIT_FLOPS = 20_000_000_000
TEXT_PIECES = 3
ACC_PIECES = 2
LAST_PIECES = 2
CORES = 2
EPS = 1e-06
LOG2E = math.log2(math.e)
MIB = 1024 * 1024

VMEM_SPEC = pl.BlockSpec(memory_space=pltpu.VMEM)
ANY_SPEC = pl.BlockSpec(memory_space=pl.ANY)
SMEM_SPEC = pl.BlockSpec(memory_space=pltpu.SMEM)


def call_kernel(
    body,
    outs,
    operands,
    scalars=0,
    anywhere=(),
    outs_anywhere=False,
    scratch=(),
    flops=0,
    moved=None,
    limit=24,
):
    if moved is None:
        moved = sum(x.size * x.dtype.itemsize for x in operands)
        moved += sum(math.prod(o.shape) * o.dtype.itemsize for o in outs)
    specs = [SMEM_SPEC] * scalars + [VMEM_SPEC] * (len(operands) - scalars)
    for at in anywhere:
        specs[at] = ANY_SPEC
    return list(
        pl.pallas_call(
            body,
            out_shape=outs,
            in_specs=specs,
            out_specs=[ANY_SPEC if outs_anywhere else VMEM_SPEC] * len(outs),
            scratch_shapes=list(scratch),
            compiler_params=pltpu.CompilerParams(vmem_limit_bytes=limit * MIB),
            cost_estimate=pl.CostEstimate(flops=flops, bytes_accessed=moved, transcendentals=0),
        )(*operands)
    )


def struct(shape, dtype):
    return jax.ShapeDtypeStruct(shape, dtype)


def row_scales(square_sum):
    return lax.rsqrt(square_sum + EPS)


def column_of(row):
    return jnp.broadcast_to(row, (TILE, TILE)).T


def dot_nt(left, right):
    return lax.dot_general(
        left, right, (((1,), (1,)), ((), ())), preferred_element_type=jnp.float32
    )


def dot_tn(left, right):
    return lax.dot_general(
        left, right, (((0,), (0,)), ((), ())), preferred_element_type=jnp.float32
    )


def far_first(k, chunks):
    return (chunks - k) % chunks


def feature_slice(peer, width):
    return pl.ds(pl.multiple_of(peer * width, width), width)


def pick_body(text_ref, *out_refs):
    place = lax.axis_index("tp")
    rows = out_refs[0].shape[0]
    for k, out_ref in enumerate(out_refs):
        out_ref[...] = text_ref[pl.ds(pl.multiple_of((place ^ k) * rows, rows), rows), :]


def unit_text_body(chunks, *refs):
    chunk_refs, (unit_ref, scale_ref) = refs[:chunks], refs[chunks : chunks + 2]
    piece_refs = refs[chunks + 2 :]
    place = lax.axis_index("tp")
    rows, width = chunk_refs[0].shape
    for first in range(0, rows, TILE):
        part = pl.ds(first, TILE)
        parts = [ref[part, :].astype(jnp.float32) for ref in chunk_refs]
        scales = row_scales(sum(jnp.sum(x * x, axis=-1, keepdims=True) for x in parts))
        scale_ref[part, :] = jnp.broadcast_to(scales, (TILE, TILE))
        for k, x in enumerate(parts):
            unit_ref[part, feature_slice(place ^ k, width)] = (x * scales).astype(jnp.bfloat16)
    split_rows(unit_ref, piece_refs)


def split_rows(whole_ref, piece_refs):
    for at, ref in enumerate(piece_refs):
        ref[...] = whole_ref[pl.ds(at * ref.shape[0], ref.shape[0]), :]


def join_rows(piece_refs, whole_ref):
    for at, ref in enumerate(piece_refs):
        whole_ref[pl.ds(at * ref.shape[0], ref.shape[0]), :] = ref[...]


def unit_images(ref, image_ref, scale_ref=None):
    step = 64
    for first in range(0, ref.shape[0], step):
        part = pl.ds(first, step)
        values = ref[part, :].astype(jnp.float32)
        scales = row_scales(jnp.sum(values * values, axis=-1, keepdims=True))
        image_ref[part, :] = (values * scales).astype(jnp.bfloat16)
        if scale_ref is not None:
            scale_ref[part, :] = jnp.broadcast_to(scales, (step, TILE))


def unit_images_body(raw_ref, out_ref):
    unit_images(raw_ref, out_ref)


def own_images_body(raw_ref, out_ref, raw_out_ref, scale_ref):
    unit_images(raw_ref, out_ref, scale_ref)
    raw_out_ref[...] = raw_ref[...]


def near_images_body(first_ref, second_unit_ref, out_ref):
    rows = first_ref.shape[0]
    unit_images(first_ref, out_ref)
    out_ref[rows:, :] = second_unit_ref[...]


def neighbour_bits(shard):
    core = shard % CORES
    return 2 << core, 4 >> core


def list_body(groups, tiles, chips, *refs):
    scale_ref, bias_ref, blocks_ref, bucket_ref, positive_ref = refs[:5]
    line_ref, amount_ref, column_ref, row_ref, match_ref, own_ref = refs[5:]
    here, place = lax.axis_index("blk"), lax.axis_index("tp")
    scale = scale_ref[0]
    line_ref[pl.ds(0, 1), :] = jnp.full((1, TILE), -scale * LOG2E, jnp.float32)
    line_ref[pl.ds(1, 1), :] = jnp.full((1, TILE), -bias_ref[0] * LOG2E, jnp.float32)
    if chips == 4:
        first, second = neighbour_bits(here)
        shards = [here, here ^ first, here ^ second, here ^ 6]
    else:
        shards = [chip * CORES + here % CORES for chip in range(chips)]
    count = len(shards) * tiles

    def first_tile(shard):
        return (shard * groups + place) * tiles

    for n, shard in enumerate(shards):
        own_ref[pl.ds(n, 1), :] = jnp.full((1, TILE), jnp.where(shard == here, 1.0, 0.0))
        for j in range(tiles):
            column_ref[pl.ds(n * tiles + j, 1), :] = bucket_ref[pl.ds(first_tile(shard) + j, 1), :]
    for at in range(CORES * tiles):
        tile = first_tile(here ^ (at // tiles)) + at % tiles
        row_ref[pl.ds(at * TILE, TILE), :] = column_of(bucket_ref[pl.ds(tile, 1), :])
        if at < tiles:
            ids = lax.broadcasted_iota(jnp.int32, (1, TILE), 1) + tile * TILE
            matched = column_of(positive_ref[pl.ds(tile, 1), :]) == ids
            match_ref[pl.ds(at * TILE, TILE), :] = jnp.where(matched, 1.0, 0.0)
        for n, shard in enumerate(shards):
            entries = [blocks_ref[slot, shard, tile] for slot in range(SLOTS)]
            for j in range(tiles):
                listed = sum(jnp.where(entry == j, 1.0, 0.0) for entry in entries)
                amount_ref[pl.ds(at * count + n * tiles + j, 1), :] = jnp.full(
                    (1, TILE), scale * listed, jnp.float32
                )


class Pairs:
    count = 6

    def __init__(self, refs, tiles):
        self.line_ref, self.amount_ref, self.column_ref = refs[:3]
        self.row_ref, self.match_ref, self.own_ref = refs[3:6]
        self.tiles = tiles

    def weigh(self, products, half, group, weight_ref, top, left, own=None):
        tiles = self.tiles
        slope, offset = self.line_ref[pl.ds(0, 1), :], self.line_ref[pl.ds(1, 1), :]
        count = self.column_ref.shape[0]
        for a in range(tiles):
            at = half * tiles + a
            row_bucket = self.row_ref[pl.ds(at * TILE, TILE), :]
            for j in range(tiles):
                n = group * tiles + j
                amount = self.amount_ref[pl.ds(at * count + n, 1), :]
                power = (
                    products[a * TILE : (a + 1) * TILE, j * TILE : (j + 1) * TILE] * slope + offset
                )
                factor = jnp.where(row_bucket == self.column_ref[pl.ds(n, 1), :], amount, 0.0)
                if own and a == j:
                    match = self.match_ref[pl.ds(a * TILE, TILE), :]
                    if own == "search":
                        match = match * self.own_ref[pl.ds(group, 1), :]
                    power = jnp.where(match > 0.0, -power, power)
                    factor = jnp.where(match > 0.0, -amount, factor)
                below = 1.0 + jnp.exp2(power)
                inverse = pl.reciprocal(below, approx=True)
                inverse = inverse * (2.0 - below * inverse)
                weight_ref[pl.ds(top + a * TILE, TILE), pl.ds(left + j * TILE, TILE)] = (
                    factor * inverse
                ).astype(jnp.bfloat16)


def near_own_body(tiles, *refs):
    pairs = Pairs(refs, tiles)
    unit_ref, own_image_ref, near_image_ref, own_weight_ref, weight_ref = refs[Pairs.count :]
    rows = unit_ref.shape[0]
    first = dot_nt(unit_ref[...], near_image_ref[pl.ds(0, rows), :])
    second = dot_nt(unit_ref[...], near_image_ref[pl.ds(rows, rows), :])
    pairs.weigh(first, 0, 1, weight_ref, 0, 0)
    own = dot_nt(unit_ref[...], own_image_ref[...])
    pairs.weigh(second, 0, 2, weight_ref, 0, rows)
    pairs.weigh(own, 0, 0, own_weight_ref, 0, 0, "diagonal")


def first_sum_body(tiles, *refs):
    pairs = Pairs(refs, tiles)
    own_unit_ref, near_image_ref, weight_in_ref = refs[Pairs.count : Pairs.count + 3]
    piece_refs = refs[Pairs.count + 3 : Pairs.count + 3 + TEXT_PIECES]
    unit_ref, weight_ref, sum_ref = refs[Pairs.count + 3 + TEXT_PIECES :]
    rows = own_unit_ref.shape[0]
    for at, ref in enumerate(piece_refs):
        unit_ref[pl.ds(rows + at * ref.shape[0], ref.shape[0]), :] = ref[...]
    unit_ref[:rows, :] = own_unit_ref[...]
    weight_ref[:rows, :] = weight_in_ref[:, :rows]
    products = dot_nt(unit_ref[rows:, :], near_image_ref[pl.ds(0, rows), :])
    pairs.weigh(products, 1, 1, weight_ref, rows, 0)
    sum_ref[...] = dot_tn(weight_ref[...], unit_ref[...]).astype(jnp.bfloat16)


def near_sum_body(tiles, *refs):
    pairs = Pairs(refs, tiles)
    unit_ref, own_image_ref, near_image_ref, own_weight_in_ref, weight_in_ref, first_ref = refs[
        Pairs.count : Pairs.count + 6
    ]
    own_weight_ref, acc_ref, weight_ref = refs[Pairs.count + 6 :]
    rows = own_image_ref.shape[0]
    second = dot_nt(unit_ref[rows:, :], near_image_ref[pl.ds(rows, rows), :])
    own = dot_nt(unit_ref[rows:, :], own_image_ref[...])
    own_weight_ref[:rows, :] = own_weight_in_ref[...]
    weight_ref[:, :rows] = first_ref[...]
    weight_ref[:rows, rows:] = weight_in_ref[:, rows:]
    pairs.weigh(second, 1, 2, weight_ref, rows, rows)
    pairs.weigh(own, 1, 0, own_weight_ref, rows, 0)
    acc_ref[...] = jnp.dot(
        weight_ref[...], near_image_ref[...], preferred_element_type=jnp.float32
    )


def far_weights_body(tiles, *refs):
    pairs = Pairs(refs, tiles)
    unit_ref, own_image_ref, own_weight_ref, raw_ref = refs[Pairs.count : Pairs.count + 4]
    weight_ref, image_ref = refs[Pairs.count + 4 :]
    rows = raw_ref.shape[0]
    unit_images(raw_ref, image_ref.at[pl.ds(rows, rows), :])
    products = dot_nt(unit_ref[...], image_ref[rows:, :])
    for half in range(CORES):
        part = products[half * rows : (half + 1) * rows, :]
        pairs.weigh(part, half, 3, weight_ref, half * rows, rows)
    image_ref[:rows, :] = own_image_ref[...]
    weight_ref[:, :rows] = own_weight_ref[...]


def far_sum_body(weight_ref, unit_ref, *out_refs):
    rows = weight_ref.shape[1] // 2
    total = dot_tn(weight_ref[:, rows:], unit_ref[...]).astype(jnp.bfloat16)
    size = rows // len(out_refs)
    for at, ref in enumerate(out_refs):
        ref[...] = total[at * size : (at + 1) * size, :]


def text_sum_body(half, weight_ref, image_ref, acc_ref, *out_refs):
    rows = weight_ref.shape[0] // CORES
    size = out_refs[0].shape[0]
    part = pl.ds(half * rows, rows)
    acc = acc_ref[part, :] + jnp.dot(
        weight_ref[part, :], image_ref[...], preferred_element_type=jnp.float32
    )
    for at, ref in enumerate(out_refs):
        ref[...] = acc[at * size : (at + 1) * size, :].astype(ref.dtype)


def own_sum_body(own_weight_ref, near_weight_ref, unit_ref, add_ref, own_ref, second_ref):
    rows = own_ref.shape[0]
    second_ref[...] = dot_tn(near_weight_ref[:, rows:], unit_ref[...])
    own_ref[...] = dot_tn(own_weight_ref[...], unit_ref[...]) + add_ref[...].astype(jnp.float32)


def all_body(tiles, chips, *refs):
    pairs = Pairs(refs, tiles)
    own_ref, other_ref, piece_ref = refs[Pairs.count : Pairs.count + 3]
    outs = refs[Pairs.count + 3 :]
    spread_ref, acc_ref, acc_piece_refs = outs[0], outs[1], outs[2 : 2 + ACC_PIECES]
    image_ref, weight_ref = outs[2 + ACC_PIECES :]
    rows = own_ref.shape[0]
    unit_images(piece_ref, image_ref)
    for half, text_ref in enumerate((own_ref, other_ref)):
        for chip in range(chips):
            products = dot_nt(text_ref[...], image_ref[pl.ds(chip * rows, rows), :])
            pairs.weigh(
                products, half, chip, weight_ref, half * rows, chip * rows, None if half else "search"
            )
        acc = jnp.dot(
            weight_ref[pl.ds(half * rows, rows), :],
            image_ref[...],
            preferred_element_type=jnp.float32,
        )
        if half == 0:
            acc_ref[...] = acc
            continue
        size = rows // ACC_PIECES
        for at, ref in enumerate(acc_piece_refs):
            ref[...] = acc[at * size : (at + 1) * size, :].astype(jnp.bfloat16)
    for chip in range(chips):
        columns = pl.ds(chip * rows, rows)
        total = dot_tn(weight_ref[pl.ds(0, rows), columns], own_ref[...])
        total += dot_tn(weight_ref[pl.ds(rows, rows), columns], other_ref[...])
        spread_ref[columns, :] = total.astype(jnp.bfloat16)


def relay_body(at, sum_ref, in_ref, out_ref):
    size = in_ref.shape[0]
    part = sum_ref[pl.ds(at * size, size), :]
    out_ref[...] = (part + in_ref[...].astype(jnp.float32)).astype(jnp.bfloat16)


def text_grad_body(chunks, *refs):
    scale_ref, raw_refs, acc_ref = refs[0], refs[1 : 1 + chunks], refs[1 + chunks]
    add_refs, out_refs = refs[2 + chunks : -chunks], refs[-chunks:]
    place = lax.axis_index("tp")
    rows, width = raw_refs[0].shape
    size = add_refs[0].shape[0]
    for first in range(0, rows, TILE // 2):
        part = pl.ds(first, TILE // 2)
        scales = scale_ref[part, :1]
        raws = [ref[part, :].astype(jnp.float32) for ref in raw_refs]
        accs = []
        for k in range(chunks):
            features = feature_slice(place ^ k, width)
            added = add_refs[first // size][pl.ds(first % size, TILE // 2), features]
            accs.append(acc_ref[part, features] + added.astype(jnp.float32))
        inner = sum(jnp.sum(x * a, axis=-1, keepdims=True) for x, a in zip(raws, accs))
        inner = inner * scales * scales
        for k in range(chunks):
            out_refs[far_first(k, chunks)][part, :] = (
                scales * (accs[k] - raws[k] * inner)
            ).astype(jnp.bfloat16)


def place_text_body(chunks, *refs):
    part_refs, out_ref, sems = refs[:chunks], refs[chunks], refs[chunks + 1]
    place = lax.axis_index("tp")
    rows = part_refs[0].shape[0]
    copies = []
    for k in range(chunks):
        peer = place ^ far_first(k, chunks)
        block = pl.ds(pl.multiple_of(peer * rows, rows), rows)
        copies.append(pltpu.make_async_copy(part_refs[k], out_ref.at[block, :], sems.at[k]))
    for copy in copies:
        copy.start()
    for copy in copies:
        copy.wait()


def image_grad_body(piece_count, raw_ref, scale_ref, sum_ref, *refs):
    piece_refs, (out_ref, grad_ref, sems) = refs[:piece_count], refs[piece_count:]
    copies = []
    for block in range(raw_ref.shape[0] // TILE):
        for first in range(block * TILE, (block + 1) * TILE, TILE // 2):
            part = pl.ds(first, TILE // 2)
            raw = raw_ref[part, :].astype(jnp.float32)
            scales = scale_ref[part, :1]
            acc = sum_ref[part, :]
            if piece_refs:
                size = piece_refs[0].shape[0]
                piece = piece_refs[first // size][pl.ds(first % size, TILE // 2), :]
                acc = acc + piece.astype(jnp.float32)
            inner = jnp.sum(raw * acc, axis=-1, keepdims=True) * scales * scales
            grad_ref[part, :] = (scales * (acc - raw * inner)).astype(jnp.bfloat16)
        part = pl.ds(block * TILE, TILE)
        copies.append(
            pltpu.make_async_copy(grad_ref.at[part, :], out_ref.at[part, :], sems.at[block])
        )
        copies[-1].start()
    for copy in copies:
        copy.wait()


def swap(value, axis, bits):
    count = lax.axis_size(axis)
    return lax.ppermute(value, axis, [(i, i ^ bits) for i in range(count)])


def swap_near(value, which):
    count = lax.axis_size("blk")
    return lax.ppermute(value, "blk", [(i, i ^ neighbour_bits(i)[which]) for i in range(count)])


def per_device(text_emb, image_emb, logit_scale, logit_bias, bucket, positive, blocks):
    groups = lax.axis_size("tp")
    shards = lax.axis_size("blk")
    chips = shards // CORES
    rows, embed = image_emb.shape
    tiles = rows // TILE
    width = text_emb.shape[1]
    square = chips == 4

    def bf16(count, columns=embed):
        return struct((count, columns), jnp.bfloat16)

    def f32(count, columns=embed):
        return struct((count, columns), jnp.float32)

    def i32(count, columns):
        return struct((count, columns), jnp.int32)

    picked = call_kernel(pick_body, [bf16(rows, width)] * groups, [text_emb], limit=8)
    text_raw = picked[:1] + [swap(picked[k], "tp", k) for k in range(1, groups)]
    if square:
        from_second = swap_near(image_emb, 1)
    else:
        same_core = [[chip * CORES + core for chip in range(chips)] for core in range(CORES)]
        gathered = lax.all_gather(
            image_emb, "blk", axis=0, tiled=True, axis_index_groups=same_core
        )
        _, image_raw, image_scales = call_kernel(
            own_images_body, [bf16(rows), bf16(rows), f32(rows, TILE)], [image_emb], limit=8
        )
    lists = call_kernel(
        functools.partial(list_body, groups, tiles, chips),
        [
            f32(2, TILE),
            f32(CORES * tiles * chips * tiles, TILE),
            i32(chips * tiles, TILE),
            i32(CORES * rows, TILE),
            f32(rows, TILE),
            f32(chips, TILE),
        ],
        [
            logit_scale,
            logit_bias,
            blocks.transpose(2, 1, 0),
            bucket.reshape(-1, TILE),
            positive.reshape(-1, TILE),
        ],
        scalars=3,
        limit=8,
    )
    if square:
        own_images, image_raw, image_scales = call_kernel(
            own_images_body, [bf16(rows), bf16(rows), f32(rows, TILE)], [image_emb], limit=8
        )
        image_sent, own_images = lax.optimization_barrier((image_emb, own_images))
        from_first = swap_near(image_sent, 0)
        from_second, own_images, *lists = lax.optimization_barrier(
            (from_second, own_images, *lists)
        )
        from_far = swap_near(from_second, 0)
        second_images = call_kernel(
            unit_images_body, [bf16(rows)], [from_second], flops=WAIT_FLOPS // 2, limit=8
        )[0]
        text_raw[-1], second_images = lax.optimization_barrier((text_raw[-1], second_images))
    text_own, text_scales, *pieces = call_kernel(
        functools.partial(unit_text_body, groups),
        [bf16(rows), f32(rows, TILE)] + [bf16(rows // TEXT_PIECES)] * TEXT_PIECES,
        text_raw,
        limit=8,
    )
    text_other = [swap(piece, "blk", 1) for piece in pieces]
    if square:
        from_first, text_own = lax.optimization_barrier((from_first, text_own))
        near_images = call_kernel(
            near_images_body, [bf16(2 * rows)], [from_first, second_images], limit=8
        )[0]
    unit_flops = 2 * rows * rows * embed

    def finish_text(acc_own, acc_other):
        parts = call_kernel(
            functools.partial(text_grad_body, groups),
            [bf16(rows, width)] * groups,
            [text_scales] + text_raw + [acc_own] + [swap(piece, "blk", 1) for piece in acc_other],
            limit=16,
        )
        return parts[:1] + [
            swap(parts[k], "tp", far_first(k, groups)) for k in range(1, groups)
        ]

    def place_text(text_parts):
        return call_kernel(
            functools.partial(place_text_body, groups),
            [bf16(groups * rows, width)],
            text_parts,
            outs_anywhere=True,
            scratch=[pltpu.SemaphoreType.DMA((groups,))],
            flops=WAIT_FLOPS,
            limit=8,
        )[0]

    def finish_image(total, pieces):
        return call_kernel(
            functools.partial(image_grad_body, len(pieces)),
            [bf16(rows)],
            [image_raw, image_scales, total] + pieces,
            outs_anywhere=True,
            scratch=[pltpu.VMEM((rows, embed), jnp.bfloat16), pltpu.SemaphoreType.DMA((tiles,))],
            limit=8,
        )[0]

    if not square:
        columns = gathered.shape[0]
        spread, acc_own, *acc_other = call_kernel(
            functools.partial(all_body, tiles, chips),
            [bf16(columns), f32(rows)] + [bf16(rows // ACC_PIECES)] * ACC_PIECES,
            lists + [text_own, jnp.concatenate(text_other), gathered],
            scratch=[
                pltpu.VMEM((columns, embed), jnp.bfloat16),
                pltpu.VMEM((2 * rows, columns), jnp.bfloat16),
            ],
            flops=6 * chips * unit_flops,
            limit=56,
        )
        text_parts = finish_text(acc_own, acc_other)
        parts = lax.all_to_all(
            spread, "blk", split_axis=0, concat_axis=0, tiled=True, axis_index_groups=same_core
        )
        total = jnp.sum(parts.reshape(-1, rows, embed).astype(jnp.float32), axis=0)
        return (place_text(text_parts), finish_image(total, []))

    own_weights, near_weights = call_kernel(
        functools.partial(near_own_body, tiles),
        [bf16(rows, rows), bf16(rows, 2 * rows)],
        lists + [text_own, own_images, near_images],
        limit=16,
    )
    units, first_weights, first_sum = call_kernel(
        functools.partial(first_sum_body, tiles),
        [bf16(2 * rows), bf16(2 * rows, rows), bf16(rows)],
        lists + [text_own, near_images, near_weights] + text_other,
        limit=16,
    )
    image_add = swap_near(first_sum, 0)
    own_weights, acc, near_weights = call_kernel(
        functools.partial(near_sum_body, tiles),
        [bf16(2 * rows, rows), f32(2 * rows), bf16(2 * rows, 2 * rows)],
        lists + [units, own_images, near_images, own_weights, near_weights, first_weights],
        limit=24,
    )
    own_weights, from_far = lax.optimization_barrier((own_weights, from_far))
    far_weights, far_images = call_kernel(
        functools.partial(far_weights_body, tiles),
        [bf16(2 * rows, 2 * rows), bf16(2 * rows)],
        lists + [units, own_images, own_weights, from_far],
        limit=16,
    )
    acc_other = call_kernel(
        functools.partial(text_sum_body, 1),
        [bf16(rows // ACC_PIECES)] * ACC_PIECES,
        [far_weights, far_images, acc],
        limit=16,
    )
    far_images, acc_other[0] = lax.optimization_barrier((far_images, acc_other[0]))
    acc_own = call_kernel(
        functools.partial(text_sum_body, 0),
        [f32(rows)],
        [far_weights, far_images, acc],
        limit=16,
    )[0]
    far_weights, acc_own = lax.optimization_barrier((far_weights, acc_own))
    far_sum = call_kernel(
        far_sum_body, [bf16(rows // LAST_PIECES)] * LAST_PIECES, [far_weights, units], limit=16
    )
    acc_own, far_sum[0] = lax.optimization_barrier((acc_own, far_sum[0]))
    text_parts = finish_text(acc_own, acc_other)
    own_weights, text_parts[0] = lax.optimization_barrier((own_weights, text_parts[0]))
    base, second_sum = call_kernel(
        own_sum_body,
        [f32(rows), f32(rows)],
        [own_weights, near_weights, units, image_add],
        flops=WAIT_FLOPS,
        limit=16,
    )
    image_last = []
    for at, piece in enumerate(far_sum):
        relayed = call_kernel(
            functools.partial(relay_body, at),
            [bf16(rows // LAST_PIECES)],
            [second_sum, swap_near(piece, 0)],
            limit=8,
        )[0]
        image_last.append(swap_near(relayed, 1))
    text_grad = place_text(text_parts)
    base, _ = lax.optimization_barrier((base, text_grad))
    return (text_grad, finish_image(base, image_last))


def solution(mesh):
    in_specs = (P("blk", "tp"), P(("blk", "tp"), None), P(), P(), P(), P(), P())
    out_specs = (P("blk", "tp"), P(("blk", "tp"), None))
    return jax.shard_map(
        per_device, mesh=mesh, in_specs=in_specs, out_specs=out_specs, check_vma=False
    )
```

```python
import functools
import math

import jax
import jax.numpy as jnp
from jax import lax
from jax.experimental import pallas as pl
from jax.experimental.pallas import tpu as pltpu
from jax.sharding import PartitionSpec as P

TILE = 128
SLOTS = 3
WAIT_FLOPS = 20_000_000_000
TEXT_PIECES = 3
ACC_PIECES = 2
LAST_PIECES = 2
CORES = 2
EPS = 1e-06
LOG2E = math.log2(math.e)
MIB = 1024 * 1024

VMEM_SPEC = pl.BlockSpec(memory_space=pltpu.VMEM)
ANY_SPEC = pl.BlockSpec(memory_space=pl.ANY)
SMEM_SPEC = pl.BlockSpec(memory_space=pltpu.SMEM)


def call_kernel(
    body,
    outs,
    operands,
    scalars=0,
    anywhere=(),
    outs_anywhere=False,
    scratch=(),
    flops=0,
    moved=None,
    limit=24,
):
    if moved is None:
        moved = sum(x.size * x.dtype.itemsize for x in operands)
        moved += sum(math.prod(o.shape) * o.dtype.itemsize for o in outs)
    specs = [SMEM_SPEC] * scalars + [VMEM_SPEC] * (len(operands) - scalars)
    for at in anywhere:
        specs[at] = ANY_SPEC
    return list(
        pl.pallas_call(
            body,
            out_shape=outs,
            in_specs=specs,
            out_specs=[ANY_SPEC if outs_anywhere else VMEM_SPEC] * len(outs),
            scratch_shapes=list(scratch),
            compiler_params=pltpu.CompilerParams(vmem_limit_bytes=limit * MIB),
            cost_estimate=pl.CostEstimate(flops=flops, bytes_accessed=moved, transcendentals=0),
        )(*operands)
    )


def struct(shape, dtype):
    return jax.ShapeDtypeStruct(shape, dtype)


def row_scales(square_sum):
    return lax.rsqrt(square_sum + EPS)


def column_of(row):
    return jnp.broadcast_to(row, (TILE, TILE)).T


def dot_nt(left, right):
    return lax.dot_general(
        left, right, (((1,), (1,)), ((), ())), preferred_element_type=jnp.float32
    )


def dot_tn(left, right):
    return lax.dot_general(
        left, right, (((0,), (0,)), ((), ())), preferred_element_type=jnp.float32
    )


def far_first(k, chunks):
    return (chunks - k) % chunks


def feature_slice(peer, width):
    return pl.ds(pl.multiple_of(peer * width, width), width)


def pick_body(text_ref, *out_refs):
    place = lax.axis_index("tp")
    rows = out_refs[0].shape[0]
    for k, out_ref in enumerate(out_refs):
        peer = place ^ far_first(k, len(out_refs))
        out_ref[...] = text_ref[pl.ds(pl.multiple_of(peer * rows, rows), rows), :]


def unit_text_body(chunks, *refs):
    chunk_refs, (unit_ref, scale_ref) = refs[:chunks], refs[chunks : chunks + 2]
    piece_refs = refs[chunks + 2 :]
    place = lax.axis_index("tp")
    rows, width = chunk_refs[0].shape
    for first in range(0, rows, TILE):
        part = pl.ds(first, TILE)
        parts = [ref[part, :].astype(jnp.float32) for ref in chunk_refs]
        scales = row_scales(sum(jnp.sum(x * x, axis=-1, keepdims=True) for x in parts))
        scale_ref[part, :] = jnp.broadcast_to(scales, (TILE, TILE))
        for k, x in enumerate(parts):
            unit_ref[part, feature_slice(place ^ far_first(k, chunks), width)] = (x * scales).astype(jnp.bfloat16)
    split_rows(unit_ref, piece_refs)


def split_rows(whole_ref, piece_refs):
    for at, ref in enumerate(piece_refs):
        ref[...] = whole_ref[pl.ds(at * ref.shape[0], ref.shape[0]), :]


def join_rows(piece_refs, whole_ref):
    for at, ref in enumerate(piece_refs):
        whole_ref[pl.ds(at * ref.shape[0], ref.shape[0]), :] = ref[...]


def unit_images(ref, image_ref, scale_ref=None):
    step = 64
    for first in range(0, ref.shape[0], step):
        part = pl.ds(first, step)
        values = ref[part, :].astype(jnp.float32)
        scales = row_scales(jnp.sum(values * values, axis=-1, keepdims=True))
        image_ref[part, :] = (values * scales).astype(jnp.bfloat16)
        if scale_ref is not None:
            scale_ref[part, :] = jnp.broadcast_to(scales, (step, TILE))


def unit_images_body(raw_ref, out_ref):
    unit_images(raw_ref, out_ref)


def own_images_body(raw_ref, out_ref, raw_out_ref, scale_ref):
    unit_images(raw_ref, out_ref, scale_ref)
    raw_out_ref[...] = raw_ref[...]


def near_images_body(first_ref, second_unit_ref, out_ref):
    rows = first_ref.shape[0]
    unit_images(first_ref, out_ref)
    out_ref[rows:, :] = second_unit_ref[...]


def neighbour_bits(shard):
    core = shard % CORES
    return 2 << core, 4 >> core


def list_body(groups, tiles, chips, *refs):
    scale_ref, bias_ref, blocks_ref, bucket_ref, positive_ref = refs[:5]
    line_ref, amount_ref, column_ref, row_ref, match_ref, own_ref = refs[5:]
    here, place = lax.axis_index("blk"), lax.axis_index("tp")
    scale = scale_ref[0]
    line_ref[pl.ds(0, 1), :] = jnp.full((1, TILE), -scale * LOG2E, jnp.float32)
    line_ref[pl.ds(1, 1), :] = jnp.full((1, TILE), -bias_ref[0] * LOG2E, jnp.float32)
    if chips == 4:
        first, second = neighbour_bits(here)
        shards = [here, here ^ first, here ^ second, here ^ 6]
    else:
        shards = [chip * CORES + here % CORES for chip in range(chips)]
    count = len(shards) * tiles

    def first_tile(shard):
        return (shard * groups + place) * tiles

    for n, shard in enumerate(shards):
        own_ref[pl.ds(n, 1), :] = jnp.full((1, TILE), jnp.where(shard == here, 1.0, 0.0))
        for j in range(tiles):
            column_ref[pl.ds(n * tiles + j, 1), :] = bucket_ref[pl.ds(first_tile(shard) + j, 1), :]
    for at in range(CORES * tiles):
        tile = first_tile(here ^ (at // tiles)) + at % tiles
        row_ref[pl.ds(at * TILE, TILE), :] = column_of(bucket_ref[pl.ds(tile, 1), :])
        if at < tiles:
            ids = lax.broadcasted_iota(jnp.int32, (1, TILE), 1) + tile * TILE
            matched = column_of(positive_ref[pl.ds(tile, 1), :]) == ids
            match_ref[pl.ds(at * TILE, TILE), :] = jnp.where(matched, 1.0, 0.0)
        for n, shard in enumerate(shards):
            entries = [blocks_ref[slot, shard, tile] for slot in range(SLOTS)]
            for j in range(tiles):
                listed = sum(jnp.where(entry == j, 1.0, 0.0) for entry in entries)
                amount_ref[pl.ds(at * count + n * tiles + j, 1), :] = jnp.full(
                    (1, TILE), scale * listed, jnp.float32
                )


class Pairs:
    count = 6

    def __init__(self, refs, tiles):
        self.line_ref, self.amount_ref, self.column_ref = refs[:3]
        self.row_ref, self.match_ref, self.own_ref = refs[3:6]
        self.tiles = tiles

    def weigh(self, products, half, group, weight_ref, top, left, own=None):
        tiles = self.tiles
        slope, offset = self.line_ref[pl.ds(0, 1), :], self.line_ref[pl.ds(1, 1), :]
        count = self.column_ref.shape[0]
        for a in range(tiles):
            at = half * tiles + a
            row_bucket = self.row_ref[pl.ds(at * TILE, TILE), :]
            for j in range(tiles):
                n = group * tiles + j
                amount = self.amount_ref[pl.ds(at * count + n, 1), :]
                power = (
                    products[a * TILE : (a + 1) * TILE, j * TILE : (j + 1) * TILE] * slope + offset
                )
                factor = jnp.where(row_bucket == self.column_ref[pl.ds(n, 1), :], amount, 0.0)
                if own and a == j:
                    match = self.match_ref[pl.ds(a * TILE, TILE), :]
                    if own == "search":
                        match = match * self.own_ref[pl.ds(group, 1), :]
                    power = jnp.where(match > 0.0, -power, power)
                    factor = jnp.where(match > 0.0, -amount, factor)
                below = 1.0 + jnp.exp2(power)
                inverse = pl.reciprocal(below, approx=True)
                inverse = inverse * (2.0 - below * inverse)
                weight_ref[pl.ds(top + a * TILE, TILE), pl.ds(left + j * TILE, TILE)] = (
                    factor * inverse
                ).astype(jnp.bfloat16)


def near_own_body(tiles, *refs):
    pairs = Pairs(refs, tiles)
    unit_ref, own_image_ref, near_image_ref, own_weight_ref, weight_ref = refs[Pairs.count :]
    rows = unit_ref.shape[0]
    first = dot_nt(unit_ref[...], near_image_ref[pl.ds(0, rows), :])
    second = dot_nt(unit_ref[...], near_image_ref[pl.ds(rows, rows), :])
    pairs.weigh(first, 0, 1, weight_ref, 0, 0)
    own = dot_nt(unit_ref[...], own_image_ref[...])
    pairs.weigh(second, 0, 2, weight_ref, 0, rows)
    pairs.weigh(own, 0, 0, own_weight_ref, 0, 0, "diagonal")


def first_sum_body(tiles, *refs):
    pairs = Pairs(refs, tiles)
    own_unit_ref, near_image_ref, weight_in_ref = refs[Pairs.count : Pairs.count + 3]
    piece_refs = refs[Pairs.count + 3 : Pairs.count + 3 + TEXT_PIECES]
    unit_ref, weight_ref, sum_ref = refs[Pairs.count + 3 + TEXT_PIECES :]
    rows = own_unit_ref.shape[0]
    for at, ref in enumerate(piece_refs):
        unit_ref[pl.ds(rows + at * ref.shape[0], ref.shape[0]), :] = ref[...]
    unit_ref[:rows, :] = own_unit_ref[...]
    weight_ref[:rows, :] = weight_in_ref[:, :rows]
    products = dot_nt(unit_ref[rows:, :], near_image_ref[pl.ds(0, rows), :])
    pairs.weigh(products, 1, 1, weight_ref, rows, 0)
    sum_ref[...] = dot_tn(weight_ref[...], unit_ref[...]).astype(jnp.bfloat16)


def near_sum_body(tiles, *refs):
    pairs = Pairs(refs, tiles)
    unit_ref, own_image_ref, near_image_ref, own_weight_in_ref, weight_in_ref, first_ref = refs[
        Pairs.count : Pairs.count + 6
    ]
    own_weight_ref, acc_ref, weight_ref = refs[Pairs.count + 6 :]
    rows = own_image_ref.shape[0]
    second = dot_nt(unit_ref[rows:, :], near_image_ref[pl.ds(rows, rows), :])
    own = dot_nt(unit_ref[rows:, :], own_image_ref[...])
    own_weight_ref[:rows, :] = own_weight_in_ref[...]
    weight_ref[:, :rows] = first_ref[...]
    weight_ref[:rows, rows:] = weight_in_ref[:, rows:]
    pairs.weigh(second, 1, 2, weight_ref, rows, rows)
    pairs.weigh(own, 1, 0, own_weight_ref, rows, 0)
    acc_ref[...] = jnp.dot(
        weight_ref[...], near_image_ref[...], preferred_element_type=jnp.float32
    )


def far_weights_body(tiles, *refs):
    pairs = Pairs(refs, tiles)
    unit_ref, own_image_ref, own_weight_ref, raw_ref = refs[Pairs.count : Pairs.count + 4]
    weight_ref, image_ref = refs[Pairs.count + 4 :]
    rows = raw_ref.shape[0]
    unit_images(raw_ref, image_ref.at[pl.ds(rows, rows), :])
    products = dot_nt(unit_ref[...], image_ref[rows:, :])
    for half in range(CORES):
        part = products[half * rows : (half + 1) * rows, :]
        pairs.weigh(part, half, 3, weight_ref, half * rows, rows)
    image_ref[:rows, :] = own_image_ref[...]
    weight_ref[:, :rows] = own_weight_ref[...]


def far_sum_body(weight_ref, unit_ref, *out_refs):
    rows = weight_ref.shape[1] // 2
    total = dot_tn(weight_ref[:, rows:], unit_ref[...]).astype(jnp.bfloat16)
    size = rows // len(out_refs)
    for at, ref in enumerate(out_refs):
        ref[...] = total[at * size : (at + 1) * size, :]


def text_sum_body(half, weight_ref, image_ref, acc_ref, *out_refs):
    rows = weight_ref.shape[0] // CORES
    size = out_refs[0].shape[0]
    part = pl.ds(half * rows, rows)
    acc = acc_ref[part, :] + jnp.dot(
        weight_ref[part, :], image_ref[...], preferred_element_type=jnp.float32
    )
    for at, ref in enumerate(out_refs):
        ref[...] = acc[at * size : (at + 1) * size, :].astype(ref.dtype)


def own_sum_body(own_weight_ref, near_weight_ref, unit_ref, add_ref, own_ref, second_ref):
    rows = own_ref.shape[0]
    second_ref[...] = dot_tn(near_weight_ref[:, rows:], unit_ref[...])
    own_ref[...] = dot_tn(own_weight_ref[...], unit_ref[...]) + add_ref[...].astype(jnp.float32)


def all_body(tiles, chips, *refs):
    pairs = Pairs(refs, tiles)
    own_ref, other_ref, piece_ref = refs[Pairs.count : Pairs.count + 3]
    outs = refs[Pairs.count + 3 :]
    spread_ref, acc_ref, acc_piece_refs = outs[0], outs[1], outs[2 : 2 + ACC_PIECES]
    image_ref, weight_ref = outs[2 + ACC_PIECES :]
    rows = own_ref.shape[0]
    unit_images(piece_ref, image_ref)
    for half, text_ref in enumerate((own_ref, other_ref)):
        for chip in range(chips):
            products = dot_nt(text_ref[...], image_ref[pl.ds(chip * rows, rows), :])
            pairs.weigh(
                products, half, chip, weight_ref, half * rows, chip * rows, None if half else "search"
            )
        acc = jnp.dot(
            weight_ref[pl.ds(half * rows, rows), :],
            image_ref[...],
            preferred_element_type=jnp.float32,
        )
        if half == 0:
            acc_ref[...] = acc
            continue
        size = rows // ACC_PIECES
        for at, ref in enumerate(acc_piece_refs):
            ref[...] = acc[at * size : (at + 1) * size, :].astype(jnp.bfloat16)
    for chip in range(chips):
        columns = pl.ds(chip * rows, rows)
        total = dot_tn(weight_ref[pl.ds(0, rows), columns], own_ref[...])
        total += dot_tn(weight_ref[pl.ds(rows, rows), columns], other_ref[...])
        spread_ref[columns, :] = total.astype(jnp.bfloat16)


def relay_body(at, sum_ref, in_ref, out_ref):
    size = in_ref.shape[0]
    part = sum_ref[pl.ds(at * size, size), :]
    out_ref[...] = (part + in_ref[...].astype(jnp.float32)).astype(jnp.bfloat16)


def text_grad_body(chunks, *refs):
    scale_ref, raw_refs, acc_ref = refs[0], refs[1 : 1 + chunks], refs[1 + chunks]
    add_refs, out_refs = refs[2 + chunks : -chunks], refs[-chunks:]
    place = lax.axis_index("tp")
    rows, width = raw_refs[0].shape
    size = add_refs[0].shape[0]
    for first in range(0, rows, TILE // 2):
        part = pl.ds(first, TILE // 2)
        scales = scale_ref[part, :1]
        raws = [ref[part, :].astype(jnp.float32) for ref in raw_refs]
        accs = []
        for k in range(chunks):
            features = feature_slice(place ^ far_first(k, chunks), width)
            added = add_refs[first // size][pl.ds(first % size, TILE // 2), features]
            accs.append(acc_ref[part, features] + added.astype(jnp.float32))
        inner = sum(jnp.sum(x * a, axis=-1, keepdims=True) for x, a in zip(raws, accs))
        inner = inner * scales * scales
        for k in range(chunks):
            out_refs[k][part, :] = (scales * (accs[k] - raws[k] * inner)).astype(jnp.bfloat16)


def arrived_body(*refs):
    out_ref = refs[-1]
    out_ref[...] = sum(ref[: out_ref.shape[0], : out_ref.shape[1]] for ref in refs[:-1])


def finish_body(chunks, adds, *refs):
    part_refs, (raw_ref, scale_ref, sum_ref) = refs[:chunks], refs[chunks : chunks + 3]
    piece_refs = refs[chunks + 3 : chunks + 3 + adds]
    text_ref, image_ref, grad_ref, sems = refs[-4:]
    place = lax.axis_index("tp")
    rows = part_refs[0].shape[0]
    copies = []
    for k in range(chunks):
        peer = place ^ far_first(k, chunks)
        block = pl.ds(pl.multiple_of(peer * rows, rows), rows)
        copies.append(pltpu.make_async_copy(part_refs[k], text_ref.at[block, :], sems.at[k]))
        copies[-1].start()
    for block in range(rows // TILE):
        for first in range(block * TILE, (block + 1) * TILE, TILE // 2):
            part = pl.ds(first, TILE // 2)
            raw = raw_ref[part, :].astype(jnp.float32)
            scales = scale_ref[part, :1]
            acc = sum_ref[part, :]
            if piece_refs:
                size = piece_refs[0].shape[0]
                piece = piece_refs[first // size][pl.ds(first % size, TILE // 2), :]
                acc = acc + piece.astype(jnp.float32)
            inner = jnp.sum(raw * acc, axis=-1, keepdims=True) * scales * scales
            grad_ref[part, :] = (scales * (acc - raw * inner)).astype(jnp.bfloat16)
        part = pl.ds(block * TILE, TILE)
        copies.append(
            pltpu.make_async_copy(
                grad_ref.at[part, :], image_ref.at[part, :], sems.at[chunks + block]
            )
        )
        copies[-1].start()
    for copy in copies:
        copy.wait()


def swap(value, axis, bits):
    count = lax.axis_size(axis)
    return lax.ppermute(value, axis, [(i, i ^ bits) for i in range(count)])


def swap_near(value, which):
    count = lax.axis_size("blk")
    return lax.ppermute(value, "blk", [(i, i ^ neighbour_bits(i)[which]) for i in range(count)])


def swap_chunks(chunks):
    count = len(chunks)
    return chunks[:1] + [swap(chunks[k], "tp", far_first(k, count)) for k in range(1, count)]


def per_device(text_emb, image_emb, logit_scale, logit_bias, bucket, positive, blocks):
    groups = lax.axis_size("tp")
    shards = lax.axis_size("blk")
    chips = shards // CORES
    rows, embed = image_emb.shape
    tiles = rows // TILE
    width = text_emb.shape[1]
    square = chips == 4

    def bf16(count, columns=embed):
        return struct((count, columns), jnp.bfloat16)

    def f32(count, columns=embed):
        return struct((count, columns), jnp.float32)

    def i32(count, columns):
        return struct((count, columns), jnp.int32)

    picked = call_kernel(pick_body, [bf16(rows, width)] * groups, [text_emb], limit=8)
    text_raw = swap_chunks(picked)
    if square:
        from_second = swap_near(image_emb, 1)
    else:
        same_core = [[chip * CORES + core for chip in range(chips)] for core in range(CORES)]
        gathered = lax.all_gather(
            image_emb, "blk", axis=0, tiled=True, axis_index_groups=same_core
        )
        _, image_raw, image_scales = call_kernel(
            own_images_body, [bf16(rows), bf16(rows), f32(rows, TILE)], [image_emb], limit=8
        )
    lists = call_kernel(
        functools.partial(list_body, groups, tiles, chips),
        [
            f32(2, TILE),
            f32(CORES * tiles * chips * tiles, TILE),
            i32(chips * tiles, TILE),
            i32(CORES * rows, TILE),
            f32(rows, TILE),
            f32(chips, TILE),
        ],
        [
            logit_scale,
            logit_bias,
            blocks.transpose(2, 1, 0),
            bucket.reshape(-1, TILE),
            positive.reshape(-1, TILE),
        ],
        scalars=3,
        limit=8,
    )
    if square:
        own_images, image_raw, image_scales = call_kernel(
            own_images_body, [bf16(rows), bf16(rows), f32(rows, TILE)], [image_emb], limit=8
        )
        image_sent, own_images = lax.optimization_barrier((image_emb, own_images))
        from_first = swap_near(image_sent, 0)
        from_second, own_images, *lists = lax.optimization_barrier(
            (from_second, own_images, *lists)
        )
        from_far = swap_near(from_second, 0)
        second_images = call_kernel(
            unit_images_body, [bf16(rows)], [from_second], flops=WAIT_FLOPS // 2, limit=8
        )[0]
        text_raw[-1], second_images = lax.optimization_barrier((text_raw[-1], second_images))
    text_own, text_scales, *pieces = call_kernel(
        functools.partial(unit_text_body, groups),
        [bf16(rows), f32(rows, TILE)] + [bf16(rows // TEXT_PIECES)] * TEXT_PIECES,
        text_raw,
        limit=8,
    )
    text_other = [swap(piece, "blk", 1) for piece in pieces]
    if square:
        from_first, text_own = lax.optimization_barrier((from_first, text_own))
        near_images = call_kernel(
            near_images_body, [bf16(2 * rows)], [from_first, second_images], limit=8
        )[0]
    unit_flops = 2 * rows * rows * embed

    def finish_text(acc_own, acc_other):
        parts = call_kernel(
            functools.partial(text_grad_body, groups),
            [bf16(rows, width)] * groups,
            [text_scales] + text_raw + [acc_own] + [swap(piece, "blk", 1) for piece in acc_other],
            limit=16,
        )
        return swap_chunks(parts)

    def finish(text_parts, total, pieces):
        arrived = call_kernel(
            arrived_body,
            [struct((16, TILE), jnp.bfloat16)],
            text_parts[1:],
            flops=WAIT_FLOPS,
            limit=8,
        )
        return tuple(
            call_kernel(
                functools.partial(finish_body, groups, len(pieces)),
                [bf16(groups * rows, width), bf16(rows)],
                text_parts + [image_raw, image_scales, total] + pieces + arrived,
                outs_anywhere=True,
                scratch=[
                    pltpu.VMEM((rows, embed), jnp.bfloat16),
                    pltpu.SemaphoreType.DMA((groups + tiles,)),
                ],
                limit=8,
            )
        )

    if not square:
        columns = gathered.shape[0]
        spread, acc_own, *acc_other = call_kernel(
            functools.partial(all_body, tiles, chips),
            [bf16(columns), f32(rows)] + [bf16(rows // ACC_PIECES)] * ACC_PIECES,
            lists + [text_own, jnp.concatenate(text_other), gathered],
            scratch=[
                pltpu.VMEM((columns, embed), jnp.bfloat16),
                pltpu.VMEM((2 * rows, columns), jnp.bfloat16),
            ],
            flops=6 * chips * unit_flops,
            limit=56,
        )
        text_parts = finish_text(acc_own, acc_other)
        parts = lax.all_to_all(
            spread, "blk", split_axis=0, concat_axis=0, tiled=True, axis_index_groups=same_core
        )
        total = jnp.sum(parts.reshape(-1, rows, embed).astype(jnp.float32), axis=0)
        return finish(text_parts, total, [])

    own_weights, near_weights = call_kernel(
        functools.partial(near_own_body, tiles),
        [bf16(rows, rows), bf16(rows, 2 * rows)],
        lists + [text_own, own_images, near_images],
        limit=16,
    )
    units, first_weights, first_sum = call_kernel(
        functools.partial(first_sum_body, tiles),
        [bf16(2 * rows), bf16(2 * rows, rows), bf16(rows)],
        lists + [text_own, near_images, near_weights] + text_other,
        limit=16,
    )
    image_add = swap_near(first_sum, 0)
    own_weights, acc, near_weights = call_kernel(
        functools.partial(near_sum_body, tiles),
        [bf16(2 * rows, rows), f32(2 * rows), bf16(2 * rows, 2 * rows)],
        lists + [units, own_images, near_images, own_weights, near_weights, first_weights],
        limit=24,
    )
    own_weights, from_far = lax.optimization_barrier((own_weights, from_far))
    far_weights, far_images = call_kernel(
        functools.partial(far_weights_body, tiles),
        [bf16(2 * rows, 2 * rows), bf16(2 * rows)],
        lists + [units, own_images, own_weights, from_far],
        limit=16,
    )
    acc_other = call_kernel(
        functools.partial(text_sum_body, 1),
        [bf16(rows // ACC_PIECES)] * ACC_PIECES,
        [far_weights, far_images, acc],
        limit=16,
    )
    far_images, acc_other[0] = lax.optimization_barrier((far_images, acc_other[0]))
    acc_own = call_kernel(
        functools.partial(text_sum_body, 0),
        [f32(rows)],
        [far_weights, far_images, acc],
        limit=16,
    )[0]
    far_weights, acc_own = lax.optimization_barrier((far_weights, acc_own))
    far_sum = call_kernel(
        far_sum_body, [bf16(rows // LAST_PIECES)] * LAST_PIECES, [far_weights, units], limit=16
    )
    acc_own, far_sum[0] = lax.optimization_barrier((acc_own, far_sum[0]))
    text_parts = finish_text(acc_own, acc_other)
    own_weights, text_parts[0] = lax.optimization_barrier((own_weights, text_parts[0]))
    base, second_sum = call_kernel(
        own_sum_body,
        [f32(rows), f32(rows)],
        [own_weights, near_weights, units, image_add],
        flops=WAIT_FLOPS,
        limit=16,
    )
    image_last = []
    for at, piece in enumerate(far_sum):
        relayed = call_kernel(
            functools.partial(relay_body, at),
            [bf16(rows // LAST_PIECES)],
            [second_sum, swap_near(piece, 0)],
            limit=8,
        )[0]
        image_last.append(swap_near(relayed, 1))
    return finish(text_parts, base, image_last)


def solution(mesh):
    in_specs = (P("blk", "tp"), P(("blk", "tp"), None), P(), P(), P(), P(), P())
    out_specs = (P("blk", "tp"), P(("blk", "tp"), None))
    return jax.shard_map(
        per_device, mesh=mesh, in_specs=in_specs, out_specs=out_specs, check_vma=False
    )
```

```python
import functools
import math

import jax
import jax.numpy as jnp
from jax import lax
from jax.experimental import pallas as pl
from jax.experimental.pallas import tpu as pltpu
from jax.sharding import PartitionSpec as P

TILE = 128
SLOTS = 3
WAIT_FLOPS = 20_000_000_000
TEXT_PIECES = 3
ACC_PIECES = 2
LAST_PIECES = 2
CORES = 2
EPS = 1e-06
LOG2E = math.log2(math.e)
MIB = 1024 * 1024

VMEM_SPEC = pl.BlockSpec(memory_space=pltpu.VMEM)
ANY_SPEC = pl.BlockSpec(memory_space=pl.ANY)
SMEM_SPEC = pl.BlockSpec(memory_space=pltpu.SMEM)


def call_kernel(
    body,
    outs,
    operands,
    scalars=0,
    anywhere=(),
    outs_anywhere=False,
    scratch=(),
    flops=0,
    moved=None,
    limit=24,
):
    if moved is None:
        moved = sum(x.size * x.dtype.itemsize for x in operands)
        moved += sum(math.prod(o.shape) * o.dtype.itemsize for o in outs)
    specs = [SMEM_SPEC] * scalars + [VMEM_SPEC] * (len(operands) - scalars)
    for at in anywhere:
        specs[at] = ANY_SPEC
    return list(
        pl.pallas_call(
            body,
            out_shape=outs,
            in_specs=specs,
            out_specs=[ANY_SPEC if outs_anywhere else VMEM_SPEC] * len(outs),
            scratch_shapes=list(scratch),
            compiler_params=pltpu.CompilerParams(vmem_limit_bytes=limit * MIB),
            cost_estimate=pl.CostEstimate(flops=flops, bytes_accessed=moved, transcendentals=0),
        )(*operands)
    )


def struct(shape, dtype):
    return jax.ShapeDtypeStruct(shape, dtype)


def row_scales(square_sum):
    return lax.rsqrt(square_sum + EPS)


def column_of(row):
    return jnp.broadcast_to(row, (TILE, TILE)).T


def dot_nt(left, right):
    return lax.dot_general(
        left, right, (((1,), (1,)), ((), ())), preferred_element_type=jnp.float32
    )


def dot_tn(left, right):
    return lax.dot_general(
        left, right, (((0,), (0,)), ((), ())), preferred_element_type=jnp.float32
    )


def far_first(k, chunks):
    return (chunks - k) % chunks


def feature_slice(peer, width):
    return pl.ds(pl.multiple_of(peer * width, width), width)


def pick_body(text_ref, *out_refs):
    place = lax.axis_index("tp")
    rows = out_refs[0].shape[0]
    for k, out_ref in enumerate(out_refs):
        peer = place ^ far_first(k, len(out_refs))
        out_ref[...] = text_ref[pl.ds(pl.multiple_of(peer * rows, rows), rows), :]


def unit_text_body(chunks, *refs):
    chunk_refs, (unit_ref, scale_ref) = refs[:chunks], refs[chunks : chunks + 2]
    piece_refs = refs[chunks + 2 :]
    place = lax.axis_index("tp")
    rows, width = chunk_refs[0].shape
    for first in range(0, rows, TILE):
        part = pl.ds(first, TILE)
        parts = [ref[part, :].astype(jnp.float32) for ref in chunk_refs]
        scales = row_scales(sum(jnp.sum(x * x, axis=-1, keepdims=True) for x in parts))
        scale_ref[part, :] = jnp.broadcast_to(scales, (TILE, TILE))
        for k, x in enumerate(parts):
            unit_ref[part, feature_slice(place ^ far_first(k, chunks), width)] = (x * scales).astype(jnp.bfloat16)
    split_rows(unit_ref, piece_refs)


def split_rows(whole_ref, piece_refs):
    for at, ref in enumerate(piece_refs):
        ref[...] = whole_ref[pl.ds(at * ref.shape[0], ref.shape[0]), :]


def join_rows(piece_refs, whole_ref):
    for at, ref in enumerate(piece_refs):
        whole_ref[pl.ds(at * ref.shape[0], ref.shape[0]), :] = ref[...]


def unit_images(ref, image_ref, scale_ref=None):
    step = 64
    for first in range(0, ref.shape[0], step):
        part = pl.ds(first, step)
        values = ref[part, :].astype(jnp.float32)
        scales = row_scales(jnp.sum(values * values, axis=-1, keepdims=True))
        image_ref[part, :] = (values * scales).astype(jnp.bfloat16)
        if scale_ref is not None:
            scale_ref[part, :] = jnp.broadcast_to(scales, (step, TILE))


def unit_images_body(raw_ref, out_ref):
    unit_images(raw_ref, out_ref)


def own_images_body(raw_ref, out_ref, raw_out_ref, scale_ref):
    unit_images(raw_ref, out_ref, scale_ref)
    raw_out_ref[...] = raw_ref[...]


def near_images_body(first_ref, second_unit_ref, out_ref):
    rows = first_ref.shape[0]
    unit_images(first_ref, out_ref)
    out_ref[rows:, :] = second_unit_ref[...]


def neighbour_bits(shard):
    core = shard % CORES
    return 2 << core, 4 >> core


def list_body(groups, tiles, chips, *refs):
    scale_ref, bias_ref, blocks_ref, bucket_ref, positive_ref = refs[:5]
    line_ref, amount_ref, column_ref, row_ref, match_ref, own_ref = refs[5:]
    here, place = lax.axis_index("blk"), lax.axis_index("tp")
    scale = scale_ref[0]
    line_ref[pl.ds(0, 1), :] = jnp.full((1, TILE), -scale * LOG2E, jnp.float32)
    line_ref[pl.ds(1, 1), :] = jnp.full((1, TILE), -bias_ref[0] * LOG2E, jnp.float32)
    if chips == 4:
        first, second = neighbour_bits(here)
        shards = [here, here ^ first, here ^ second, here ^ 6]
    else:
        shards = [chip * CORES + here % CORES for chip in range(chips)]
    count = len(shards) * tiles

    def first_tile(shard):
        return (shard * groups + place) * tiles

    for n, shard in enumerate(shards):
        own_ref[pl.ds(n, 1), :] = jnp.full((1, TILE), jnp.where(shard == here, 1.0, 0.0))
        for j in range(tiles):
            column_ref[pl.ds(n * tiles + j, 1), :] = bucket_ref[pl.ds(first_tile(shard) + j, 1), :]
    for at in range(CORES * tiles):
        tile = first_tile(here ^ (at // tiles)) + at % tiles
        row_ref[pl.ds(at * TILE, TILE), :] = column_of(bucket_ref[pl.ds(tile, 1), :])
        if at < tiles:
            ids = lax.broadcasted_iota(jnp.int32, (1, TILE), 1) + tile * TILE
            matched = column_of(positive_ref[pl.ds(tile, 1), :]) == ids
            match_ref[pl.ds(at * TILE, TILE), :] = jnp.where(matched, 1.0, 0.0)
        for n, shard in enumerate(shards):
            entries = [blocks_ref[slot, shard, tile] for slot in range(SLOTS)]
            for j in range(tiles):
                listed = sum(jnp.where(entry == j, 1.0, 0.0) for entry in entries)
                amount_ref[pl.ds(at * count + n * tiles + j, 1), :] = jnp.full(
                    (1, TILE), scale * listed, jnp.float32
                )


class Pairs:
    count = 6

    def __init__(self, refs, tiles):
        self.line_ref, self.amount_ref, self.column_ref = refs[:3]
        self.row_ref, self.match_ref, self.own_ref = refs[3:6]
        self.tiles = tiles

    def weigh(self, products, half, group, weight_ref, top, left, own=None):
        tiles = self.tiles
        slope, offset = self.line_ref[pl.ds(0, 1), :], self.line_ref[pl.ds(1, 1), :]
        count = self.column_ref.shape[0]
        for a in range(tiles):
            at = half * tiles + a
            row_bucket = self.row_ref[pl.ds(at * TILE, TILE), :]
            for j in range(tiles):
                n = group * tiles + j
                amount = self.amount_ref[pl.ds(at * count + n, 1), :]
                power = (
                    products[a * TILE : (a + 1) * TILE, j * TILE : (j + 1) * TILE] * slope + offset
                )
                factor = jnp.where(row_bucket == self.column_ref[pl.ds(n, 1), :], amount, 0.0)
                if own and a == j:
                    match = self.match_ref[pl.ds(a * TILE, TILE), :]
                    if own == "search":
                        match = match * self.own_ref[pl.ds(group, 1), :]
                    power = jnp.where(match > 0.0, -power, power)
                    factor = jnp.where(match > 0.0, -amount, factor)
                inverse = pl.reciprocal(1.0 + jnp.exp2(power), approx=True)
                weight_ref[pl.ds(top + a * TILE, TILE), pl.ds(left + j * TILE, TILE)] = (
                    factor * inverse
                ).astype(jnp.bfloat16)


def near_own_body(tiles, *refs):
    pairs = Pairs(refs, tiles)
    unit_ref, own_image_ref, near_image_ref, own_weight_ref, weight_ref = refs[Pairs.count :]
    rows = unit_ref.shape[0]
    first = dot_nt(unit_ref[...], near_image_ref[pl.ds(0, rows), :])
    second = dot_nt(unit_ref[...], near_image_ref[pl.ds(rows, rows), :])
    pairs.weigh(first, 0, 1, weight_ref, 0, 0)
    own = dot_nt(unit_ref[...], own_image_ref[...])
    pairs.weigh(second, 0, 2, weight_ref, 0, rows)
    pairs.weigh(own, 0, 0, own_weight_ref, 0, 0, "diagonal")


def first_sum_body(tiles, *refs):
    pairs = Pairs(refs, tiles)
    own_unit_ref, near_image_ref, weight_in_ref = refs[Pairs.count : Pairs.count + 3]
    piece_refs = refs[Pairs.count + 3 : Pairs.count + 3 + TEXT_PIECES]
    unit_ref, weight_ref, sum_ref = refs[Pairs.count + 3 + TEXT_PIECES :]
    rows = own_unit_ref.shape[0]
    for at, ref in enumerate(piece_refs):
        unit_ref[pl.ds(rows + at * ref.shape[0], ref.shape[0]), :] = ref[...]
    unit_ref[:rows, :] = own_unit_ref[...]
    weight_ref[:rows, :] = weight_in_ref[:, :rows]
    products = dot_nt(unit_ref[rows:, :], near_image_ref[pl.ds(0, rows), :])
    pairs.weigh(products, 1, 1, weight_ref, rows, 0)
    sum_ref[...] = dot_tn(weight_ref[...], unit_ref[...]).astype(jnp.bfloat16)


def near_sum_body(tiles, *refs):
    pairs = Pairs(refs, tiles)
    unit_ref, own_image_ref, near_image_ref, own_weight_in_ref, weight_in_ref, first_ref = refs[
        Pairs.count : Pairs.count + 6
    ]
    own_weight_ref, acc_ref, weight_ref = refs[Pairs.count + 6 :]
    rows = own_image_ref.shape[0]
    second = dot_nt(unit_ref[rows:, :], near_image_ref[pl.ds(rows, rows), :])
    own = dot_nt(unit_ref[rows:, :], own_image_ref[...])
    own_weight_ref[:rows, :] = own_weight_in_ref[...]
    weight_ref[:, :rows] = first_ref[...]
    weight_ref[:rows, rows:] = weight_in_ref[:, rows:]
    pairs.weigh(second, 1, 2, weight_ref, rows, rows)
    pairs.weigh(own, 1, 0, own_weight_ref, rows, 0)
    acc_ref[...] = jnp.dot(
        weight_ref[...], near_image_ref[...], preferred_element_type=jnp.float32
    )


def far_weights_body(tiles, *refs):
    pairs = Pairs(refs, tiles)
    unit_ref, own_image_ref, own_weight_ref, raw_ref = refs[Pairs.count : Pairs.count + 4]
    weight_ref, image_ref = refs[Pairs.count + 4 :]
    rows = raw_ref.shape[0]
    unit_images(raw_ref, image_ref.at[pl.ds(rows, rows), :])
    products = dot_nt(unit_ref[...], image_ref[rows:, :])
    for half in range(CORES):
        part = products[half * rows : (half + 1) * rows, :]
        pairs.weigh(part, half, 3, weight_ref, half * rows, rows)
    image_ref[:rows, :] = own_image_ref[...]
    weight_ref[:, :rows] = own_weight_ref[...]


def far_sum_body(weight_ref, unit_ref, *out_refs):
    rows = weight_ref.shape[1] // 2
    total = dot_tn(weight_ref[:, rows:], unit_ref[...]).astype(jnp.bfloat16)
    size = rows // len(out_refs)
    for at, ref in enumerate(out_refs):
        ref[...] = total[at * size : (at + 1) * size, :]


def text_sum_body(half, weight_ref, image_ref, acc_ref, *out_refs):
    rows = weight_ref.shape[0] // CORES
    size = out_refs[0].shape[0]
    part = pl.ds(half * rows, rows)
    acc = acc_ref[part, :] + jnp.dot(
        weight_ref[part, :], image_ref[...], preferred_element_type=jnp.float32
    )
    for at, ref in enumerate(out_refs):
        ref[...] = acc[at * size : (at + 1) * size, :].astype(ref.dtype)


def own_sum_body(own_weight_ref, near_weight_ref, unit_ref, add_ref, own_ref, second_ref):
    rows = own_ref.shape[0]
    second_ref[...] = dot_tn(near_weight_ref[:, rows:], unit_ref[...])
    own_ref[...] = dot_tn(own_weight_ref[...], unit_ref[...]) + add_ref[...].astype(jnp.float32)


def all_body(tiles, chips, *refs):
    pairs = Pairs(refs, tiles)
    own_ref, other_ref, piece_ref = refs[Pairs.count : Pairs.count + 3]
    outs = refs[Pairs.count + 3 :]
    spread_ref, acc_ref, acc_piece_refs = outs[0], outs[1], outs[2 : 2 + ACC_PIECES]
    image_ref, weight_ref = outs[2 + ACC_PIECES :]
    rows = own_ref.shape[0]
    unit_images(piece_ref, image_ref)
    for half, text_ref in enumerate((own_ref, other_ref)):
        for chip in range(chips):
            products = dot_nt(text_ref[...], image_ref[pl.ds(chip * rows, rows), :])
            pairs.weigh(
                products, half, chip, weight_ref, half * rows, chip * rows, None if half else "search"
            )
        acc = jnp.dot(
            weight_ref[pl.ds(half * rows, rows), :],
            image_ref[...],
            preferred_element_type=jnp.float32,
        )
        if half == 0:
            acc_ref[...] = acc
            continue
        size = rows // ACC_PIECES
        for at, ref in enumerate(acc_piece_refs):
            ref[...] = acc[at * size : (at + 1) * size, :].astype(jnp.bfloat16)
    for chip in range(chips):
        columns = pl.ds(chip * rows, rows)
        total = dot_tn(weight_ref[pl.ds(0, rows), columns], own_ref[...])
        total += dot_tn(weight_ref[pl.ds(rows, rows), columns], other_ref[...])
        spread_ref[columns, :] = total.astype(jnp.bfloat16)


def relay_body(at, sum_ref, in_ref, out_ref):
    size = in_ref.shape[0]
    part = sum_ref[pl.ds(at * size, size), :]
    out_ref[...] = (part + in_ref[...].astype(jnp.float32)).astype(jnp.bfloat16)


def text_grad_body(chunks, *refs):
    scale_ref, raw_refs, acc_ref = refs[0], refs[1 : 1 + chunks], refs[1 + chunks]
    add_refs, out_refs = refs[2 + chunks : -chunks], refs[-chunks:]
    place = lax.axis_index("tp")
    rows, width = raw_refs[0].shape
    size = add_refs[0].shape[0]
    for first in range(0, rows, TILE // 2):
        part = pl.ds(first, TILE // 2)
        scales = scale_ref[part, :1]
        raws = [ref[part, :].astype(jnp.float32) for ref in raw_refs]
        accs = []
        for k in range(chunks):
            features = feature_slice(place ^ far_first(k, chunks), width)
            added = add_refs[first // size][pl.ds(first % size, TILE // 2), features]
            accs.append(acc_ref[part, features] + added.astype(jnp.float32))
        inner = sum(jnp.sum(x * a, axis=-1, keepdims=True) for x, a in zip(raws, accs))
        inner = inner * scales * scales
        for k in range(chunks):
            out_refs[k][part, :] = (scales * (accs[k] - raws[k] * inner)).astype(jnp.bfloat16)


def arrived_body(*refs):
    out_ref = refs[-1]
    out_ref[...] = sum(ref[: out_ref.shape[0], : out_ref.shape[1]] for ref in refs[:-1])


def finish_body(chunks, adds, *refs):
    part_refs, (raw_ref, scale_ref, sum_ref) = refs[:chunks], refs[chunks : chunks + 3]
    piece_refs = refs[chunks + 3 : chunks + 3 + adds]
    text_ref, image_ref, grad_ref, sems = refs[-4:]
    place = lax.axis_index("tp")
    rows = part_refs[0].shape[0]
    copies = []
    for k in range(chunks):
        peer = place ^ far_first(k, chunks)
        for first in range(0, rows, TILE):
            block = pl.ds(pl.multiple_of(peer * rows + first, TILE), TILE)
            copies.append(
                pltpu.make_async_copy(
                    part_refs[k].at[pl.ds(first, TILE), :],
                    text_ref.at[block, :],
                    sems.at[len(copies)],
                )
            )
            copies[-1].start()
    for first in range(0, rows, TILE // 2):
        part = pl.ds(first, TILE // 2)
        raw = raw_ref[part, :].astype(jnp.float32)
        scales = scale_ref[part, :1]
        acc = sum_ref[part, :]
        if piece_refs:
            size = piece_refs[0].shape[0]
            piece = piece_refs[first // size][pl.ds(first % size, TILE // 2), :]
            acc = acc + piece.astype(jnp.float32)
        inner = jnp.sum(raw * acc, axis=-1, keepdims=True) * scales * scales
        grad_ref[part, :] = (scales * (acc - raw * inner)).astype(jnp.bfloat16)
        copies.append(
            pltpu.make_async_copy(
                grad_ref.at[part, :], image_ref.at[part, :], sems.at[len(copies)]
            )
        )
        copies[-1].start()
    for copy in copies:
        copy.wait()


def swap(value, axis, bits):
    count = lax.axis_size(axis)
    return lax.ppermute(value, axis, [(i, i ^ bits) for i in range(count)])


def swap_near(value, which):
    count = lax.axis_size("blk")
    return lax.ppermute(value, "blk", [(i, i ^ neighbour_bits(i)[which]) for i in range(count)])


def swap_chunks(chunks):
    count = len(chunks)
    return chunks[:1] + [swap(chunks[k], "tp", far_first(k, count)) for k in range(1, count)]


def per_device(text_emb, image_emb, logit_scale, logit_bias, bucket, positive, blocks):
    groups = lax.axis_size("tp")
    shards = lax.axis_size("blk")
    chips = shards // CORES
    rows, embed = image_emb.shape
    tiles = rows // TILE
    width = text_emb.shape[1]
    square = chips == 4

    def bf16(count, columns=embed):
        return struct((count, columns), jnp.bfloat16)

    def f32(count, columns=embed):
        return struct((count, columns), jnp.float32)

    def i32(count, columns):
        return struct((count, columns), jnp.int32)

    picked = call_kernel(pick_body, [bf16(rows, width)] * groups, [text_emb], limit=8)
    text_raw = swap_chunks(picked)
    if square:
        from_second = swap_near(image_emb, 1)
    else:
        same_core = [[chip * CORES + core for chip in range(chips)] for core in range(CORES)]
        gathered = lax.all_gather(
            image_emb, "blk", axis=0, tiled=True, axis_index_groups=same_core
        )
        _, image_raw, image_scales = call_kernel(
            own_images_body, [bf16(rows), bf16(rows), f32(rows, TILE)], [image_emb], limit=8
        )
    lists = call_kernel(
        functools.partial(list_body, groups, tiles, chips),
        [
            f32(2, TILE),
            f32(CORES * tiles * chips * tiles, TILE),
            i32(chips * tiles, TILE),
            i32(CORES * rows, TILE),
            f32(rows, TILE),
            f32(chips, TILE),
        ],
        [
            logit_scale,
            logit_bias,
            blocks.transpose(2, 1, 0),
            bucket.reshape(-1, TILE),
            positive.reshape(-1, TILE),
        ],
        scalars=3,
        limit=8,
    )
    if square:
        own_images, image_raw, image_scales = call_kernel(
            own_images_body, [bf16(rows), bf16(rows), f32(rows, TILE)], [image_emb], limit=8
        )
        image_sent, own_images = lax.optimization_barrier((image_emb, own_images))
        from_first = swap_near(image_sent, 0)
        from_second, own_images, *lists = lax.optimization_barrier(
            (from_second, own_images, *lists)
        )
        from_far = swap_near(from_second, 0)
        second_images = call_kernel(
            unit_images_body, [bf16(rows)], [from_second], flops=WAIT_FLOPS // 2, limit=8
        )[0]
        near_images = call_kernel(
            near_images_body, [bf16(2 * rows)], [from_first, second_images], limit=8
        )[0]
        text_raw[-1], near_images = lax.optimization_barrier((text_raw[-1], near_images))
    text_own, text_scales, *pieces = call_kernel(
        functools.partial(unit_text_body, groups),
        [bf16(rows), f32(rows, TILE)] + [bf16(rows // TEXT_PIECES)] * TEXT_PIECES,
        text_raw,
        limit=8,
    )
    text_other = [swap(piece, "blk", 1) for piece in pieces]
    unit_flops = 2 * rows * rows * embed

    def finish_text(acc_own, acc_other):
        parts = call_kernel(
            functools.partial(text_grad_body, groups),
            [bf16(rows, width)] * groups,
            [text_scales] + text_raw + [acc_own] + [swap(piece, "blk", 1) for piece in acc_other],
            limit=16,
        )
        return swap_chunks(parts)

    def finish(text_parts, total, pieces):
        arrived = call_kernel(
            arrived_body,
            [struct((16, TILE), jnp.bfloat16)],
            text_parts[1:],
            flops=WAIT_FLOPS,
            limit=8,
        )
        return tuple(
            call_kernel(
                functools.partial(finish_body, groups, len(pieces)),
                [bf16(groups * rows, width), bf16(rows)],
                text_parts + [image_raw, image_scales, total] + pieces + arrived,
                outs_anywhere=True,
                scratch=[
                    pltpu.VMEM((rows, embed), jnp.bfloat16),
                    pltpu.SemaphoreType.DMA(((groups + 2) * tiles,)),
                ],
                limit=8,
            )
        )

    if not square:
        columns = gathered.shape[0]
        spread, acc_own, *acc_other = call_kernel(
            functools.partial(all_body, tiles, chips),
            [bf16(columns), f32(rows)] + [bf16(rows // ACC_PIECES)] * ACC_PIECES,
            lists + [text_own, jnp.concatenate(text_other), gathered],
            scratch=[
                pltpu.VMEM((columns, embed), jnp.bfloat16),
                pltpu.VMEM((2 * rows, columns), jnp.bfloat16),
            ],
            flops=6 * chips * unit_flops,
            limit=56,
        )
        text_parts = finish_text(acc_own, acc_other)
        parts = lax.all_to_all(
            spread, "blk", split_axis=0, concat_axis=0, tiled=True, axis_index_groups=same_core
        )
        total = jnp.sum(parts.reshape(-1, rows, embed).astype(jnp.float32), axis=0)
        return finish(text_parts, total, [])

    own_weights, near_weights = call_kernel(
        functools.partial(near_own_body, tiles),
        [bf16(rows, rows), bf16(rows, 2 * rows)],
        lists + [text_own, own_images, near_images],
        limit=16,
    )
    units, first_weights, first_sum = call_kernel(
        functools.partial(first_sum_body, tiles),
        [bf16(2 * rows), bf16(2 * rows, rows), bf16(rows)],
        lists + [text_own, near_images, near_weights] + text_other,
        limit=16,
    )
    image_add = swap_near(first_sum, 0)
    own_weights, acc, near_weights = call_kernel(
        functools.partial(near_sum_body, tiles),
        [bf16(2 * rows, rows), f32(2 * rows), bf16(2 * rows, 2 * rows)],
        lists + [units, own_images, near_images, own_weights, near_weights, first_weights],
        limit=24,
    )
    own_weights, from_far = lax.optimization_barrier((own_weights, from_far))
    far_weights, far_images = call_kernel(
        functools.partial(far_weights_body, tiles),
        [bf16(2 * rows, 2 * rows), bf16(2 * rows)],
        lists + [units, own_images, own_weights, from_far],
        limit=16,
    )
    acc_other = call_kernel(
        functools.partial(text_sum_body, 1),
        [bf16(rows // ACC_PIECES)] * ACC_PIECES,
        [far_weights, far_images, acc],
        limit=16,
    )
    far_images, acc_other[0] = lax.optimization_barrier((far_images, acc_other[0]))
    acc_own = call_kernel(
        functools.partial(text_sum_body, 0),
        [f32(rows)],
        [far_weights, far_images, acc],
        limit=16,
    )[0]
    far_weights, acc_own = lax.optimization_barrier((far_weights, acc_own))
    far_sum = call_kernel(
        far_sum_body, [bf16(rows // LAST_PIECES)] * LAST_PIECES, [far_weights, units], limit=16
    )
    acc_own, far_sum[0] = lax.optimization_barrier((acc_own, far_sum[0]))
    text_parts = finish_text(acc_own, acc_other)
    own_weights, text_parts[0] = lax.optimization_barrier((own_weights, text_parts[0]))
    base, second_sum = call_kernel(
        own_sum_body,
        [f32(rows), f32(rows)],
        [own_weights, near_weights, units, image_add],
        flops=WAIT_FLOPS,
        limit=16,
    )
    far_sum[1], text_parts[0] = lax.optimization_barrier((far_sum[1], text_parts[0]))
    image_last = []
    for at, piece in enumerate(far_sum):
        relayed = call_kernel(
            functools.partial(relay_body, at),
            [bf16(rows // LAST_PIECES)],
            [second_sum, swap_near(piece, 0)],
            limit=8,
        )[0]
        image_last.append(swap_near(relayed, 1))
    return finish(text_parts, base, image_last)


def solution(mesh):
    in_specs = (P("blk", "tp"), P(("blk", "tp"), None), P(), P(), P(), P(), P())
    out_specs = (P("blk", "tp"), P(("blk", "tp"), None))
    return jax.shard_map(
        per_device, mesh=mesh, in_specs=in_specs, out_specs=out_specs, check_vma=False
    )
```

```python
import functools
import math

import jax
import jax.numpy as jnp
from jax import lax
from jax.experimental import pallas as pl
from jax.experimental.pallas import tpu as pltpu
from jax.sharding import PartitionSpec as P

TILE = 128
SLOTS = 3
WAIT_FLOPS = 20_000_000_000
TEXT_PIECES = 3
ACC_PIECES = 2
LAST_PIECES = 2
CORES = 2
EPS = 1e-06
LOG2E = math.log2(math.e)
MIB = 1024 * 1024

VMEM_SPEC = pl.BlockSpec(memory_space=pltpu.VMEM)
ANY_SPEC = pl.BlockSpec(memory_space=pl.ANY)
SMEM_SPEC = pl.BlockSpec(memory_space=pltpu.SMEM)


def call_kernel(
    body,
    outs,
    operands,
    scalars=0,
    anywhere=(),
    outs_anywhere=False,
    scratch=(),
    flops=0,
    moved=None,
    limit=24,
):
    if moved is None:
        moved = sum(x.size * x.dtype.itemsize for x in operands)
        moved += sum(math.prod(o.shape) * o.dtype.itemsize for o in outs)
    specs = [SMEM_SPEC] * scalars + [VMEM_SPEC] * (len(operands) - scalars)
    for at in anywhere:
        specs[at] = ANY_SPEC
    return list(
        pl.pallas_call(
            body,
            out_shape=outs,
            in_specs=specs,
            out_specs=[ANY_SPEC if outs_anywhere else VMEM_SPEC] * len(outs),
            scratch_shapes=list(scratch),
            compiler_params=pltpu.CompilerParams(vmem_limit_bytes=limit * MIB),
            cost_estimate=pl.CostEstimate(flops=flops, bytes_accessed=moved, transcendentals=0),
        )(*operands)
    )


def struct(shape, dtype):
    return jax.ShapeDtypeStruct(shape, dtype)


def row_scales(square_sum):
    return lax.rsqrt(square_sum + EPS)


def column_of(row):
    return jnp.broadcast_to(row, (TILE, TILE)).T


def dot_nt(left, right):
    return lax.dot_general(
        left, right, (((1,), (1,)), ((), ())), preferred_element_type=jnp.float32
    )


def dot_tn(left, right):
    return lax.dot_general(
        left, right, (((0,), (0,)), ((), ())), preferred_element_type=jnp.float32
    )


def far_first(k, chunks):
    return (chunks - k) % chunks


def feature_slice(peer, width):
    return pl.ds(pl.multiple_of(peer * width, width), width)


def pick_body(text_ref, *out_refs):
    place = lax.axis_index("tp")
    rows = out_refs[0].shape[0]
    for k, out_ref in enumerate(out_refs):
        peer = place ^ far_first(k, len(out_refs))
        out_ref[...] = text_ref[pl.ds(pl.multiple_of(peer * rows, rows), rows), :]


def unit_text_body(chunks, *refs):
    chunk_refs, (unit_ref, scale_ref) = refs[:chunks], refs[chunks : chunks + 2]
    piece_refs = refs[chunks + 2 :]
    place = lax.axis_index("tp")
    rows, width = chunk_refs[0].shape
    for first in range(0, rows, TILE):
        part = pl.ds(first, TILE)
        parts = [ref[part, :].astype(jnp.float32) for ref in chunk_refs]
        scales = row_scales(sum(jnp.sum(x * x, axis=-1, keepdims=True) for x in parts))
        scale_ref[part, :] = jnp.broadcast_to(scales, (TILE, TILE))
        for k, x in enumerate(parts):
            unit_ref[part, feature_slice(place ^ far_first(k, chunks), width)] = (x * scales).astype(jnp.bfloat16)
    split_rows(unit_ref, piece_refs)


def split_rows(whole_ref, piece_refs):
    for at, ref in enumerate(piece_refs):
        ref[...] = whole_ref[pl.ds(at * ref.shape[0], ref.shape[0]), :]


def join_rows(piece_refs, whole_ref):
    for at, ref in enumerate(piece_refs):
        whole_ref[pl.ds(at * ref.shape[0], ref.shape[0]), :] = ref[...]


def unit_images(ref, image_ref, scale_ref=None):
    step = 64
    for first in range(0, ref.shape[0], step):
        part = pl.ds(first, step)
        values = ref[part, :].astype(jnp.float32)
        scales = row_scales(jnp.sum(values * values, axis=-1, keepdims=True))
        image_ref[part, :] = (values * scales).astype(jnp.bfloat16)
        if scale_ref is not None:
            scale_ref[part, :] = jnp.broadcast_to(scales, (step, TILE))


def unit_images_body(raw_ref, out_ref):
    unit_images(raw_ref, out_ref)


def own_images_body(raw_ref, out_ref, raw_out_ref, scale_ref):
    unit_images(raw_ref, out_ref, scale_ref)
    raw_out_ref[...] = raw_ref[...]


def near_images_body(first_ref, second_unit_ref, out_ref):
    rows = first_ref.shape[0]
    unit_images(first_ref, out_ref)
    out_ref[rows:, :] = second_unit_ref[...]


def neighbour_bits(shard):
    core = shard % CORES
    return 2 << core, 4 >> core


def list_body(groups, tiles, chips, *refs):
    scale_ref, bias_ref, blocks_ref, bucket_ref, positive_ref = refs[:5]
    line_ref, amount_ref, column_ref, row_ref, match_ref, own_ref = refs[5:]
    here, place = lax.axis_index("blk"), lax.axis_index("tp")
    scale = scale_ref[0]
    line_ref[pl.ds(0, 1), :] = jnp.full((1, TILE), -scale * LOG2E, jnp.float32)
    line_ref[pl.ds(1, 1), :] = jnp.full((1, TILE), -bias_ref[0] * LOG2E, jnp.float32)
    if chips == 4:
        first, second = neighbour_bits(here)
        shards = [here, here ^ first, here ^ second, here ^ 6]
    else:
        shards = [chip * CORES + here % CORES for chip in range(chips)]
    count = len(shards) * tiles

    def first_tile(shard):
        return (shard * groups + place) * tiles

    for n, shard in enumerate(shards):
        own_ref[pl.ds(n, 1), :] = jnp.full((1, TILE), jnp.where(shard == here, 1.0, 0.0))
        for j in range(tiles):
            column_ref[pl.ds(n * tiles + j, 1), :] = bucket_ref[pl.ds(first_tile(shard) + j, 1), :]
    for at in range(CORES * tiles):
        tile = first_tile(here ^ (at // tiles)) + at % tiles
        row_ref[pl.ds(at * TILE, TILE), :] = column_of(bucket_ref[pl.ds(tile, 1), :])
        if at < tiles:
            ids = lax.broadcasted_iota(jnp.int32, (1, TILE), 1) + tile * TILE
            matched = column_of(positive_ref[pl.ds(tile, 1), :]) == ids
            match_ref[pl.ds(at * TILE, TILE), :] = jnp.where(matched, 1.0, 0.0)
        for n, shard in enumerate(shards):
            entries = [blocks_ref[slot, shard, tile] for slot in range(SLOTS)]
            for j in range(tiles):
                listed = sum(jnp.where(entry == j, 1.0, 0.0) for entry in entries)
                amount_ref[pl.ds(at * count + n * tiles + j, 1), :] = jnp.full(
                    (1, TILE), scale * listed, jnp.float32
                )


class Pairs:
    count = 6

    def __init__(self, refs, tiles):
        self.line_ref, self.amount_ref, self.column_ref = refs[:3]
        self.row_ref, self.match_ref, self.own_ref = refs[3:6]
        self.tiles = tiles

    def weigh(self, products, half, group, weight_ref, top, left, own=None):
        tiles = self.tiles
        slope, offset = self.line_ref[pl.ds(0, 1), :], self.line_ref[pl.ds(1, 1), :]
        count = self.column_ref.shape[0]
        for a in range(tiles):
            at = half * tiles + a
            row_bucket = self.row_ref[pl.ds(at * TILE, TILE), :]
            for j in range(tiles):
                n = group * tiles + j
                amount = self.amount_ref[pl.ds(at * count + n, 1), :]
                power = (
                    products[a * TILE : (a + 1) * TILE, j * TILE : (j + 1) * TILE] * slope + offset
                )
                factor = jnp.where(row_bucket == self.column_ref[pl.ds(n, 1), :], amount, 0.0)
                if own and a == j:
                    match = self.match_ref[pl.ds(a * TILE, TILE), :]
                    if own == "search":
                        match = match * self.own_ref[pl.ds(group, 1), :]
                    power = jnp.where(match > 0.0, -power, power)
                    factor = jnp.where(match > 0.0, -amount, factor)
                inverse = pl.reciprocal(1.0 + jnp.exp2(power), approx=True)
                weight_ref[pl.ds(top + a * TILE, TILE), pl.ds(left + j * TILE, TILE)] = (
                    factor * inverse
                ).astype(jnp.bfloat16)


def near_own_body(tiles, *refs):
    pairs = Pairs(refs, tiles)
    unit_ref, own_image_ref, near_image_ref, own_weight_ref, weight_ref = refs[Pairs.count :]
    rows = unit_ref.shape[0]
    first = dot_nt(unit_ref[...], near_image_ref[pl.ds(0, rows), :])
    second = dot_nt(unit_ref[...], near_image_ref[pl.ds(rows, rows), :])
    pairs.weigh(first, 0, 1, weight_ref, 0, 0)
    own = dot_nt(unit_ref[...], own_image_ref[...])
    pairs.weigh(second, 0, 2, weight_ref, 0, rows)
    pairs.weigh(own, 0, 0, own_weight_ref, 0, 0, "diagonal")


def first_sum_body(tiles, *refs):
    pairs = Pairs(refs, tiles)
    own_unit_ref, near_image_ref, weight_in_ref = refs[Pairs.count : Pairs.count + 3]
    piece_refs = refs[Pairs.count + 3 : Pairs.count + 3 + TEXT_PIECES]
    unit_ref, weight_ref, sum_ref = refs[Pairs.count + 3 + TEXT_PIECES :]
    rows = own_unit_ref.shape[0]
    for at, ref in enumerate(piece_refs):
        unit_ref[pl.ds(rows + at * ref.shape[0], ref.shape[0]), :] = ref[...]
    unit_ref[:rows, :] = own_unit_ref[...]
    weight_ref[:rows, :] = weight_in_ref[:, :rows]
    products = dot_nt(unit_ref[rows:, :], near_image_ref[pl.ds(0, rows), :])
    pairs.weigh(products, 1, 1, weight_ref, rows, 0)
    sum_ref[...] = dot_tn(weight_ref[...], unit_ref[...]).astype(jnp.bfloat16)


def near_sum_body(tiles, *refs):
    pairs = Pairs(refs, tiles)
    unit_ref, own_image_ref, near_image_ref, own_weight_in_ref, weight_in_ref, first_ref = refs[
        Pairs.count : Pairs.count + 6
    ]
    own_weight_ref, acc_ref, weight_ref = refs[Pairs.count + 6 :]
    rows = own_image_ref.shape[0]
    second = dot_nt(unit_ref[rows:, :], near_image_ref[pl.ds(rows, rows), :])
    own = dot_nt(unit_ref[rows:, :], own_image_ref[...])
    own_weight_ref[:rows, :] = own_weight_in_ref[...]
    weight_ref[:, :rows] = first_ref[...]
    weight_ref[:rows, rows:] = weight_in_ref[:, rows:]
    pairs.weigh(second, 1, 2, weight_ref, rows, rows)
    pairs.weigh(own, 1, 0, own_weight_ref, rows, 0)
    acc_ref[...] = jnp.dot(
        weight_ref[...], near_image_ref[...], preferred_element_type=jnp.float32
    )


def far_weights_body(tiles, *refs):
    pairs = Pairs(refs, tiles)
    unit_ref, own_image_ref, own_weight_ref, raw_ref = refs[Pairs.count : Pairs.count + 4]
    weight_ref, image_ref = refs[Pairs.count + 4 :]
    rows = raw_ref.shape[0]
    unit_images(raw_ref, image_ref.at[pl.ds(rows, rows), :])
    products = dot_nt(unit_ref[...], image_ref[rows:, :])
    for half in range(CORES):
        part = products[half * rows : (half + 1) * rows, :]
        pairs.weigh(part, half, 3, weight_ref, half * rows, rows)
    image_ref[:rows, :] = own_image_ref[...]
    weight_ref[:, :rows] = own_weight_ref[...]


def far_sum_body(weight_ref, unit_ref, *out_refs):
    rows = weight_ref.shape[1] // 2
    total = dot_tn(weight_ref[:, rows:], unit_ref[...]).astype(jnp.bfloat16)
    size = rows // len(out_refs)
    for at, ref in enumerate(out_refs):
        ref[...] = total[at * size : (at + 1) * size, :]


def text_sum_body(half, weight_ref, image_ref, acc_ref, *out_refs):
    rows = weight_ref.shape[0] // CORES
    size = out_refs[0].shape[0]
    part = pl.ds(half * rows, rows)
    acc = acc_ref[part, :] + jnp.dot(
        weight_ref[part, :], image_ref[...], preferred_element_type=jnp.float32
    )
    for at, ref in enumerate(out_refs):
        ref[...] = acc[at * size : (at + 1) * size, :].astype(ref.dtype)


def second_sum_body(weight_ref, unit_ref, add_ref, out_ref, add_out_ref):
    rows = out_ref.shape[0]
    out_ref[...] = dot_tn(weight_ref[:, rows:], unit_ref[...])
    add_out_ref[...] = add_ref[...]


def own_sum_body(weight_ref, unit_ref, add_ref, out_ref):
    out_ref[...] = dot_tn(weight_ref[...], unit_ref[...]) + add_ref[...].astype(jnp.float32)


def all_body(tiles, chips, *refs):
    pairs = Pairs(refs, tiles)
    own_ref, other_ref, piece_ref = refs[Pairs.count : Pairs.count + 3]
    outs = refs[Pairs.count + 3 :]
    spread_ref, acc_ref, acc_piece_refs = outs[0], outs[1], outs[2 : 2 + ACC_PIECES]
    image_ref, weight_ref = outs[2 + ACC_PIECES :]
    rows = own_ref.shape[0]
    unit_images(piece_ref, image_ref)
    for half, text_ref in enumerate((own_ref, other_ref)):
        for chip in range(chips):
            products = dot_nt(text_ref[...], image_ref[pl.ds(chip * rows, rows), :])
            pairs.weigh(
                products, half, chip, weight_ref, half * rows, chip * rows, None if half else "search"
            )
        acc = jnp.dot(
            weight_ref[pl.ds(half * rows, rows), :],
            image_ref[...],
            preferred_element_type=jnp.float32,
        )
        if half == 0:
            acc_ref[...] = acc
            continue
        size = rows // ACC_PIECES
        for at, ref in enumerate(acc_piece_refs):
            ref[...] = acc[at * size : (at + 1) * size, :].astype(jnp.bfloat16)
    for chip in range(chips):
        columns = pl.ds(chip * rows, rows)
        total = dot_tn(weight_ref[pl.ds(0, rows), columns], own_ref[...])
        total += dot_tn(weight_ref[pl.ds(rows, rows), columns], other_ref[...])
        spread_ref[columns, :] = total.astype(jnp.bfloat16)


def relay_body(at, sum_ref, in_ref, out_ref):
    size = in_ref.shape[0]
    part = sum_ref[pl.ds(at * size, size), :]
    out_ref[...] = (part + in_ref[...].astype(jnp.float32)).astype(jnp.bfloat16)


def text_grad_body(chunks, *refs):
    scale_ref, raw_refs, acc_ref = refs[0], refs[1 : 1 + chunks], refs[1 + chunks]
    add_refs, out_refs = refs[2 + chunks : -chunks], refs[-chunks:]
    place = lax.axis_index("tp")
    rows, width = raw_refs[0].shape
    size = add_refs[0].shape[0]
    for first in range(0, rows, TILE // 2):
        part = pl.ds(first, TILE // 2)
        scales = scale_ref[part, :1]
        raws = [ref[part, :].astype(jnp.float32) for ref in raw_refs]
        accs = []
        for k in range(chunks):
            features = feature_slice(place ^ far_first(k, chunks), width)
            added = add_refs[first // size][pl.ds(first % size, TILE // 2), features]
            accs.append(acc_ref[part, features] + added.astype(jnp.float32))
        inner = sum(jnp.sum(x * a, axis=-1, keepdims=True) for x, a in zip(raws, accs))
        inner = inner * scales * scales
        for k in range(chunks):
            out_refs[k][part, :] = (scales * (accs[k] - raws[k] * inner)).astype(jnp.bfloat16)


def arrived_body(*refs):
    out_ref = refs[-1]
    out_ref[...] = sum(ref[: out_ref.shape[0], : out_ref.shape[1]] for ref in refs[:-1])


def finish_body(chunks, adds, *refs):
    part_refs, (raw_ref, scale_ref, sum_ref) = refs[:chunks], refs[chunks : chunks + 3]
    piece_refs = refs[chunks + 3 : chunks + 3 + adds]
    text_ref, image_ref, grad_ref, sems = refs[-4:]
    place = lax.axis_index("tp")
    rows = part_refs[0].shape[0]
    copies = []
    for k in range(chunks):
        peer = place ^ far_first(k, chunks)
        for first in range(0, rows, TILE):
            block = pl.ds(pl.multiple_of(peer * rows + first, TILE), TILE)
            copies.append(
                pltpu.make_async_copy(
                    part_refs[k].at[pl.ds(first, TILE), :],
                    text_ref.at[block, :],
                    sems.at[len(copies)],
                )
            )
            copies[-1].start()
    for first in range(0, rows, TILE // 2):
        part = pl.ds(first, TILE // 2)
        raw = raw_ref[part, :].astype(jnp.float32)
        scales = scale_ref[part, :1]
        acc = sum_ref[part, :]
        if piece_refs:
            size = piece_refs[0].shape[0]
            piece = piece_refs[first // size][pl.ds(first % size, TILE // 2), :]
            acc = acc + piece.astype(jnp.float32)
        inner = jnp.sum(raw * acc, axis=-1, keepdims=True) * scales * scales
        grad_ref[part, :] = (scales * (acc - raw * inner)).astype(jnp.bfloat16)
        copies.append(
            pltpu.make_async_copy(
                grad_ref.at[part, :], image_ref.at[part, :], sems.at[len(copies)]
            )
        )
        copies[-1].start()
    for copy in copies:
        copy.wait()


def swap(value, axis, bits):
    count = lax.axis_size(axis)
    return lax.ppermute(value, axis, [(i, i ^ bits) for i in range(count)])


def swap_near(value, which):
    count = lax.axis_size("blk")
    return lax.ppermute(value, "blk", [(i, i ^ neighbour_bits(i)[which]) for i in range(count)])


def swap_chunks(chunks):
    count = len(chunks)
    return chunks[:1] + [swap(chunks[k], "tp", far_first(k, count)) for k in range(1, count)]


def per_device(text_emb, image_emb, logit_scale, logit_bias, bucket, positive, blocks):
    groups = lax.axis_size("tp")
    shards = lax.axis_size("blk")
    chips = shards // CORES
    rows, embed = image_emb.shape
    tiles = rows // TILE
    width = text_emb.shape[1]
    square = chips == 4

    def bf16(count, columns=embed):
        return struct((count, columns), jnp.bfloat16)

    def f32(count, columns=embed):
        return struct((count, columns), jnp.float32)

    def i32(count, columns):
        return struct((count, columns), jnp.int32)

    picked = call_kernel(pick_body, [bf16(rows, width)] * groups, [text_emb], limit=8)
    text_raw = swap_chunks(picked)
    if square:
        from_second = swap_near(image_emb, 1)
    else:
        same_core = [[chip * CORES + core for chip in range(chips)] for core in range(CORES)]
        gathered = lax.all_gather(
            image_emb, "blk", axis=0, tiled=True, axis_index_groups=same_core
        )
        _, image_raw, image_scales = call_kernel(
            own_images_body, [bf16(rows), bf16(rows), f32(rows, TILE)], [image_emb], limit=8
        )
    lists = call_kernel(
        functools.partial(list_body, groups, tiles, chips),
        [
            f32(2, TILE),
            f32(CORES * tiles * chips * tiles, TILE),
            i32(chips * tiles, TILE),
            i32(CORES * rows, TILE),
            f32(rows, TILE),
            f32(chips, TILE),
        ],
        [
            logit_scale,
            logit_bias,
            blocks.transpose(2, 1, 0),
            bucket.reshape(-1, TILE),
            positive.reshape(-1, TILE),
        ],
        scalars=3,
        limit=8,
    )
    if square:
        own_images, image_raw, image_scales = call_kernel(
            own_images_body, [bf16(rows), bf16(rows), f32(rows, TILE)], [image_emb], limit=8
        )
        image_sent, own_images = lax.optimization_barrier((image_emb, own_images))
        from_first = swap_near(image_sent, 0)
        from_second, own_images, *lists = lax.optimization_barrier(
            (from_second, own_images, *lists)
        )
        from_far = swap_near(from_second, 0)
        second_images = call_kernel(
            unit_images_body, [bf16(rows)], [from_second], flops=WAIT_FLOPS // 2, limit=8
        )[0]
        near_images = call_kernel(
            near_images_body, [bf16(2 * rows)], [from_first, second_images], limit=8
        )[0]
        text_raw[-1], near_images = lax.optimization_barrier((text_raw[-1], near_images))
    text_own, text_scales, *pieces = call_kernel(
        functools.partial(unit_text_body, groups),
        [bf16(rows), f32(rows, TILE)] + [bf16(rows // TEXT_PIECES)] * TEXT_PIECES,
        text_raw,
        limit=8,
    )
    text_other = [swap(piece, "blk", 1) for piece in pieces]
    unit_flops = 2 * rows * rows * embed

    def finish_text(acc_own, acc_other):
        parts = call_kernel(
            functools.partial(text_grad_body, groups),
            [bf16(rows, width)] * groups,
            [text_scales] + text_raw + [acc_own] + [swap(piece, "blk", 1) for piece in acc_other],
            limit=16,
        )
        return swap_chunks(parts)

    def finish(text_parts, total, pieces):
        arrived = call_kernel(
            arrived_body,
            [struct((16, TILE), jnp.bfloat16)],
            text_parts[1:],
            flops=WAIT_FLOPS,
            limit=8,
        )
        return tuple(
            call_kernel(
                functools.partial(finish_body, groups, len(pieces)),
                [bf16(groups * rows, width), bf16(rows)],
                text_parts + [image_raw, image_scales, total] + pieces + arrived,
                outs_anywhere=True,
                scratch=[
                    pltpu.VMEM((rows, embed), jnp.bfloat16),
                    pltpu.SemaphoreType.DMA(((groups + 2) * tiles,)),
                ],
                limit=8,
            )
        )

    if not square:
        columns = gathered.shape[0]
        spread, acc_own, *acc_other = call_kernel(
            functools.partial(all_body, tiles, chips),
            [bf16(columns), f32(rows)] + [bf16(rows // ACC_PIECES)] * ACC_PIECES,
            lists + [text_own, jnp.concatenate(text_other), gathered],
            scratch=[
                pltpu.VMEM((columns, embed), jnp.bfloat16),
                pltpu.VMEM((2 * rows, columns), jnp.bfloat16),
            ],
            flops=6 * chips * unit_flops,
            limit=56,
        )
        text_parts = finish_text(acc_own, acc_other)
        parts = lax.all_to_all(
            spread, "blk", split_axis=0, concat_axis=0, tiled=True, axis_index_groups=same_core
        )
        total = jnp.sum(parts.reshape(-1, rows, embed).astype(jnp.float32), axis=0)
        return finish(text_parts, total, [])

    own_weights, near_weights = call_kernel(
        functools.partial(near_own_body, tiles),
        [bf16(rows, rows), bf16(rows, 2 * rows)],
        lists + [text_own, own_images, near_images],
        limit=16,
    )
    units, first_weights, first_sum = call_kernel(
        functools.partial(first_sum_body, tiles),
        [bf16(2 * rows), bf16(2 * rows, rows), bf16(rows)],
        lists + [text_own, near_images, near_weights] + text_other,
        limit=16,
    )
    image_add = swap_near(first_sum, 0)
    own_weights, acc, near_weights = call_kernel(
        functools.partial(near_sum_body, tiles),
        [bf16(2 * rows, rows), f32(2 * rows), bf16(2 * rows, 2 * rows)],
        lists + [units, own_images, near_images, own_weights, near_weights, first_weights],
        limit=24,
    )
    own_weights, from_far = lax.optimization_barrier((own_weights, from_far))
    far_weights, far_images = call_kernel(
        functools.partial(far_weights_body, tiles),
        [bf16(2 * rows, 2 * rows), bf16(2 * rows)],
        lists + [units, own_images, own_weights, from_far],
        limit=16,
    )
    acc_other = call_kernel(
        functools.partial(text_sum_body, 1),
        [bf16(rows // ACC_PIECES)] * ACC_PIECES,
        [far_weights, far_images, acc],
        limit=16,
    )
    far_images, acc_other[0] = lax.optimization_barrier((far_images, acc_other[0]))
    acc_own = call_kernel(
        functools.partial(text_sum_body, 0),
        [f32(rows)],
        [far_weights, far_images, acc],
        limit=16,
    )[0]
    far_weights, acc_own = lax.optimization_barrier((far_weights, acc_own))
    far_sum = call_kernel(
        far_sum_body, [bf16(rows // LAST_PIECES)] * LAST_PIECES, [far_weights, units], limit=16
    )
    acc_own, far_sum[0] = lax.optimization_barrier((acc_own, far_sum[0]))
    text_parts = finish_text(acc_own, acc_other)
    near_weights, text_parts[0] = lax.optimization_barrier((near_weights, text_parts[0]))
    second_sum, image_add = call_kernel(
        second_sum_body,
        [f32(rows), bf16(rows)],
        [near_weights, units, image_add],
        flops=WAIT_FLOPS,
        limit=16,
    )
    image_last = []
    far_in = [swap_near(piece, 0) for piece in far_sum]
    for at, piece in enumerate(far_in):
        relayed = call_kernel(
            functools.partial(relay_body, at),
            [bf16(rows // LAST_PIECES)],
            [second_sum, piece],
            limit=8,
        )[0]
        image_last.append(swap_near(relayed, 1))
        second_sum, relayed = lax.optimization_barrier((second_sum, relayed))
    own_weights, relayed = lax.optimization_barrier((own_weights, relayed))
    base = call_kernel(
        own_sum_body, [f32(rows)], [own_weights, units, image_add], moved=0, limit=16
    )[0]
    return finish(text_parts, base, image_last)


def solution(mesh):
    in_specs = (P("blk", "tp"), P(("blk", "tp"), None), P(), P(), P(), P(), P())
    out_specs = (P("blk", "tp"), P(("blk", "tp"), None))
    return jax.shard_map(
        per_device, mesh=mesh, in_specs=in_specs, out_specs=out_specs, check_vma=False
    )
```

```python
import functools
import math

import jax
import jax.numpy as jnp
from jax import lax
from jax.experimental import pallas as pl
from jax.experimental.pallas import tpu as pltpu
from jax.sharding import PartitionSpec as P

TILE = 128
SLOTS = 3
WAIT_FLOPS = 20_000_000_000
TEXT_PIECES = 3
ACC_PIECES = 2
LAST_PIECES = 1
CORES = 2
EPS = 1e-06
LOG2E = math.log2(math.e)
MIB = 1024 * 1024

VMEM_SPEC = pl.BlockSpec(memory_space=pltpu.VMEM)
ANY_SPEC = pl.BlockSpec(memory_space=pl.ANY)
SMEM_SPEC = pl.BlockSpec(memory_space=pltpu.SMEM)


def call_kernel(
    body,
    outs,
    operands,
    scalars=0,
    anywhere=(),
    outs_anywhere=False,
    scratch=(),
    flops=0,
    moved=None,
    limit=24,
):
    if moved is None:
        moved = sum(x.size * x.dtype.itemsize for x in operands)
        moved += sum(math.prod(o.shape) * o.dtype.itemsize for o in outs)
    specs = [SMEM_SPEC] * scalars + [VMEM_SPEC] * (len(operands) - scalars)
    for at in anywhere:
        specs[at] = ANY_SPEC
    return list(
        pl.pallas_call(
            body,
            out_shape=outs,
            in_specs=specs,
            out_specs=[ANY_SPEC if outs_anywhere else VMEM_SPEC] * len(outs),
            scratch_shapes=list(scratch),
            compiler_params=pltpu.CompilerParams(vmem_limit_bytes=limit * MIB),
            cost_estimate=pl.CostEstimate(flops=flops, bytes_accessed=moved, transcendentals=0),
        )(*operands)
    )


def struct(shape, dtype):
    return jax.ShapeDtypeStruct(shape, dtype)


def row_scales(square_sum):
    return lax.rsqrt(square_sum + EPS)


def column_of(row):
    return jnp.broadcast_to(row, (TILE, TILE)).T


def dot_nt(left, right):
    return lax.dot_general(
        left, right, (((1,), (1,)), ((), ())), preferred_element_type=jnp.float32
    )


def dot_tn(left, right):
    return lax.dot_general(
        left, right, (((0,), (0,)), ((), ())), preferred_element_type=jnp.float32
    )


def far_first(k, chunks):
    return (chunks - k) % chunks


def feature_slice(peer, width):
    return pl.ds(pl.multiple_of(peer * width, width), width)


def pick_body(text_ref, *out_refs):
    place = lax.axis_index("tp")
    rows = out_refs[0].shape[0]
    for k, out_ref in enumerate(out_refs):
        peer = place ^ far_first(k, len(out_refs))
        out_ref[...] = text_ref[pl.ds(pl.multiple_of(peer * rows, rows), rows), :]


def unit_text_body(chunks, *refs):
    chunk_refs, (unit_ref, scale_ref) = refs[:chunks], refs[chunks : chunks + 2]
    piece_refs = refs[chunks + 2 :]
    place = lax.axis_index("tp")
    rows, width = chunk_refs[0].shape
    for first in range(0, rows, TILE):
        part = pl.ds(first, TILE)
        parts = [ref[part, :].astype(jnp.float32) for ref in chunk_refs]
        scales = row_scales(sum(jnp.sum(x * x, axis=-1, keepdims=True) for x in parts))
        scale_ref[part, :] = jnp.broadcast_to(scales, (TILE, TILE))
        for k, x in enumerate(parts):
            unit_ref[part, feature_slice(place ^ far_first(k, chunks), width)] = (x * scales).astype(jnp.bfloat16)
    split_rows(unit_ref, piece_refs)


def split_rows(whole_ref, piece_refs):
    for at, ref in enumerate(piece_refs):
        ref[...] = whole_ref[pl.ds(at * ref.shape[0], ref.shape[0]), :]


def join_rows(piece_refs, whole_ref):
    for at, ref in enumerate(piece_refs):
        whole_ref[pl.ds(at * ref.shape[0], ref.shape[0]), :] = ref[...]


def unit_images(ref, image_ref, scale_ref=None):
    step = 64
    for first in range(0, ref.shape[0], step):
        part = pl.ds(first, step)
        values = ref[part, :].astype(jnp.float32)
        scales = row_scales(jnp.sum(values * values, axis=-1, keepdims=True))
        image_ref[part, :] = (values * scales).astype(jnp.bfloat16)
        if scale_ref is not None:
            scale_ref[part, :] = jnp.broadcast_to(scales, (step, TILE))


def unit_images_body(raw_ref, out_ref):
    unit_images(raw_ref, out_ref)


def own_images_body(raw_ref, out_ref, raw_out_ref, scale_ref):
    unit_images(raw_ref, out_ref, scale_ref)
    raw_out_ref[...] = raw_ref[...]


def near_images_body(first_ref, second_unit_ref, out_ref):
    rows = first_ref.shape[0]
    unit_images(first_ref, out_ref)
    out_ref[rows:, :] = second_unit_ref[...]


def neighbour_bits(shard):
    core = shard % CORES
    return 2 << core, 4 >> core


def list_body(groups, tiles, chips, *refs):
    scale_ref, bias_ref, blocks_ref, bucket_ref, positive_ref = refs[:5]
    line_ref, amount_ref, column_ref, row_ref, match_ref, own_ref = refs[5:]
    here, place = lax.axis_index("blk"), lax.axis_index("tp")
    scale = scale_ref[0]
    line_ref[pl.ds(0, 1), :] = jnp.full((1, TILE), -scale * LOG2E, jnp.float32)
    line_ref[pl.ds(1, 1), :] = jnp.full((1, TILE), -bias_ref[0] * LOG2E, jnp.float32)
    if chips == 4:
        first, second = neighbour_bits(here)
        shards = [here, here ^ first, here ^ second, here ^ 6]
    else:
        shards = [chip * CORES + here % CORES for chip in range(chips)]
    count = len(shards) * tiles

    def first_tile(shard):
        return (shard * groups + place) * tiles

    for n, shard in enumerate(shards):
        own_ref[pl.ds(n, 1), :] = jnp.full((1, TILE), jnp.where(shard == here, 1.0, 0.0))
        for j in range(tiles):
            column_ref[pl.ds(n * tiles + j, 1), :] = bucket_ref[pl.ds(first_tile(shard) + j, 1), :]
    for at in range(CORES * tiles):
        tile = first_tile(here ^ (at // tiles)) + at % tiles
        row_ref[pl.ds(at * TILE, TILE), :] = column_of(bucket_ref[pl.ds(tile, 1), :])
        if at < tiles:
            ids = lax.broadcasted_iota(jnp.int32, (1, TILE), 1) + tile * TILE
            matched = column_of(positive_ref[pl.ds(tile, 1), :]) == ids
            match_ref[pl.ds(at * TILE, TILE), :] = jnp.where(matched, 1.0, 0.0)
        for n, shard in enumerate(shards):
            entries = [blocks_ref[slot, shard, tile] for slot in range(SLOTS)]
            for j in range(tiles):
                listed = sum(jnp.where(entry == j, 1.0, 0.0) for entry in entries)
                amount_ref[pl.ds(at * count + n * tiles + j, 1), :] = jnp.full(
                    (1, TILE), scale * listed, jnp.float32
                )


class Pairs:
    count = 6

    def __init__(self, refs, tiles):
        self.line_ref, self.amount_ref, self.column_ref = refs[:3]
        self.row_ref, self.match_ref, self.own_ref = refs[3:6]
        self.tiles = tiles

    def weigh(self, products, half, group, weight_ref, top, left, own=None):
        tiles = self.tiles
        slope, offset = self.line_ref[pl.ds(0, 1), :], self.line_ref[pl.ds(1, 1), :]
        count = self.column_ref.shape[0]
        for a in range(tiles):
            at = half * tiles + a
            row_bucket = self.row_ref[pl.ds(at * TILE, TILE), :]
            for j in range(tiles):
                n = group * tiles + j
                amount = self.amount_ref[pl.ds(at * count + n, 1), :]
                power = (
                    products[a * TILE : (a + 1) * TILE, j * TILE : (j + 1) * TILE] * slope + offset
                )
                factor = jnp.where(row_bucket == self.column_ref[pl.ds(n, 1), :], amount, 0.0)
                if own and a == j:
                    match = self.match_ref[pl.ds(a * TILE, TILE), :]
                    if own == "search":
                        match = match * self.own_ref[pl.ds(group, 1), :]
                    power = jnp.where(match > 0.0, -power, power)
                    factor = jnp.where(match > 0.0, -amount, factor)
                inverse = pl.reciprocal(1.0 + jnp.exp2(power), approx=True)
                weight_ref[pl.ds(top + a * TILE, TILE), pl.ds(left + j * TILE, TILE)] = (
                    factor * inverse
                ).astype(jnp.bfloat16)


def near_own_body(tiles, *refs):
    pairs = Pairs(refs, tiles)
    unit_ref, own_image_ref, near_image_ref, own_weight_ref, weight_ref = refs[Pairs.count :]
    rows = unit_ref.shape[0]
    first = dot_nt(unit_ref[...], near_image_ref[pl.ds(0, rows), :])
    second = dot_nt(unit_ref[...], near_image_ref[pl.ds(rows, rows), :])
    pairs.weigh(first, 0, 1, weight_ref, 0, 0)
    own = dot_nt(unit_ref[...], own_image_ref[...])
    pairs.weigh(second, 0, 2, weight_ref, 0, rows)
    pairs.weigh(own, 0, 0, own_weight_ref, 0, 0, "diagonal")


def first_sum_body(tiles, *refs):
    pairs = Pairs(refs, tiles)
    own_unit_ref, near_image_ref, weight_in_ref = refs[Pairs.count : Pairs.count + 3]
    piece_refs = refs[Pairs.count + 3 : Pairs.count + 3 + TEXT_PIECES]
    unit_ref, weight_ref, sum_ref = refs[Pairs.count + 3 + TEXT_PIECES :]
    rows = own_unit_ref.shape[0]
    for at, ref in enumerate(piece_refs):
        unit_ref[pl.ds(rows + at * ref.shape[0], ref.shape[0]), :] = ref[...]
    unit_ref[:rows, :] = own_unit_ref[...]
    weight_ref[:rows, :] = weight_in_ref[:, :rows]
    products = dot_nt(unit_ref[rows:, :], near_image_ref[pl.ds(0, rows), :])
    pairs.weigh(products, 1, 1, weight_ref, rows, 0)
    sum_ref[...] = dot_tn(weight_ref[...], unit_ref[...]).astype(jnp.bfloat16)


def near_sum_body(tiles, *refs):
    pairs = Pairs(refs, tiles)
    unit_ref, own_image_ref, near_image_ref, own_weight_in_ref, weight_in_ref, first_ref = refs[
        Pairs.count : Pairs.count + 6
    ]
    own_weight_ref, acc_ref, weight_ref = refs[Pairs.count + 6 :]
    rows = own_image_ref.shape[0]
    second = dot_nt(unit_ref[rows:, :], near_image_ref[pl.ds(rows, rows), :])
    own = dot_nt(unit_ref[rows:, :], own_image_ref[...])
    own_weight_ref[:rows, :] = own_weight_in_ref[...]
    weight_ref[:, :rows] = first_ref[...]
    weight_ref[:rows, rows:] = weight_in_ref[:, rows:]
    pairs.weigh(second, 1, 2, weight_ref, rows, rows)
    pairs.weigh(own, 1, 0, own_weight_ref, rows, 0)
    acc_ref[...] = jnp.dot(
        weight_ref[...], near_image_ref[...], preferred_element_type=jnp.float32
    )


def far_weights_body(tiles, *refs):
    pairs = Pairs(refs, tiles)
    unit_ref, own_image_ref, own_weight_ref, raw_ref = refs[Pairs.count : Pairs.count + 4]
    weight_ref, image_ref = refs[Pairs.count + 4 :]
    rows = raw_ref.shape[0]
    unit_images(raw_ref, image_ref.at[pl.ds(rows, rows), :])
    products = dot_nt(unit_ref[...], image_ref[rows:, :])
    for half in range(CORES):
        part = products[half * rows : (half + 1) * rows, :]
        pairs.weigh(part, half, 3, weight_ref, half * rows, rows)
    image_ref[:rows, :] = own_image_ref[...]
    weight_ref[:, :rows] = own_weight_ref[...]


def far_sum_body(weight_ref, unit_ref, *out_refs):
    rows = weight_ref.shape[1] // 2
    total = dot_tn(weight_ref[:, rows:], unit_ref[...]).astype(jnp.bfloat16)
    size = rows // len(out_refs)
    for at, ref in enumerate(out_refs):
        ref[...] = total[at * size : (at + 1) * size, :]


def text_sum_body(half, weight_ref, image_ref, acc_ref, *out_refs):
    rows = weight_ref.shape[0] // CORES
    size = out_refs[0].shape[0]
    part = pl.ds(half * rows, rows)
    acc = acc_ref[part, :] + jnp.dot(
        weight_ref[part, :], image_ref[...], preferred_element_type=jnp.float32
    )
    for at, ref in enumerate(out_refs):
        ref[...] = acc[at * size : (at + 1) * size, :].astype(ref.dtype)


def second_sum_body(weight_ref, unit_ref, add_ref, out_ref, add_out_ref):
    rows = out_ref.shape[0]
    out_ref[...] = dot_tn(weight_ref[:, rows:], unit_ref[...])
    add_out_ref[...] = add_ref[...]


def own_sum_body(weight_ref, unit_ref, add_ref, out_ref):
    out_ref[...] = dot_tn(weight_ref[...], unit_ref[...]) + add_ref[...].astype(jnp.float32)


def all_body(tiles, chips, *refs):
    pairs = Pairs(refs, tiles)
    own_ref, other_ref, piece_ref = refs[Pairs.count : Pairs.count + 3]
    outs = refs[Pairs.count + 3 :]
    spread_ref, acc_ref, acc_piece_refs = outs[0], outs[1], outs[2 : 2 + ACC_PIECES]
    image_ref, weight_ref = outs[2 + ACC_PIECES :]
    rows = own_ref.shape[0]
    unit_images(piece_ref, image_ref)
    for half, text_ref in enumerate((own_ref, other_ref)):
        for chip in range(chips):
            products = dot_nt(text_ref[...], image_ref[pl.ds(chip * rows, rows), :])
            pairs.weigh(
                products, half, chip, weight_ref, half * rows, chip * rows, None if half else "search"
            )
        acc = jnp.dot(
            weight_ref[pl.ds(half * rows, rows), :],
            image_ref[...],
            preferred_element_type=jnp.float32,
        )
        if half == 0:
            acc_ref[...] = acc
            continue
        size = rows // ACC_PIECES
        for at, ref in enumerate(acc_piece_refs):
            ref[...] = acc[at * size : (at + 1) * size, :].astype(jnp.bfloat16)
    for chip in range(chips):
        columns = pl.ds(chip * rows, rows)
        total = dot_tn(weight_ref[pl.ds(0, rows), columns], own_ref[...])
        total += dot_tn(weight_ref[pl.ds(rows, rows), columns], other_ref[...])
        spread_ref[columns, :] = total.astype(jnp.bfloat16)


def relay_body(at, sum_ref, in_ref, out_ref):
    size = in_ref.shape[0]
    part = sum_ref[pl.ds(at * size, size), :]
    out_ref[...] = (part + in_ref[...].astype(jnp.float32)).astype(jnp.bfloat16)


def text_grad_body(chunks, *refs):
    scale_ref, raw_refs, acc_ref = refs[0], refs[1 : 1 + chunks], refs[1 + chunks]
    add_refs, out_refs = refs[2 + chunks : -chunks], refs[-chunks:]
    place = lax.axis_index("tp")
    rows, width = raw_refs[0].shape
    size = add_refs[0].shape[0]
    for first in range(0, rows, TILE // 2):
        part = pl.ds(first, TILE // 2)
        scales = scale_ref[part, :1]
        raws = [ref[part, :].astype(jnp.float32) for ref in raw_refs]
        accs = []
        for k in range(chunks):
            features = feature_slice(place ^ far_first(k, chunks), width)
            added = add_refs[first // size][pl.ds(first % size, TILE // 2), features]
            accs.append(acc_ref[part, features] + added.astype(jnp.float32))
        inner = sum(jnp.sum(x * a, axis=-1, keepdims=True) for x, a in zip(raws, accs))
        inner = inner * scales * scales
        for k in range(chunks):
            out_refs[k][part, :] = (scales * (accs[k] - raws[k] * inner)).astype(jnp.bfloat16)


def arrived_body(*refs):
    out_ref = refs[-1]
    out_ref[...] = sum(ref[: out_ref.shape[0], : out_ref.shape[1]] for ref in refs[:-1])


def finish_body(chunks, adds, *refs):
    part_refs, (raw_ref, scale_ref, sum_ref) = refs[:chunks], refs[chunks : chunks + 3]
    piece_refs = refs[chunks + 3 : chunks + 3 + adds]
    text_ref, image_ref, grad_ref, sems = refs[-4:]
    place = lax.axis_index("tp")
    rows = part_refs[0].shape[0]
    copies = []
    for k in range(chunks):
        peer = place ^ far_first(k, chunks)
        for first in range(0, rows, TILE):
            block = pl.ds(pl.multiple_of(peer * rows + first, TILE), TILE)
            copies.append(
                pltpu.make_async_copy(
                    part_refs[k].at[pl.ds(first, TILE), :],
                    text_ref.at[block, :],
                    sems.at[len(copies)],
                )
            )
            copies[-1].start()
    for first in range(0, rows, TILE // 2):
        part = pl.ds(first, TILE // 2)
        raw = raw_ref[part, :].astype(jnp.float32)
        scales = scale_ref[part, :1]
        acc = sum_ref[part, :]
        if piece_refs:
            size = piece_refs[0].shape[0]
            piece = piece_refs[first // size][pl.ds(first % size, TILE // 2), :]
            acc = acc + piece.astype(jnp.float32)
        inner = jnp.sum(raw * acc, axis=-1, keepdims=True) * scales * scales
        grad_ref[part, :] = (scales * (acc - raw * inner)).astype(jnp.bfloat16)
        copies.append(
            pltpu.make_async_copy(
                grad_ref.at[part, :], image_ref.at[part, :], sems.at[len(copies)]
            )
        )
        copies[-1].start()
    for copy in copies:
        copy.wait()


def swap(value, axis, bits):
    count = lax.axis_size(axis)
    return lax.ppermute(value, axis, [(i, i ^ bits) for i in range(count)])


def swap_near(value, which):
    count = lax.axis_size("blk")
    return lax.ppermute(value, "blk", [(i, i ^ neighbour_bits(i)[which]) for i in range(count)])


def swap_chunks(chunks):
    count = len(chunks)
    return chunks[:1] + [swap(chunks[k], "tp", far_first(k, count)) for k in range(1, count)]


def per_device(text_emb, image_emb, logit_scale, logit_bias, bucket, positive, blocks):
    groups = lax.axis_size("tp")
    shards = lax.axis_size("blk")
    chips = shards // CORES
    rows, embed = image_emb.shape
    tiles = rows // TILE
    width = text_emb.shape[1]
    square = chips == 4

    def bf16(count, columns=embed):
        return struct((count, columns), jnp.bfloat16)

    def f32(count, columns=embed):
        return struct((count, columns), jnp.float32)

    def i32(count, columns):
        return struct((count, columns), jnp.int32)

    picked = call_kernel(pick_body, [bf16(rows, width)] * groups, [text_emb], limit=8)
    text_raw = swap_chunks(picked)
    if square:
        from_second = swap_near(image_emb, 1)
    else:
        same_core = [[chip * CORES + core for chip in range(chips)] for core in range(CORES)]
        gathered = lax.all_gather(
            image_emb, "blk", axis=0, tiled=True, axis_index_groups=same_core
        )
        _, image_raw, image_scales = call_kernel(
            own_images_body, [bf16(rows), bf16(rows), f32(rows, TILE)], [image_emb], limit=8
        )
    lists = call_kernel(
        functools.partial(list_body, groups, tiles, chips),
        [
            f32(2, TILE),
            f32(CORES * tiles * chips * tiles, TILE),
            i32(chips * tiles, TILE),
            i32(CORES * rows, TILE),
            f32(rows, TILE),
            f32(chips, TILE),
        ],
        [
            logit_scale,
            logit_bias,
            blocks.transpose(2, 1, 0),
            bucket.reshape(-1, TILE),
            positive.reshape(-1, TILE),
        ],
        scalars=3,
        limit=8,
    )
    if square:
        own_images, image_raw, image_scales = call_kernel(
            own_images_body, [bf16(rows), bf16(rows), f32(rows, TILE)], [image_emb], limit=8
        )
        image_sent, own_images = lax.optimization_barrier((image_emb, own_images))
        from_first = swap_near(image_sent, 0)
        from_second, own_images, *lists = lax.optimization_barrier(
            (from_second, own_images, *lists)
        )
        from_far = swap_near(from_second, 0)
        second_images = call_kernel(
            unit_images_body, [bf16(rows)], [from_second], flops=WAIT_FLOPS // 2, limit=8
        )[0]
        near_images = call_kernel(
            near_images_body, [bf16(2 * rows)], [from_first, second_images], limit=8
        )[0]
        text_raw[-1], near_images = lax.optimization_barrier((text_raw[-1], near_images))
    text_own, text_scales, *pieces = call_kernel(
        functools.partial(unit_text_body, groups),
        [bf16(rows), f32(rows, TILE)] + [bf16(rows // TEXT_PIECES)] * TEXT_PIECES,
        text_raw,
        limit=8,
    )
    text_other = [swap(piece, "blk", 1) for piece in pieces]
    unit_flops = 2 * rows * rows * embed

    def finish_text(acc_own, acc_other):
        parts = call_kernel(
            functools.partial(text_grad_body, groups),
            [bf16(rows, width)] * groups,
            [text_scales] + text_raw + [acc_own] + [swap(piece, "blk", 1) for piece in acc_other],
            limit=16,
        )
        return swap_chunks(parts)

    def finish(text_parts, total, pieces):
        arrived = call_kernel(
            arrived_body,
            [struct((16, TILE), jnp.bfloat16)],
            text_parts[1:],
            flops=WAIT_FLOPS,
            limit=8,
        )
        return tuple(
            call_kernel(
                functools.partial(finish_body, groups, len(pieces)),
                [bf16(groups * rows, width), bf16(rows)],
                text_parts + [image_raw, image_scales, total] + pieces + arrived,
                outs_anywhere=True,
                scratch=[
                    pltpu.VMEM((rows, embed), jnp.bfloat16),
                    pltpu.SemaphoreType.DMA(((groups + 2) * tiles,)),
                ],
                limit=8,
            )
        )

    if not square:
        columns = gathered.shape[0]
        spread, acc_own, *acc_other = call_kernel(
            functools.partial(all_body, tiles, chips),
            [bf16(columns), f32(rows)] + [bf16(rows // ACC_PIECES)] * ACC_PIECES,
            lists + [text_own, jnp.concatenate(text_other), gathered],
            scratch=[
                pltpu.VMEM((columns, embed), jnp.bfloat16),
                pltpu.VMEM((2 * rows, columns), jnp.bfloat16),
            ],
            flops=6 * chips * unit_flops,
            limit=56,
        )
        text_parts = finish_text(acc_own, acc_other)
        parts = lax.all_to_all(
            spread, "blk", split_axis=0, concat_axis=0, tiled=True, axis_index_groups=same_core
        )
        total = jnp.sum(parts.reshape(-1, rows, embed).astype(jnp.float32), axis=0)
        return finish(text_parts, total, [])

    own_weights, near_weights = call_kernel(
        functools.partial(near_own_body, tiles),
        [bf16(rows, rows), bf16(rows, 2 * rows)],
        lists + [text_own, own_images, near_images],
        limit=16,
    )
    units, first_weights, first_sum = call_kernel(
        functools.partial(first_sum_body, tiles),
        [bf16(2 * rows), bf16(2 * rows, rows), bf16(rows)],
        lists + [text_own, near_images, near_weights] + text_other,
        limit=16,
    )
    image_add = swap_near(first_sum, 0)
    own_weights, acc, near_weights = call_kernel(
        functools.partial(near_sum_body, tiles),
        [bf16(2 * rows, rows), f32(2 * rows), bf16(2 * rows, 2 * rows)],
        lists + [units, own_images, near_images, own_weights, near_weights, first_weights],
        limit=24,
    )
    own_weights, from_far = lax.optimization_barrier((own_weights, from_far))
    far_weights, far_images = call_kernel(
        functools.partial(far_weights_body, tiles),
        [bf16(2 * rows, 2 * rows), bf16(2 * rows)],
        lists + [units, own_images, own_weights, from_far],
        limit=16,
    )
    far_sum = call_kernel(
        far_sum_body, [bf16(rows // LAST_PIECES)] * LAST_PIECES, [far_weights, units], limit=16
    )
    far_images, far_sum[0] = lax.optimization_barrier((far_images, far_sum[0]))
    acc_other = call_kernel(
        functools.partial(text_sum_body, 1),
        [bf16(rows // ACC_PIECES)] * ACC_PIECES,
        [far_weights, far_images, acc],
        limit=16,
    )
    far_images, acc_other[0] = lax.optimization_barrier((far_images, acc_other[0]))
    acc_own = call_kernel(
        functools.partial(text_sum_body, 0),
        [f32(rows)],
        [far_weights, far_images, acc],
        limit=16,
    )[0]
    text_parts = finish_text(acc_own, acc_other)
    near_weights, text_parts[0] = lax.optimization_barrier((near_weights, text_parts[0]))
    second_sum, image_add = call_kernel(
        second_sum_body,
        [f32(rows), bf16(rows)],
        [near_weights, units, image_add],
        flops=0,
        limit=16,
    )
    image_last = []
    far_in = [swap_near(piece, 0) for piece in far_sum]
    for at, piece in enumerate(far_in):
        relayed = call_kernel(
            functools.partial(relay_body, at),
            [bf16(rows // LAST_PIECES)],
            [second_sum, piece],
            limit=8,
        )[0]
        image_last.append(swap_near(relayed, 1))
        second_sum, relayed = lax.optimization_barrier((second_sum, relayed))
    own_weights, relayed = lax.optimization_barrier((own_weights, relayed))
    base = call_kernel(
        own_sum_body, [f32(rows)], [own_weights, units, image_add], moved=0, limit=16
    )[0]
    return finish(text_parts, base, image_last)


def solution(mesh):
    in_specs = (P("blk", "tp"), P(("blk", "tp"), None), P(), P(), P(), P(), P())
    out_specs = (P("blk", "tp"), P(("blk", "tp"), None))
    return jax.shard_map(
        per_device, mesh=mesh, in_specs=in_specs, out_specs=out_specs, check_vma=False
    )
```

```python
import functools
import math

import jax
import jax.numpy as jnp
from jax import lax
from jax.experimental import pallas as pl
from jax.experimental.pallas import tpu as pltpu
from jax.sharding import PartitionSpec as P

TILE = 128
SLOTS = 3
WAIT_FLOPS = 20_000_000_000
TEXT_PIECES = 3
ACC_PIECES = 2
LAST_PIECES = 2
CORES = 2
EPS = 1e-06
LOG2E = math.log2(math.e)
MIB = 1024 * 1024

VMEM_SPEC = pl.BlockSpec(memory_space=pltpu.VMEM)
ANY_SPEC = pl.BlockSpec(memory_space=pl.ANY)
SMEM_SPEC = pl.BlockSpec(memory_space=pltpu.SMEM)


def call_kernel(
    body,
    outs,
    operands,
    scalars=0,
    anywhere=(),
    outs_anywhere=False,
    scratch=(),
    flops=0,
    moved=None,
    limit=24,
):
    if moved is None:
        moved = sum(x.size * x.dtype.itemsize for x in operands)
        moved += sum(math.prod(o.shape) * o.dtype.itemsize for o in outs)
    specs = [SMEM_SPEC] * scalars + [VMEM_SPEC] * (len(operands) - scalars)
    for at in anywhere:
        specs[at] = ANY_SPEC
    return list(
        pl.pallas_call(
            body,
            out_shape=outs,
            in_specs=specs,
            out_specs=[ANY_SPEC if outs_anywhere else VMEM_SPEC] * len(outs),
            scratch_shapes=list(scratch),
            compiler_params=pltpu.CompilerParams(vmem_limit_bytes=limit * MIB),
            cost_estimate=pl.CostEstimate(flops=flops, bytes_accessed=moved, transcendentals=0),
        )(*operands)
    )


def struct(shape, dtype):
    return jax.ShapeDtypeStruct(shape, dtype)


def row_scales(square_sum):
    return lax.rsqrt(square_sum + EPS)


def column_of(row):
    return jnp.broadcast_to(row, (TILE, TILE)).T


def dot_nt(left, right):
    return lax.dot_general(
        left, right, (((1,), (1,)), ((), ())), preferred_element_type=jnp.float32
    )


def dot_tn(left, right):
    return lax.dot_general(
        left, right, (((0,), (0,)), ((), ())), preferred_element_type=jnp.float32
    )


def far_first(k, chunks):
    return (chunks - k) % chunks


def feature_slice(peer, width):
    return pl.ds(pl.multiple_of(peer * width, width), width)


def pick_body(text_ref, *out_refs):
    place = lax.axis_index("tp")
    rows = out_refs[0].shape[0]
    for k, out_ref in enumerate(out_refs):
        peer = place ^ far_first(k, len(out_refs))
        out_ref[...] = text_ref[pl.ds(pl.multiple_of(peer * rows, rows), rows), :]


def unit_text_body(chunks, *refs):
    chunk_refs, (unit_ref, scale_ref) = refs[:chunks], refs[chunks : chunks + 2]
    piece_refs = refs[chunks + 2 :]
    place = lax.axis_index("tp")
    rows, width = chunk_refs[0].shape
    for first in range(0, rows, TILE):
        part = pl.ds(first, TILE)
        parts = [ref[part, :].astype(jnp.float32) for ref in chunk_refs]
        scales = row_scales(sum(jnp.sum(x * x, axis=-1, keepdims=True) for x in parts))
        scale_ref[part, :] = jnp.broadcast_to(scales, (TILE, TILE))
        for k, x in enumerate(parts):
            unit_ref[part, feature_slice(place ^ far_first(k, chunks), width)] = (x * scales).astype(jnp.bfloat16)
    split_rows(unit_ref, piece_refs)


def split_rows(whole_ref, piece_refs):
    for at, ref in enumerate(piece_refs):
        ref[...] = whole_ref[pl.ds(at * ref.shape[0], ref.shape[0]), :]


def join_rows(piece_refs, whole_ref):
    for at, ref in enumerate(piece_refs):
        whole_ref[pl.ds(at * ref.shape[0], ref.shape[0]), :] = ref[...]


def unit_images(ref, image_ref, scale_ref=None):
    step = 64
    for first in range(0, ref.shape[0], step):
        part = pl.ds(first, step)
        values = ref[part, :].astype(jnp.float32)
        scales = row_scales(jnp.sum(values * values, axis=-1, keepdims=True))
        image_ref[part, :] = (values * scales).astype(jnp.bfloat16)
        if scale_ref is not None:
            scale_ref[part, :] = jnp.broadcast_to(scales, (step, TILE))


def unit_images_body(raw_ref, out_ref):
    unit_images(raw_ref, out_ref)


def own_images_body(raw_ref, out_ref, raw_out_ref, scale_ref):
    unit_images(raw_ref, out_ref, scale_ref)
    raw_out_ref[...] = raw_ref[...]


def near_images_body(first_ref, second_unit_ref, out_ref):
    rows = first_ref.shape[0]
    unit_images(first_ref, out_ref)
    out_ref[rows:, :] = second_unit_ref[...]


def neighbour_bits(shard):
    core = shard % CORES
    return 2 << core, 4 >> core


def list_body(groups, tiles, chips, *refs):
    scale_ref, bias_ref, blocks_ref, bucket_ref, positive_ref = refs[:5]
    line_ref, amount_ref, column_ref, row_ref, match_ref, own_ref = refs[5:]
    here, place = lax.axis_index("blk"), lax.axis_index("tp")
    scale = scale_ref[0]
    line_ref[pl.ds(0, 1), :] = jnp.full((1, TILE), -scale * LOG2E, jnp.float32)
    line_ref[pl.ds(1, 1), :] = jnp.full((1, TILE), -bias_ref[0] * LOG2E, jnp.float32)
    if chips == 4:
        first, second = neighbour_bits(here)
        shards = [here, here ^ first, here ^ second, here ^ 6]
    else:
        shards = [chip * CORES + here % CORES for chip in range(chips)]
    count = len(shards) * tiles

    def first_tile(shard):
        return (shard * groups + place) * tiles

    for n, shard in enumerate(shards):
        own_ref[pl.ds(n, 1), :] = jnp.full((1, TILE), jnp.where(shard == here, 1.0, 0.0))
        for j in range(tiles):
            column_ref[pl.ds(n * tiles + j, 1), :] = bucket_ref[pl.ds(first_tile(shard) + j, 1), :]
    for at in range(CORES * tiles):
        tile = first_tile(here ^ (at // tiles)) + at % tiles
        row_ref[pl.ds(at * TILE, TILE), :] = column_of(bucket_ref[pl.ds(tile, 1), :])
        if at < tiles:
            ids = lax.broadcasted_iota(jnp.int32, (1, TILE), 1) + tile * TILE
            matched = column_of(positive_ref[pl.ds(tile, 1), :]) == ids
            match_ref[pl.ds(at * TILE, TILE), :] = jnp.where(matched, 1.0, 0.0)
        for n, shard in enumerate(shards):
            entries = [blocks_ref[slot, shard, tile] for slot in range(SLOTS)]
            for j in range(tiles):
                listed = sum(jnp.where(entry == j, 1.0, 0.0) for entry in entries)
                amount_ref[pl.ds(at * count + n * tiles + j, 1), :] = jnp.full(
                    (1, TILE), scale * listed, jnp.float32
                )


class Pairs:
    count = 6

    def __init__(self, refs, tiles):
        self.line_ref, self.amount_ref, self.column_ref = refs[:3]
        self.row_ref, self.match_ref, self.own_ref = refs[3:6]
        self.tiles = tiles

    def weigh(self, products, half, group, weight_ref, top, left, own=None):
        tiles = self.tiles
        slope, offset = self.line_ref[pl.ds(0, 1), :], self.line_ref[pl.ds(1, 1), :]
        count = self.column_ref.shape[0]
        for a in range(tiles):
            at = half * tiles + a
            row_bucket = self.row_ref[pl.ds(at * TILE, TILE), :]
            for j in range(tiles):
                n = group * tiles + j
                amount = self.amount_ref[pl.ds(at * count + n, 1), :]
                power = (
                    products[a * TILE : (a + 1) * TILE, j * TILE : (j + 1) * TILE] * slope + offset
                )
                factor = jnp.where(row_bucket == self.column_ref[pl.ds(n, 1), :], amount, 0.0)
                if own and a == j:
                    match = self.match_ref[pl.ds(a * TILE, TILE), :]
                    if own == "search":
                        match = match * self.own_ref[pl.ds(group, 1), :]
                    power = jnp.where(match > 0.0, -power, power)
                    factor = jnp.where(match > 0.0, -amount, factor)
                inverse = pl.reciprocal(1.0 + jnp.exp2(power), approx=True)
                weight_ref[pl.ds(top + a * TILE, TILE), pl.ds(left + j * TILE, TILE)] = (
                    factor * inverse
                ).astype(jnp.bfloat16)


def near_own_body(tiles, *refs):
    pairs = Pairs(refs, tiles)
    unit_ref, own_image_ref, near_image_ref, own_weight_ref, weight_ref = refs[Pairs.count :]
    rows = unit_ref.shape[0]
    first = dot_nt(unit_ref[...], near_image_ref[pl.ds(0, rows), :])
    second = dot_nt(unit_ref[...], near_image_ref[pl.ds(rows, rows), :])
    pairs.weigh(first, 0, 1, weight_ref, 0, 0)
    own = dot_nt(unit_ref[...], own_image_ref[...])
    pairs.weigh(second, 0, 2, weight_ref, 0, rows)
    pairs.weigh(own, 0, 0, own_weight_ref, 0, 0, "diagonal")


def first_sum_body(tiles, *refs):
    pairs = Pairs(refs, tiles)
    own_unit_ref, near_image_ref, weight_in_ref = refs[Pairs.count : Pairs.count + 3]
    piece_refs = refs[Pairs.count + 3 : Pairs.count + 3 + TEXT_PIECES]
    unit_ref, weight_ref, sum_ref = refs[Pairs.count + 3 + TEXT_PIECES :]
    rows = own_unit_ref.shape[0]
    for at, ref in enumerate(piece_refs):
        unit_ref[pl.ds(rows + at * ref.shape[0], ref.shape[0]), :] = ref[...]
    unit_ref[:rows, :] = own_unit_ref[...]
    weight_ref[:rows, :] = weight_in_ref[:, :rows]
    products = dot_nt(unit_ref[rows:, :], near_image_ref[pl.ds(0, rows), :])
    pairs.weigh(products, 1, 1, weight_ref, rows, 0)
    sum_ref[...] = dot_tn(weight_ref[...], unit_ref[...]).astype(jnp.bfloat16)


def near_sum_body(tiles, *refs):
    pairs = Pairs(refs, tiles)
    unit_ref, own_image_ref, near_image_ref, own_weight_in_ref, weight_in_ref, first_ref = refs[
        Pairs.count : Pairs.count + 6
    ]
    own_weight_ref, acc_ref, weight_ref = refs[Pairs.count + 6 :]
    rows = own_image_ref.shape[0]
    second = dot_nt(unit_ref[rows:, :], near_image_ref[pl.ds(rows, rows), :])
    own = dot_nt(unit_ref[rows:, :], own_image_ref[...])
    own_weight_ref[:rows, :] = own_weight_in_ref[...]
    weight_ref[:, :rows] = first_ref[...]
    weight_ref[:rows, rows:] = weight_in_ref[:, rows:]
    pairs.weigh(second, 1, 2, weight_ref, rows, rows)
    pairs.weigh(own, 1, 0, own_weight_ref, rows, 0)
    acc_ref[...] = jnp.dot(
        weight_ref[...], near_image_ref[...], preferred_element_type=jnp.float32
    )


def far_weights_body(tiles, *refs):
    pairs = Pairs(refs, tiles)
    unit_ref, own_image_ref, own_weight_ref, raw_ref = refs[Pairs.count : Pairs.count + 4]
    weight_ref, image_ref = refs[Pairs.count + 4 :]
    rows = raw_ref.shape[0]
    unit_images(raw_ref, image_ref.at[pl.ds(rows, rows), :])
    products = dot_nt(unit_ref[...], image_ref[rows:, :])
    for half in range(CORES):
        part = products[half * rows : (half + 1) * rows, :]
        pairs.weigh(part, half, 3, weight_ref, half * rows, rows)
    image_ref[:rows, :] = own_image_ref[...]
    weight_ref[:, :rows] = own_weight_ref[...]


def far_sum_body(weight_ref, unit_ref, *out_refs):
    rows = weight_ref.shape[1] // 2
    total = dot_tn(weight_ref[:, rows:], unit_ref[...]).astype(jnp.bfloat16)
    size = rows // len(out_refs)
    for at, ref in enumerate(out_refs):
        ref[...] = total[at * size : (at + 1) * size, :]


def text_sum_body(half, weight_ref, image_ref, acc_ref, *out_refs):
    rows = weight_ref.shape[0] // CORES
    size = out_refs[0].shape[0]
    part = pl.ds(half * rows, rows)
    acc = acc_ref[part, :] + jnp.dot(
        weight_ref[part, :], image_ref[...], preferred_element_type=jnp.float32
    )
    for at, ref in enumerate(out_refs):
        ref[...] = acc[at * size : (at + 1) * size, :].astype(ref.dtype)


def second_sum_body(weight_ref, unit_ref, add_ref, out_ref, add_out_ref):
    rows = out_ref.shape[0]
    out_ref[...] = dot_tn(weight_ref[:, rows:], unit_ref[...])
    add_out_ref[...] = add_ref[...]


def own_sum_body(weight_ref, unit_ref, add_ref, out_ref):
    out_ref[...] = dot_tn(weight_ref[...], unit_ref[...]) + add_ref[...].astype(jnp.float32)


def all_body(tiles, chips, *refs):
    pairs = Pairs(refs, tiles)
    own_ref, other_ref, piece_ref = refs[Pairs.count : Pairs.count + 3]
    outs = refs[Pairs.count + 3 :]
    spread_ref, acc_ref, acc_piece_refs = outs[0], outs[1], outs[2 : 2 + ACC_PIECES]
    image_ref, weight_ref = outs[2 + ACC_PIECES :]
    rows = own_ref.shape[0]
    unit_images(piece_ref, image_ref)
    for half, text_ref in enumerate((own_ref, other_ref)):
        for chip in range(chips):
            products = dot_nt(text_ref[...], image_ref[pl.ds(chip * rows, rows), :])
            pairs.weigh(
                products, half, chip, weight_ref, half * rows, chip * rows, None if half else "search"
            )
        acc = jnp.dot(
            weight_ref[pl.ds(half * rows, rows), :],
            image_ref[...],
            preferred_element_type=jnp.float32,
        )
        if half == 0:
            acc_ref[...] = acc
            continue
        size = rows // ACC_PIECES
        for at, ref in enumerate(acc_piece_refs):
            ref[...] = acc[at * size : (at + 1) * size, :].astype(jnp.bfloat16)
    for chip in range(chips):
        columns = pl.ds(chip * rows, rows)
        total = dot_tn(weight_ref[pl.ds(0, rows), columns], own_ref[...])
        total += dot_tn(weight_ref[pl.ds(rows, rows), columns], other_ref[...])
        spread_ref[columns, :] = total.astype(jnp.bfloat16)


def relay_body(at, sum_ref, in_ref, out_ref):
    size = in_ref.shape[0]
    part = sum_ref[pl.ds(at * size, size), :]
    out_ref[...] = (part + in_ref[...].astype(jnp.float32)).astype(jnp.bfloat16)


def text_grad_body(chunks, *refs):
    scale_ref, raw_refs, acc_ref = refs[0], refs[1 : 1 + chunks], refs[1 + chunks]
    add_refs, out_refs = refs[2 + chunks : -chunks], refs[-chunks:]
    place = lax.axis_index("tp")
    rows, width = raw_refs[0].shape
    size = add_refs[0].shape[0]
    for first in range(0, rows, TILE // 2):
        part = pl.ds(first, TILE // 2)
        scales = scale_ref[part, :1]
        raws = [ref[part, :].astype(jnp.float32) for ref in raw_refs]
        accs = []
        for k in range(chunks):
            features = feature_slice(place ^ far_first(k, chunks), width)
            added = add_refs[first // size][pl.ds(first % size, TILE // 2), features]
            accs.append(acc_ref[part, features] + added.astype(jnp.float32))
        inner = sum(jnp.sum(x * a, axis=-1, keepdims=True) for x, a in zip(raws, accs))
        inner = inner * scales * scales
        for k in range(chunks):
            out_refs[k][part, :] = (scales * (accs[k] - raws[k] * inner)).astype(jnp.bfloat16)


def arrived_body(*refs):
    out_ref = refs[-1]
    out_ref[...] = sum(ref[: out_ref.shape[0], : out_ref.shape[1]] for ref in refs[:-1])


def finish_body(chunks, adds, *refs):
    part_refs, (raw_ref, scale_ref, sum_ref) = refs[:chunks], refs[chunks : chunks + 3]
    piece_refs = refs[chunks + 3 : chunks + 3 + adds]
    text_ref, image_ref, grad_ref, sems = refs[-4:]
    place = lax.axis_index("tp")
    rows = part_refs[0].shape[0]
    copies = []
    for k in range(chunks):
        peer = place ^ far_first(k, chunks)
        for first in range(0, rows, TILE):
            block = pl.ds(pl.multiple_of(peer * rows + first, TILE), TILE)
            copies.append(
                pltpu.make_async_copy(
                    part_refs[k].at[pl.ds(first, TILE), :],
                    text_ref.at[block, :],
                    sems.at[len(copies)],
                )
            )
            copies[-1].start()
    for first in range(0, rows, TILE // 2):
        part = pl.ds(first, TILE // 2)
        raw = raw_ref[part, :].astype(jnp.float32)
        scales = scale_ref[part, :1]
        acc = sum_ref[part, :]
        if piece_refs:
            size = piece_refs[0].shape[0]
            piece = piece_refs[first // size][pl.ds(first % size, TILE // 2), :]
            acc = acc + piece.astype(jnp.float32)
        inner = jnp.sum(raw * acc, axis=-1, keepdims=True) * scales * scales
        grad_ref[part, :] = (scales * (acc - raw * inner)).astype(jnp.bfloat16)
        copies.append(
            pltpu.make_async_copy(
                grad_ref.at[part, :], image_ref.at[part, :], sems.at[len(copies)]
            )
        )
        copies[-1].start()
    for copy in copies:
        copy.wait()


def swap(value, axis, bits):
    count = lax.axis_size(axis)
    return lax.ppermute(value, axis, [(i, i ^ bits) for i in range(count)])


def swap_near(value, which):
    count = lax.axis_size("blk")
    return lax.ppermute(value, "blk", [(i, i ^ neighbour_bits(i)[which]) for i in range(count)])


def swap_chunks(chunks):
    count = len(chunks)
    return chunks[:1] + [swap(chunks[k], "tp", far_first(k, count)) for k in range(1, count)]


def per_device(text_emb, image_emb, logit_scale, logit_bias, bucket, positive, blocks):
    groups = lax.axis_size("tp")
    shards = lax.axis_size("blk")
    chips = shards // CORES
    rows, embed = image_emb.shape
    tiles = rows // TILE
    width = text_emb.shape[1]
    square = chips == 4

    def bf16(count, columns=embed):
        return struct((count, columns), jnp.bfloat16)

    def f32(count, columns=embed):
        return struct((count, columns), jnp.float32)

    def i32(count, columns):
        return struct((count, columns), jnp.int32)

    picked = call_kernel(pick_body, [bf16(rows, width)] * groups, [text_emb], limit=8)
    text_raw = swap_chunks(picked)
    if square:
        from_second = swap_near(image_emb, 1)
    else:
        same_core = [[chip * CORES + core for chip in range(chips)] for core in range(CORES)]
        gathered = lax.all_gather(
            image_emb, "blk", axis=0, tiled=True, axis_index_groups=same_core
        )
        _, image_raw, image_scales = call_kernel(
            own_images_body, [bf16(rows), bf16(rows), f32(rows, TILE)], [image_emb], limit=8
        )
    lists = call_kernel(
        functools.partial(list_body, groups, tiles, chips),
        [
            f32(2, TILE),
            f32(CORES * tiles * chips * tiles, TILE),
            i32(chips * tiles, TILE),
            i32(CORES * rows, TILE),
            f32(rows, TILE),
            f32(chips, TILE),
        ],
        [
            logit_scale,
            logit_bias,
            blocks.transpose(2, 1, 0),
            bucket.reshape(-1, TILE),
            positive.reshape(-1, TILE),
        ],
        scalars=3,
        limit=8,
    )
    if square:
        own_images, image_raw, image_scales = call_kernel(
            own_images_body, [bf16(rows), bf16(rows), f32(rows, TILE)], [image_emb], limit=8
        )
        image_sent, own_images = lax.optimization_barrier((image_emb, own_images))
        from_first = swap_near(image_sent, 0)
        from_second, own_images, *lists = lax.optimization_barrier(
            (from_second, own_images, *lists)
        )
        from_far = swap_near(from_second, 0)
        second_images = call_kernel(
            unit_images_body, [bf16(rows)], [from_second], flops=WAIT_FLOPS // 2, limit=8
        )[0]
        near_images = call_kernel(
            near_images_body, [bf16(2 * rows)], [from_first, second_images], limit=8
        )[0]
        text_raw[-1], near_images = lax.optimization_barrier((text_raw[-1], near_images))
    text_own, text_scales, *pieces = call_kernel(
        functools.partial(unit_text_body, groups),
        [bf16(rows), f32(rows, TILE)] + [bf16(rows // TEXT_PIECES)] * TEXT_PIECES,
        text_raw,
        limit=8,
    )
    text_other = [swap(piece, "blk", 1) for piece in pieces]
    unit_flops = 2 * rows * rows * embed

    def finish_text(acc_own, acc_other):
        parts = call_kernel(
            functools.partial(text_grad_body, groups),
            [bf16(rows, width)] * groups,
            [text_scales] + text_raw + [acc_own] + [swap(piece, "blk", 1) for piece in acc_other],
            limit=16,
        )
        return swap_chunks(parts)

    def finish(text_parts, total, pieces):
        arrived = call_kernel(
            arrived_body,
            [struct((16, TILE), jnp.bfloat16)],
            text_parts[1:],
            flops=WAIT_FLOPS,
            limit=8,
        )
        return tuple(
            call_kernel(
                functools.partial(finish_body, groups, len(pieces)),
                [bf16(groups * rows, width), bf16(rows)],
                text_parts + [image_raw, image_scales, total] + pieces + arrived,
                outs_anywhere=True,
                scratch=[
                    pltpu.VMEM((rows, embed), jnp.bfloat16),
                    pltpu.SemaphoreType.DMA(((groups + 2) * tiles,)),
                ],
                limit=8,
            )
        )

    if not square:
        columns = gathered.shape[0]
        spread, acc_own, *acc_other = call_kernel(
            functools.partial(all_body, tiles, chips),
            [bf16(columns), f32(rows)] + [bf16(rows // ACC_PIECES)] * ACC_PIECES,
            lists + [text_own, jnp.concatenate(text_other), gathered],
            scratch=[
                pltpu.VMEM((columns, embed), jnp.bfloat16),
                pltpu.VMEM((2 * rows, columns), jnp.bfloat16),
            ],
            flops=6 * chips * unit_flops,
            limit=56,
        )
        text_parts = finish_text(acc_own, acc_other)
        parts = lax.all_to_all(
            spread, "blk", split_axis=0, concat_axis=0, tiled=True, axis_index_groups=same_core
        )
        total = jnp.sum(parts.reshape(-1, rows, embed).astype(jnp.float32), axis=0)
        return finish(text_parts, total, [])

    own_weights, near_weights = call_kernel(
        functools.partial(near_own_body, tiles),
        [bf16(rows, rows), bf16(rows, 2 * rows)],
        lists + [text_own, own_images, near_images],
        limit=16,
    )
    units, first_weights, first_sum = call_kernel(
        functools.partial(first_sum_body, tiles),
        [bf16(2 * rows), bf16(2 * rows, rows), bf16(rows)],
        lists + [text_own, near_images, near_weights] + text_other,
        limit=16,
    )
    image_add = swap_near(first_sum, 0)
    own_weights, acc, near_weights = call_kernel(
        functools.partial(near_sum_body, tiles),
        [bf16(2 * rows, rows), f32(2 * rows), bf16(2 * rows, 2 * rows)],
        lists + [units, own_images, near_images, own_weights, near_weights, first_weights],
        limit=24,
    )
    own_weights, from_far = lax.optimization_barrier((own_weights, from_far))
    far_weights, far_images = call_kernel(
        functools.partial(far_weights_body, tiles),
        [bf16(2 * rows, 2 * rows), bf16(2 * rows)],
        lists + [units, own_images, own_weights, from_far],
        limit=16,
    )
    far_sum = call_kernel(
        far_sum_body, [bf16(rows // LAST_PIECES)] * LAST_PIECES, [far_weights, units], limit=16
    )
    far_images, far_sum[0] = lax.optimization_barrier((far_images, far_sum[0]))
    acc_other = call_kernel(
        functools.partial(text_sum_body, 1),
        [bf16(rows // ACC_PIECES)] * ACC_PIECES,
        [far_weights, far_images, acc],
        limit=16,
    )
    far_images, acc_other[0] = lax.optimization_barrier((far_images, acc_other[0]))
    acc_own = call_kernel(
        functools.partial(text_sum_body, 0),
        [f32(rows)],
        [far_weights, far_images, acc],
        limit=16,
    )[0]
    text_parts = finish_text(acc_own, acc_other)
    near_weights, text_parts[0] = lax.optimization_barrier((near_weights, text_parts[0]))
    second_sum, image_add = call_kernel(
        second_sum_body,
        [f32(rows), bf16(rows)],
        [near_weights, units, image_add],
        limit=16,
    )
    image_last = []
    far_in = [swap_near(piece, 0) for piece in far_sum]
    for at, piece in enumerate(far_in):
        relayed = call_kernel(
            functools.partial(relay_body, at),
            [bf16(rows // LAST_PIECES)],
            [second_sum, piece],
            limit=8,
        )[0]
        image_last.append(swap_near(relayed, 1))
        second_sum, relayed = lax.optimization_barrier((second_sum, relayed))
    own_weights, relayed = lax.optimization_barrier((own_weights, relayed))
    base = call_kernel(
        own_sum_body, [f32(rows)], [own_weights, units, image_add], moved=0, limit=16
    )[0]
    return finish(text_parts, base, image_last)


def solution(mesh):
    in_specs = (P("blk", "tp"), P(("blk", "tp"), None), P(), P(), P(), P(), P())
    out_specs = (P("blk", "tp"), P(("blk", "tp"), None))
    return jax.shard_map(
        per_device, mesh=mesh, in_specs=in_specs, out_specs=out_specs, check_vma=False
    )
```

```python
import functools
import math

import jax
import jax.numpy as jnp
from jax import lax
from jax.experimental import pallas as pl
from jax.experimental.pallas import tpu as pltpu
from jax.sharding import PartitionSpec as P

TILE = 128
SLOTS = 3
WAIT_FLOPS = 20_000_000_000
TEXT_PIECES = 3
ACC_PIECES = 2
CORES = 2
EPS = 1e-06
LOG2E = math.log2(math.e)
MIB = 1024 * 1024

VMEM_SPEC = pl.BlockSpec(memory_space=pltpu.VMEM)
ANY_SPEC = pl.BlockSpec(memory_space=pl.ANY)
SMEM_SPEC = pl.BlockSpec(memory_space=pltpu.SMEM)


def call_kernel(
    body,
    outs,
    operands,
    scalars=0,
    anywhere=(),
    outs_anywhere=False,
    scratch=(),
    flops=0,
    moved=None,
    aliases=None,
    limit=24,
):
    if moved is None:
        moved = sum(x.size * x.dtype.itemsize for x in operands)
        moved += sum(math.prod(o.shape) * o.dtype.itemsize for o in outs)
    specs = [SMEM_SPEC] * scalars + [VMEM_SPEC] * (len(operands) - scalars)
    for at in anywhere:
        specs[at] = ANY_SPEC
    return list(
        pl.pallas_call(
            body,
            out_shape=outs,
            in_specs=specs,
            out_specs=[ANY_SPEC if outs_anywhere else VMEM_SPEC] * len(outs),
            scratch_shapes=list(scratch),
            input_output_aliases=aliases or {},
            compiler_params=pltpu.CompilerParams(vmem_limit_bytes=limit * MIB),
            cost_estimate=pl.CostEstimate(flops=flops, bytes_accessed=moved, transcendentals=0),
        )(*operands)
    )


def struct(shape, dtype):
    return jax.ShapeDtypeStruct(shape, dtype)


def row_scales(square_sum):
    return lax.rsqrt(square_sum + EPS)


def column_of(row):
    return jnp.broadcast_to(row, (TILE, TILE)).T


def dot_nt(left, right):
    return lax.dot_general(
        left, right, (((1,), (1,)), ((), ())), preferred_element_type=jnp.float32
    )


def dot_tn(left, right):
    return lax.dot_general(
        left, right, (((0,), (0,)), ((), ())), preferred_element_type=jnp.float32
    )


def far_first(k, chunks):
    return (chunks - k) % chunks


def feature_slice(peer, width):
    return pl.ds(pl.multiple_of(peer * width, width), width)


def pick_body(text_ref, *out_refs):
    place = lax.axis_index("tp")
    rows = out_refs[0].shape[0]
    for k, out_ref in enumerate(out_refs):
        peer = place ^ far_first(k, len(out_refs))
        out_ref[...] = text_ref[pl.ds(pl.multiple_of(peer * rows, rows), rows), :]


def unit_text_body(chunks, *refs):
    chunk_refs, (unit_ref, scale_ref) = refs[:chunks], refs[chunks : chunks + 2]
    piece_refs = refs[chunks + 2 :]
    place = lax.axis_index("tp")
    rows, width = chunk_refs[0].shape
    for first in range(0, rows, TILE):
        part = pl.ds(first, TILE)
        parts = [ref[part, :].astype(jnp.float32) for ref in chunk_refs]
        scales = row_scales(sum(jnp.sum(x * x, axis=-1, keepdims=True) for x in parts))
        scale_ref[part, :] = jnp.broadcast_to(scales, (TILE, TILE))
        for k, x in enumerate(parts):
            unit_ref[part, feature_slice(place ^ far_first(k, chunks), width)] = (x * scales).astype(jnp.bfloat16)
    split_rows(unit_ref, piece_refs)


def split_rows(whole_ref, piece_refs):
    for at, ref in enumerate(piece_refs):
        ref[...] = whole_ref[pl.ds(at * ref.shape[0], ref.shape[0]), :]


def join_rows(piece_refs, whole_ref):
    for at, ref in enumerate(piece_refs):
        whole_ref[pl.ds(at * ref.shape[0], ref.shape[0]), :] = ref[...]


def unit_images(ref, image_ref, scale_ref=None):
    step = 64
    for first in range(0, ref.shape[0], step):
        part = pl.ds(first, step)
        values = ref[part, :].astype(jnp.float32)
        scales = row_scales(jnp.sum(values * values, axis=-1, keepdims=True))
        image_ref[part, :] = (values * scales).astype(jnp.bfloat16)
        if scale_ref is not None:
            scale_ref[part, :] = jnp.broadcast_to(scales, (step, TILE))


def unit_images_body(raw_ref, out_ref):
    unit_images(raw_ref, out_ref)


def own_images_body(raw_ref, out_ref, raw_out_ref, scale_ref):
    unit_images(raw_ref, out_ref, scale_ref)
    raw_out_ref[...] = raw_ref[...]


def near_images_body(first_ref, second_unit_ref, out_ref):
    rows = first_ref.shape[0]
    unit_images(first_ref, out_ref)
    out_ref[rows:, :] = second_unit_ref[...]


def neighbour_bits(shard):
    core = shard % CORES
    return 2 << core, 4 >> core


def list_body(groups, tiles, chips, *refs):
    scale_ref, bias_ref, blocks_ref, bucket_ref, positive_ref = refs[:5]
    line_ref, amount_ref, column_ref, row_ref, match_ref, own_ref = refs[5:]
    here, place = lax.axis_index("blk"), lax.axis_index("tp")
    scale = scale_ref[0]
    line_ref[pl.ds(0, 1), :] = jnp.full((1, TILE), -scale * LOG2E, jnp.float32)
    line_ref[pl.ds(1, 1), :] = jnp.full((1, TILE), -bias_ref[0] * LOG2E, jnp.float32)
    if chips == 4:
        first, second = neighbour_bits(here)
        shards = [here, here ^ first, here ^ second, here ^ 6]
    else:
        shards = [chip * CORES + here % CORES for chip in range(chips)]
    count = len(shards) * tiles

    def first_tile(shard):
        return (shard * groups + place) * tiles

    for n, shard in enumerate(shards):
        own_ref[pl.ds(n, 1), :] = jnp.full((1, TILE), jnp.where(shard == here, 1.0, 0.0))
        for j in range(tiles):
            column_ref[pl.ds(n * tiles + j, 1), :] = bucket_ref[pl.ds(first_tile(shard) + j, 1), :]
    for at in range(CORES * tiles):
        tile = first_tile(here ^ (at // tiles)) + at % tiles
        row_ref[pl.ds(at * TILE, TILE), :] = column_of(bucket_ref[pl.ds(tile, 1), :])
        if at < tiles:
            ids = lax.broadcasted_iota(jnp.int32, (1, TILE), 1) + tile * TILE
            matched = column_of(positive_ref[pl.ds(tile, 1), :]) == ids
            match_ref[pl.ds(at * TILE, TILE), :] = jnp.where(matched, 1.0, 0.0)
        for n, shard in enumerate(shards):
            entries = [blocks_ref[slot, shard, tile] for slot in range(SLOTS)]
            for j in range(tiles):
                listed = sum(jnp.where(entry == j, 1.0, 0.0) for entry in entries)
                amount_ref[pl.ds(at * count + n * tiles + j, 1), :] = jnp.full(
                    (1, TILE), scale * listed, jnp.float32
                )


class Pairs:
    count = 6

    def __init__(self, refs, tiles):
        self.line_ref, self.amount_ref, self.column_ref = refs[:3]
        self.row_ref, self.match_ref, self.own_ref = refs[3:6]
        self.tiles = tiles

    def weigh(self, products, half, group, weight_ref, top, left, own=None):
        tiles = self.tiles
        slope, offset = self.line_ref[pl.ds(0, 1), :], self.line_ref[pl.ds(1, 1), :]
        count = self.column_ref.shape[0]
        for a in range(tiles):
            at = half * tiles + a
            row_bucket = self.row_ref[pl.ds(at * TILE, TILE), :]
            for j in range(tiles):
                n = group * tiles + j
                amount = self.amount_ref[pl.ds(at * count + n, 1), :]
                power = (
                    products[a * TILE : (a + 1) * TILE, j * TILE : (j + 1) * TILE] * slope + offset
                )
                factor = jnp.where(row_bucket == self.column_ref[pl.ds(n, 1), :], amount, 0.0)
                if own and a == j:
                    match = self.match_ref[pl.ds(a * TILE, TILE), :]
                    if own == "search":
                        match = match * self.own_ref[pl.ds(group, 1), :]
                    power = jnp.where(match > 0.0, -power, power)
                    factor = jnp.where(match > 0.0, -amount, factor)
                inverse = pl.reciprocal(1.0 + jnp.exp2(power), approx=True)
                weight_ref[pl.ds(top + a * TILE, TILE), pl.ds(left + j * TILE, TILE)] = (
                    factor * inverse
                ).astype(jnp.bfloat16)


def near_own_body(tiles, *refs):
    pairs = Pairs(refs, tiles)
    unit_ref, own_image_ref, near_image_ref, own_weight_ref, weight_ref = refs[Pairs.count :]
    rows = unit_ref.shape[0]
    first = dot_nt(unit_ref[...], near_image_ref[pl.ds(0, rows), :])
    second = dot_nt(unit_ref[...], near_image_ref[pl.ds(rows, rows), :])
    pairs.weigh(first, 0, 1, weight_ref, 0, 0)
    own = dot_nt(unit_ref[...], own_image_ref[...])
    pairs.weigh(second, 0, 2, weight_ref, 0, rows)
    pairs.weigh(own, 0, 0, own_weight_ref, 0, 0, "diagonal")


def first_sum_body(tiles, *refs):
    pairs = Pairs(refs, tiles)
    own_unit_ref, near_image_ref, weight_in_ref = refs[Pairs.count : Pairs.count + 3]
    piece_refs = refs[Pairs.count + 3 : Pairs.count + 3 + TEXT_PIECES]
    unit_ref, weight_ref, sum_ref = refs[Pairs.count + 3 + TEXT_PIECES :]
    rows = own_unit_ref.shape[0]
    for at, ref in enumerate(piece_refs):
        unit_ref[pl.ds(rows + at * ref.shape[0], ref.shape[0]), :] = ref[...]
    unit_ref[:rows, :] = own_unit_ref[...]
    weight_ref[:rows, :] = weight_in_ref[:, :rows]
    products = dot_nt(unit_ref[rows:, :], near_image_ref[pl.ds(0, rows), :])
    pairs.weigh(products, 1, 1, weight_ref, rows, 0)
    sum_ref[...] = dot_tn(weight_ref[...], unit_ref[...]).astype(jnp.bfloat16)


def near_sum_body(tiles, *refs):
    pairs = Pairs(refs, tiles)
    unit_ref, own_image_ref, near_image_ref, own_weight_in_ref, weight_in_ref, first_ref = refs[
        Pairs.count : Pairs.count + 6
    ]
    own_weight_ref, acc_ref, weight_ref = refs[Pairs.count + 6 :]
    rows = own_image_ref.shape[0]
    second = dot_nt(unit_ref[rows:, :], near_image_ref[pl.ds(rows, rows), :])
    own = dot_nt(unit_ref[rows:, :], own_image_ref[...])
    own_weight_ref[:rows, :] = own_weight_in_ref[...]
    weight_ref[:, :rows] = first_ref[...]
    weight_ref[:rows, rows:] = weight_in_ref[:, rows:]
    pairs.weigh(second, 1, 2, weight_ref, rows, rows)
    pairs.weigh(own, 1, 0, own_weight_ref, rows, 0)
    acc_ref[...] = jnp.dot(
        weight_ref[...], near_image_ref[...], preferred_element_type=jnp.float32
    )


def far_weights_body(tiles, *refs):
    pairs = Pairs(refs, tiles)
    unit_ref, own_image_ref, own_weight_ref, raw_ref = refs[Pairs.count : Pairs.count + 4]
    weight_ref, image_ref = refs[Pairs.count + 4 :]
    rows = raw_ref.shape[0]
    unit_images(raw_ref, image_ref.at[pl.ds(rows, rows), :])
    products = dot_nt(unit_ref[...], image_ref[rows:, :])
    for half in range(CORES):
        part = products[half * rows : (half + 1) * rows, :]
        pairs.weigh(part, half, 3, weight_ref, half * rows, rows)
    image_ref[:rows, :] = own_image_ref[...]
    weight_ref[:, :rows] = own_weight_ref[...]


def far_sum_body(weight_ref, unit_ref, *out_refs):
    rows = weight_ref.shape[1] // 2
    total = dot_tn(weight_ref[:, rows:], unit_ref[...]).astype(jnp.bfloat16)
    start = 0
    for ref in out_refs:
        ref[...] = total[start : start + ref.shape[0], :]
        start += ref.shape[0]


def text_sum_body(half, weight_ref, image_ref, acc_ref, *out_refs):
    rows = weight_ref.shape[0] // CORES
    size = out_refs[0].shape[0]
    part = pl.ds(half * rows, rows)
    acc = acc_ref[part, :] + jnp.dot(
        weight_ref[part, :], image_ref[...], preferred_element_type=jnp.float32
    )
    for at, ref in enumerate(out_refs):
        ref[...] = acc[at * size : (at + 1) * size, :].astype(ref.dtype)


def second_sum_body(weight_ref, unit_ref, add_ref, out_ref, add_out_ref):
    rows = out_ref.shape[0]
    out_ref[...] = dot_tn(weight_ref[:, rows:], unit_ref[...])
    add_out_ref[...] = add_ref[...]


def own_sum_body(weight_ref, unit_ref, add_ref, out_ref):
    out_ref[...] = dot_tn(weight_ref[...], unit_ref[...]) + add_ref[...].astype(jnp.float32)


def all_body(tiles, chips, *refs):
    pairs = Pairs(refs, tiles)
    own_ref, other_ref, piece_ref = refs[Pairs.count : Pairs.count + 3]
    outs = refs[Pairs.count + 3 :]
    spread_ref, acc_ref, acc_piece_refs = outs[0], outs[1], outs[2 : 2 + ACC_PIECES]
    image_ref, weight_ref = outs[2 + ACC_PIECES :]
    rows = own_ref.shape[0]
    unit_images(piece_ref, image_ref)
    for half, text_ref in enumerate((own_ref, other_ref)):
        for chip in range(chips):
            products = dot_nt(text_ref[...], image_ref[pl.ds(chip * rows, rows), :])
            pairs.weigh(
                products, half, chip, weight_ref, half * rows, chip * rows, None if half else "search"
            )
        acc = jnp.dot(
            weight_ref[pl.ds(half * rows, rows), :],
            image_ref[...],
            preferred_element_type=jnp.float32,
        )
        if half == 0:
            acc_ref[...] = acc
            continue
        size = rows // ACC_PIECES
        for at, ref in enumerate(acc_piece_refs):
            ref[...] = acc[at * size : (at + 1) * size, :].astype(jnp.bfloat16)
    for chip in range(chips):
        columns = pl.ds(chip * rows, rows)
        total = dot_tn(weight_ref[pl.ds(0, rows), columns], own_ref[...])
        total += dot_tn(weight_ref[pl.ds(rows, rows), columns], other_ref[...])
        spread_ref[columns, :] = total.astype(jnp.bfloat16)


def relay_body(start, sum_ref, in_ref, out_ref):
    part = sum_ref[pl.ds(start, in_ref.shape[0]), :]
    out_ref[...] = (part + in_ref[...].astype(jnp.float32)).astype(jnp.bfloat16)


def text_grad_body(chunks, *refs):
    scale_ref, raw_refs, acc_ref = refs[0], refs[1 : 1 + chunks], refs[1 + chunks]
    add_refs, out_refs = refs[2 + chunks : -chunks], refs[-chunks:]
    place = lax.axis_index("tp")
    rows, width = raw_refs[0].shape
    size = add_refs[0].shape[0]
    for first in range(0, rows, TILE // 2):
        part = pl.ds(first, TILE // 2)
        scales = scale_ref[part, :1]
        raws = [ref[part, :].astype(jnp.float32) for ref in raw_refs]
        accs = []
        for k in range(chunks):
            features = feature_slice(place ^ far_first(k, chunks), width)
            added = add_refs[first // size][pl.ds(first % size, TILE // 2), features]
            accs.append(acc_ref[part, features] + added.astype(jnp.float32))
        inner = sum(jnp.sum(x * a, axis=-1, keepdims=True) for x, a in zip(raws, accs))
        inner = inner * scales * scales
        for k in range(chunks):
            out_refs[k][part, :] = (scales * (accs[k] - raws[k] * inner)).astype(jnp.bfloat16)


def arrived_body(*refs):
    out_ref = refs[-1]
    out_ref[...] = sum(ref[: out_ref.shape[0], : out_ref.shape[1]] for ref in refs[:-1])


def finish_rows(start, count, raw_ref, scale_ref, sum_ref, add_ref, grad_ref, out_ref, sems, copies):
    step = TILE // 2
    for first in range(0, count, step):
        part = pl.ds(start + first, step)
        raw = raw_ref[part, :].astype(jnp.float32)
        scales = scale_ref[part, :1]
        acc = sum_ref[part, :]
        if add_ref is not None:
            acc = acc + add_ref[pl.ds(first, step), :].astype(jnp.float32)
        inner = jnp.sum(raw * acc, axis=-1, keepdims=True) * scales * scales
        grad_ref[part, :] = (scales * (acc - raw * inner)).astype(jnp.bfloat16)
        copies.append(
            pltpu.make_async_copy(
                grad_ref.at[part, :], out_ref.at[part, :], sems.at[len(copies)]
            )
        )
        copies[-1].start()


def finish_body(chunks, count, *refs):
    part_refs, (raw_ref, scale_ref, sum_ref) = refs[:chunks], refs[chunks : chunks + 3]
    add_ref = refs[chunks + 3] if len(refs) == chunks + 9 else None
    text_ref, image_ref, grad_ref, sems = refs[-4:]
    place = lax.axis_index("tp")
    rows = part_refs[0].shape[0]
    copies = []
    for k in range(chunks):
        peer = place ^ far_first(k, chunks)
        for first in range(0, rows, TILE):
            block = pl.ds(pl.multiple_of(peer * rows + first, TILE), TILE)
            copies.append(
                pltpu.make_async_copy(
                    part_refs[k].at[pl.ds(first, TILE), :],
                    text_ref.at[block, :],
                    sems.at[len(copies)],
                )
            )
            copies[-1].start()
    finish_rows(
        0, count, raw_ref, scale_ref, sum_ref, add_ref, grad_ref, image_ref, sems, copies
    )
    for copy in copies:
        copy.wait()


def finish_last_body(start, raw_ref, scale_ref, sum_ref, add_ref, _, image_ref, grad_ref, sems):
    copies = []
    count = add_ref.shape[0]
    finish_rows(
        start, count, raw_ref, scale_ref, sum_ref, add_ref, grad_ref, image_ref, sems, copies
    )
    for copy in copies:
        copy.wait()


def swap(value, axis, bits):
    count = lax.axis_size(axis)
    return lax.ppermute(value, axis, [(i, i ^ bits) for i in range(count)])


def swap_near(value, which):
    count = lax.axis_size("blk")
    return lax.ppermute(value, "blk", [(i, i ^ neighbour_bits(i)[which]) for i in range(count)])


def swap_chunks(chunks):
    count = len(chunks)
    return chunks[:1] + [swap(chunks[k], "tp", far_first(k, count)) for k in range(1, count)]


def per_device(text_emb, image_emb, logit_scale, logit_bias, bucket, positive, blocks):
    groups = lax.axis_size("tp")
    shards = lax.axis_size("blk")
    chips = shards // CORES
    rows, embed = image_emb.shape
    tiles = rows // TILE
    width = text_emb.shape[1]
    square = chips == 4

    def bf16(count, columns=embed):
        return struct((count, columns), jnp.bfloat16)

    def f32(count, columns=embed):
        return struct((count, columns), jnp.float32)

    def i32(count, columns):
        return struct((count, columns), jnp.int32)

    picked = call_kernel(pick_body, [bf16(rows, width)] * groups, [text_emb], limit=8)
    text_raw = swap_chunks(picked)
    if square:
        from_second = swap_near(image_emb, 1)
    else:
        same_core = [[chip * CORES + core for chip in range(chips)] for core in range(CORES)]
        gathered = lax.all_gather(
            image_emb, "blk", axis=0, tiled=True, axis_index_groups=same_core
        )
        _, image_raw, image_scales = call_kernel(
            own_images_body, [bf16(rows), bf16(rows), f32(rows, TILE)], [image_emb], limit=8
        )
    lists = call_kernel(
        functools.partial(list_body, groups, tiles, chips),
        [
            f32(2, TILE),
            f32(CORES * tiles * chips * tiles, TILE),
            i32(chips * tiles, TILE),
            i32(CORES * rows, TILE),
            f32(rows, TILE),
            f32(chips, TILE),
        ],
        [
            logit_scale,
            logit_bias,
            blocks.transpose(2, 1, 0),
            bucket.reshape(-1, TILE),
            positive.reshape(-1, TILE),
        ],
        scalars=3,
        limit=8,
    )
    if square:
        own_images, image_raw, image_scales = call_kernel(
            own_images_body, [bf16(rows), bf16(rows), f32(rows, TILE)], [image_emb], limit=8
        )
        image_sent, own_images = lax.optimization_barrier((image_emb, own_images))
        from_first = swap_near(image_sent, 0)
        from_second, own_images, *lists = lax.optimization_barrier(
            (from_second, own_images, *lists)
        )
        from_far = swap_near(from_second, 0)
        second_images = call_kernel(
            unit_images_body, [bf16(rows)], [from_second], flops=WAIT_FLOPS // 2, limit=8
        )[0]
        near_images = call_kernel(
            near_images_body, [bf16(2 * rows)], [from_first, second_images], limit=8
        )[0]
        text_raw[-1], near_images = lax.optimization_barrier((text_raw[-1], near_images))
    text_own, text_scales, *pieces = call_kernel(
        functools.partial(unit_text_body, groups),
        [bf16(rows), f32(rows, TILE)] + [bf16(rows // TEXT_PIECES)] * TEXT_PIECES,
        text_raw,
        limit=8,
    )
    text_other = [swap(piece, "blk", 1) for piece in pieces]
    unit_flops = 2 * rows * rows * embed

    def finish_text(acc_own, acc_other):
        parts = call_kernel(
            functools.partial(text_grad_body, groups),
            [bf16(rows, width)] * groups,
            [text_scales] + text_raw + [acc_own] + [swap(piece, "blk", 1) for piece in acc_other],
            limit=16,
        )
        return swap_chunks(parts)

    def finish(text_parts, total, pieces):
        arrived = call_kernel(
            arrived_body,
            [struct((16, TILE), jnp.bfloat16)],
            text_parts[1:],
            flops=WAIT_FLOPS,
            limit=8,
        )
        head = pieces[0].shape[0] if pieces else rows
        text_grad, image_grad = call_kernel(
            functools.partial(finish_body, groups, head),
            [bf16(groups * rows, width), bf16(rows)],
            text_parts + [image_raw, image_scales, total] + pieces[:1] + arrived,
            outs_anywhere=True,
            scratch=[
                pltpu.VMEM((rows, embed), jnp.bfloat16),
                pltpu.SemaphoreType.DMA(((groups + 2) * tiles,)),
            ],
            limit=8,
        )
        if pieces:
            image_grad = call_kernel(
                functools.partial(finish_last_body, head),
                [bf16(rows)],
                [image_raw, image_scales, total, pieces[1], image_grad],
                anywhere=(4,),
                outs_anywhere=True,
                aliases={4: 0},
                scratch=[
                    pltpu.VMEM((rows, embed), jnp.bfloat16),
                    pltpu.SemaphoreType.DMA((2 * tiles,)),
                ],
                limit=8,
            )[0]
        return (text_grad, image_grad)

    if not square:
        columns = gathered.shape[0]
        spread, acc_own, *acc_other = call_kernel(
            functools.partial(all_body, tiles, chips),
            [bf16(columns), f32(rows)] + [bf16(rows // ACC_PIECES)] * ACC_PIECES,
            lists + [text_own, jnp.concatenate(text_other), gathered],
            scratch=[
                pltpu.VMEM((columns, embed), jnp.bfloat16),
                pltpu.VMEM((2 * rows, columns), jnp.bfloat16),
            ],
            flops=6 * chips * unit_flops,
            limit=56,
        )
        text_parts = finish_text(acc_own, acc_other)
        parts = lax.all_to_all(
            spread, "blk", split_axis=0, concat_axis=0, tiled=True, axis_index_groups=same_core
        )
        total = jnp.sum(parts.reshape(-1, rows, embed).astype(jnp.float32), axis=0)
        return finish(text_parts, total, [])

    own_weights, near_weights = call_kernel(
        functools.partial(near_own_body, tiles),
        [bf16(rows, rows), bf16(rows, 2 * rows)],
        lists + [text_own, own_images, near_images],
        limit=16,
    )
    units, first_weights, first_sum = call_kernel(
        functools.partial(first_sum_body, tiles),
        [bf16(2 * rows), bf16(2 * rows, rows), bf16(rows)],
        lists + [text_own, near_images, near_weights] + text_other,
        limit=16,
    )
    image_add = swap_near(first_sum, 0)
    own_weights, acc, near_weights = call_kernel(
        functools.partial(near_sum_body, tiles),
        [bf16(2 * rows, rows), f32(2 * rows), bf16(2 * rows, 2 * rows)],
        lists + [units, own_images, near_images, own_weights, near_weights, first_weights],
        limit=24,
    )
    own_weights, from_far = lax.optimization_barrier((own_weights, from_far))
    far_weights, far_images = call_kernel(
        functools.partial(far_weights_body, tiles),
        [bf16(2 * rows, 2 * rows), bf16(2 * rows)],
        lists + [units, own_images, own_weights, from_far],
        limit=16,
    )
    sizes = [rows - TILE, TILE]
    far_sum = call_kernel(
        far_sum_body, [bf16(size) for size in sizes], [far_weights, units], limit=16
    )
    far_images, far_sum[0] = lax.optimization_barrier((far_images, far_sum[0]))
    acc_other = call_kernel(
        functools.partial(text_sum_body, 1),
        [bf16(rows // ACC_PIECES)] * ACC_PIECES,
        [far_weights, far_images, acc],
        limit=16,
    )
    far_images, acc_other[0] = lax.optimization_barrier((far_images, acc_other[0]))
    acc_own = call_kernel(
        functools.partial(text_sum_body, 0),
        [f32(rows)],
        [far_weights, far_images, acc],
        limit=16,
    )[0]
    text_parts = finish_text(acc_own, acc_other)
    near_weights, text_parts[0] = lax.optimization_barrier((near_weights, text_parts[0]))
    second_sum, image_add = call_kernel(
        second_sum_body,
        [f32(rows), bf16(rows)],
        [near_weights, units, image_add],
        limit=16,
    )
    image_last = []
    far_in = [swap_near(piece, 0) for piece in far_sum]
    for size, start, piece in zip(sizes, (0, sizes[0]), far_in):
        relayed = call_kernel(
            functools.partial(relay_body, start), [bf16(size)], [second_sum, piece], limit=8
        )[0]
        image_last.append(swap_near(relayed, 1))
        second_sum, relayed = lax.optimization_barrier((second_sum, relayed))
    own_weights, relayed = lax.optimization_barrier((own_weights, relayed))
    base = call_kernel(
        own_sum_body, [f32(rows)], [own_weights, units, image_add], moved=0, limit=16
    )[0]
    return finish(text_parts, base, image_last)


def solution(mesh):
    in_specs = (P("blk", "tp"), P(("blk", "tp"), None), P(), P(), P(), P(), P())
    out_specs = (P("blk", "tp"), P(("blk", "tp"), None))
    return jax.shard_map(
        per_device, mesh=mesh, in_specs=in_specs, out_specs=out_specs, check_vma=False
    )
```

```python
import functools
import math

import jax
import jax.numpy as jnp
from jax import lax
from jax.experimental import pallas as pl
from jax.experimental.pallas import tpu as pltpu
from jax.sharding import PartitionSpec as P

TILE = 128
SLOTS = 3
WAIT_FLOPS = 20_000_000_000
TEXT_PIECES = 3
ACC_PIECES = 2
CORES = 2
EPS = 1e-06
LOG2E = math.log2(math.e)
MIB = 1024 * 1024

VMEM_SPEC = pl.BlockSpec(memory_space=pltpu.VMEM)
ANY_SPEC = pl.BlockSpec(memory_space=pl.ANY)
SMEM_SPEC = pl.BlockSpec(memory_space=pltpu.SMEM)


def call_kernel(
    body,
    outs,
    operands,
    scalars=0,
    anywhere=(),
    outs_anywhere=False,
    scratch=(),
    flops=0,
    moved=None,
    limit=24,
):
    if moved is None:
        moved = sum(x.size * x.dtype.itemsize for x in operands)
        moved += sum(math.prod(o.shape) * o.dtype.itemsize for o in outs)
    specs = [SMEM_SPEC] * scalars + [VMEM_SPEC] * (len(operands) - scalars)
    for at in anywhere:
        specs[at] = ANY_SPEC
    return list(
        pl.pallas_call(
            body,
            out_shape=outs,
            in_specs=specs,
            out_specs=[ANY_SPEC if outs_anywhere else VMEM_SPEC] * len(outs),
            scratch_shapes=list(scratch),
            compiler_params=pltpu.CompilerParams(vmem_limit_bytes=limit * MIB),
            cost_estimate=pl.CostEstimate(flops=flops, bytes_accessed=moved, transcendentals=0),
        )(*operands)
    )


def struct(shape, dtype):
    return jax.ShapeDtypeStruct(shape, dtype)


def row_scales(square_sum):
    return lax.rsqrt(square_sum + EPS)


def column_of(row):
    return jnp.broadcast_to(row, (TILE, TILE)).T


def dot_nt(left, right):
    return lax.dot_general(
        left, right, (((1,), (1,)), ((), ())), preferred_element_type=jnp.float32
    )


def dot_tn(left, right):
    return lax.dot_general(
        left, right, (((0,), (0,)), ((), ())), preferred_element_type=jnp.float32
    )


def far_first(k, chunks):
    return (chunks - k) % chunks


def feature_slice(peer, width):
    return pl.ds(pl.multiple_of(peer * width, width), width)


def pick_body(text_ref, *out_refs):
    place = lax.axis_index("tp")
    rows = out_refs[0].shape[0]
    for k, out_ref in enumerate(out_refs):
        peer = place ^ far_first(k, len(out_refs))
        out_ref[...] = text_ref[pl.ds(pl.multiple_of(peer * rows, rows), rows), :]


def unit_text_body(chunks, *refs):
    chunk_refs, (unit_ref, scale_ref) = refs[:chunks], refs[chunks : chunks + 2]
    piece_refs = refs[chunks + 2 :]
    place = lax.axis_index("tp")
    rows, width = chunk_refs[0].shape
    for first in range(0, rows, TILE):
        part = pl.ds(first, TILE)
        parts = [ref[part, :].astype(jnp.float32) for ref in chunk_refs]
        scales = row_scales(sum(jnp.sum(x * x, axis=-1, keepdims=True) for x in parts))
        scale_ref[part, :] = jnp.broadcast_to(scales, (TILE, TILE))
        for k, x in enumerate(parts):
            unit_ref[part, feature_slice(place ^ far_first(k, chunks), width)] = (x * scales).astype(jnp.bfloat16)
    split_rows(unit_ref, piece_refs)


def split_rows(whole_ref, piece_refs):
    for at, ref in enumerate(piece_refs):
        ref[...] = whole_ref[pl.ds(at * ref.shape[0], ref.shape[0]), :]


def join_rows(piece_refs, whole_ref):
    for at, ref in enumerate(piece_refs):
        whole_ref[pl.ds(at * ref.shape[0], ref.shape[0]), :] = ref[...]


def unit_images(ref, image_ref, scale_ref=None):
    step = 64
    for first in range(0, ref.shape[0], step):
        part = pl.ds(first, step)
        values = ref[part, :].astype(jnp.float32)
        scales = row_scales(jnp.sum(values * values, axis=-1, keepdims=True))
        image_ref[part, :] = (values * scales).astype(jnp.bfloat16)
        if scale_ref is not None:
            scale_ref[part, :] = jnp.broadcast_to(scales, (step, TILE))


def unit_images_body(raw_ref, out_ref):
    unit_images(raw_ref, out_ref)


def own_images_body(raw_ref, out_ref, raw_out_ref, scale_ref):
    unit_images(raw_ref, out_ref, scale_ref)
    raw_out_ref[...] = raw_ref[...]


def near_images_body(first_ref, second_unit_ref, own_unit_ref, out_ref):
    rows = first_ref.shape[0]
    unit_images(first_ref, out_ref)
    out_ref[rows : 2 * rows, :] = second_unit_ref[...]
    out_ref[2 * rows :, :] = own_unit_ref[...]


def neighbour_bits(shard):
    core = shard % CORES
    return 2 << core, 4 >> core


def list_body(groups, tiles, chips, *refs):
    scale_ref, bias_ref, blocks_ref, bucket_ref, positive_ref = refs[:5]
    line_ref, amount_ref, column_ref, row_ref, match_ref, own_ref = refs[5:]
    here, place = lax.axis_index("blk"), lax.axis_index("tp")
    scale = scale_ref[0]
    line_ref[pl.ds(0, 1), :] = jnp.full((1, TILE), -scale * LOG2E, jnp.float32)
    line_ref[pl.ds(1, 1), :] = jnp.full((1, TILE), -bias_ref[0] * LOG2E, jnp.float32)
    if chips == 4:
        first, second = neighbour_bits(here)
        shards = [here, here ^ first, here ^ second, here ^ 6]
    else:
        shards = [chip * CORES + here % CORES for chip in range(chips)]
    count = len(shards) * tiles

    def first_tile(shard):
        return (shard * groups + place) * tiles

    for n, shard in enumerate(shards):
        own_ref[pl.ds(n, 1), :] = jnp.full((1, TILE), jnp.where(shard == here, 1.0, 0.0))
        for j in range(tiles):
            column_ref[pl.ds(n * tiles + j, 1), :] = bucket_ref[pl.ds(first_tile(shard) + j, 1), :]
    for at in range(CORES * tiles):
        tile = first_tile(here ^ (at // tiles)) + at % tiles
        row_ref[pl.ds(at * TILE, TILE), :] = column_of(bucket_ref[pl.ds(tile, 1), :])
        if at < tiles:
            ids = lax.broadcasted_iota(jnp.int32, (1, TILE), 1) + tile * TILE
            matched = column_of(positive_ref[pl.ds(tile, 1), :]) == ids
            match_ref[pl.ds(at * TILE, TILE), :] = jnp.where(matched, 1.0, 0.0)
        for n, shard in enumerate(shards):
            entries = [blocks_ref[slot, shard, tile] for slot in range(SLOTS)]
            for j in range(tiles):
                listed = sum(jnp.where(entry == j, 1.0, 0.0) for entry in entries)
                amount_ref[pl.ds(at * count + n * tiles + j, 1), :] = jnp.full(
                    (1, TILE), scale * listed, jnp.float32
                )


class Pairs:
    count = 6

    def __init__(self, refs, tiles):
        self.line_ref, self.amount_ref, self.column_ref = refs[:3]
        self.row_ref, self.match_ref, self.own_ref = refs[3:6]
        self.tiles = tiles

    def weigh(self, products, half, group, weight_ref, top, left, own=None):
        tiles = self.tiles
        slope, offset = self.line_ref[pl.ds(0, 1), :], self.line_ref[pl.ds(1, 1), :]
        count = self.column_ref.shape[0]
        for a in range(tiles):
            at = half * tiles + a
            row_bucket = self.row_ref[pl.ds(at * TILE, TILE), :]
            for j in range(tiles):
                n = group * tiles + j
                amount = self.amount_ref[pl.ds(at * count + n, 1), :]
                power = (
                    products[a * TILE : (a + 1) * TILE, j * TILE : (j + 1) * TILE] * slope + offset
                )
                factor = jnp.where(row_bucket == self.column_ref[pl.ds(n, 1), :], amount, 0.0)
                if own and a == j:
                    match = self.match_ref[pl.ds(a * TILE, TILE), :]
                    if own == "search":
                        match = match * self.own_ref[pl.ds(group, 1), :]
                    power = jnp.where(match > 0.0, -power, power)
                    factor = jnp.where(match > 0.0, -amount, factor)
                inverse = pl.reciprocal(1.0 + jnp.exp2(power), approx=True)
                weight_ref[pl.ds(top + a * TILE, TILE), pl.ds(left + j * TILE, TILE)] = (
                    factor * inverse
                ).astype(jnp.bfloat16)


def near_own_body(tiles, *refs):
    pairs = Pairs(refs, tiles)
    unit_ref, image_ref, own_weight_ref, weight_ref = refs[Pairs.count :]
    rows = unit_ref.shape[0]
    products = dot_nt(unit_ref[...], image_ref[...])
    pairs.weigh(products[:, :rows], 0, 1, weight_ref, 0, 0)
    pairs.weigh(products[:, rows : 2 * rows], 0, 2, weight_ref, 0, rows)
    pairs.weigh(products[:, 2 * rows :], 0, 0, own_weight_ref, 0, 0, "diagonal")


def first_sum_body(tiles, *refs):
    pairs = Pairs(refs, tiles)
    own_unit_ref, near_image_ref, weight_in_ref = refs[Pairs.count : Pairs.count + 3]
    piece_refs = refs[Pairs.count + 3 : Pairs.count + 3 + TEXT_PIECES]
    unit_ref, weight_ref, sum_ref = refs[Pairs.count + 3 + TEXT_PIECES :]
    rows = own_unit_ref.shape[0]
    for at, ref in enumerate(piece_refs):
        unit_ref[pl.ds(rows + at * ref.shape[0], ref.shape[0]), :] = ref[...]
    unit_ref[:rows, :] = own_unit_ref[...]
    weight_ref[:rows, :] = weight_in_ref[:, :rows]
    products = dot_nt(unit_ref[rows:, :], near_image_ref[pl.ds(0, rows), :])
    pairs.weigh(products, 1, 1, weight_ref, rows, 0)
    sum_ref[...] = dot_tn(weight_ref[...], unit_ref[...]).astype(jnp.bfloat16)


def near_sum_body(tiles, *refs):
    pairs = Pairs(refs, tiles)
    unit_ref, image_ref, own_weight_in_ref, weight_in_ref, first_ref = refs[
        Pairs.count : Pairs.count + 5
    ]
    own_weight_ref, acc_ref, weight_ref = refs[Pairs.count + 5 :]
    rows = first_ref.shape[1]
    products = dot_nt(unit_ref[rows:, :], image_ref[rows:, :])
    own_weight_ref[:rows, :] = own_weight_in_ref[...]
    weight_ref[:, :rows] = first_ref[...]
    weight_ref[:rows, rows:] = weight_in_ref[:, rows:]
    pairs.weigh(products[:, :rows], 1, 2, weight_ref, rows, rows)
    pairs.weigh(products[:, rows:], 1, 0, own_weight_ref, rows, 0)
    acc_ref[...] = jnp.dot(
        weight_ref[...], image_ref[: 2 * rows, :], preferred_element_type=jnp.float32
    )


def far_weights_body(tiles, *refs):
    pairs = Pairs(refs, tiles)
    unit_ref, own_image_ref, own_weight_ref, raw_ref = refs[Pairs.count : Pairs.count + 4]
    weight_ref, image_ref = refs[Pairs.count + 4 :]
    rows = raw_ref.shape[0]
    unit_images(raw_ref, image_ref.at[pl.ds(rows, rows), :])
    products = dot_nt(unit_ref[...], image_ref[rows:, :])
    for half in range(CORES):
        part = products[half * rows : (half + 1) * rows, :]
        pairs.weigh(part, half, 3, weight_ref, half * rows, rows)
    image_ref[:rows, :] = own_image_ref[...]
    weight_ref[:, :rows] = own_weight_ref[...]


def far_sum_body(weight_ref, unit_ref, *out_refs):
    rows = weight_ref.shape[1] // 2
    total = dot_tn(weight_ref[:, rows:], unit_ref[...]).astype(jnp.bfloat16)
    start = 0
    for ref in out_refs:
        ref[...] = total[start : start + ref.shape[0], :]
        start += ref.shape[0]


def text_sum_body(half, weight_ref, image_ref, acc_ref, *out_refs):
    rows = weight_ref.shape[0] // CORES
    size = out_refs[0].shape[0]
    part = pl.ds(half * rows, rows)
    acc = acc_ref[part, :] + jnp.dot(
        weight_ref[part, :], image_ref[...], preferred_element_type=jnp.float32
    )
    for at, ref in enumerate(out_refs):
        ref[...] = acc[at * size : (at + 1) * size, :].astype(ref.dtype)


def second_sum_body(weight_ref, unit_ref, add_ref, out_ref, add_out_ref):
    rows = out_ref.shape[0]
    out_ref[...] = dot_tn(weight_ref[:, rows:], unit_ref[...])
    add_out_ref[...] = add_ref[...]


def own_sum_body(weight_ref, unit_ref, add_ref, out_ref):
    out_ref[...] = dot_tn(weight_ref[...], unit_ref[...]) + add_ref[...].astype(jnp.float32)


def all_body(tiles, chips, *refs):
    pairs = Pairs(refs, tiles)
    own_ref, other_ref, piece_ref = refs[Pairs.count : Pairs.count + 3]
    outs = refs[Pairs.count + 3 :]
    spread_ref, acc_ref, acc_piece_refs = outs[0], outs[1], outs[2 : 2 + ACC_PIECES]
    image_ref, weight_ref = outs[2 + ACC_PIECES :]
    rows = own_ref.shape[0]
    unit_images(piece_ref, image_ref)
    for half, text_ref in enumerate((own_ref, other_ref)):
        for chip in range(chips):
            products = dot_nt(text_ref[...], image_ref[pl.ds(chip * rows, rows), :])
            pairs.weigh(
                products, half, chip, weight_ref, half * rows, chip * rows, None if half else "search"
            )
        acc = jnp.dot(
            weight_ref[pl.ds(half * rows, rows), :],
            image_ref[...],
            preferred_element_type=jnp.float32,
        )
        if half == 0:
            acc_ref[...] = acc
            continue
        size = rows // ACC_PIECES
        for at, ref in enumerate(acc_piece_refs):
            ref[...] = acc[at * size : (at + 1) * size, :].astype(jnp.bfloat16)
    for chip in range(chips):
        columns = pl.ds(chip * rows, rows)
        total = dot_tn(weight_ref[pl.ds(0, rows), columns], own_ref[...])
        total += dot_tn(weight_ref[pl.ds(rows, rows), columns], other_ref[...])
        spread_ref[columns, :] = total.astype(jnp.bfloat16)


def relay_body(start, sum_ref, in_ref, out_ref):
    part = sum_ref[pl.ds(start, in_ref.shape[0]), :]
    out_ref[...] = (part + in_ref[...].astype(jnp.float32)).astype(jnp.bfloat16)


def text_grad_body(chunks, *refs):
    scale_ref, raw_refs, acc_ref = refs[0], refs[1 : 1 + chunks], refs[1 + chunks]
    add_refs, out_refs = refs[2 + chunks : -chunks], refs[-chunks:]
    place = lax.axis_index("tp")
    rows, width = raw_refs[0].shape
    size = add_refs[0].shape[0]
    for first in range(0, rows, TILE // 2):
        part = pl.ds(first, TILE // 2)
        scales = scale_ref[part, :1]
        raws = [ref[part, :].astype(jnp.float32) for ref in raw_refs]
        accs = []
        for k in range(chunks):
            features = feature_slice(place ^ far_first(k, chunks), width)
            added = add_refs[first // size][pl.ds(first % size, TILE // 2), features]
            accs.append(acc_ref[part, features] + added.astype(jnp.float32))
        inner = sum(jnp.sum(x * a, axis=-1, keepdims=True) for x, a in zip(raws, accs))
        inner = inner * scales * scales
        for k in range(chunks):
            out_refs[k][part, :] = (scales * (accs[k] - raws[k] * inner)).astype(jnp.bfloat16)


def arrived_body(*refs):
    out_ref = refs[-1]
    out_ref[...] = sum(ref[: out_ref.shape[0], : out_ref.shape[1]] for ref in refs[:-1])


def finish_rows(start, count, raw_ref, scale_ref, sum_ref, add_ref, grad_ref, out_ref, sems, copies):
    step = TILE // 2
    for first in range(0, count, step):
        part = pl.ds(start + first, step)
        raw = raw_ref[part, :].astype(jnp.float32)
        scales = scale_ref[part, :1]
        acc = sum_ref[part, :]
        if add_ref is not None:
            acc = acc + add_ref[pl.ds(first, step), :].astype(jnp.float32)
        inner = jnp.sum(raw * acc, axis=-1, keepdims=True) * scales * scales
        grad_ref[part, :] = (scales * (acc - raw * inner)).astype(jnp.bfloat16)
        copies.append(
            pltpu.make_async_copy(
                grad_ref.at[part, :], out_ref.at[part, :], sems.at[len(copies)]
            )
        )
        copies[-1].start()


def finish_body(chunks, adds, *refs):
    part_refs, (raw_ref, scale_ref, sum_ref) = refs[:chunks], refs[chunks : chunks + 3]
    add_refs = refs[chunks + 3 : chunks + 3 + adds]
    text_ref, image_ref, grad_ref, sems = refs[-4:]
    place = lax.axis_index("tp")
    rows = part_refs[0].shape[0]
    copies = []
    for k in range(chunks):
        peer = place ^ far_first(k, chunks)
        for first in range(0, rows, TILE):
            block = pl.ds(pl.multiple_of(peer * rows + first, TILE), TILE)
            copies.append(
                pltpu.make_async_copy(
                    part_refs[k].at[pl.ds(first, TILE), :],
                    text_ref.at[block, :],
                    sems.at[len(copies)],
                )
            )
            copies[-1].start()
    start = 0
    for add_ref in add_refs or [None]:
        count = rows if add_ref is None else add_ref.shape[0]
        finish_rows(
            start, count, raw_ref, scale_ref, sum_ref, add_ref, grad_ref, image_ref, sems, copies
        )
        start += count
    for copy in copies:
        copy.wait()


def swap(value, axis, bits):
    count = lax.axis_size(axis)
    return lax.ppermute(value, axis, [(i, i ^ bits) for i in range(count)])


def swap_near(value, which):
    count = lax.axis_size("blk")
    return lax.ppermute(value, "blk", [(i, i ^ neighbour_bits(i)[which]) for i in range(count)])


def swap_chunks(chunks):
    count = len(chunks)
    return chunks[:1] + [swap(chunks[k], "tp", far_first(k, count)) for k in range(1, count)]


def per_device(text_emb, image_emb, logit_scale, logit_bias, bucket, positive, blocks):
    groups = lax.axis_size("tp")
    shards = lax.axis_size("blk")
    chips = shards // CORES
    rows, embed = image_emb.shape
    tiles = rows // TILE
    width = text_emb.shape[1]
    square = chips == 4

    def bf16(count, columns=embed):
        return struct((count, columns), jnp.bfloat16)

    def f32(count, columns=embed):
        return struct((count, columns), jnp.float32)

    def i32(count, columns):
        return struct((count, columns), jnp.int32)

    picked = call_kernel(pick_body, [bf16(rows, width)] * groups, [text_emb], limit=8)
    text_raw = swap_chunks(picked)
    if square:
        from_second = swap_near(image_emb, 1)
    else:
        same_core = [[chip * CORES + core for chip in range(chips)] for core in range(CORES)]
        gathered = lax.all_gather(
            image_emb, "blk", axis=0, tiled=True, axis_index_groups=same_core
        )
        _, image_raw, image_scales = call_kernel(
            own_images_body, [bf16(rows), bf16(rows), f32(rows, TILE)], [image_emb], limit=8
        )
    lists = call_kernel(
        functools.partial(list_body, groups, tiles, chips),
        [
            f32(2, TILE),
            f32(CORES * tiles * chips * tiles, TILE),
            i32(chips * tiles, TILE),
            i32(CORES * rows, TILE),
            f32(rows, TILE),
            f32(chips, TILE),
        ],
        [
            logit_scale,
            logit_bias,
            blocks.transpose(2, 1, 0),
            bucket.reshape(-1, TILE),
            positive.reshape(-1, TILE),
        ],
        scalars=3,
        limit=8,
    )
    if square:
        own_images, image_raw, image_scales = call_kernel(
            own_images_body, [bf16(rows), bf16(rows), f32(rows, TILE)], [image_emb], limit=8
        )
        image_sent, own_images = lax.optimization_barrier((image_emb, own_images))
        from_first = swap_near(image_sent, 0)
        from_second, own_images, *lists = lax.optimization_barrier(
            (from_second, own_images, *lists)
        )
        from_far = swap_near(from_second, 0)
        second_images = call_kernel(
            unit_images_body, [bf16(rows)], [from_second], flops=WAIT_FLOPS // 2, limit=8
        )[0]
        near_images = call_kernel(
            near_images_body, [bf16(3 * rows)], [from_first, second_images, own_images], limit=8
        )[0]
        text_raw[-1], near_images = lax.optimization_barrier((text_raw[-1], near_images))
    text_own, text_scales, *pieces = call_kernel(
        functools.partial(unit_text_body, groups),
        [bf16(rows), f32(rows, TILE)] + [bf16(rows // TEXT_PIECES)] * TEXT_PIECES,
        text_raw,
        limit=8,
    )
    text_other = [swap(piece, "blk", 1) for piece in pieces]
    unit_flops = 2 * rows * rows * embed

    def finish_text(acc_own, acc_other):
        parts = call_kernel(
            functools.partial(text_grad_body, groups),
            [bf16(rows, width)] * groups,
            [text_scales] + text_raw + [acc_own] + [swap(piece, "blk", 1) for piece in acc_other],
            limit=16,
        )
        return swap_chunks(parts)

    def finish(text_parts, total, pieces):
        arrived = call_kernel(
            arrived_body,
            [struct((16, TILE), jnp.bfloat16)],
            text_parts[1:],
            flops=WAIT_FLOPS,
            limit=8,
        )
        return tuple(
            call_kernel(
                functools.partial(finish_body, groups, len(pieces)),
                [bf16(groups * rows, width), bf16(rows)],
                text_parts + [image_raw, image_scales, total] + pieces + arrived,
                outs_anywhere=True,
                scratch=[
                    pltpu.VMEM((rows, embed), jnp.bfloat16),
                    pltpu.SemaphoreType.DMA(((groups + 2) * tiles,)),
                ],
                limit=8,
            )
        )

    if not square:
        columns = gathered.shape[0]
        spread, acc_own, *acc_other = call_kernel(
            functools.partial(all_body, tiles, chips),
            [bf16(columns), f32(rows)] + [bf16(rows // ACC_PIECES)] * ACC_PIECES,
            lists + [text_own, jnp.concatenate(text_other), gathered],
            scratch=[
                pltpu.VMEM((columns, embed), jnp.bfloat16),
                pltpu.VMEM((2 * rows, columns), jnp.bfloat16),
            ],
            flops=6 * chips * unit_flops,
            limit=56,
        )
        text_parts = finish_text(acc_own, acc_other)
        parts = lax.all_to_all(
            spread, "blk", split_axis=0, concat_axis=0, tiled=True, axis_index_groups=same_core
        )
        total = jnp.sum(parts.reshape(-1, rows, embed).astype(jnp.float32), axis=0)
        return finish(text_parts, total, [])

    own_weights, near_weights = call_kernel(
        functools.partial(near_own_body, tiles),
        [bf16(rows, rows), bf16(rows, 2 * rows)],
        lists + [text_own, near_images],
        limit=16,
    )
    units, first_weights, first_sum = call_kernel(
        functools.partial(first_sum_body, tiles),
        [bf16(2 * rows), bf16(2 * rows, rows), bf16(rows)],
        lists + [text_own, near_images, near_weights] + text_other,
        limit=16,
    )
    image_add = swap_near(first_sum, 0)
    own_weights, acc, near_weights = call_kernel(
        functools.partial(near_sum_body, tiles),
        [bf16(2 * rows, rows), f32(2 * rows), bf16(2 * rows, 2 * rows)],
        lists + [units, near_images, own_weights, near_weights, first_weights],
        limit=24,
    )
    own_weights, from_far = lax.optimization_barrier((own_weights, from_far))
    far_weights, far_images = call_kernel(
        functools.partial(far_weights_body, tiles),
        [bf16(2 * rows, 2 * rows), bf16(2 * rows)],
        lists + [units, own_images, own_weights, from_far],
        limit=16,
    )
    sizes = [rows - TILE, TILE]
    far_sum = call_kernel(
        far_sum_body, [bf16(size) for size in sizes], [far_weights, units], limit=16
    )
    far_images, far_sum[0] = lax.optimization_barrier((far_images, far_sum[0]))
    acc_other = call_kernel(
        functools.partial(text_sum_body, 1),
        [bf16(rows // ACC_PIECES)] * ACC_PIECES,
        [far_weights, far_images, acc],
        limit=16,
    )
    far_images, acc_other[0] = lax.optimization_barrier((far_images, acc_other[0]))
    acc_own = call_kernel(
        functools.partial(text_sum_body, 0),
        [f32(rows)],
        [far_weights, far_images, acc],
        limit=16,
    )[0]
    text_parts = finish_text(acc_own, acc_other)
    near_weights, text_parts[0] = lax.optimization_barrier((near_weights, text_parts[0]))
    second_sum, image_add = call_kernel(
        second_sum_body,
        [f32(rows), bf16(rows)],
        [near_weights, units, image_add],
        limit=16,
    )
    image_last = []
    far_in = [swap_near(piece, 0) for piece in far_sum]
    for size, start, piece in zip(sizes, (0, sizes[0]), far_in):
        relayed = call_kernel(
            functools.partial(relay_body, start), [bf16(size)], [second_sum, piece], limit=8
        )[0]
        image_last.append(swap_near(relayed, 1))
        second_sum, relayed = lax.optimization_barrier((second_sum, relayed))
    own_weights, relayed = lax.optimization_barrier((own_weights, relayed))
    base = call_kernel(
        own_sum_body, [f32(rows)], [own_weights, units, image_add], moved=0, limit=16
    )[0]
    return finish(text_parts, base, image_last)


def solution(mesh):
    in_specs = (P("blk", "tp"), P(("blk", "tp"), None), P(), P(), P(), P(), P())
    out_specs = (P("blk", "tp"), P(("blk", "tp"), None))
    return jax.shard_map(
        per_device, mesh=mesh, in_specs=in_specs, out_specs=out_specs, check_vma=False
    )
```

```python
import functools
import math

import jax
import jax.numpy as jnp
from jax import lax
from jax.experimental import pallas as pl
from jax.experimental.pallas import tpu as pltpu
from jax.sharding import PartitionSpec as P

TILE = 128
SLOTS = 3
WAIT_FLOPS = 20_000_000_000
TEXT_PIECES = 3
ACC_PIECES = 2
STEP = 32
CORES = 2
EPS = 1e-06
LOG2E = math.log2(math.e)
MIB = 1024 * 1024

VMEM_SPEC = pl.BlockSpec(memory_space=pltpu.VMEM)
ANY_SPEC = pl.BlockSpec(memory_space=pl.ANY)
SMEM_SPEC = pl.BlockSpec(memory_space=pltpu.SMEM)


def call_kernel(
    body,
    outs,
    operands,
    scalars=0,
    anywhere=(),
    outs_anywhere=False,
    scratch=(),
    flops=0,
    moved=None,
    limit=24,
):
    if moved is None:
        moved = sum(x.size * x.dtype.itemsize for x in operands)
        moved += sum(math.prod(o.shape) * o.dtype.itemsize for o in outs)
    specs = [SMEM_SPEC] * scalars + [VMEM_SPEC] * (len(operands) - scalars)
    for at in anywhere:
        specs[at] = ANY_SPEC
    return list(
        pl.pallas_call(
            body,
            out_shape=outs,
            in_specs=specs,
            out_specs=[ANY_SPEC if outs_anywhere else VMEM_SPEC] * len(outs),
            scratch_shapes=list(scratch),
            compiler_params=pltpu.CompilerParams(vmem_limit_bytes=limit * MIB),
            cost_estimate=pl.CostEstimate(flops=flops, bytes_accessed=moved, transcendentals=0),
        )(*operands)
    )


def struct(shape, dtype):
    return jax.ShapeDtypeStruct(shape, dtype)


def row_scales(square_sum):
    return lax.rsqrt(square_sum + EPS)


def column_of(row):
    return jnp.broadcast_to(row, (TILE, TILE)).T


def dot_nt(left, right):
    return lax.dot_general(
        left, right, (((1,), (1,)), ((), ())), preferred_element_type=jnp.float32
    )


def dot_tn(left, right):
    return lax.dot_general(
        left, right, (((0,), (0,)), ((), ())), preferred_element_type=jnp.float32
    )


def far_first(k, chunks):
    return (chunks - k) % chunks


def feature_slice(peer, width):
    return pl.ds(pl.multiple_of(peer * width, width), width)


def pick_body(text_ref, *out_refs):
    place = lax.axis_index("tp")
    rows = out_refs[0].shape[0]
    for k, out_ref in enumerate(out_refs):
        peer = place ^ far_first(k, len(out_refs))
        out_ref[...] = text_ref[pl.ds(pl.multiple_of(peer * rows, rows), rows), :]


def unit_text_body(chunks, *refs):
    chunk_refs, (unit_ref, scale_ref) = refs[:chunks], refs[chunks : chunks + 2]
    piece_refs = refs[chunks + 2 :]
    place = lax.axis_index("tp")
    rows, width = chunk_refs[0].shape
    for first in range(0, rows, STEP):
        part = pl.ds(first, STEP)
        parts = [ref[part, :].astype(jnp.float32) for ref in chunk_refs]
        scales = row_scales(sum(jnp.sum(x * x, axis=-1, keepdims=True) for x in parts))
        scale_ref[part, :] = jnp.broadcast_to(scales, (STEP, TILE))
        for k, x in enumerate(parts):
            unit_ref[part, feature_slice(place ^ far_first(k, chunks), width)] = (x * scales).astype(jnp.bfloat16)
    split_rows(unit_ref, piece_refs)


def split_rows(whole_ref, piece_refs):
    for at, ref in enumerate(piece_refs):
        ref[...] = whole_ref[pl.ds(at * ref.shape[0], ref.shape[0]), :]


def join_rows(piece_refs, whole_ref):
    for at, ref in enumerate(piece_refs):
        whole_ref[pl.ds(at * ref.shape[0], ref.shape[0]), :] = ref[...]


def unit_images(ref, image_ref, scale_ref=None):
    for first in range(0, ref.shape[0], STEP):
        part = pl.ds(first, STEP)
        values = ref[part, :].astype(jnp.float32)
        scales = row_scales(jnp.sum(values * values, axis=-1, keepdims=True))
        image_ref[part, :] = (values * scales).astype(jnp.bfloat16)
        if scale_ref is not None:
            scale_ref[part, :] = jnp.broadcast_to(scales, (STEP, TILE))


def unit_images_body(raw_ref, out_ref):
    unit_images(raw_ref, out_ref)


def own_images_body(raw_ref, out_ref, raw_out_ref, scale_ref):
    unit_images(raw_ref, out_ref, scale_ref)
    raw_out_ref[...] = raw_ref[...]


def near_images_body(first_ref, second_unit_ref, own_unit_ref, out_ref):
    rows = first_ref.shape[0]
    unit_images(first_ref, out_ref)
    out_ref[rows : 2 * rows, :] = second_unit_ref[...]
    out_ref[2 * rows :, :] = own_unit_ref[...]


def neighbour_bits(shard):
    core = shard % CORES
    return 2 << core, 4 >> core


def list_body(groups, tiles, chips, *refs):
    scale_ref, bias_ref, blocks_ref, bucket_ref, positive_ref = refs[:5]
    line_ref, amount_ref, column_ref, row_ref, match_ref, own_ref = refs[5:]
    here, place = lax.axis_index("blk"), lax.axis_index("tp")
    scale = scale_ref[0]
    line_ref[pl.ds(0, 1), :] = jnp.full((1, TILE), -scale * LOG2E, jnp.float32)
    line_ref[pl.ds(1, 1), :] = jnp.full((1, TILE), -bias_ref[0] * LOG2E, jnp.float32)
    if chips == 4:
        first, second = neighbour_bits(here)
        shards = [here, here ^ first, here ^ second, here ^ 6]
    else:
        shards = [chip * CORES + here % CORES for chip in range(chips)]
    count = len(shards) * tiles

    def first_tile(shard):
        return (shard * groups + place) * tiles

    for n, shard in enumerate(shards):
        own_ref[pl.ds(n, 1), :] = jnp.full((1, TILE), jnp.where(shard == here, 1.0, 0.0))
        for j in range(tiles):
            column_ref[pl.ds(n * tiles + j, 1), :] = bucket_ref[pl.ds(first_tile(shard) + j, 1), :]
    for at in range(CORES * tiles):
        tile = first_tile(here ^ (at // tiles)) + at % tiles
        row_ref[pl.ds(at * TILE, TILE), :] = column_of(bucket_ref[pl.ds(tile, 1), :])
        if at < tiles:
            ids = lax.broadcasted_iota(jnp.int32, (1, TILE), 1) + tile * TILE
            matched = column_of(positive_ref[pl.ds(tile, 1), :]) == ids
            match_ref[pl.ds(at * TILE, TILE), :] = jnp.where(matched, 1.0, 0.0)
        for n, shard in enumerate(shards):
            entries = [blocks_ref[slot, shard, tile] for slot in range(SLOTS)]
            for j in range(tiles):
                listed = sum(jnp.where(entry == j, 1.0, 0.0) for entry in entries)
                amount_ref[pl.ds(at * count + n * tiles + j, 1), :] = jnp.full(
                    (1, TILE), scale * listed, jnp.float32
                )


class Pairs:
    count = 6

    def __init__(self, refs, tiles):
        self.line_ref, self.amount_ref, self.column_ref = refs[:3]
        self.row_ref, self.match_ref, self.own_ref = refs[3:6]
        self.tiles = tiles

    def weigh(self, products, half, group, weight_ref, top, left, own=None):
        tiles = self.tiles
        slope, offset = self.line_ref[pl.ds(0, 1), :], self.line_ref[pl.ds(1, 1), :]
        count = self.column_ref.shape[0]
        for a in range(tiles):
            at = half * tiles + a
            row_bucket = self.row_ref[pl.ds(at * TILE, TILE), :]
            for j in range(tiles):
                n = group * tiles + j
                amount = self.amount_ref[pl.ds(at * count + n, 1), :]
                power = (
                    products[a * TILE : (a + 1) * TILE, j * TILE : (j + 1) * TILE] * slope + offset
                )
                factor = jnp.where(row_bucket == self.column_ref[pl.ds(n, 1), :], amount, 0.0)
                if own and a == j:
                    match = self.match_ref[pl.ds(a * TILE, TILE), :]
                    if own == "search":
                        match = match * self.own_ref[pl.ds(group, 1), :]
                    power = jnp.where(match > 0.0, -power, power)
                    factor = jnp.where(match > 0.0, -amount, factor)
                inverse = pl.reciprocal(1.0 + jnp.exp2(power), approx=True)
                weight_ref[pl.ds(top + a * TILE, TILE), pl.ds(left + j * TILE, TILE)] = (
                    factor * inverse
                ).astype(jnp.bfloat16)


def near_own_body(tiles, *refs):
    pairs = Pairs(refs, tiles)
    unit_ref, image_ref, own_weight_ref, weight_ref = refs[Pairs.count :]
    rows = unit_ref.shape[0]
    products = dot_nt(unit_ref[...], image_ref[...])
    pairs.weigh(products[:, :rows], 0, 1, weight_ref, 0, 0)
    pairs.weigh(products[:, rows : 2 * rows], 0, 2, weight_ref, 0, rows)
    pairs.weigh(products[:, 2 * rows :], 0, 0, own_weight_ref, 0, 0, "diagonal")


def first_sum_body(tiles, *refs):
    pairs = Pairs(refs, tiles)
    own_unit_ref, near_image_ref, weight_in_ref = refs[Pairs.count : Pairs.count + 3]
    piece_refs = refs[Pairs.count + 3 : Pairs.count + 3 + TEXT_PIECES]
    unit_ref, weight_ref, sum_ref = refs[Pairs.count + 3 + TEXT_PIECES :]
    rows = own_unit_ref.shape[0]
    for at, ref in enumerate(piece_refs):
        unit_ref[pl.ds(rows + at * ref.shape[0], ref.shape[0]), :] = ref[...]
    unit_ref[:rows, :] = own_unit_ref[...]
    weight_ref[:rows, :] = weight_in_ref[:, :rows]
    products = dot_nt(unit_ref[rows:, :], near_image_ref[pl.ds(0, rows), :])
    pairs.weigh(products, 1, 1, weight_ref, rows, 0)
    sum_ref[...] = dot_tn(weight_ref[...], unit_ref[...]).astype(jnp.bfloat16)


def near_sum_body(tiles, *refs):
    pairs = Pairs(refs, tiles)
    unit_ref, image_ref, own_weight_in_ref, weight_in_ref, first_ref = refs[
        Pairs.count : Pairs.count + 5
    ]
    own_weight_ref, acc_ref, weight_ref = refs[Pairs.count + 5 :]
    rows = first_ref.shape[1]
    products = dot_nt(unit_ref[rows:, :], image_ref[rows:, :])
    own_weight_ref[:rows, :] = own_weight_in_ref[...]
    weight_ref[:, :rows] = first_ref[...]
    weight_ref[:rows, rows:] = weight_in_ref[:, rows:]
    pairs.weigh(products[:, :rows], 1, 2, weight_ref, rows, rows)
    pairs.weigh(products[:, rows:], 1, 0, own_weight_ref, rows, 0)
    acc_ref[...] = jnp.dot(
        weight_ref[...], image_ref[: 2 * rows, :], preferred_element_type=jnp.float32
    )


def far_weights_body(tiles, *refs):
    pairs = Pairs(refs, tiles)
    unit_ref, own_image_ref, own_weight_ref, raw_ref = refs[Pairs.count : Pairs.count + 4]
    weight_ref, image_ref = refs[Pairs.count + 4 :]
    rows = raw_ref.shape[0]
    unit_images(raw_ref, image_ref.at[pl.ds(rows, rows), :])
    products = dot_nt(unit_ref[...], image_ref[rows:, :])
    for half in range(CORES):
        part = products[half * rows : (half + 1) * rows, :]
        pairs.weigh(part, half, 3, weight_ref, half * rows, rows)
    image_ref[:rows, :] = own_image_ref[...]
    weight_ref[:, :rows] = own_weight_ref[...]


def far_sum_body(weight_ref, unit_ref, *out_refs):
    rows = weight_ref.shape[1] // 2
    total = dot_tn(weight_ref[:, rows:], unit_ref[...]).astype(jnp.bfloat16)
    start = 0
    for ref in out_refs:
        ref[...] = total[start : start + ref.shape[0], :]
        start += ref.shape[0]


def text_sum_body(half, weight_ref, image_ref, acc_ref, *out_refs):
    rows = weight_ref.shape[0] // CORES
    size = out_refs[0].shape[0]
    part = pl.ds(half * rows, rows)
    acc = acc_ref[part, :] + jnp.dot(
        weight_ref[part, :], image_ref[...], preferred_element_type=jnp.float32
    )
    for at, ref in enumerate(out_refs):
        ref[...] = acc[at * size : (at + 1) * size, :].astype(ref.dtype)


def second_sum_body(weight_ref, unit_ref, add_ref, out_ref, add_out_ref):
    rows = out_ref.shape[0]
    out_ref[...] = dot_tn(weight_ref[:, rows:], unit_ref[...])
    add_out_ref[...] = add_ref[...]


def own_sum_body(weight_ref, unit_ref, add_ref, out_ref):
    out_ref[...] = dot_tn(weight_ref[...], unit_ref[...]) + add_ref[...].astype(jnp.float32)


def all_body(tiles, chips, *refs):
    pairs = Pairs(refs, tiles)
    own_ref, other_ref, piece_ref = refs[Pairs.count : Pairs.count + 3]
    outs = refs[Pairs.count + 3 :]
    spread_ref, acc_ref, acc_piece_refs = outs[0], outs[1], outs[2 : 2 + ACC_PIECES]
    image_ref, weight_ref = outs[2 + ACC_PIECES :]
    rows = own_ref.shape[0]
    unit_images(piece_ref, image_ref)
    for half, text_ref in enumerate((own_ref, other_ref)):
        for chip in range(chips):
            products = dot_nt(text_ref[...], image_ref[pl.ds(chip * rows, rows), :])
            pairs.weigh(
                products, half, chip, weight_ref, half * rows, chip * rows, None if half else "search"
            )
        acc = jnp.dot(
            weight_ref[pl.ds(half * rows, rows), :],
            image_ref[...],
            preferred_element_type=jnp.float32,
        )
        if half == 0:
            acc_ref[...] = acc
            continue
        size = rows // ACC_PIECES
        for at, ref in enumerate(acc_piece_refs):
            ref[...] = acc[at * size : (at + 1) * size, :].astype(jnp.bfloat16)
    for chip in range(chips):
        columns = pl.ds(chip * rows, rows)
        total = dot_tn(weight_ref[pl.ds(0, rows), columns], own_ref[...])
        total += dot_tn(weight_ref[pl.ds(rows, rows), columns], other_ref[...])
        spread_ref[columns, :] = total.astype(jnp.bfloat16)


def relay_body(start, sum_ref, in_ref, out_ref):
    part = sum_ref[pl.ds(start, in_ref.shape[0]), :]
    out_ref[...] = (part + in_ref[...].astype(jnp.float32)).astype(jnp.bfloat16)


def text_grad_body(chunks, *refs):
    scale_ref, raw_refs, acc_ref = refs[0], refs[1 : 1 + chunks], refs[1 + chunks]
    add_refs, out_refs = refs[2 + chunks : -chunks], refs[-chunks:]
    place = lax.axis_index("tp")
    rows, width = raw_refs[0].shape
    size = add_refs[0].shape[0]
    for first in range(0, rows, STEP):
        part = pl.ds(first, STEP)
        scales = scale_ref[part, :1]
        raws = [ref[part, :].astype(jnp.float32) for ref in raw_refs]
        accs = []
        for k in range(chunks):
            features = feature_slice(place ^ far_first(k, chunks), width)
            added = add_refs[first // size][pl.ds(first % size, STEP), features]
            accs.append(acc_ref[part, features] + added.astype(jnp.float32))
        inner = sum(jnp.sum(x * a, axis=-1, keepdims=True) for x, a in zip(raws, accs))
        inner = inner * scales * scales
        for k in range(chunks):
            out_refs[k][part, :] = (scales * (accs[k] - raws[k] * inner)).astype(jnp.bfloat16)


def arrived_body(*refs):
    out_ref = refs[-1]
    out_ref[...] = sum(ref[: out_ref.shape[0], : out_ref.shape[1]] for ref in refs[:-1])


def finish_rows(start, count, raw_ref, scale_ref, sum_ref, add_ref, grad_ref, out_ref, sems, copies):
    for block in range(0, count, TILE // 2):
        for first in range(block, block + TILE // 2, STEP):
            part = pl.ds(start + first, STEP)
            raw = raw_ref[part, :].astype(jnp.float32)
            scales = scale_ref[part, :1]
            acc = sum_ref[part, :]
            if add_ref is not None:
                acc = acc + add_ref[pl.ds(first, STEP), :].astype(jnp.float32)
            inner = jnp.sum(raw * acc, axis=-1, keepdims=True) * scales * scales
            grad_ref[part, :] = (scales * (acc - raw * inner)).astype(jnp.bfloat16)
        part = pl.ds(start + block, TILE // 2)
        copies.append(
            pltpu.make_async_copy(
                grad_ref.at[part, :], out_ref.at[part, :], sems.at[len(copies)]
            )
        )
        copies[-1].start()


def finish_body(chunks, adds, *refs):
    part_refs, (raw_ref, scale_ref, sum_ref) = refs[:chunks], refs[chunks : chunks + 3]
    add_refs = refs[chunks + 3 : chunks + 3 + adds]
    text_ref, image_ref, grad_ref, sems = refs[-4:]
    place = lax.axis_index("tp")
    rows = part_refs[0].shape[0]
    copies = []
    for k in range(chunks):
        peer = place ^ far_first(k, chunks)
        for first in range(0, rows, TILE):
            block = pl.ds(pl.multiple_of(peer * rows + first, TILE), TILE)
            copies.append(
                pltpu.make_async_copy(
                    part_refs[k].at[pl.ds(first, TILE), :],
                    text_ref.at[block, :],
                    sems.at[len(copies)],
                )
            )
            copies[-1].start()
    start = 0
    for add_ref in add_refs or [None]:
        count = rows if add_ref is None else add_ref.shape[0]
        finish_rows(
            start, count, raw_ref, scale_ref, sum_ref, add_ref, grad_ref, image_ref, sems, copies
        )
        start += count
    for copy in copies:
        copy.wait()


def swap(value, axis, bits):
    count = lax.axis_size(axis)
    return lax.ppermute(value, axis, [(i, i ^ bits) for i in range(count)])


def swap_near(value, which):
    count = lax.axis_size("blk")
    return lax.ppermute(value, "blk", [(i, i ^ neighbour_bits(i)[which]) for i in range(count)])


def swap_chunks(chunks):
    count = len(chunks)
    return chunks[:1] + [swap(chunks[k], "tp", far_first(k, count)) for k in range(1, count)]


def per_device(text_emb, image_emb, logit_scale, logit_bias, bucket, positive, blocks):
    groups = lax.axis_size("tp")
    shards = lax.axis_size("blk")
    chips = shards // CORES
    rows, embed = image_emb.shape
    tiles = rows // TILE
    width = text_emb.shape[1]
    square = chips == 4

    def bf16(count, columns=embed):
        return struct((count, columns), jnp.bfloat16)

    def f32(count, columns=embed):
        return struct((count, columns), jnp.float32)

    def i32(count, columns):
        return struct((count, columns), jnp.int32)

    picked = call_kernel(pick_body, [bf16(rows, width)] * groups, [text_emb], limit=8)
    text_raw = swap_chunks(picked)
    if square:
        from_second = swap_near(image_emb, 1)
    else:
        same_core = [[chip * CORES + core for chip in range(chips)] for core in range(CORES)]
        gathered = lax.all_gather(
            image_emb, "blk", axis=0, tiled=True, axis_index_groups=same_core
        )
        _, image_raw, image_scales = call_kernel(
            own_images_body, [bf16(rows), bf16(rows), f32(rows, TILE)], [image_emb], limit=8
        )
    lists = call_kernel(
        functools.partial(list_body, groups, tiles, chips),
        [
            f32(2, TILE),
            f32(CORES * tiles * chips * tiles, TILE),
            i32(chips * tiles, TILE),
            i32(CORES * rows, TILE),
            f32(rows, TILE),
            f32(chips, TILE),
        ],
        [
            logit_scale,
            logit_bias,
            blocks.transpose(2, 1, 0),
            bucket.reshape(-1, TILE),
            positive.reshape(-1, TILE),
        ],
        scalars=3,
        limit=8,
    )
    if square:
        own_images, image_raw, image_scales = call_kernel(
            own_images_body, [bf16(rows), bf16(rows), f32(rows, TILE)], [image_emb], limit=8
        )
        image_sent, own_images = lax.optimization_barrier((image_emb, own_images))
        from_first = swap_near(image_sent, 0)
        from_second, own_images, *lists = lax.optimization_barrier(
            (from_second, own_images, *lists)
        )
        from_far = swap_near(from_second, 0)
        second_images = call_kernel(
            unit_images_body, [bf16(rows)], [from_second], flops=WAIT_FLOPS // 2, limit=8
        )[0]
        near_images = call_kernel(
            near_images_body, [bf16(3 * rows)], [from_first, second_images, own_images], limit=8
        )[0]
        text_raw[-1], near_images = lax.optimization_barrier((text_raw[-1], near_images))
    text_own, text_scales, *pieces = call_kernel(
        functools.partial(unit_text_body, groups),
        [bf16(rows), f32(rows, TILE)] + [bf16(rows // TEXT_PIECES)] * TEXT_PIECES,
        text_raw,
        limit=8,
    )
    text_other = [swap(piece, "blk", 1) for piece in pieces]
    unit_flops = 2 * rows * rows * embed

    def finish_text(acc_own, acc_other):
        parts = call_kernel(
            functools.partial(text_grad_body, groups),
            [bf16(rows, width)] * groups,
            [text_scales] + text_raw + [acc_own] + [swap(piece, "blk", 1) for piece in acc_other],
            limit=16,
        )
        return swap_chunks(parts)

    def finish(text_parts, total, pieces):
        arrived = call_kernel(
            arrived_body,
            [struct((16, TILE), jnp.bfloat16)],
            text_parts[1:],
            flops=WAIT_FLOPS,
            limit=8,
        )
        return tuple(
            call_kernel(
                functools.partial(finish_body, groups, len(pieces)),
                [bf16(groups * rows, width), bf16(rows)],
                text_parts + [image_raw, image_scales, total] + pieces + arrived,
                outs_anywhere=True,
                scratch=[
                    pltpu.VMEM((rows, embed), jnp.bfloat16),
                    pltpu.SemaphoreType.DMA(((groups + 2) * tiles,)),
                ],
                limit=8,
            )
        )

    if not square:
        columns = gathered.shape[0]
        spread, acc_own, *acc_other = call_kernel(
            functools.partial(all_body, tiles, chips),
            [bf16(columns), f32(rows)] + [bf16(rows // ACC_PIECES)] * ACC_PIECES,
            lists + [text_own, jnp.concatenate(text_other), gathered],
            scratch=[
                pltpu.VMEM((columns, embed), jnp.bfloat16),
                pltpu.VMEM((2 * rows, columns), jnp.bfloat16),
            ],
            flops=6 * chips * unit_flops,
            limit=56,
        )
        text_parts = finish_text(acc_own, acc_other)
        parts = lax.all_to_all(
            spread, "blk", split_axis=0, concat_axis=0, tiled=True, axis_index_groups=same_core
        )
        total = jnp.sum(parts.reshape(-1, rows, embed).astype(jnp.float32), axis=0)
        return finish(text_parts, total, [])

    own_weights, near_weights = call_kernel(
        functools.partial(near_own_body, tiles),
        [bf16(rows, rows), bf16(rows, 2 * rows)],
        lists + [text_own, near_images],
        limit=16,
    )
    units, first_weights, first_sum = call_kernel(
        functools.partial(first_sum_body, tiles),
        [bf16(2 * rows), bf16(2 * rows, rows), bf16(rows)],
        lists + [text_own, near_images, near_weights] + text_other,
        limit=16,
    )
    image_add = swap_near(first_sum, 0)
    own_weights, acc, near_weights = call_kernel(
        functools.partial(near_sum_body, tiles),
        [bf16(2 * rows, rows), f32(2 * rows), bf16(2 * rows, 2 * rows)],
        lists + [units, near_images, own_weights, near_weights, first_weights],
        limit=24,
    )
    own_weights, from_far = lax.optimization_barrier((own_weights, from_far))
    far_weights, far_images = call_kernel(
        functools.partial(far_weights_body, tiles),
        [bf16(2 * rows, 2 * rows), bf16(2 * rows)],
        lists + [units, own_images, own_weights, from_far],
        limit=16,
    )
    sizes = [rows - TILE, TILE]
    far_sum = call_kernel(
        far_sum_body, [bf16(size) for size in sizes], [far_weights, units], limit=16
    )
    far_images, far_sum[0] = lax.optimization_barrier((far_images, far_sum[0]))
    acc_other = call_kernel(
        functools.partial(text_sum_body, 1),
        [bf16(rows // ACC_PIECES)] * ACC_PIECES,
        [far_weights, far_images, acc],
        limit=16,
    )
    far_images, acc_other[0] = lax.optimization_barrier((far_images, acc_other[0]))
    acc_own = call_kernel(
        functools.partial(text_sum_body, 0),
        [f32(rows)],
        [far_weights, far_images, acc],
        limit=16,
    )[0]
    text_parts = finish_text(acc_own, acc_other)
    near_weights, text_parts[0] = lax.optimization_barrier((near_weights, text_parts[0]))
    second_sum, image_add = call_kernel(
        second_sum_body,
        [f32(rows), bf16(rows)],
        [near_weights, units, image_add],
        limit=16,
    )
    image_last = []
    far_in = [swap_near(piece, 0) for piece in far_sum]
    for size, start, piece in zip(sizes, (0, sizes[0]), far_in):
        relayed = call_kernel(
            functools.partial(relay_body, start), [bf16(size)], [second_sum, piece], limit=8
        )[0]
        image_last.append(swap_near(relayed, 1))
        second_sum, relayed = lax.optimization_barrier((second_sum, relayed))
    own_weights, relayed = lax.optimization_barrier((own_weights, relayed))
    base = call_kernel(
        own_sum_body, [f32(rows)], [own_weights, units, image_add], moved=0, limit=16
    )[0]
    return finish(text_parts, base, image_last)


def solution(mesh):
    in_specs = (P("blk", "tp"), P(("blk", "tp"), None), P(), P(), P(), P(), P())
    out_specs = (P("blk", "tp"), P(("blk", "tp"), None))
    return jax.shard_map(
        per_device, mesh=mesh, in_specs=in_specs, out_specs=out_specs, check_vma=False
    )
```

```python
import functools
import math

import jax
import jax.numpy as jnp
from jax import lax
from jax.experimental import pallas as pl
from jax.experimental.pallas import tpu as pltpu
from jax.sharding import PartitionSpec as P

TILE = 128
SLOTS = 3
WAIT_FLOPS = 20_000_000_000
TEXT_PIECES = 3
ACC_PIECES = 2
STEP = 32
CORES = 2
EPS = 1e-06
LOG2E = math.log2(math.e)
MIB = 1024 * 1024

VMEM_SPEC = pl.BlockSpec(memory_space=pltpu.VMEM)
ANY_SPEC = pl.BlockSpec(memory_space=pl.ANY)
SMEM_SPEC = pl.BlockSpec(memory_space=pltpu.SMEM)


def call_kernel(
    body,
    outs,
    operands,
    scalars=0,
    anywhere=(),
    outs_anywhere=False,
    scratch=(),
    flops=0,
    moved=None,
    limit=24,
):
    if moved is None:
        moved = sum(x.size * x.dtype.itemsize for x in operands)
        moved += sum(math.prod(o.shape) * o.dtype.itemsize for o in outs)
    specs = [SMEM_SPEC] * scalars + [VMEM_SPEC] * (len(operands) - scalars)
    for at in anywhere:
        specs[at] = ANY_SPEC
    return list(
        pl.pallas_call(
            body,
            out_shape=outs,
            in_specs=specs,
            out_specs=[ANY_SPEC if outs_anywhere else VMEM_SPEC] * len(outs),
            scratch_shapes=list(scratch),
            compiler_params=pltpu.CompilerParams(vmem_limit_bytes=limit * MIB),
            cost_estimate=pl.CostEstimate(flops=flops, bytes_accessed=moved, transcendentals=0),
        )(*operands)
    )


def struct(shape, dtype):
    return jax.ShapeDtypeStruct(shape, dtype)


def row_scales(square_sum):
    return lax.rsqrt(square_sum + EPS)


def column_of(row):
    return jnp.broadcast_to(row, (TILE, TILE)).T


def dot_nt(left, right):
    return lax.dot_general(
        left, right, (((1,), (1,)), ((), ())), preferred_element_type=jnp.float32
    )


def dot_tn(left, right):
    return lax.dot_general(
        left, right, (((0,), (0,)), ((), ())), preferred_element_type=jnp.float32
    )


def far_first(k, chunks):
    return (chunks - k) % chunks


def feature_slice(peer, width):
    return pl.ds(pl.multiple_of(peer * width, width), width)


def pick_body(text_ref, *out_refs):
    place = lax.axis_index("tp")
    rows = out_refs[0].shape[0]
    for k, out_ref in enumerate(out_refs):
        peer = place ^ far_first(k, len(out_refs))
        out_ref[...] = text_ref[pl.ds(pl.multiple_of(peer * rows, rows), rows), :]


def unit_text_body(chunks, *refs):
    chunk_refs, (unit_ref, scale_ref) = refs[:chunks], refs[chunks : chunks + 2]
    piece_refs = refs[chunks + 2 :]
    place = lax.axis_index("tp")
    rows, width = chunk_refs[0].shape
    for first in range(0, rows, STEP):
        part = pl.ds(first, STEP)
        parts = [ref[part, :].astype(jnp.float32) for ref in chunk_refs]
        scales = row_scales(sum(jnp.sum(x * x, axis=-1, keepdims=True) for x in parts))
        scale_ref[part, :] = jnp.broadcast_to(scales, (STEP, TILE))
        for k, x in enumerate(parts):
            unit_ref[part, feature_slice(place ^ far_first(k, chunks), width)] = (x * scales).astype(jnp.bfloat16)
    split_rows(unit_ref, piece_refs)


def split_rows(whole_ref, piece_refs):
    for at, ref in enumerate(piece_refs):
        ref[...] = whole_ref[pl.ds(at * ref.shape[0], ref.shape[0]), :]


def join_rows(piece_refs, whole_ref):
    for at, ref in enumerate(piece_refs):
        whole_ref[pl.ds(at * ref.shape[0], ref.shape[0]), :] = ref[...]


def unit_images(ref, image_ref, scale_ref=None):
    for first in range(0, ref.shape[0], STEP):
        part = pl.ds(first, STEP)
        values = ref[part, :].astype(jnp.float32)
        scales = row_scales(jnp.sum(values * values, axis=-1, keepdims=True))
        image_ref[part, :] = (values * scales).astype(jnp.bfloat16)
        if scale_ref is not None:
            scale_ref[part, :] = jnp.broadcast_to(scales, (STEP, TILE))


def unit_images_body(raw_ref, out_ref):
    unit_images(raw_ref, out_ref)


def own_images_body(raw_ref, out_ref, raw_out_ref, scale_ref):
    unit_images(raw_ref, out_ref, scale_ref)
    raw_out_ref[...] = raw_ref[...]


def near_images_body(first_ref, second_unit_ref, own_unit_ref, out_ref):
    rows = first_ref.shape[0]
    unit_images(first_ref, out_ref)
    out_ref[rows : 2 * rows, :] = second_unit_ref[...]
    out_ref[2 * rows :, :] = own_unit_ref[...]


def neighbour_bits(shard):
    core = shard % CORES
    return 2 << core, 4 >> core


def list_body(groups, tiles, chips, *refs):
    scale_ref, bias_ref, blocks_ref, bucket_ref, positive_ref = refs[:5]
    line_ref, amount_ref, column_ref, row_ref, match_ref, own_ref = refs[5:]
    here, place = lax.axis_index("blk"), lax.axis_index("tp")
    scale = scale_ref[0]
    line_ref[pl.ds(0, 1), :] = jnp.full((1, TILE), -scale * LOG2E, jnp.float32)
    line_ref[pl.ds(1, 1), :] = jnp.full((1, TILE), -bias_ref[0] * LOG2E, jnp.float32)
    if chips == 4:
        first, second = neighbour_bits(here)
        shards = [here, here ^ first, here ^ second, here ^ 6]
    else:
        shards = [chip * CORES + here % CORES for chip in range(chips)]
    count = len(shards) * tiles

    def first_tile(shard):
        return (shard * groups + place) * tiles

    for n, shard in enumerate(shards):
        own_ref[pl.ds(n, 1), :] = jnp.full((1, TILE), jnp.where(shard == here, 1.0, 0.0))
        for j in range(tiles):
            column_ref[pl.ds(n * tiles + j, 1), :] = bucket_ref[pl.ds(first_tile(shard) + j, 1), :]
    for at in range(CORES * tiles):
        tile = first_tile(here ^ (at // tiles)) + at % tiles
        row_ref[pl.ds(at * TILE, TILE), :] = column_of(bucket_ref[pl.ds(tile, 1), :])
        if at < tiles:
            ids = lax.broadcasted_iota(jnp.int32, (1, TILE), 1) + tile * TILE
            matched = column_of(positive_ref[pl.ds(tile, 1), :]) == ids
            match_ref[pl.ds(at * TILE, TILE), :] = jnp.where(matched, 1.0, 0.0)
        for n, shard in enumerate(shards):
            entries = [blocks_ref[slot, shard, tile] for slot in range(SLOTS)]
            for j in range(tiles):
                listed = sum(jnp.where(entry == j, 1.0, 0.0) for entry in entries)
                amount_ref[pl.ds(at * count + n * tiles + j, 1), :] = jnp.full(
                    (1, TILE), scale * listed, jnp.float32
                )


class Pairs:
    count = 6

    def __init__(self, refs, tiles):
        self.line_ref, self.amount_ref, self.column_ref = refs[:3]
        self.row_ref, self.match_ref, self.own_ref = refs[3:6]
        self.tiles = tiles

    def weigh(self, products, half, group, weight_ref, top, left, own=None):
        tiles = self.tiles
        slope, offset = self.line_ref[pl.ds(0, 1), :], self.line_ref[pl.ds(1, 1), :]
        count = self.column_ref.shape[0]
        for a in range(tiles):
            at = half * tiles + a
            row_bucket = self.row_ref[pl.ds(at * TILE, TILE), :]
            for j in range(tiles):
                n = group * tiles + j
                amount = self.amount_ref[pl.ds(at * count + n, 1), :]
                power = (
                    products[a * TILE : (a + 1) * TILE, j * TILE : (j + 1) * TILE] * slope + offset
                )
                factor = jnp.where(row_bucket == self.column_ref[pl.ds(n, 1), :], amount, 0.0)
                if own and a == j:
                    match = self.match_ref[pl.ds(a * TILE, TILE), :]
                    if own == "search":
                        match = match * self.own_ref[pl.ds(group, 1), :]
                    power = jnp.where(match > 0.0, -power, power)
                    factor = jnp.where(match > 0.0, -amount, factor)
                inverse = pl.reciprocal(1.0 + jnp.exp2(power), approx=True)
                weight_ref[pl.ds(top + a * TILE, TILE), pl.ds(left + j * TILE, TILE)] = (
                    factor * inverse
                ).astype(jnp.bfloat16)


def near_own_body(tiles, *refs):
    pairs = Pairs(refs, tiles)
    unit_ref, image_ref, own_weight_ref, weight_ref = refs[Pairs.count :]
    rows = unit_ref.shape[0]
    products = dot_nt(unit_ref[...], image_ref[...])
    pairs.weigh(products[:, :rows], 0, 1, weight_ref, 0, 0)
    pairs.weigh(products[:, rows : 2 * rows], 0, 2, weight_ref, 0, rows)
    pairs.weigh(products[:, 2 * rows :], 0, 0, own_weight_ref, 0, 0, "diagonal")


def first_sum_body(tiles, *refs):
    pairs = Pairs(refs, tiles)
    own_unit_ref, near_image_ref, weight_in_ref = refs[Pairs.count : Pairs.count + 3]
    piece_refs = refs[Pairs.count + 3 : Pairs.count + 3 + TEXT_PIECES]
    unit_ref, weight_ref, sum_ref = refs[Pairs.count + 3 + TEXT_PIECES :]
    rows = own_unit_ref.shape[0]
    for at, ref in enumerate(piece_refs):
        unit_ref[pl.ds(rows + at * ref.shape[0], ref.shape[0]), :] = ref[...]
    unit_ref[:rows, :] = own_unit_ref[...]
    weight_ref[:rows, :] = weight_in_ref[:, :rows]
    products = dot_nt(unit_ref[rows:, :], near_image_ref[pl.ds(0, rows), :])
    pairs.weigh(products, 1, 1, weight_ref, rows, 0)
    sum_ref[...] = dot_tn(weight_ref[...], unit_ref[...]).astype(jnp.bfloat16)


def near_sum_body(tiles, *refs):
    pairs = Pairs(refs, tiles)
    unit_ref, image_ref, own_weight_in_ref, weight_in_ref, first_ref = refs[
        Pairs.count : Pairs.count + 5
    ]
    own_weight_ref, acc_ref, weight_ref = refs[Pairs.count + 5 :]
    rows = first_ref.shape[1]
    products = dot_nt(unit_ref[rows:, :], image_ref[rows:, :])
    own_weight_ref[:rows, :] = own_weight_in_ref[...]
    weight_ref[:, :rows] = first_ref[...]
    weight_ref[:rows, rows:] = weight_in_ref[:, rows:]
    pairs.weigh(products[:, :rows], 1, 2, weight_ref, rows, rows)
    pairs.weigh(products[:, rows:], 1, 0, own_weight_ref, rows, 0)
    acc_ref[...] = jnp.dot(
        weight_ref[...], image_ref[: 2 * rows, :], preferred_element_type=jnp.float32
    )


def far_weights_body(tiles, *refs):
    pairs = Pairs(refs, tiles)
    unit_ref, own_image_ref, own_weight_ref, raw_ref = refs[Pairs.count : Pairs.count + 4]
    weight_ref, image_ref = refs[Pairs.count + 4 :]
    rows = raw_ref.shape[0]
    unit_images(raw_ref, image_ref.at[pl.ds(rows, rows), :])
    products = dot_nt(unit_ref[...], image_ref[rows:, :])
    for half in range(CORES):
        part = products[half * rows : (half + 1) * rows, :]
        pairs.weigh(part, half, 3, weight_ref, half * rows, rows)
    image_ref[:rows, :] = own_image_ref[...]
    weight_ref[:, :rows] = own_weight_ref[...]


def far_sum_body(weight_ref, unit_ref, *out_refs):
    rows = weight_ref.shape[1] // 2
    total = dot_tn(weight_ref[:, rows:], unit_ref[...]).astype(jnp.bfloat16)
    start = 0
    for ref in out_refs:
        ref[...] = total[start : start + ref.shape[0], :]
        start += ref.shape[0]


def text_sum_body(half, weight_ref, image_ref, acc_ref, *out_refs):
    rows = weight_ref.shape[0] // CORES
    size = out_refs[0].shape[0]
    part = pl.ds(half * rows, rows)
    acc = acc_ref[part, :] + jnp.dot(
        weight_ref[part, :], image_ref[...], preferred_element_type=jnp.float32
    )
    for at, ref in enumerate(out_refs):
        ref[...] = acc[at * size : (at + 1) * size, :].astype(ref.dtype)


def second_sum_body(weight_ref, unit_ref, add_ref, out_ref, add_out_ref):
    rows = out_ref.shape[0]
    out_ref[...] = dot_tn(weight_ref[:, rows:], unit_ref[...])
    add_out_ref[...] = add_ref[...]


def own_sum_body(weight_ref, unit_ref, add_ref, out_ref):
    out_ref[...] = dot_tn(weight_ref[...], unit_ref[...]) + add_ref[...].astype(jnp.float32)


def all_body(tiles, chips, *refs):
    pairs = Pairs(refs, tiles)
    own_ref, other_ref, piece_ref = refs[Pairs.count : Pairs.count + 3]
    outs = refs[Pairs.count + 3 :]
    spread_ref, acc_ref, acc_piece_refs = outs[0], outs[1], outs[2 : 2 + ACC_PIECES]
    image_ref, weight_ref = outs[2 + ACC_PIECES :]
    rows = own_ref.shape[0]
    unit_images(piece_ref, image_ref)
    for half, text_ref in enumerate((own_ref, other_ref)):
        for chip in range(chips):
            products = dot_nt(text_ref[...], image_ref[pl.ds(chip * rows, rows), :])
            pairs.weigh(
                products, half, chip, weight_ref, half * rows, chip * rows, None if half else "search"
            )
        acc = jnp.dot(
            weight_ref[pl.ds(half * rows, rows), :],
            image_ref[...],
            preferred_element_type=jnp.float32,
        )
        if half == 0:
            acc_ref[...] = acc
            continue
        size = rows // ACC_PIECES
        for at, ref in enumerate(acc_piece_refs):
            ref[...] = acc[at * size : (at + 1) * size, :].astype(jnp.bfloat16)
    for chip in range(chips):
        columns = pl.ds(chip * rows, rows)
        total = dot_tn(weight_ref[pl.ds(0, rows), columns], own_ref[...])
        total += dot_tn(weight_ref[pl.ds(rows, rows), columns], other_ref[...])
        spread_ref[columns, :] = total.astype(jnp.bfloat16)


def relay_body(start, sum_ref, in_ref, out_ref):
    part = sum_ref[pl.ds(start, in_ref.shape[0]), :]
    out_ref[...] = (part + in_ref[...].astype(jnp.float32)).astype(jnp.bfloat16)


def text_grad_body(chunks, *refs):
    scale_ref, raw_refs, acc_ref = refs[0], refs[1 : 1 + chunks], refs[1 + chunks]
    add_refs, out_refs = refs[2 + chunks : -chunks], refs[-chunks:]
    place = lax.axis_index("tp")
    rows, width = raw_refs[0].shape
    size = add_refs[0].shape[0]
    for first in range(0, rows, STEP):
        part = pl.ds(first, STEP)
        scales = scale_ref[part, :1]
        raws = [ref[part, :].astype(jnp.float32) for ref in raw_refs]
        accs = []
        for k in range(chunks):
            features = feature_slice(place ^ far_first(k, chunks), width)
            added = add_refs[first // size][pl.ds(first % size, STEP), features]
            accs.append(acc_ref[part, features] + added.astype(jnp.float32))
        inner = sum(jnp.sum(x * a, axis=-1, keepdims=True) for x, a in zip(raws, accs))
        inner = inner * scales * scales
        for k in range(chunks):
            out_refs[k][part, :] = (scales * (accs[k] - raws[k] * inner)).astype(jnp.bfloat16)


def arrived_body(*refs):
    out_ref = refs[-1]
    out_ref[...] = sum(ref[: out_ref.shape[0], : out_ref.shape[1]] for ref in refs[:-1])


def finish_rows(start, count, raw_ref, scale_ref, sum_ref, add_ref, grad_ref):
    for first in range(0, count, STEP):
        part = pl.ds(start + first, STEP)
        raw = raw_ref[part, :].astype(jnp.float32)
        scales = scale_ref[part, :1]
        acc = sum_ref[part, :]
        if add_ref is not None:
            acc = acc + add_ref[pl.ds(first, STEP), :].astype(jnp.float32)
        inner = jnp.sum(raw * acc, axis=-1, keepdims=True) * scales * scales
        grad_ref[part, :] = (scales * (acc - raw * inner)).astype(jnp.bfloat16)


def finish_body(chunks, adds, *refs):
    part_refs, (raw_ref, scale_ref, sum_ref) = refs[:chunks], refs[chunks : chunks + 3]
    add_refs = refs[chunks + 3 : chunks + 3 + adds]
    text_ref, image_ref, grad_ref, sems = refs[-4:]
    place = lax.axis_index("tp")
    rows = part_refs[0].shape[0]
    copies = []
    for k in range(chunks):
        peer = place ^ far_first(k, chunks)
        for first in range(0, rows, TILE):
            block = pl.ds(pl.multiple_of(peer * rows + first, TILE), TILE)
            copies.append(
                pltpu.make_async_copy(
                    part_refs[k].at[pl.ds(first, TILE), :],
                    text_ref.at[block, :],
                    sems.at[len(copies)],
                )
            )
            copies[-1].start()
    start = 0
    for add_ref in add_refs or [None]:
        count = rows if add_ref is None else add_ref.shape[0]
        finish_rows(start, count, raw_ref, scale_ref, sum_ref, add_ref, grad_ref)
        part = pl.ds(start, count)
        copies.append(
            pltpu.make_async_copy(
                grad_ref.at[part, :], image_ref.at[part, :], sems.at[len(copies)]
            )
        )
        copies[-1].start()
        start += count
    for copy in copies:
        copy.wait()


def swap(value, axis, bits):
    count = lax.axis_size(axis)
    return lax.ppermute(value, axis, [(i, i ^ bits) for i in range(count)])


def swap_near(value, which):
    count = lax.axis_size("blk")
    return lax.ppermute(value, "blk", [(i, i ^ neighbour_bits(i)[which]) for i in range(count)])


def swap_chunks(chunks):
    count = len(chunks)
    return chunks[:1] + [swap(chunks[k], "tp", far_first(k, count)) for k in range(1, count)]


def per_device(text_emb, image_emb, logit_scale, logit_bias, bucket, positive, blocks):
    groups = lax.axis_size("tp")
    shards = lax.axis_size("blk")
    chips = shards // CORES
    rows, embed = image_emb.shape
    tiles = rows // TILE
    width = text_emb.shape[1]
    square = chips == 4

    def bf16(count, columns=embed):
        return struct((count, columns), jnp.bfloat16)

    def f32(count, columns=embed):
        return struct((count, columns), jnp.float32)

    def i32(count, columns):
        return struct((count, columns), jnp.int32)

    picked = call_kernel(pick_body, [bf16(rows, width)] * groups, [text_emb], limit=8)
    text_raw = swap_chunks(picked)
    if square:
        from_second = swap_near(image_emb, 1)
    else:
        same_core = [[chip * CORES + core for chip in range(chips)] for core in range(CORES)]
        gathered = lax.all_gather(
            image_emb, "blk", axis=0, tiled=True, axis_index_groups=same_core
        )
        _, image_raw, image_scales = call_kernel(
            own_images_body, [bf16(rows), bf16(rows), f32(rows, TILE)], [image_emb], limit=8
        )
    lists = call_kernel(
        functools.partial(list_body, groups, tiles, chips),
        [
            f32(2, TILE),
            f32(CORES * tiles * chips * tiles, TILE),
            i32(chips * tiles, TILE),
            i32(CORES * rows, TILE),
            f32(rows, TILE),
            f32(chips, TILE),
        ],
        [
            logit_scale,
            logit_bias,
            blocks.transpose(2, 1, 0),
            bucket.reshape(-1, TILE),
            positive.reshape(-1, TILE),
        ],
        scalars=3,
        limit=8,
    )
    if square:
        own_images, image_raw, image_scales = call_kernel(
            own_images_body, [bf16(rows), bf16(rows), f32(rows, TILE)], [image_emb], limit=8
        )
        image_sent, own_images = lax.optimization_barrier((image_emb, own_images))
        from_first = swap_near(image_sent, 0)
        from_second, own_images, *lists = lax.optimization_barrier(
            (from_second, own_images, *lists)
        )
        from_far = swap_near(from_second, 0)
        second_images = call_kernel(
            unit_images_body, [bf16(rows)], [from_second], flops=WAIT_FLOPS // 2, limit=8
        )[0]
        near_images = call_kernel(
            near_images_body, [bf16(3 * rows)], [from_first, second_images, own_images], limit=8
        )[0]
        text_raw[-1], near_images = lax.optimization_barrier((text_raw[-1], near_images))
    text_own, text_scales, *pieces = call_kernel(
        functools.partial(unit_text_body, groups),
        [bf16(rows), f32(rows, TILE)] + [bf16(rows // TEXT_PIECES)] * TEXT_PIECES,
        text_raw,
        limit=8,
    )
    text_other = [swap(piece, "blk", 1) for piece in pieces]
    unit_flops = 2 * rows * rows * embed

    def finish_text(acc_own, acc_other):
        parts = call_kernel(
            functools.partial(text_grad_body, groups),
            [bf16(rows, width)] * groups,
            [text_scales] + text_raw + [acc_own] + [swap(piece, "blk", 1) for piece in acc_other],
            limit=16,
        )
        return swap_chunks(parts)

    def finish(text_parts, total, pieces):
        arrived = call_kernel(
            arrived_body,
            [struct((16, TILE), jnp.bfloat16)],
            text_parts[1:],
            flops=WAIT_FLOPS,
            limit=8,
        )
        return tuple(
            call_kernel(
                functools.partial(finish_body, groups, len(pieces)),
                [bf16(groups * rows, width), bf16(rows)],
                text_parts + [image_raw, image_scales, total] + pieces + arrived,
                outs_anywhere=True,
                scratch=[
                    pltpu.VMEM((rows, embed), jnp.bfloat16),
                    pltpu.SemaphoreType.DMA(((groups + 2) * tiles,)),
                ],
                limit=8,
            )
        )

    if not square:
        columns = gathered.shape[0]
        spread, acc_own, *acc_other = call_kernel(
            functools.partial(all_body, tiles, chips),
            [bf16(columns), f32(rows)] + [bf16(rows // ACC_PIECES)] * ACC_PIECES,
            lists + [text_own, jnp.concatenate(text_other), gathered],
            scratch=[
                pltpu.VMEM((columns, embed), jnp.bfloat16),
                pltpu.VMEM((2 * rows, columns), jnp.bfloat16),
            ],
            flops=6 * chips * unit_flops,
            limit=56,
        )
        text_parts = finish_text(acc_own, acc_other)
        parts = lax.all_to_all(
            spread, "blk", split_axis=0, concat_axis=0, tiled=True, axis_index_groups=same_core
        )
        total = jnp.sum(parts.reshape(-1, rows, embed).astype(jnp.float32), axis=0)
        return finish(text_parts, total, [])

    own_weights, near_weights = call_kernel(
        functools.partial(near_own_body, tiles),
        [bf16(rows, rows), bf16(rows, 2 * rows)],
        lists + [text_own, near_images],
        limit=16,
    )
    units, first_weights, first_sum = call_kernel(
        functools.partial(first_sum_body, tiles),
        [bf16(2 * rows), bf16(2 * rows, rows), bf16(rows)],
        lists + [text_own, near_images, near_weights] + text_other,
        limit=16,
    )
    image_add = swap_near(first_sum, 0)
    own_weights, acc, near_weights = call_kernel(
        functools.partial(near_sum_body, tiles),
        [bf16(2 * rows, rows), f32(2 * rows), bf16(2 * rows, 2 * rows)],
        lists + [units, near_images, own_weights, near_weights, first_weights],
        limit=24,
    )
    own_weights, from_far = lax.optimization_barrier((own_weights, from_far))
    far_weights, far_images = call_kernel(
        functools.partial(far_weights_body, tiles),
        [bf16(2 * rows, 2 * rows), bf16(2 * rows)],
        lists + [units, own_images, own_weights, from_far],
        limit=16,
    )
    sizes = [rows - TILE, TILE]
    far_sum = call_kernel(
        far_sum_body, [bf16(size) for size in sizes], [far_weights, units], limit=16
    )
    far_images, far_sum[0] = lax.optimization_barrier((far_images, far_sum[0]))
    acc_other = call_kernel(
        functools.partial(text_sum_body, 1),
        [bf16(rows // ACC_PIECES)] * ACC_PIECES,
        [far_weights, far_images, acc],
        limit=16,
    )
    far_images, acc_other[0] = lax.optimization_barrier((far_images, acc_other[0]))
    acc_own = call_kernel(
        functools.partial(text_sum_body, 0),
        [f32(rows)],
        [far_weights, far_images, acc],
        limit=16,
    )[0]
    text_parts = finish_text(acc_own, acc_other)
    near_weights, text_parts[0] = lax.optimization_barrier((near_weights, text_parts[0]))
    second_sum, image_add = call_kernel(
        second_sum_body,
        [f32(rows), bf16(rows)],
        [near_weights, units, image_add],
        limit=16,
    )
    image_last = []
    far_in = [swap_near(piece, 0) for piece in far_sum]
    for size, start, piece in zip(sizes, (0, sizes[0]), far_in):
        relayed = call_kernel(
            functools.partial(relay_body, start), [bf16(size)], [second_sum, piece], limit=8
        )[0]
        image_last.append(swap_near(relayed, 1))
        second_sum, relayed = lax.optimization_barrier((second_sum, relayed))
    own_weights, relayed = lax.optimization_barrier((own_weights, relayed))
    base = call_kernel(
        own_sum_body, [f32(rows)], [own_weights, units, image_add], moved=0, limit=16
    )[0]
    return finish(text_parts, base, image_last)


def solution(mesh):
    in_specs = (P("blk", "tp"), P(("blk", "tp"), None), P(), P(), P(), P(), P())
    out_specs = (P("blk", "tp"), P(("blk", "tp"), None))
    return jax.shard_map(
        per_device, mesh=mesh, in_specs=in_specs, out_specs=out_specs, check_vma=False
    )
```

```python
import functools
import math

import jax
import jax.numpy as jnp
from jax import lax
from jax.experimental import pallas as pl
from jax.experimental.pallas import tpu as pltpu
from jax.sharding import PartitionSpec as P

TILE = 128
SLOTS = 3
WAIT_FLOPS = 20_000_000_000
TEXT_PIECES = 3
ACC_PIECES = 2
STEP = 32
CORES = 2
EPS = 1e-06
LOG2E = math.log2(math.e)
MIB = 1024 * 1024

VMEM_SPEC = pl.BlockSpec(memory_space=pltpu.VMEM)
ANY_SPEC = pl.BlockSpec(memory_space=pl.ANY)
SMEM_SPEC = pl.BlockSpec(memory_space=pltpu.SMEM)


def call_kernel(
    body,
    outs,
    operands,
    scalars=0,
    anywhere=(),
    outs_anywhere=False,
    scratch=(),
    flops=0,
    moved=None,
    limit=24,
):
    if moved is None:
        moved = sum(x.size * x.dtype.itemsize for x in operands)
        moved += sum(math.prod(o.shape) * o.dtype.itemsize for o in outs)
    specs = [SMEM_SPEC] * scalars + [VMEM_SPEC] * (len(operands) - scalars)
    for at in anywhere:
        specs[at] = ANY_SPEC
    return list(
        pl.pallas_call(
            body,
            out_shape=outs,
            in_specs=specs,
            out_specs=[ANY_SPEC if outs_anywhere else VMEM_SPEC] * len(outs),
            scratch_shapes=list(scratch),
            compiler_params=pltpu.CompilerParams(vmem_limit_bytes=limit * MIB),
            cost_estimate=pl.CostEstimate(flops=flops, bytes_accessed=moved, transcendentals=0),
        )(*operands)
    )


def struct(shape, dtype):
    return jax.ShapeDtypeStruct(shape, dtype)


def row_scales(square_sum):
    return lax.rsqrt(square_sum + EPS)


def column_of(row):
    return jnp.broadcast_to(row, (TILE, TILE)).T


def dot_nt(left, right):
    return lax.dot_general(
        left, right, (((1,), (1,)), ((), ())), preferred_element_type=jnp.float32
    )


def dot_tn(left, right):
    return lax.dot_general(
        left, right, (((0,), (0,)), ((), ())), preferred_element_type=jnp.float32
    )


def far_first(k, chunks):
    if chunks > 2 and k in (1, 2):
        return chunks - 3 + k
    return (chunks - k) % chunks


def feature_slice(peer, width):
    return pl.ds(pl.multiple_of(peer * width, width), width)


def pick_body(text_ref, *out_refs):
    place = lax.axis_index("tp")
    rows = out_refs[0].shape[0]
    for k, out_ref in enumerate(out_refs):
        peer = place ^ far_first(k, len(out_refs))
        out_ref[...] = text_ref[pl.ds(pl.multiple_of(peer * rows, rows), rows), :]


def unit_text_body(chunks, *refs):
    chunk_refs, (unit_ref, scale_ref) = refs[:chunks], refs[chunks : chunks + 2]
    piece_refs = refs[chunks + 2 :]
    place = lax.axis_index("tp")
    rows, width = chunk_refs[0].shape
    for first in range(0, rows, STEP):
        part = pl.ds(first, STEP)
        parts = [ref[part, :].astype(jnp.float32) for ref in chunk_refs]
        scales = row_scales(sum(jnp.sum(x * x, axis=-1, keepdims=True) for x in parts))
        scale_ref[part, :] = jnp.broadcast_to(scales, (STEP, TILE))
        for k, x in enumerate(parts):
            unit_ref[part, feature_slice(place ^ far_first(k, chunks), width)] = (x * scales).astype(jnp.bfloat16)
    split_rows(unit_ref, piece_refs)


def split_rows(whole_ref, piece_refs):
    for at, ref in enumerate(piece_refs):
        ref[...] = whole_ref[pl.ds(at * ref.shape[0], ref.shape[0]), :]


def join_rows(piece_refs, whole_ref):
    for at, ref in enumerate(piece_refs):
        whole_ref[pl.ds(at * ref.shape[0], ref.shape[0]), :] = ref[...]


def unit_images(ref, image_ref, scale_ref=None):
    for first in range(0, ref.shape[0], STEP):
        part = pl.ds(first, STEP)
        values = ref[part, :].astype(jnp.float32)
        scales = row_scales(jnp.sum(values * values, axis=-1, keepdims=True))
        image_ref[part, :] = (values * scales).astype(jnp.bfloat16)
        if scale_ref is not None:
            scale_ref[part, :] = jnp.broadcast_to(scales, (STEP, TILE))


def unit_images_body(raw_ref, out_ref):
    unit_images(raw_ref, out_ref)


def own_images_body(raw_ref, out_ref, raw_out_ref, scale_ref):
    unit_images(raw_ref, out_ref, scale_ref)
    raw_out_ref[...] = raw_ref[...]


def near_images_body(first_ref, second_unit_ref, own_unit_ref, out_ref):
    rows = first_ref.shape[0]
    unit_images(first_ref, out_ref)
    out_ref[rows : 2 * rows, :] = second_unit_ref[...]
    out_ref[2 * rows :, :] = own_unit_ref[...]


def neighbour_bits(shard):
    core = shard % CORES
    return 2 << core, 4 >> core


def list_body(groups, tiles, chips, *refs):
    scale_ref, bias_ref, blocks_ref, bucket_ref, positive_ref = refs[:5]
    line_ref, amount_ref, column_ref, row_ref, match_ref, own_ref = refs[5:]
    here, place = lax.axis_index("blk"), lax.axis_index("tp")
    scale = scale_ref[0]
    line_ref[pl.ds(0, 1), :] = jnp.full((1, TILE), -scale * LOG2E, jnp.float32)
    line_ref[pl.ds(1, 1), :] = jnp.full((1, TILE), -bias_ref[0] * LOG2E, jnp.float32)
    if chips == 4:
        first, second = neighbour_bits(here)
        shards = [here, here ^ first, here ^ second, here ^ 6]
    else:
        shards = [chip * CORES + here % CORES for chip in range(chips)]
    count = len(shards) * tiles

    def first_tile(shard):
        return (shard * groups + place) * tiles

    for n, shard in enumerate(shards):
        own_ref[pl.ds(n, 1), :] = jnp.full((1, TILE), jnp.where(shard == here, 1.0, 0.0))
        for j in range(tiles):
            column_ref[pl.ds(n * tiles + j, 1), :] = bucket_ref[pl.ds(first_tile(shard) + j, 1), :]
    for at in range(CORES * tiles):
        tile = first_tile(here ^ (at // tiles)) + at % tiles
        row_ref[pl.ds(at * TILE, TILE), :] = column_of(bucket_ref[pl.ds(tile, 1), :])
        if at < tiles:
            ids = lax.broadcasted_iota(jnp.int32, (1, TILE), 1) + tile * TILE
            matched = column_of(positive_ref[pl.ds(tile, 1), :]) == ids
            match_ref[pl.ds(at * TILE, TILE), :] = jnp.where(matched, 1.0, 0.0)
        for n, shard in enumerate(shards):
            entries = [blocks_ref[slot, shard, tile] for slot in range(SLOTS)]
            for j in range(tiles):
                listed = sum(jnp.where(entry == j, 1.0, 0.0) for entry in entries)
                amount_ref[pl.ds(at * count + n * tiles + j, 1), :] = jnp.full(
                    (1, TILE), scale * listed, jnp.float32
                )


class Pairs:
    count = 6

    def __init__(self, refs, tiles):
        self.line_ref, self.amount_ref, self.column_ref = refs[:3]
        self.row_ref, self.match_ref, self.own_ref = refs[3:6]
        self.tiles = tiles

    def weigh(self, products, half, group, weight_ref, top, left, own=None):
        tiles = self.tiles
        slope, offset = self.line_ref[pl.ds(0, 1), :], self.line_ref[pl.ds(1, 1), :]
        count = self.column_ref.shape[0]
        for a in range(tiles):
            at = half * tiles + a
            row_bucket = self.row_ref[pl.ds(at * TILE, TILE), :]
            for j in range(tiles):
                n = group * tiles + j
                amount = self.amount_ref[pl.ds(at * count + n, 1), :]
                power = (
                    products[a * TILE : (a + 1) * TILE, j * TILE : (j + 1) * TILE] * slope + offset
                )
                factor = jnp.where(row_bucket == self.column_ref[pl.ds(n, 1), :], amount, 0.0)
                if own and a == j:
                    match = self.match_ref[pl.ds(a * TILE, TILE), :]
                    if own == "search":
                        match = match * self.own_ref[pl.ds(group, 1), :]
                    power = jnp.where(match > 0.0, -power, power)
                    factor = jnp.where(match > 0.0, -amount, factor)
                inverse = pl.reciprocal(1.0 + jnp.exp2(power), approx=True)
                weight_ref[pl.ds(top + a * TILE, TILE), pl.ds(left + j * TILE, TILE)] = (
                    factor * inverse
                ).astype(jnp.bfloat16)


def near_own_body(tiles, *refs):
    pairs = Pairs(refs, tiles)
    unit_ref, image_ref, own_weight_ref, weight_ref = refs[Pairs.count :]
    rows = unit_ref.shape[0]
    products = dot_nt(unit_ref[...], image_ref[...])
    pairs.weigh(products[:, :rows], 0, 1, weight_ref, 0, 0)
    pairs.weigh(products[:, rows : 2 * rows], 0, 2, weight_ref, 0, rows)
    pairs.weigh(products[:, 2 * rows :], 0, 0, own_weight_ref, 0, 0, "diagonal")


def first_sum_body(tiles, *refs):
    pairs = Pairs(refs, tiles)
    own_unit_ref, near_image_ref, weight_in_ref = refs[Pairs.count : Pairs.count + 3]
    piece_refs = refs[Pairs.count + 3 : Pairs.count + 3 + TEXT_PIECES]
    unit_ref, weight_ref, sum_ref = refs[Pairs.count + 3 + TEXT_PIECES :]
    rows = own_unit_ref.shape[0]
    for at, ref in enumerate(piece_refs):
        unit_ref[pl.ds(rows + at * ref.shape[0], ref.shape[0]), :] = ref[...]
    unit_ref[:rows, :] = own_unit_ref[...]
    weight_ref[:rows, :] = weight_in_ref[:, :rows]
    products = dot_nt(unit_ref[rows:, :], near_image_ref[pl.ds(0, rows), :])
    pairs.weigh(products, 1, 1, weight_ref, rows, 0)
    sum_ref[...] = dot_tn(weight_ref[...], unit_ref[...]).astype(jnp.bfloat16)


def near_sum_body(tiles, *refs):
    pairs = Pairs(refs, tiles)
    unit_ref, image_ref, own_weight_in_ref, weight_in_ref, first_ref = refs[
        Pairs.count : Pairs.count + 5
    ]
    own_weight_ref, acc_ref, weight_ref = refs[Pairs.count + 5 :]
    rows = first_ref.shape[1]
    products = dot_nt(unit_ref[rows:, :], image_ref[rows:, :])
    own_weight_ref[:rows, :] = own_weight_in_ref[...]
    weight_ref[:, :rows] = first_ref[...]
    weight_ref[:rows, rows:] = weight_in_ref[:, rows:]
    pairs.weigh(products[:, :rows], 1, 2, weight_ref, rows, rows)
    pairs.weigh(products[:, rows:], 1, 0, own_weight_ref, rows, 0)
    acc_ref[...] = jnp.dot(
        weight_ref[...], image_ref[: 2 * rows, :], preferred_element_type=jnp.float32
    )


def far_weights_body(tiles, *refs):
    pairs = Pairs(refs, tiles)
    unit_ref, own_image_ref, own_weight_ref, raw_ref = refs[Pairs.count : Pairs.count + 4]
    weight_ref, image_ref = refs[Pairs.count + 4 :]
    rows = raw_ref.shape[0]
    unit_images(raw_ref, image_ref.at[pl.ds(rows, rows), :])
    products = dot_nt(unit_ref[...], image_ref[rows:, :])
    for half in range(CORES):
        part = products[half * rows : (half + 1) * rows, :]
        pairs.weigh(part, half, 3, weight_ref, half * rows, rows)
    image_ref[:rows, :] = own_image_ref[...]
    weight_ref[:, :rows] = own_weight_ref[...]


def far_sum_body(weight_ref, unit_ref, *out_refs):
    rows = weight_ref.shape[1] // 2
    total = dot_tn(weight_ref[:, rows:], unit_ref[...]).astype(jnp.bfloat16)
    start = 0
    for ref in out_refs:
        ref[...] = total[start : start + ref.shape[0], :]
        start += ref.shape[0]


def text_sum_body(half, weight_ref, image_ref, acc_ref, *out_refs):
    rows = weight_ref.shape[0] // CORES
    size = out_refs[0].shape[0]
    part = pl.ds(half * rows, rows)
    acc = acc_ref[part, :] + jnp.dot(
        weight_ref[part, :], image_ref[...], preferred_element_type=jnp.float32
    )
    for at, ref in enumerate(out_refs):
        ref[...] = acc[at * size : (at + 1) * size, :].astype(ref.dtype)


def second_sum_body(weight_ref, unit_ref, add_ref, out_ref, add_out_ref):
    rows = out_ref.shape[0]
    out_ref[...] = dot_tn(weight_ref[:, rows:], unit_ref[...])
    add_out_ref[...] = add_ref[...]


def own_sum_body(weight_ref, unit_ref, add_ref, out_ref):
    out_ref[...] = dot_tn(weight_ref[...], unit_ref[...]) + add_ref[...].astype(jnp.float32)


def all_body(tiles, chips, *refs):
    pairs = Pairs(refs, tiles)
    own_ref, other_ref, piece_ref = refs[Pairs.count : Pairs.count + 3]
    outs = refs[Pairs.count + 3 :]
    spread_ref, acc_ref, acc_piece_refs = outs[0], outs[1], outs[2 : 2 + ACC_PIECES]
    image_ref, weight_ref = outs[2 + ACC_PIECES :]
    rows = own_ref.shape[0]
    unit_images(piece_ref, image_ref)
    for half, text_ref in enumerate((own_ref, other_ref)):
        for chip in range(chips):
            products = dot_nt(text_ref[...], image_ref[pl.ds(chip * rows, rows), :])
            pairs.weigh(
                products, half, chip, weight_ref, half * rows, chip * rows, None if half else "search"
            )
        acc = jnp.dot(
            weight_ref[pl.ds(half * rows, rows), :],
            image_ref[...],
            preferred_element_type=jnp.float32,
        )
        if half == 0:
            acc_ref[...] = acc
            continue
        size = rows // ACC_PIECES
        for at, ref in enumerate(acc_piece_refs):
            ref[...] = acc[at * size : (at + 1) * size, :].astype(jnp.bfloat16)
    for chip in range(chips):
        columns = pl.ds(chip * rows, rows)
        total = dot_tn(weight_ref[pl.ds(0, rows), columns], own_ref[...])
        total += dot_tn(weight_ref[pl.ds(rows, rows), columns], other_ref[...])
        spread_ref[columns, :] = total.astype(jnp.bfloat16)


def relay_body(start, sum_ref, in_ref, out_ref):
    part = sum_ref[pl.ds(start, in_ref.shape[0]), :]
    out_ref[...] = (part + in_ref[...].astype(jnp.float32)).astype(jnp.bfloat16)


def text_grad_body(chunks, *refs):
    scale_ref, raw_refs, acc_ref = refs[0], refs[1 : 1 + chunks], refs[1 + chunks]
    add_refs, out_refs = refs[2 + chunks : -chunks], refs[-chunks:]
    place = lax.axis_index("tp")
    rows, width = raw_refs[0].shape
    size = add_refs[0].shape[0]
    for first in range(0, rows, STEP):
        part = pl.ds(first, STEP)
        scales = scale_ref[part, :1]
        raws = [ref[part, :].astype(jnp.float32) for ref in raw_refs]
        accs = []
        for k in range(chunks):
            features = feature_slice(place ^ far_first(k, chunks), width)
            added = add_refs[first // size][pl.ds(first % size, STEP), features]
            accs.append(acc_ref[part, features] + added.astype(jnp.float32))
        inner = sum(jnp.sum(x * a, axis=-1, keepdims=True) for x, a in zip(raws, accs))
        inner = inner * scales * scales
        for k in range(chunks):
            out_refs[k][part, :] = (scales * (accs[k] - raws[k] * inner)).astype(jnp.bfloat16)


def arrived_body(*refs):
    out_ref = refs[-1]
    out_ref[...] = sum(ref[: out_ref.shape[0], : out_ref.shape[1]] for ref in refs[:-1])


def finish_rows(start, count, raw_ref, scale_ref, sum_ref, add_ref, grad_ref, out_ref, sems, copies):
    for block in range(0, count, TILE // 2):
        for first in range(block, block + TILE // 2, STEP):
            part = pl.ds(start + first, STEP)
            raw = raw_ref[part, :].astype(jnp.float32)
            scales = scale_ref[part, :1]
            acc = sum_ref[part, :]
            if add_ref is not None:
                acc = acc + add_ref[pl.ds(first, STEP), :].astype(jnp.float32)
            inner = jnp.sum(raw * acc, axis=-1, keepdims=True) * scales * scales
            grad_ref[part, :] = (scales * (acc - raw * inner)).astype(jnp.bfloat16)
        part = pl.ds(start + block, TILE // 2)
        copies.append(
            pltpu.make_async_copy(
                grad_ref.at[part, :], out_ref.at[part, :], sems.at[len(copies)]
            )
        )
        copies[-1].start()


def finish_body(chunks, adds, *refs):
    part_refs, (raw_ref, scale_ref, sum_ref) = refs[:chunks], refs[chunks : chunks + 3]
    add_refs = refs[chunks + 3 : chunks + 3 + adds]
    text_ref, image_ref, grad_ref, sems = refs[-4:]
    place = lax.axis_index("tp")
    rows = part_refs[0].shape[0]
    copies = []
    for k in range(chunks):
        peer = place ^ far_first(k, chunks)
        for first in range(0, rows, TILE):
            block = pl.ds(pl.multiple_of(peer * rows + first, TILE), TILE)
            copies.append(
                pltpu.make_async_copy(
                    part_refs[k].at[pl.ds(first, TILE), :],
                    text_ref.at[block, :],
                    sems.at[len(copies)],
                )
            )
            copies[-1].start()
    start = 0
    for add_ref in add_refs or [None]:
        count = rows if add_ref is None else add_ref.shape[0]
        finish_rows(
            start, count, raw_ref, scale_ref, sum_ref, add_ref, grad_ref, image_ref, sems, copies
        )
        start += count
    for copy in copies:
        copy.wait()


def swap(value, axis, bits):
    count = lax.axis_size(axis)
    return lax.ppermute(value, axis, [(i, i ^ bits) for i in range(count)])


def swap_near(value, which):
    count = lax.axis_size("blk")
    return lax.ppermute(value, "blk", [(i, i ^ neighbour_bits(i)[which]) for i in range(count)])


def swap_chunks(chunks):
    count = len(chunks)
    return chunks[:1] + [swap(chunks[k], "tp", far_first(k, count)) for k in range(1, count)]


def per_device(text_emb, image_emb, logit_scale, logit_bias, bucket, positive, blocks):
    groups = lax.axis_size("tp")
    shards = lax.axis_size("blk")
    chips = shards // CORES
    rows, embed = image_emb.shape
    tiles = rows // TILE
    width = text_emb.shape[1]
    square = chips == 4

    def bf16(count, columns=embed):
        return struct((count, columns), jnp.bfloat16)

    def f32(count, columns=embed):
        return struct((count, columns), jnp.float32)

    def i32(count, columns):
        return struct((count, columns), jnp.int32)

    picked = call_kernel(pick_body, [bf16(rows, width)] * groups, [text_emb], limit=8)
    text_raw = swap_chunks(picked)
    if square:
        from_second = swap_near(image_emb, 1)
    else:
        same_core = [[chip * CORES + core for chip in range(chips)] for core in range(CORES)]
        gathered = lax.all_gather(
            image_emb, "blk", axis=0, tiled=True, axis_index_groups=same_core
        )
        _, image_raw, image_scales = call_kernel(
            own_images_body, [bf16(rows), bf16(rows), f32(rows, TILE)], [image_emb], limit=8
        )
    lists = call_kernel(
        functools.partial(list_body, groups, tiles, chips),
        [
            f32(2, TILE),
            f32(CORES * tiles * chips * tiles, TILE),
            i32(chips * tiles, TILE),
            i32(CORES * rows, TILE),
            f32(rows, TILE),
            f32(chips, TILE),
        ],
        [
            logit_scale,
            logit_bias,
            blocks.transpose(2, 1, 0),
            bucket.reshape(-1, TILE),
            positive.reshape(-1, TILE),
        ],
        scalars=3,
        limit=8,
    )
    if square:
        own_images, image_raw, image_scales = call_kernel(
            own_images_body, [bf16(rows), bf16(rows), f32(rows, TILE)], [image_emb], limit=8
        )
        image_sent, own_images = lax.optimization_barrier((image_emb, own_images))
        from_first = swap_near(image_sent, 0)
        from_second, own_images, *lists = lax.optimization_barrier(
            (from_second, own_images, *lists)
        )
        from_far = swap_near(from_second, 0)
        second_images = call_kernel(
            unit_images_body, [bf16(rows)], [from_second], flops=WAIT_FLOPS // 2, limit=8
        )[0]
        near_images = call_kernel(
            near_images_body, [bf16(3 * rows)], [from_first, second_images, own_images], limit=8
        )[0]
        text_raw[-1], near_images = lax.optimization_barrier((text_raw[-1], near_images))
    text_own, text_scales, *pieces = call_kernel(
        functools.partial(unit_text_body, groups),
        [bf16(rows), f32(rows, TILE)] + [bf16(rows // TEXT_PIECES)] * TEXT_PIECES,
        text_raw,
        limit=8,
    )
    text_other = [swap(piece, "blk", 1) for piece in pieces]
    unit_flops = 2 * rows * rows * embed

    def finish_text(acc_own, acc_other):
        parts = call_kernel(
            functools.partial(text_grad_body, groups),
            [bf16(rows, width)] * groups,
            [text_scales] + text_raw + [acc_own] + [swap(piece, "blk", 1) for piece in acc_other],
            limit=16,
        )
        return swap_chunks(parts)

    def finish(text_parts, total, pieces):
        arrived = call_kernel(
            arrived_body,
            [struct((16, TILE), jnp.bfloat16)],
            text_parts[1:],
            flops=WAIT_FLOPS,
            limit=8,
        )
        return tuple(
            call_kernel(
                functools.partial(finish_body, groups, len(pieces)),
                [bf16(groups * rows, width), bf16(rows)],
                text_parts + [image_raw, image_scales, total] + pieces + arrived,
                outs_anywhere=True,
                scratch=[
                    pltpu.VMEM((rows, embed), jnp.bfloat16),
                    pltpu.SemaphoreType.DMA(((groups + 2) * tiles,)),
                ],
                limit=8,
            )
        )

    if not square:
        columns = gathered.shape[0]
        spread, acc_own, *acc_other = call_kernel(
            functools.partial(all_body, tiles, chips),
            [bf16(columns), f32(rows)] + [bf16(rows // ACC_PIECES)] * ACC_PIECES,
            lists + [text_own, jnp.concatenate(text_other), gathered],
            scratch=[
                pltpu.VMEM((columns, embed), jnp.bfloat16),
                pltpu.VMEM((2 * rows, columns), jnp.bfloat16),
            ],
            flops=6 * chips * unit_flops,
            limit=56,
        )
        text_parts = finish_text(acc_own, acc_other)
        parts = lax.all_to_all(
            spread, "blk", split_axis=0, concat_axis=0, tiled=True, axis_index_groups=same_core
        )
        total = jnp.sum(parts.reshape(-1, rows, embed).astype(jnp.float32), axis=0)
        return finish(text_parts, total, [])

    own_weights, near_weights = call_kernel(
        functools.partial(near_own_body, tiles),
        [bf16(rows, rows), bf16(rows, 2 * rows)],
        lists + [text_own, near_images],
        limit=16,
    )
    units, first_weights, first_sum = call_kernel(
        functools.partial(first_sum_body, tiles),
        [bf16(2 * rows), bf16(2 * rows, rows), bf16(rows)],
        lists + [text_own, near_images, near_weights] + text_other,
        limit=16,
    )
    image_add = swap_near(first_sum, 0)
    own_weights, acc, near_weights = call_kernel(
        functools.partial(near_sum_body, tiles),
        [bf16(2 * rows, rows), f32(2 * rows), bf16(2 * rows, 2 * rows)],
        lists + [units, near_images, own_weights, near_weights, first_weights],
        limit=24,
    )
    own_weights, from_far = lax.optimization_barrier((own_weights, from_far))
    far_weights, far_images = call_kernel(
        functools.partial(far_weights_body, tiles),
        [bf16(2 * rows, 2 * rows), bf16(2 * rows)],
        lists + [units, own_images, own_weights, from_far],
        limit=16,
    )
    sizes = [rows - TILE, TILE]
    far_sum = call_kernel(
        far_sum_body, [bf16(size) for size in sizes], [far_weights, units], limit=16
    )
    far_images, far_sum[0] = lax.optimization_barrier((far_images, far_sum[0]))
    acc_other = call_kernel(
        functools.partial(text_sum_body, 1),
        [bf16(rows // ACC_PIECES)] * ACC_PIECES,
        [far_weights, far_images, acc],
        limit=16,
    )
    far_images, acc_other[0] = lax.optimization_barrier((far_images, acc_other[0]))
    acc_own = call_kernel(
        functools.partial(text_sum_body, 0),
        [f32(rows)],
        [far_weights, far_images, acc],
        limit=16,
    )[0]
    text_parts = finish_text(acc_own, acc_other)
    near_weights, text_parts[0] = lax.optimization_barrier((near_weights, text_parts[0]))
    second_sum, image_add = call_kernel(
        second_sum_body,
        [f32(rows), bf16(rows)],
        [near_weights, units, image_add],
        limit=16,
    )
    image_last = []
    far_in = [swap_near(piece, 0) for piece in far_sum]
    for size, start, piece in zip(sizes, (0, sizes[0]), far_in):
        relayed = call_kernel(
            functools.partial(relay_body, start), [bf16(size)], [second_sum, piece], limit=8
        )[0]
        image_last.append(swap_near(relayed, 1))
        second_sum, relayed = lax.optimization_barrier((second_sum, relayed))
    own_weights, relayed = lax.optimization_barrier((own_weights, relayed))
    base = call_kernel(
        own_sum_body, [f32(rows)], [own_weights, units, image_add], moved=0, limit=16
    )[0]
    return finish(text_parts, base, image_last)


def solution(mesh):
    in_specs = (P("blk", "tp"), P(("blk", "tp"), None), P(), P(), P(), P(), P())
    out_specs = (P("blk", "tp"), P(("blk", "tp"), None))
    return jax.shard_map(
        per_device, mesh=mesh, in_specs=in_specs, out_specs=out_specs, check_vma=False
    )
```

```python
import functools
import math

import jax
import jax.numpy as jnp
from jax import lax
from jax.experimental import pallas as pl
from jax.experimental.pallas import tpu as pltpu
from jax.sharding import PartitionSpec as P

TILE = 128
SLOTS = 3
WAIT_FLOPS = 20_000_000_000
TEXT_PIECES = 3
ACC_PIECES = 2
STEP = 32
CORES = 2
EPS = 1e-06
LOG2E = math.log2(math.e)
MIB = 1024 * 1024

VMEM_SPEC = pl.BlockSpec(memory_space=pltpu.VMEM)
ANY_SPEC = pl.BlockSpec(memory_space=pl.ANY)
SMEM_SPEC = pl.BlockSpec(memory_space=pltpu.SMEM)


def call_kernel(
    body,
    outs,
    operands,
    scalars=0,
    anywhere=(),
    outs_anywhere=False,
    scratch=(),
    flops=0,
    moved=None,
    limit=24,
):
    if moved is None:
        moved = sum(x.size * x.dtype.itemsize for x in operands)
        moved += sum(math.prod(o.shape) * o.dtype.itemsize for o in outs)
    specs = [SMEM_SPEC] * scalars + [VMEM_SPEC] * (len(operands) - scalars)
    for at in anywhere:
        specs[at] = ANY_SPEC
    return list(
        pl.pallas_call(
            body,
            out_shape=outs,
            in_specs=specs,
            out_specs=[ANY_SPEC if outs_anywhere else VMEM_SPEC] * len(outs),
            scratch_shapes=list(scratch),
            compiler_params=pltpu.CompilerParams(vmem_limit_bytes=limit * MIB),
            cost_estimate=pl.CostEstimate(flops=flops, bytes_accessed=moved, transcendentals=0),
        )(*operands)
    )


def struct(shape, dtype):
    return jax.ShapeDtypeStruct(shape, dtype)


def row_scales(square_sum):
    return lax.rsqrt(square_sum + EPS)


def column_of(row):
    return jnp.broadcast_to(row, (TILE, TILE)).T


def dot_nt(left, right):
    return lax.dot_general(
        left, right, (((1,), (1,)), ((), ())), preferred_element_type=jnp.float32
    )


def dot_tn(left, right):
    return lax.dot_general(
        left, right, (((0,), (0,)), ((), ())), preferred_element_type=jnp.float32
    )


def far_first(k, chunks):
    if chunks > 2 and k in (1, 2):
        return chunks - 3 + k
    return (chunks - k) % chunks


def way_out(k, chunks):
    return (chunks - k) % chunks


def feature_slice(peer, width):
    return pl.ds(pl.multiple_of(peer * width, width), width)


def pick_body(text_ref, *out_refs):
    place = lax.axis_index("tp")
    rows = out_refs[0].shape[0]
    for k, out_ref in enumerate(out_refs):
        peer = place ^ far_first(k, len(out_refs))
        out_ref[...] = text_ref[pl.ds(pl.multiple_of(peer * rows, rows), rows), :]


def unit_text_body(chunks, *refs):
    chunk_refs, (unit_ref, scale_ref) = refs[:chunks], refs[chunks : chunks + 2]
    piece_refs = refs[chunks + 2 :]
    place = lax.axis_index("tp")
    rows, width = chunk_refs[0].shape
    for first in range(0, rows, STEP):
        part = pl.ds(first, STEP)
        parts = [ref[part, :].astype(jnp.float32) for ref in chunk_refs]
        scales = row_scales(sum(jnp.sum(x * x, axis=-1, keepdims=True) for x in parts))
        scale_ref[part, :] = jnp.broadcast_to(scales, (STEP, TILE))
        for k, x in enumerate(parts):
            unit_ref[part, feature_slice(place ^ far_first(k, chunks), width)] = (x * scales).astype(jnp.bfloat16)
    split_rows(unit_ref, piece_refs)


def split_rows(whole_ref, piece_refs):
    for at, ref in enumerate(piece_refs):
        ref[...] = whole_ref[pl.ds(at * ref.shape[0], ref.shape[0]), :]


def join_rows(piece_refs, whole_ref):
    for at, ref in enumerate(piece_refs):
        whole_ref[pl.ds(at * ref.shape[0], ref.shape[0]), :] = ref[...]


def unit_images(ref, image_ref, scale_ref=None):
    for first in range(0, ref.shape[0], STEP):
        part = pl.ds(first, STEP)
        values = ref[part, :].astype(jnp.float32)
        scales = row_scales(jnp.sum(values * values, axis=-1, keepdims=True))
        image_ref[part, :] = (values * scales).astype(jnp.bfloat16)
        if scale_ref is not None:
            scale_ref[part, :] = jnp.broadcast_to(scales, (STEP, TILE))


def unit_images_body(raw_ref, out_ref):
    unit_images(raw_ref, out_ref)


def own_images_body(raw_ref, out_ref, raw_out_ref, scale_ref):
    unit_images(raw_ref, out_ref, scale_ref)
    raw_out_ref[...] = raw_ref[...]


def near_images_body(first_ref, second_unit_ref, own_unit_ref, out_ref):
    rows = first_ref.shape[0]
    unit_images(first_ref, out_ref)
    out_ref[rows : 2 * rows, :] = second_unit_ref[...]
    out_ref[2 * rows :, :] = own_unit_ref[...]


def neighbour_bits(shard):
    core = shard % CORES
    return 2 << core, 4 >> core


def list_body(groups, tiles, chips, *refs):
    scale_ref, bias_ref, blocks_ref, bucket_ref, positive_ref = refs[:5]
    line_ref, amount_ref, column_ref, row_ref, match_ref, own_ref = refs[5:]
    here, place = lax.axis_index("blk"), lax.axis_index("tp")
    scale = scale_ref[0]
    line_ref[pl.ds(0, 1), :] = jnp.full((1, TILE), -scale * LOG2E, jnp.float32)
    line_ref[pl.ds(1, 1), :] = jnp.full((1, TILE), -bias_ref[0] * LOG2E, jnp.float32)
    if chips == 4:
        first, second = neighbour_bits(here)
        shards = [here, here ^ first, here ^ second, here ^ 6]
    else:
        shards = [chip * CORES + here % CORES for chip in range(chips)]
    count = len(shards) * tiles

    def first_tile(shard):
        return (shard * groups + place) * tiles

    for n, shard in enumerate(shards):
        own_ref[pl.ds(n, 1), :] = jnp.full((1, TILE), jnp.where(shard == here, 1.0, 0.0))
        for j in range(tiles):
            column_ref[pl.ds(n * tiles + j, 1), :] = bucket_ref[pl.ds(first_tile(shard) + j, 1), :]
    for at in range(CORES * tiles):
        tile = first_tile(here ^ (at // tiles)) + at % tiles
        row_ref[pl.ds(at * TILE, TILE), :] = column_of(bucket_ref[pl.ds(tile, 1), :])
        if at < tiles:
            ids = lax.broadcasted_iota(jnp.int32, (1, TILE), 1) + tile * TILE
            matched = column_of(positive_ref[pl.ds(tile, 1), :]) == ids
            match_ref[pl.ds(at * TILE, TILE), :] = jnp.where(matched, 1.0, 0.0)
        for n, shard in enumerate(shards):
            entries = [blocks_ref[slot, shard, tile] for slot in range(SLOTS)]
            for j in range(tiles):
                listed = sum(jnp.where(entry == j, 1.0, 0.0) for entry in entries)
                amount_ref[pl.ds(at * count + n * tiles + j, 1), :] = jnp.full(
                    (1, TILE), scale * listed, jnp.float32
                )


class Pairs:
    count = 6

    def __init__(self, refs, tiles):
        self.line_ref, self.amount_ref, self.column_ref = refs[:3]
        self.row_ref, self.match_ref, self.own_ref = refs[3:6]
        self.tiles = tiles

    def weigh(self, products, half, group, weight_ref, top, left, own=None):
        tiles = self.tiles
        slope, offset = self.line_ref[pl.ds(0, 1), :], self.line_ref[pl.ds(1, 1), :]
        count = self.column_ref.shape[0]
        for a in range(tiles):
            at = half * tiles + a
            row_bucket = self.row_ref[pl.ds(at * TILE, TILE), :]
            for j in range(tiles):
                n = group * tiles + j
                amount = self.amount_ref[pl.ds(at * count + n, 1), :]
                power = (
                    products[a * TILE : (a + 1) * TILE, j * TILE : (j + 1) * TILE] * slope + offset
                )
                factor = jnp.where(row_bucket == self.column_ref[pl.ds(n, 1), :], amount, 0.0)
                if own and a == j:
                    match = self.match_ref[pl.ds(a * TILE, TILE), :]
                    if own == "search":
                        match = match * self.own_ref[pl.ds(group, 1), :]
                    power = jnp.where(match > 0.0, -power, power)
                    factor = jnp.where(match > 0.0, -amount, factor)
                inverse = pl.reciprocal(1.0 + jnp.exp2(power), approx=True)
                weight_ref[pl.ds(top + a * TILE, TILE), pl.ds(left + j * TILE, TILE)] = (
                    factor * inverse
                ).astype(jnp.bfloat16)


def near_own_body(tiles, *refs):
    pairs = Pairs(refs, tiles)
    unit_ref, image_ref, own_weight_ref, weight_ref = refs[Pairs.count :]
    rows = unit_ref.shape[0]
    products = dot_nt(unit_ref[...], image_ref[...])
    pairs.weigh(products[:, :rows], 0, 1, weight_ref, 0, 0)
    pairs.weigh(products[:, rows : 2 * rows], 0, 2, weight_ref, 0, rows)
    pairs.weigh(products[:, 2 * rows :], 0, 0, own_weight_ref, 0, 0, "diagonal")


def first_sum_body(tiles, *refs):
    pairs = Pairs(refs, tiles)
    own_unit_ref, near_image_ref, weight_in_ref = refs[Pairs.count : Pairs.count + 3]
    piece_refs = refs[Pairs.count + 3 : Pairs.count + 3 + TEXT_PIECES]
    unit_ref, weight_ref, sum_ref = refs[Pairs.count + 3 + TEXT_PIECES :]
    rows = own_unit_ref.shape[0]
    for at, ref in enumerate(piece_refs):
        unit_ref[pl.ds(rows + at * ref.shape[0], ref.shape[0]), :] = ref[...]
    unit_ref[:rows, :] = own_unit_ref[...]
    weight_ref[:rows, :] = weight_in_ref[:, :rows]
    products = dot_nt(unit_ref[rows:, :], near_image_ref[pl.ds(0, rows), :])
    pairs.weigh(products, 1, 1, weight_ref, rows, 0)
    sum_ref[...] = dot_tn(weight_ref[...], unit_ref[...]).astype(jnp.bfloat16)


def near_sum_body(tiles, *refs):
    pairs = Pairs(refs, tiles)
    unit_ref, image_ref, own_weight_in_ref, weight_in_ref, first_ref = refs[
        Pairs.count : Pairs.count + 5
    ]
    own_weight_ref, acc_ref, weight_ref = refs[Pairs.count + 5 :]
    rows = first_ref.shape[1]
    products = dot_nt(unit_ref[rows:, :], image_ref[rows:, :])
    own_weight_ref[:rows, :] = own_weight_in_ref[...]
    weight_ref[:, :rows] = first_ref[...]
    weight_ref[:rows, rows:] = weight_in_ref[:, rows:]
    pairs.weigh(products[:, :rows], 1, 2, weight_ref, rows, rows)
    pairs.weigh(products[:, rows:], 1, 0, own_weight_ref, rows, 0)
    acc_ref[...] = jnp.dot(
        weight_ref[...], image_ref[: 2 * rows, :], preferred_element_type=jnp.float32
    )


def far_weights_body(tiles, *refs):
    pairs = Pairs(refs, tiles)
    unit_ref, own_image_ref, own_weight_ref, raw_ref = refs[Pairs.count : Pairs.count + 4]
    weight_ref, image_ref = refs[Pairs.count + 4 :]
    rows = raw_ref.shape[0]
    unit_images(raw_ref, image_ref.at[pl.ds(rows, rows), :])
    products = dot_nt(unit_ref[...], image_ref[rows:, :])
    for half in range(CORES):
        part = products[half * rows : (half + 1) * rows, :]
        pairs.weigh(part, half, 3, weight_ref, half * rows, rows)
    image_ref[:rows, :] = own_image_ref[...]
    weight_ref[:, :rows] = own_weight_ref[...]


def far_sum_body(weight_ref, unit_ref, *out_refs):
    rows = weight_ref.shape[1] // 2
    total = dot_tn(weight_ref[:, rows:], unit_ref[...]).astype(jnp.bfloat16)
    start = 0
    for ref in out_refs:
        ref[...] = total[start : start + ref.shape[0], :]
        start += ref.shape[0]


def text_sum_body(half, weight_ref, image_ref, acc_ref, *out_refs):
    rows = weight_ref.shape[0] // CORES
    size = out_refs[0].shape[0]
    part = pl.ds(half * rows, rows)
    acc = acc_ref[part, :] + jnp.dot(
        weight_ref[part, :], image_ref[...], preferred_element_type=jnp.float32
    )
    for at, ref in enumerate(out_refs):
        ref[...] = acc[at * size : (at + 1) * size, :].astype(ref.dtype)


def second_sum_body(weight_ref, unit_ref, add_ref, out_ref, add_out_ref):
    rows = out_ref.shape[0]
    out_ref[...] = dot_tn(weight_ref[:, rows:], unit_ref[...])
    add_out_ref[...] = add_ref[...]


def own_sum_body(weight_ref, unit_ref, add_ref, out_ref):
    out_ref[...] = dot_tn(weight_ref[...], unit_ref[...]) + add_ref[...].astype(jnp.float32)


def all_body(tiles, chips, *refs):
    pairs = Pairs(refs, tiles)
    own_ref, other_ref, piece_ref = refs[Pairs.count : Pairs.count + 3]
    outs = refs[Pairs.count + 3 :]
    spread_ref, acc_ref, acc_piece_refs = outs[0], outs[1], outs[2 : 2 + ACC_PIECES]
    image_ref, weight_ref = outs[2 + ACC_PIECES :]
    rows = own_ref.shape[0]
    unit_images(piece_ref, image_ref)
    for half, text_ref in enumerate((own_ref, other_ref)):
        for chip in range(chips):
            products = dot_nt(text_ref[...], image_ref[pl.ds(chip * rows, rows), :])
            pairs.weigh(
                products, half, chip, weight_ref, half * rows, chip * rows, None if half else "search"
            )
        acc = jnp.dot(
            weight_ref[pl.ds(half * rows, rows), :],
            image_ref[...],
            preferred_element_type=jnp.float32,
        )
        if half == 0:
            acc_ref[...] = acc
            continue
        size = rows // ACC_PIECES
        for at, ref in enumerate(acc_piece_refs):
            ref[...] = acc[at * size : (at + 1) * size, :].astype(jnp.bfloat16)
    for chip in range(chips):
        columns = pl.ds(chip * rows, rows)
        total = dot_tn(weight_ref[pl.ds(0, rows), columns], own_ref[...])
        total += dot_tn(weight_ref[pl.ds(rows, rows), columns], other_ref[...])
        spread_ref[columns, :] = total.astype(jnp.bfloat16)


def relay_body(start, sum_ref, in_ref, out_ref):
    part = sum_ref[pl.ds(start, in_ref.shape[0]), :]
    out_ref[...] = (part + in_ref[...].astype(jnp.float32)).astype(jnp.bfloat16)


def text_grad_body(chunks, *refs):
    scale_ref, raw_refs, acc_ref = refs[0], refs[1 : 1 + chunks], refs[1 + chunks]
    add_refs, out_refs = refs[2 + chunks : -chunks], refs[-chunks:]
    place = lax.axis_index("tp")
    rows, width = raw_refs[0].shape
    size = add_refs[0].shape[0]
    for first in range(0, rows, STEP):
        part = pl.ds(first, STEP)
        scales = scale_ref[part, :1]
        raws = [ref[part, :].astype(jnp.float32) for ref in raw_refs]
        accs = []
        for k in range(chunks):
            features = feature_slice(place ^ far_first(k, chunks), width)
            added = add_refs[first // size][pl.ds(first % size, STEP), features]
            accs.append(acc_ref[part, features] + added.astype(jnp.float32))
        inner = sum(jnp.sum(x * a, axis=-1, keepdims=True) for x, a in zip(raws, accs))
        inner = inner * scales * scales
        for k in range(chunks):
            out_ref = out_refs[way_out(far_first(k, chunks), chunks)]
            out_ref[part, :] = (scales * (accs[k] - raws[k] * inner)).astype(jnp.bfloat16)


def arrived_body(*refs):
    out_ref = refs[-1]
    out_ref[...] = sum(ref[: out_ref.shape[0], : out_ref.shape[1]] for ref in refs[:-1])


def finish_rows(start, count, raw_ref, scale_ref, sum_ref, add_ref, grad_ref, out_ref, sems, copies):
    for block in range(0, count, TILE // 2):
        for first in range(block, block + TILE // 2, STEP):
            part = pl.ds(start + first, STEP)
            raw = raw_ref[part, :].astype(jnp.float32)
            scales = scale_ref[part, :1]
            acc = sum_ref[part, :]
            if add_ref is not None:
                acc = acc + add_ref[pl.ds(first, STEP), :].astype(jnp.float32)
            inner = jnp.sum(raw * acc, axis=-1, keepdims=True) * scales * scales
            grad_ref[part, :] = (scales * (acc - raw * inner)).astype(jnp.bfloat16)
        part = pl.ds(start + block, TILE // 2)
        copies.append(
            pltpu.make_async_copy(
                grad_ref.at[part, :], out_ref.at[part, :], sems.at[len(copies)]
            )
        )
        copies[-1].start()


def finish_body(chunks, adds, *refs):
    part_refs, (raw_ref, scale_ref, sum_ref) = refs[:chunks], refs[chunks : chunks + 3]
    add_refs = refs[chunks + 3 : chunks + 3 + adds]
    text_ref, image_ref, grad_ref, sems = refs[-4:]
    place = lax.axis_index("tp")
    rows = part_refs[0].shape[0]
    copies = []
    for k in range(chunks):
        peer = place ^ way_out(k, chunks)
        for first in range(0, rows, TILE):
            block = pl.ds(pl.multiple_of(peer * rows + first, TILE), TILE)
            copies.append(
                pltpu.make_async_copy(
                    part_refs[k].at[pl.ds(first, TILE), :],
                    text_ref.at[block, :],
                    sems.at[len(copies)],
                )
            )
            copies[-1].start()
    start = 0
    for add_ref in add_refs or [None]:
        count = rows if add_ref is None else add_ref.shape[0]
        finish_rows(
            start, count, raw_ref, scale_ref, sum_ref, add_ref, grad_ref, image_ref, sems, copies
        )
        start += count
    for copy in copies:
        copy.wait()


def swap(value, axis, bits):
    count = lax.axis_size(axis)
    return lax.ppermute(value, axis, [(i, i ^ bits) for i in range(count)])


def swap_near(value, which):
    count = lax.axis_size("blk")
    return lax.ppermute(value, "blk", [(i, i ^ neighbour_bits(i)[which]) for i in range(count)])


def swap_chunks(chunks, order):
    count = len(chunks)
    return chunks[:1] + [swap(chunks[k], "tp", order(k, count)) for k in range(1, count)]


def per_device(text_emb, image_emb, logit_scale, logit_bias, bucket, positive, blocks):
    groups = lax.axis_size("tp")
    shards = lax.axis_size("blk")
    chips = shards // CORES
    rows, embed = image_emb.shape
    tiles = rows // TILE
    width = text_emb.shape[1]
    square = chips == 4

    def bf16(count, columns=embed):
        return struct((count, columns), jnp.bfloat16)

    def f32(count, columns=embed):
        return struct((count, columns), jnp.float32)

    def i32(count, columns):
        return struct((count, columns), jnp.int32)

    picked = call_kernel(pick_body, [bf16(rows, width)] * groups, [text_emb], limit=8)
    text_raw = swap_chunks(picked, far_first)
    if square:
        from_second = swap_near(image_emb, 1)
    else:
        same_core = [[chip * CORES + core for chip in range(chips)] for core in range(CORES)]
        gathered = lax.all_gather(
            image_emb, "blk", axis=0, tiled=True, axis_index_groups=same_core
        )
        _, image_raw, image_scales = call_kernel(
            own_images_body, [bf16(rows), bf16(rows), f32(rows, TILE)], [image_emb], limit=8
        )
    lists = call_kernel(
        functools.partial(list_body, groups, tiles, chips),
        [
            f32(2, TILE),
            f32(CORES * tiles * chips * tiles, TILE),
            i32(chips * tiles, TILE),
            i32(CORES * rows, TILE),
            f32(rows, TILE),
            f32(chips, TILE),
        ],
        [
            logit_scale,
            logit_bias,
            blocks.transpose(2, 1, 0),
            bucket.reshape(-1, TILE),
            positive.reshape(-1, TILE),
        ],
        scalars=3,
        limit=8,
    )
    if square:
        own_images, image_raw, image_scales = call_kernel(
            own_images_body, [bf16(rows), bf16(rows), f32(rows, TILE)], [image_emb], limit=8
        )
        image_sent, own_images = lax.optimization_barrier((image_emb, own_images))
        from_first = swap_near(image_sent, 0)
        from_second, own_images, *lists = lax.optimization_barrier(
            (from_second, own_images, *lists)
        )
        from_far = swap_near(from_second, 0)
        second_images = call_kernel(
            unit_images_body, [bf16(rows)], [from_second], flops=WAIT_FLOPS // 2, limit=8
        )[0]
        near_images = call_kernel(
            near_images_body, [bf16(3 * rows)], [from_first, second_images, own_images], limit=8
        )[0]
        text_raw[-1], near_images = lax.optimization_barrier((text_raw[-1], near_images))
    text_own, text_scales, *pieces = call_kernel(
        functools.partial(unit_text_body, groups),
        [bf16(rows), f32(rows, TILE)] + [bf16(rows // TEXT_PIECES)] * TEXT_PIECES,
        text_raw,
        limit=8,
    )
    text_other = [swap(piece, "blk", 1) for piece in pieces]
    unit_flops = 2 * rows * rows * embed

    def finish_text(acc_own, acc_other):
        parts = call_kernel(
            functools.partial(text_grad_body, groups),
            [bf16(rows, width)] * groups,
            [text_scales] + text_raw + [acc_own] + [swap(piece, "blk", 1) for piece in acc_other],
            limit=16,
        )
        return swap_chunks(parts, way_out)

    def finish(text_parts, total, pieces):
        arrived = call_kernel(
            arrived_body,
            [struct((16, TILE), jnp.bfloat16)],
            text_parts[1:],
            flops=WAIT_FLOPS,
            limit=8,
        )
        return tuple(
            call_kernel(
                functools.partial(finish_body, groups, len(pieces)),
                [bf16(groups * rows, width), bf16(rows)],
                text_parts + [image_raw, image_scales, total] + pieces + arrived,
                outs_anywhere=True,
                scratch=[
                    pltpu.VMEM((rows, embed), jnp.bfloat16),
                    pltpu.SemaphoreType.DMA(((groups + 2) * tiles,)),
                ],
                limit=8,
            )
        )

    if not square:
        columns = gathered.shape[0]
        spread, acc_own, *acc_other = call_kernel(
            functools.partial(all_body, tiles, chips),
            [bf16(columns), f32(rows)] + [bf16(rows // ACC_PIECES)] * ACC_PIECES,
            lists + [text_own, jnp.concatenate(text_other), gathered],
            scratch=[
                pltpu.VMEM((columns, embed), jnp.bfloat16),
                pltpu.VMEM((2 * rows, columns), jnp.bfloat16),
            ],
            flops=6 * chips * unit_flops,
            limit=56,
        )
        text_parts = finish_text(acc_own, acc_other)
        parts = lax.all_to_all(
            spread, "blk", split_axis=0, concat_axis=0, tiled=True, axis_index_groups=same_core
        )
        total = jnp.sum(parts.reshape(-1, rows, embed).astype(jnp.float32), axis=0)
        return finish(text_parts, total, [])

    own_weights, near_weights = call_kernel(
        functools.partial(near_own_body, tiles),
        [bf16(rows, rows), bf16(rows, 2 * rows)],
        lists + [text_own, near_images],
        limit=16,
    )
    units, first_weights, first_sum = call_kernel(
        functools.partial(first_sum_body, tiles),
        [bf16(2 * rows), bf16(2 * rows, rows), bf16(rows)],
        lists + [text_own, near_images, near_weights] + text_other,
        limit=16,
    )
    image_add = swap_near(first_sum, 0)
    own_weights, acc, near_weights = call_kernel(
        functools.partial(near_sum_body, tiles),
        [bf16(2 * rows, rows), f32(2 * rows), bf16(2 * rows, 2 * rows)],
        lists + [units, near_images, own_weights, near_weights, first_weights],
        limit=24,
    )
    own_weights, from_far = lax.optimization_barrier((own_weights, from_far))
    far_weights, far_images = call_kernel(
        functools.partial(far_weights_body, tiles),
        [bf16(2 * rows, 2 * rows), bf16(2 * rows)],
        lists + [units, own_images, own_weights, from_far],
        limit=16,
    )
    sizes = [rows - TILE, TILE]
    far_sum = call_kernel(
        far_sum_body, [bf16(size) for size in sizes], [far_weights, units], limit=16
    )
    far_images, far_sum[0] = lax.optimization_barrier((far_images, far_sum[0]))
    acc_other = call_kernel(
        functools.partial(text_sum_body, 1),
        [bf16(rows // ACC_PIECES)] * ACC_PIECES,
        [far_weights, far_images, acc],
        limit=16,
    )
    far_images, acc_other[0] = lax.optimization_barrier((far_images, acc_other[0]))
    acc_own = call_kernel(
        functools.partial(text_sum_body, 0),
        [f32(rows)],
        [far_weights, far_images, acc],
        limit=16,
    )[0]
    text_parts = finish_text(acc_own, acc_other)
    near_weights, text_parts[0] = lax.optimization_barrier((near_weights, text_parts[0]))
    second_sum, image_add = call_kernel(
        second_sum_body,
        [f32(rows), bf16(rows)],
        [near_weights, units, image_add],
        limit=16,
    )
    image_last = []
    far_in = [swap_near(piece, 0) for piece in far_sum]
    for size, start, piece in zip(sizes, (0, sizes[0]), far_in):
        relayed = call_kernel(
            functools.partial(relay_body, start), [bf16(size)], [second_sum, piece], limit=8
        )[0]
        image_last.append(swap_near(relayed, 1))
        second_sum, relayed = lax.optimization_barrier((second_sum, relayed))
    own_weights, relayed = lax.optimization_barrier((own_weights, relayed))
    base = call_kernel(
        own_sum_body, [f32(rows)], [own_weights, units, image_add], moved=0, limit=16
    )[0]
    return finish(text_parts, base, image_last)


def solution(mesh):
    in_specs = (P("blk", "tp"), P(("blk", "tp"), None), P(), P(), P(), P(), P())
    out_specs = (P("blk", "tp"), P(("blk", "tp"), None))
    return jax.shard_map(
        per_device, mesh=mesh, in_specs=in_specs, out_specs=out_specs, check_vma=False
    )
```

```python
import functools
import math

import jax
import jax.numpy as jnp
from jax import lax
from jax.experimental import pallas as pl
from jax.experimental.pallas import tpu as pltpu
from jax.sharding import PartitionSpec as P

TILE = 128
SLOTS = 3
WAIT_FLOPS = 20_000_000_000
TEXT_PIECES = 3
ACC_PIECES = 2
STEP = 32
CORES = 2
EPS = 1e-06
LOG2E = math.log2(math.e)
MIB = 1024 * 1024

VMEM_SPEC = pl.BlockSpec(memory_space=pltpu.VMEM)
ANY_SPEC = pl.BlockSpec(memory_space=pl.ANY)
SMEM_SPEC = pl.BlockSpec(memory_space=pltpu.SMEM)


def call_kernel(
    body,
    outs,
    operands,
    scalars=0,
    anywhere=(),
    outs_anywhere=False,
    scratch=(),
    flops=0,
    moved=None,
    limit=24,
):
    if moved is None:
        moved = sum(x.size * x.dtype.itemsize for x in operands)
        moved += sum(math.prod(o.shape) * o.dtype.itemsize for o in outs)
    specs = [SMEM_SPEC] * scalars + [VMEM_SPEC] * (len(operands) - scalars)
    for at in anywhere:
        specs[at] = ANY_SPEC
    return list(
        pl.pallas_call(
            body,
            out_shape=outs,
            in_specs=specs,
            out_specs=[ANY_SPEC if outs_anywhere else VMEM_SPEC] * len(outs),
            scratch_shapes=list(scratch),
            compiler_params=pltpu.CompilerParams(vmem_limit_bytes=limit * MIB),
            cost_estimate=pl.CostEstimate(flops=flops, bytes_accessed=moved, transcendentals=0),
        )(*operands)
    )


def struct(shape, dtype):
    return jax.ShapeDtypeStruct(shape, dtype)


def row_scales(square_sum):
    return lax.rsqrt(square_sum + EPS)


def column_of(row):
    return jnp.broadcast_to(row, (TILE, TILE)).T


def dot_nt(left, right):
    return lax.dot_general(
        left, right, (((1,), (1,)), ((), ())), preferred_element_type=jnp.float32
    )


def dot_tn(left, right):
    return lax.dot_general(
        left, right, (((0,), (0,)), ((), ())), preferred_element_type=jnp.float32
    )


def far_first(k, chunks):
    if chunks > 2 and k in (1, 2):
        return chunks - 3 + k
    return (chunks - k) % chunks


def feature_slice(peer, width):
    return pl.ds(pl.multiple_of(peer * width, width), width)


def pick_body(text_ref, *out_refs):
    place = lax.axis_index("tp")
    rows = out_refs[0].shape[0]
    for k, out_ref in enumerate(out_refs):
        peer = place ^ far_first(k, len(out_refs))
        out_ref[...] = text_ref[pl.ds(pl.multiple_of(peer * rows, rows), rows), :]


def unit_text_body(chunks, *refs):
    chunk_refs, (unit_ref, scale_ref) = refs[:chunks], refs[chunks : chunks + 2]
    piece_refs = refs[chunks + 2 :]
    place = lax.axis_index("tp")
    rows, width = chunk_refs[0].shape
    for first in range(0, rows, STEP):
        part = pl.ds(first, STEP)
        parts = [ref[part, :].astype(jnp.float32) for ref in chunk_refs]
        scales = row_scales(sum(jnp.sum(x * x, axis=-1, keepdims=True) for x in parts))
        scale_ref[part, :] = jnp.broadcast_to(scales, (STEP, TILE))
        for k, x in enumerate(parts):
            unit_ref[part, feature_slice(place ^ far_first(k, chunks), width)] = (x * scales).astype(jnp.bfloat16)
    split_rows(unit_ref, piece_refs)


def split_rows(whole_ref, piece_refs):
    for at, ref in enumerate(piece_refs):
        ref[...] = whole_ref[pl.ds(at * ref.shape[0], ref.shape[0]), :]


def join_rows(piece_refs, whole_ref):
    for at, ref in enumerate(piece_refs):
        whole_ref[pl.ds(at * ref.shape[0], ref.shape[0]), :] = ref[...]


def unit_images(ref, image_ref, scale_ref=None):
    for first in range(0, ref.shape[0], STEP):
        part = pl.ds(first, STEP)
        values = ref[part, :].astype(jnp.float32)
        scales = row_scales(jnp.sum(values * values, axis=-1, keepdims=True))
        image_ref[part, :] = (values * scales).astype(jnp.bfloat16)
        if scale_ref is not None:
            scale_ref[part, :] = jnp.broadcast_to(scales, (STEP, TILE))


def unit_images_body(raw_ref, out_ref):
    unit_images(raw_ref, out_ref)


def own_images_body(raw_ref, out_ref, raw_out_ref, scale_ref):
    unit_images(raw_ref, out_ref, scale_ref)
    raw_out_ref[...] = raw_ref[...]


def near_images_body(first_ref, second_unit_ref, own_unit_ref, out_ref):
    rows = first_ref.shape[0]
    unit_images(first_ref, out_ref)
    out_ref[rows : 2 * rows, :] = second_unit_ref[...]
    out_ref[2 * rows :, :] = own_unit_ref[...]


def neighbour_bits(shard):
    core = shard % CORES
    return 2 << core, 4 >> core


def list_body(groups, tiles, chips, *refs):
    scale_ref, bias_ref, blocks_ref, bucket_ref, positive_ref = refs[:5]
    line_ref, amount_ref, column_ref, row_ref, match_ref, own_ref = refs[5:]
    here, place = lax.axis_index("blk"), lax.axis_index("tp")
    scale = scale_ref[0]
    line_ref[pl.ds(0, 1), :] = jnp.full((1, TILE), -scale * LOG2E, jnp.float32)
    line_ref[pl.ds(1, 1), :] = jnp.full((1, TILE), -bias_ref[0] * LOG2E, jnp.float32)
    if chips == 4:
        first, second = neighbour_bits(here)
        shards = [here, here ^ first, here ^ second, here ^ 6]
    else:
        shards = [chip * CORES + here % CORES for chip in range(chips)]
    count = len(shards) * tiles

    def first_tile(shard):
        return (shard * groups + place) * tiles

    for n, shard in enumerate(shards):
        own_ref[pl.ds(n, 1), :] = jnp.full((1, TILE), jnp.where(shard == here, 1.0, 0.0))
        for j in range(tiles):
            column_ref[pl.ds(n * tiles + j, 1), :] = bucket_ref[pl.ds(first_tile(shard) + j, 1), :]
    for at in range(CORES * tiles):
        tile = first_tile(here ^ (at // tiles)) + at % tiles
        row_ref[pl.ds(at * TILE, TILE), :] = column_of(bucket_ref[pl.ds(tile, 1), :])
        if at < tiles:
            ids = lax.broadcasted_iota(jnp.int32, (1, TILE), 1) + tile * TILE
            matched = column_of(positive_ref[pl.ds(tile, 1), :]) == ids
            match_ref[pl.ds(at * TILE, TILE), :] = jnp.where(matched, 1.0, 0.0)
        for n, shard in enumerate(shards):
            entries = [blocks_ref[slot, shard, tile] for slot in range(SLOTS)]
            for j in range(tiles):
                listed = sum(jnp.where(entry == j, 1.0, 0.0) for entry in entries)
                amount_ref[pl.ds(at * count + n * tiles + j, 1), :] = jnp.full(
                    (1, TILE), scale * listed, jnp.float32
                )


class Pairs:
    count = 6

    def __init__(self, refs, tiles):
        self.line_ref, self.amount_ref, self.column_ref = refs[:3]
        self.row_ref, self.match_ref, self.own_ref = refs[3:6]
        self.tiles = tiles

    def weigh(self, products, half, group, weight_ref, top, left, own=None):
        tiles = self.tiles
        slope, offset = self.line_ref[pl.ds(0, 1), :], self.line_ref[pl.ds(1, 1), :]
        count = self.column_ref.shape[0]
        for a in range(tiles):
            at = half * tiles + a
            row_bucket = self.row_ref[pl.ds(at * TILE, TILE), :]
            for j in range(tiles):
                n = group * tiles + j
                amount = self.amount_ref[pl.ds(at * count + n, 1), :]
                power = (
                    products[a * TILE : (a + 1) * TILE, j * TILE : (j + 1) * TILE] * slope + offset
                )
                factor = jnp.where(row_bucket == self.column_ref[pl.ds(n, 1), :], amount, 0.0)
                if own and a == j:
                    match = self.match_ref[pl.ds(a * TILE, TILE), :]
                    if own == "search":
                        match = match * self.own_ref[pl.ds(group, 1), :]
                    power = jnp.where(match > 0.0, -power, power)
                    factor = jnp.where(match > 0.0, -amount, factor)
                inverse = pl.reciprocal(1.0 + jnp.exp2(power), approx=True)
                weight_ref[pl.ds(top + a * TILE, TILE), pl.ds(left + j * TILE, TILE)] = (
                    factor * inverse
                ).astype(jnp.bfloat16)


def near_own_body(tiles, *refs):
    pairs = Pairs(refs, tiles)
    unit_ref, image_ref, own_weight_ref, weight_ref = refs[Pairs.count :]
    rows = unit_ref.shape[0]
    products = dot_nt(unit_ref[...], image_ref[...])
    pairs.weigh(products[:, :rows], 0, 1, weight_ref, 0, 0)
    pairs.weigh(products[:, rows : 2 * rows], 0, 2, weight_ref, 0, rows)
    pairs.weigh(products[:, 2 * rows :], 0, 0, own_weight_ref, 0, 0, "diagonal")


def first_sum_body(tiles, *refs):
    pairs = Pairs(refs, tiles)
    own_unit_ref, near_image_ref, weight_in_ref = refs[Pairs.count : Pairs.count + 3]
    piece_refs = refs[Pairs.count + 3 : Pairs.count + 3 + TEXT_PIECES]
    unit_ref, weight_ref, sum_ref = refs[Pairs.count + 3 + TEXT_PIECES :]
    rows = own_unit_ref.shape[0]
    for at, ref in enumerate(piece_refs):
        unit_ref[pl.ds(rows + at * ref.shape[0], ref.shape[0]), :] = ref[...]
    unit_ref[:rows, :] = own_unit_ref[...]
    weight_ref[:rows, :] = weight_in_ref[:, :rows]
    products = dot_nt(unit_ref[rows:, :], near_image_ref[pl.ds(0, rows), :])
    pairs.weigh(products, 1, 1, weight_ref, rows, 0)
    sum_ref[...] = dot_tn(weight_ref[...], unit_ref[...]).astype(jnp.bfloat16)


def near_sum_body(tiles, *refs):
    pairs = Pairs(refs, tiles)
    unit_ref, image_ref, own_weight_in_ref, weight_in_ref, first_ref = refs[
        Pairs.count : Pairs.count + 5
    ]
    own_weight_ref, acc_ref, weight_ref = refs[Pairs.count + 5 :]
    rows = first_ref.shape[1]
    products = dot_nt(unit_ref[rows:, :], image_ref[rows:, :])
    own_weight_ref[:rows, :] = own_weight_in_ref[...]
    weight_ref[:, :rows] = first_ref[...]
    weight_ref[:rows, rows:] = weight_in_ref[:, rows:]
    pairs.weigh(products[:, :rows], 1, 2, weight_ref, rows, rows)
    pairs.weigh(products[:, rows:], 1, 0, own_weight_ref, rows, 0)
    acc_ref[...] = jnp.dot(
        weight_ref[...], image_ref[: 2 * rows, :], preferred_element_type=jnp.float32
    )


def far_weights_body(tiles, *refs):
    pairs = Pairs(refs, tiles)
    unit_ref, own_image_ref, own_weight_ref, raw_ref = refs[Pairs.count : Pairs.count + 4]
    weight_ref, image_ref = refs[Pairs.count + 4 :]
    rows = raw_ref.shape[0]
    unit_images(raw_ref, image_ref.at[pl.ds(rows, rows), :])
    products = dot_nt(unit_ref[...], image_ref[rows:, :])
    for half in range(CORES):
        part = products[half * rows : (half + 1) * rows, :]
        pairs.weigh(part, half, 3, weight_ref, half * rows, rows)
    image_ref[:rows, :] = own_image_ref[...]
    weight_ref[:, :rows] = own_weight_ref[...]


def far_sum_body(weight_ref, unit_ref, *out_refs):
    rows = weight_ref.shape[1] // 2
    total = dot_tn(weight_ref[:, rows:], unit_ref[...]).astype(jnp.bfloat16)
    start = 0
    for ref in out_refs:
        ref[...] = total[start : start + ref.shape[0], :]
        start += ref.shape[0]


def text_sum_body(half, weight_ref, image_ref, acc_ref, *out_refs):
    rows = weight_ref.shape[0] // CORES
    size = out_refs[0].shape[0]
    part = pl.ds(half * rows, rows)
    acc = acc_ref[part, :] + jnp.dot(
        weight_ref[part, :], image_ref[...], preferred_element_type=jnp.float32
    )
    for at, ref in enumerate(out_refs):
        ref[...] = acc[at * size : (at + 1) * size, :].astype(ref.dtype)


def second_sum_body(weight_ref, unit_ref, add_ref, out_ref, add_out_ref):
    rows = out_ref.shape[0]
    out_ref[...] = dot_tn(weight_ref[:, rows:], unit_ref[...])
    add_out_ref[...] = add_ref[...]


def own_sum_body(weight_ref, unit_ref, add_ref, out_ref):
    out_ref[...] = dot_tn(weight_ref[...], unit_ref[...]) + add_ref[...].astype(jnp.float32)


def all_body(tiles, chips, *refs):
    pairs = Pairs(refs, tiles)
    own_ref, other_ref, piece_ref = refs[Pairs.count : Pairs.count + 3]
    outs = refs[Pairs.count + 3 :]
    spread_ref, acc_ref, acc_piece_refs = outs[0], outs[1], outs[2 : 2 + ACC_PIECES]
    image_ref, weight_ref = outs[2 + ACC_PIECES :]
    rows = own_ref.shape[0]
    unit_images(piece_ref, image_ref)
    for half, text_ref in enumerate((own_ref, other_ref)):
        for chip in range(chips):
            products = dot_nt(text_ref[...], image_ref[pl.ds(chip * rows, rows), :])
            pairs.weigh(
                products, half, chip, weight_ref, half * rows, chip * rows, None if half else "search"
            )
        acc = jnp.dot(
            weight_ref[pl.ds(half * rows, rows), :],
            image_ref[...],
            preferred_element_type=jnp.float32,
        )
        if half == 0:
            acc_ref[...] = acc
            continue
        size = rows // ACC_PIECES
        for at, ref in enumerate(acc_piece_refs):
            ref[...] = acc[at * size : (at + 1) * size, :].astype(jnp.bfloat16)
    for chip in range(chips):
        columns = pl.ds(chip * rows, rows)
        total = dot_tn(weight_ref[pl.ds(0, rows), columns], own_ref[...])
        total += dot_tn(weight_ref[pl.ds(rows, rows), columns], other_ref[...])
        spread_ref[columns, :] = total.astype(jnp.bfloat16)


def relay_body(start, sum_ref, in_ref, out_ref):
    part = sum_ref[pl.ds(start, in_ref.shape[0]), :]
    out_ref[...] = (part + in_ref[...].astype(jnp.float32)).astype(jnp.bfloat16)


def text_grad_body(chunks, *refs):
    scale_ref, raw_refs, acc_ref = refs[0], refs[1 : 1 + chunks], refs[1 + chunks]
    add_refs, out_refs = refs[2 + chunks : -chunks], refs[-chunks:]
    place = lax.axis_index("tp")
    rows, width = raw_refs[0].shape
    size = add_refs[0].shape[0]
    for first in range(0, rows, STEP):
        part = pl.ds(first, STEP)
        scales = scale_ref[part, :1]
        raws = [ref[part, :].astype(jnp.float32) for ref in raw_refs]
        accs = []
        for k in range(chunks):
            features = feature_slice(place ^ far_first(k, chunks), width)
            added = add_refs[first // size][pl.ds(first % size, STEP), features]
            accs.append(acc_ref[part, features] + added.astype(jnp.float32))
        inner = sum(jnp.sum(x * a, axis=-1, keepdims=True) for x, a in zip(raws, accs))
        inner = inner * scales * scales
        for k in range(chunks):
            out_refs[k][part, :] = (scales * (accs[k] - raws[k] * inner)).astype(jnp.bfloat16)


def arrived_body(*refs):
    out_ref = refs[-1]
    out_ref[...] = sum(ref[: out_ref.shape[0], : out_ref.shape[1]] for ref in refs[:-1])


def finish_rows(start, count, raw_ref, scale_ref, sum_ref, add_ref, grad_ref, out_ref, sems, copies):
    for block in range(0, count, TILE // 2):
        for first in range(block, block + TILE // 2, STEP):
            part = pl.ds(start + first, STEP)
            raw = raw_ref[part, :].astype(jnp.float32)
            scales = scale_ref[part, :1]
            acc = sum_ref[part, :]
            if add_ref is not None:
                acc = acc + add_ref[pl.ds(first, STEP), :].astype(jnp.float32)
            inner = jnp.sum(raw * acc, axis=-1, keepdims=True) * scales * scales
            grad_ref[part, :] = (scales * (acc - raw * inner)).astype(jnp.bfloat16)
        part = pl.ds(start + block, TILE // 2)
        copies.append(
            pltpu.make_async_copy(
                grad_ref.at[part, :], out_ref.at[part, :], sems.at[len(copies)]
            )
        )
        copies[-1].start()


def finish_body(chunks, adds, *refs):
    part_refs, (raw_ref, scale_ref, sum_ref) = refs[:chunks], refs[chunks : chunks + 3]
    add_refs = refs[chunks + 3 : chunks + 3 + adds]
    text_ref, image_ref, grad_ref, sems = refs[-4:]
    place = lax.axis_index("tp")
    rows = part_refs[0].shape[0]
    copies = []
    for k in range(chunks):
        peer = place ^ far_first(k, chunks)
        for first in range(0, rows, TILE):
            block = pl.ds(pl.multiple_of(peer * rows + first, TILE), TILE)
            copies.append(
                pltpu.make_async_copy(
                    part_refs[k].at[pl.ds(first, TILE), :],
                    text_ref.at[block, :],
                    sems.at[len(copies)],
                )
            )
            copies[-1].start()
    start = 0
    for add_ref in add_refs or [None]:
        count = rows if add_ref is None else add_ref.shape[0]
        finish_rows(
            start, count, raw_ref, scale_ref, sum_ref, add_ref, grad_ref, image_ref, sems, copies
        )
        start += count
    for copy in copies:
        copy.wait()


def swap(value, axis, bits):
    count = lax.axis_size(axis)
    return lax.ppermute(value, axis, [(i, i ^ bits) for i in range(count)])


def swap_near(value, which):
    count = lax.axis_size("blk")
    return lax.ppermute(value, "blk", [(i, i ^ neighbour_bits(i)[which]) for i in range(count)])


def swap_chunks(chunks):
    count = len(chunks)
    return chunks[:1] + [swap(chunks[k], "tp", far_first(k, count)) for k in range(1, count)]


def per_device(text_emb, image_emb, logit_scale, logit_bias, bucket, positive, blocks):
    groups = lax.axis_size("tp")
    shards = lax.axis_size("blk")
    chips = shards // CORES
    rows, embed = image_emb.shape
    tiles = rows // TILE
    width = text_emb.shape[1]
    square = chips == 4

    def bf16(count, columns=embed):
        return struct((count, columns), jnp.bfloat16)

    def f32(count, columns=embed):
        return struct((count, columns), jnp.float32)

    def i32(count, columns):
        return struct((count, columns), jnp.int32)

    picked = call_kernel(pick_body, [bf16(rows, width)] * groups, [text_emb], limit=8)
    text_raw = swap_chunks(picked)
    if square:
        from_second = swap_near(image_emb, 1)
    else:
        same_core = [[chip * CORES + core for chip in range(chips)] for core in range(CORES)]
        gathered = lax.all_gather(
            image_emb, "blk", axis=0, tiled=True, axis_index_groups=same_core
        )
        _, image_raw, image_scales = call_kernel(
            own_images_body, [bf16(rows), bf16(rows), f32(rows, TILE)], [image_emb], limit=8
        )
    lists = call_kernel(
        functools.partial(list_body, groups, tiles, chips),
        [
            f32(2, TILE),
            f32(CORES * tiles * chips * tiles, TILE),
            i32(chips * tiles, TILE),
            i32(CORES * rows, TILE),
            f32(rows, TILE),
            f32(chips, TILE),
        ],
        [
            logit_scale,
            logit_bias,
            blocks.transpose(2, 1, 0),
            bucket.reshape(-1, TILE),
            positive.reshape(-1, TILE),
        ],
        scalars=3,
        limit=8,
    )
    if square:
        own_images, image_raw, image_scales = call_kernel(
            own_images_body, [bf16(rows), bf16(rows), f32(rows, TILE)], [image_emb], limit=8
        )
        image_sent, own_images = lax.optimization_barrier((image_emb, own_images))
        from_first = swap_near(image_sent, 0)
        from_second, own_images, *lists = lax.optimization_barrier(
            (from_second, own_images, *lists)
        )
        from_far = swap_near(from_second, 0)
        second_images = call_kernel(
            unit_images_body, [bf16(rows)], [from_second], flops=WAIT_FLOPS // 2, limit=8
        )[0]
        near_images = call_kernel(
            near_images_body, [bf16(3 * rows)], [from_first, second_images, own_images], limit=8
        )[0]
        text_raw[-1], near_images = lax.optimization_barrier((text_raw[-1], near_images))
    text_own, text_scales, *pieces = call_kernel(
        functools.partial(unit_text_body, groups),
        [bf16(rows), f32(rows, TILE)] + [bf16(rows // TEXT_PIECES)] * TEXT_PIECES,
        text_raw,
        limit=8,
    )
    text_other = [swap(piece, "blk", 1) for piece in pieces]
    unit_flops = 2 * rows * rows * embed

    def finish_text(acc_own, acc_other):
        parts = call_kernel(
            functools.partial(text_grad_body, groups),
            [bf16(rows, width)] * groups,
            [text_scales] + text_raw + [acc_own] + [swap(piece, "blk", 1) for piece in acc_other],
            limit=16,
        )
        return swap_chunks(parts)

    def finish(text_parts, total, pieces):
        arrived = call_kernel(
            arrived_body,
            [struct((16, TILE), jnp.bfloat16)],
            text_parts[1:],
            flops=WAIT_FLOPS,
            limit=8,
        )
        return tuple(
            call_kernel(
                functools.partial(finish_body, groups, len(pieces)),
                [bf16(groups * rows, width), bf16(rows)],
                text_parts + [image_raw, image_scales, total] + pieces + arrived,
                outs_anywhere=True,
                scratch=[
                    pltpu.VMEM((rows, embed), jnp.bfloat16),
                    pltpu.SemaphoreType.DMA(((groups + 2) * tiles,)),
                ],
                limit=8,
            )
        )

    if not square:
        columns = gathered.shape[0]
        spread, acc_own, *acc_other = call_kernel(
            functools.partial(all_body, tiles, chips),
            [bf16(columns), f32(rows)] + [bf16(rows // ACC_PIECES)] * ACC_PIECES,
            lists + [text_own, jnp.concatenate(text_other), gathered],
            scratch=[
                pltpu.VMEM((columns, embed), jnp.bfloat16),
                pltpu.VMEM((2 * rows, columns), jnp.bfloat16),
            ],
            flops=6 * chips * unit_flops,
            limit=56,
        )
        text_parts = finish_text(acc_own, acc_other)
        parts = lax.all_to_all(
            spread, "blk", split_axis=0, concat_axis=0, tiled=True, axis_index_groups=same_core
        )
        total = jnp.sum(parts.reshape(-1, rows, embed).astype(jnp.float32), axis=0)
        return finish(text_parts, total, [])

    own_weights, near_weights = call_kernel(
        functools.partial(near_own_body, tiles),
        [bf16(rows, rows), bf16(rows, 2 * rows)],
        lists + [text_own, near_images],
        limit=16,
    )
    units, first_weights, first_sum = call_kernel(
        functools.partial(first_sum_body, tiles),
        [bf16(2 * rows), bf16(2 * rows, rows), bf16(rows)],
        lists + [text_own, near_images, near_weights] + text_other,
        limit=16,
    )
    image_add = swap_near(first_sum, 0)
    own_weights, acc, near_weights = call_kernel(
        functools.partial(near_sum_body, tiles),
        [bf16(2 * rows, rows), f32(2 * rows), bf16(2 * rows, 2 * rows)],
        lists + [units, near_images, own_weights, near_weights, first_weights],
        limit=24,
    )
    own_weights, from_far = lax.optimization_barrier((own_weights, from_far))
    far_weights, far_images = call_kernel(
        functools.partial(far_weights_body, tiles),
        [bf16(2 * rows, 2 * rows), bf16(2 * rows)],
        lists + [units, own_images, own_weights, from_far],
        limit=16,
    )
    sizes = [rows // 2] * 2
    far_sum = call_kernel(
        far_sum_body, [bf16(size) for size in sizes], [far_weights, units], limit=16
    )
    far_images, far_sum[0] = lax.optimization_barrier((far_images, far_sum[0]))
    acc_other = call_kernel(
        functools.partial(text_sum_body, 1),
        [bf16(rows // ACC_PIECES)] * ACC_PIECES,
        [far_weights, far_images, acc],
        limit=16,
    )
    far_images, acc_other[0] = lax.optimization_barrier((far_images, acc_other[0]))
    acc_own = call_kernel(
        functools.partial(text_sum_body, 0),
        [f32(rows)],
        [far_weights, far_images, acc],
        limit=16,
    )[0]
    text_parts = finish_text(acc_own, acc_other)
    near_weights, text_parts[0] = lax.optimization_barrier((near_weights, text_parts[0]))
    second_sum, image_add = call_kernel(
        second_sum_body,
        [f32(rows), bf16(rows)],
        [near_weights, units, image_add],
        limit=16,
    )
    image_last = []
    far_in = [swap_near(piece, 0) for piece in far_sum]
    for size, start, piece in zip(sizes, (0, sizes[0]), far_in):
        relayed = call_kernel(
            functools.partial(relay_body, start), [bf16(size)], [second_sum, piece], limit=8
        )[0]
        image_last.append(swap_near(relayed, 1))
        second_sum, relayed = lax.optimization_barrier((second_sum, relayed))
    own_weights, relayed = lax.optimization_barrier((own_weights, relayed))
    base = call_kernel(
        own_sum_body, [f32(rows)], [own_weights, units, image_add], moved=0, limit=16
    )[0]
    return finish(text_parts, base, image_last)


def solution(mesh):
    in_specs = (P("blk", "tp"), P(("blk", "tp"), None), P(), P(), P(), P(), P())
    out_specs = (P("blk", "tp"), P(("blk", "tp"), None))
    return jax.shard_map(
        per_device, mesh=mesh, in_specs=in_specs, out_specs=out_specs, check_vma=False
    )
```

```python
import functools
import math

import jax
import jax.numpy as jnp
from jax import lax
from jax.experimental import pallas as pl
from jax.experimental.pallas import tpu as pltpu
from jax.sharding import PartitionSpec as P

TILE = 128
SLOTS = 3
WAIT_FLOPS = 20_000_000_000
TEXT_PIECES = 3
ACC_PIECES = 2
STEP = 32
CORES = 2
EPS = 1e-06
LOG2E = math.log2(math.e)
MIB = 1024 * 1024

VMEM_SPEC = pl.BlockSpec(memory_space=pltpu.VMEM)
ANY_SPEC = pl.BlockSpec(memory_space=pl.ANY)
SMEM_SPEC = pl.BlockSpec(memory_space=pltpu.SMEM)


def call_kernel(
    body,
    outs,
    operands,
    scalars=0,
    anywhere=(),
    outs_anywhere=False,
    scratch=(),
    flops=0,
    moved=None,
    limit=24,
):
    if moved is None:
        moved = sum(x.size * x.dtype.itemsize for x in operands)
        moved += sum(math.prod(o.shape) * o.dtype.itemsize for o in outs)
    specs = [SMEM_SPEC] * scalars + [VMEM_SPEC] * (len(operands) - scalars)
    for at in anywhere:
        specs[at] = ANY_SPEC
    return list(
        pl.pallas_call(
            body,
            out_shape=outs,
            in_specs=specs,
            out_specs=[ANY_SPEC if outs_anywhere else VMEM_SPEC] * len(outs),
            scratch_shapes=list(scratch),
            compiler_params=pltpu.CompilerParams(vmem_limit_bytes=limit * MIB),
            cost_estimate=pl.CostEstimate(flops=flops, bytes_accessed=moved, transcendentals=0),
        )(*operands)
    )


def struct(shape, dtype):
    return jax.ShapeDtypeStruct(shape, dtype)


def row_scales(square_sum):
    return lax.rsqrt(square_sum + EPS)


def column_of(row):
    return jnp.broadcast_to(row, (TILE, TILE)).T


def dot_nt(left, right):
    return lax.dot_general(
        left, right, (((1,), (1,)), ((), ())), preferred_element_type=jnp.float32
    )


def dot_tn(left, right):
    return lax.dot_general(
        left, right, (((0,), (0,)), ((), ())), preferred_element_type=jnp.float32
    )


def far_first(k, chunks):
    if chunks > 2 and k in (1, 2):
        return chunks - 3 + k
    return (chunks - k) % chunks


def feature_slice(peer, width):
    return pl.ds(pl.multiple_of(peer * width, width), width)


def pick_body(text_ref, *out_refs):
    place = lax.axis_index("tp")
    rows = out_refs[0].shape[0]
    for k, out_ref in enumerate(out_refs):
        peer = place ^ far_first(k, len(out_refs))
        out_ref[...] = text_ref[pl.ds(pl.multiple_of(peer * rows, rows), rows), :]


def unit_text_body(chunks, *refs):
    chunk_refs, (unit_ref, scale_ref) = refs[:chunks], refs[chunks : chunks + 2]
    piece_refs = refs[chunks + 2 :]
    place = lax.axis_index("tp")
    rows, width = chunk_refs[0].shape
    for first in range(0, rows, STEP):
        part = pl.ds(first, STEP)
        parts = [ref[part, :].astype(jnp.float32) for ref in chunk_refs]
        scales = row_scales(sum(jnp.sum(x * x, axis=-1, keepdims=True) for x in parts))
        scale_ref[part, :] = jnp.broadcast_to(scales, (STEP, TILE))
        for k, x in enumerate(parts):
            unit_ref[part, feature_slice(place ^ far_first(k, chunks), width)] = (x * scales).astype(jnp.bfloat16)
    split_rows(unit_ref, piece_refs)


def split_rows(whole_ref, piece_refs):
    for at, ref in enumerate(piece_refs):
        ref[...] = whole_ref[pl.ds(at * ref.shape[0], ref.shape[0]), :]


def join_rows(piece_refs, whole_ref):
    for at, ref in enumerate(piece_refs):
        whole_ref[pl.ds(at * ref.shape[0], ref.shape[0]), :] = ref[...]


def unit_images(ref, image_ref, scale_ref=None):
    for first in range(0, ref.shape[0], STEP):
        part = pl.ds(first, STEP)
        values = ref[part, :].astype(jnp.float32)
        scales = row_scales(jnp.sum(values * values, axis=-1, keepdims=True))
        image_ref[part, :] = (values * scales).astype(jnp.bfloat16)
        if scale_ref is not None:
            scale_ref[part, :] = jnp.broadcast_to(scales, (STEP, TILE))


def unit_images_body(raw_ref, out_ref):
    unit_images(raw_ref, out_ref)


def own_images_body(raw_ref, out_ref, raw_out_ref, scale_ref):
    unit_images(raw_ref, out_ref, scale_ref)
    raw_out_ref[...] = raw_ref[...]


def near_images_body(first_ref, second_unit_ref, own_unit_ref, out_ref):
    rows = first_ref.shape[0]
    unit_images(first_ref, out_ref)
    out_ref[rows : 2 * rows, :] = second_unit_ref[...]
    out_ref[2 * rows :, :] = own_unit_ref[...]


def neighbour_bits(shard):
    core = shard % CORES
    return 2 << core, 4 >> core


def list_body(groups, tiles, chips, *refs):
    scale_ref, bias_ref, blocks_ref, bucket_ref, positive_ref = refs[:5]
    line_ref, amount_ref, column_ref, row_ref, match_ref, own_ref = refs[5:]
    here, place = lax.axis_index("blk"), lax.axis_index("tp")
    scale = scale_ref[0]
    line_ref[pl.ds(0, 1), :] = jnp.full((1, TILE), -scale * LOG2E, jnp.float32)
    line_ref[pl.ds(1, 1), :] = jnp.full((1, TILE), -bias_ref[0] * LOG2E, jnp.float32)
    if chips == 4:
        first, second = neighbour_bits(here)
        shards = [here, here ^ first, here ^ second, here ^ 6]
    else:
        shards = [chip * CORES + here % CORES for chip in range(chips)]
    count = len(shards) * tiles

    def first_tile(shard):
        return (shard * groups + place) * tiles

    for n, shard in enumerate(shards):
        own_ref[pl.ds(n, 1), :] = jnp.full((1, TILE), jnp.where(shard == here, 1.0, 0.0))
        for j in range(tiles):
            column_ref[pl.ds(n * tiles + j, 1), :] = bucket_ref[pl.ds(first_tile(shard) + j, 1), :]
    for at in range(CORES * tiles):
        tile = first_tile(here ^ (at // tiles)) + at % tiles
        row_ref[pl.ds(at * TILE, TILE), :] = column_of(bucket_ref[pl.ds(tile, 1), :])
        if at < tiles:
            ids = lax.broadcasted_iota(jnp.int32, (1, TILE), 1) + tile * TILE
            matched = column_of(positive_ref[pl.ds(tile, 1), :]) == ids
            match_ref[pl.ds(at * TILE, TILE), :] = jnp.where(matched, 1.0, 0.0)
        for n, shard in enumerate(shards):
            entries = [blocks_ref[slot, shard, tile] for slot in range(SLOTS)]
            for j in range(tiles):
                listed = sum(jnp.where(entry == j, 1.0, 0.0) for entry in entries)
                amount_ref[pl.ds(at * count + n * tiles + j, 1), :] = jnp.full(
                    (1, TILE), scale * listed, jnp.float32
                )


class Pairs:
    count = 6

    def __init__(self, refs, tiles):
        self.line_ref, self.amount_ref, self.column_ref = refs[:3]
        self.row_ref, self.match_ref, self.own_ref = refs[3:6]
        self.tiles = tiles

    def weigh(self, products, half, group, weight_ref, top, left, own=None):
        tiles = self.tiles
        slope, offset = self.line_ref[pl.ds(0, 1), :], self.line_ref[pl.ds(1, 1), :]
        count = self.column_ref.shape[0]
        for a in range(tiles):
            at = half * tiles + a
            row_bucket = self.row_ref[pl.ds(at * TILE, TILE), :]
            for j in range(tiles):
                n = group * tiles + j
                amount = self.amount_ref[pl.ds(at * count + n, 1), :]
                power = (
                    products[a * TILE : (a + 1) * TILE, j * TILE : (j + 1) * TILE] * slope + offset
                )
                factor = jnp.where(row_bucket == self.column_ref[pl.ds(n, 1), :], amount, 0.0)
                if own and a == j:
                    match = self.match_ref[pl.ds(a * TILE, TILE), :]
                    if own == "search":
                        match = match * self.own_ref[pl.ds(group, 1), :]
                    power = jnp.where(match > 0.0, -power, power)
                    factor = jnp.where(match > 0.0, -amount, factor)
                inverse = pl.reciprocal(1.0 + jnp.exp2(power), approx=True)
                weight_ref[pl.ds(top + a * TILE, TILE), pl.ds(left + j * TILE, TILE)] = (
                    factor * inverse
                ).astype(jnp.bfloat16)


def near_own_body(tiles, *refs):
    pairs = Pairs(refs, tiles)
    unit_ref, image_ref, own_weight_ref, weight_ref = refs[Pairs.count :]
    rows = unit_ref.shape[0]
    products = dot_nt(unit_ref[...], image_ref[...])
    pairs.weigh(products[:, :rows], 0, 1, weight_ref, 0, 0)
    pairs.weigh(products[:, rows : 2 * rows], 0, 2, weight_ref, 0, rows)
    pairs.weigh(products[:, 2 * rows :], 0, 0, own_weight_ref, 0, 0, "diagonal")


def first_sum_body(tiles, *refs):
    pairs = Pairs(refs, tiles)
    own_unit_ref, near_image_ref, weight_in_ref = refs[Pairs.count : Pairs.count + 3]
    piece_refs = refs[Pairs.count + 3 : Pairs.count + 3 + TEXT_PIECES]
    unit_ref, weight_ref, sum_ref = refs[Pairs.count + 3 + TEXT_PIECES :]
    rows = own_unit_ref.shape[0]
    for at, ref in enumerate(piece_refs):
        unit_ref[pl.ds(rows + at * ref.shape[0], ref.shape[0]), :] = ref[...]
    unit_ref[:rows, :] = own_unit_ref[...]
    weight_ref[:rows, :] = weight_in_ref[:, :rows]
    products = dot_nt(unit_ref[rows:, :], near_image_ref[pl.ds(0, rows), :])
    pairs.weigh(products, 1, 1, weight_ref, rows, 0)
    sum_ref[...] = dot_tn(weight_ref[...], unit_ref[...]).astype(jnp.bfloat16)


def near_sum_body(tiles, *refs):
    pairs = Pairs(refs, tiles)
    unit_ref, image_ref, own_weight_in_ref, weight_in_ref, first_ref = refs[
        Pairs.count : Pairs.count + 5
    ]
    own_weight_ref, acc_ref, weight_ref = refs[Pairs.count + 5 :]
    rows = first_ref.shape[1]
    products = dot_nt(unit_ref[rows:, :], image_ref[rows:, :])
    own_weight_ref[:rows, :] = own_weight_in_ref[...]
    weight_ref[:, :rows] = first_ref[...]
    weight_ref[:rows, rows:] = weight_in_ref[:, rows:]
    pairs.weigh(products[:, :rows], 1, 2, weight_ref, rows, rows)
    pairs.weigh(products[:, rows:], 1, 0, own_weight_ref, rows, 0)
    acc_ref[...] = jnp.dot(
        weight_ref[...], image_ref[: 2 * rows, :], preferred_element_type=jnp.float32
    )


def far_body(tiles, pieces, *refs):
    pairs = Pairs(refs, tiles)
    unit_ref, own_image_ref, own_weight_ref, raw_ref, acc_ref = refs[Pairs.count : Pairs.count + 5]
    weight_ref, image_ref = refs[Pairs.count + 5 : Pairs.count + 7]
    sum_refs, text_refs = refs[Pairs.count + 7 : Pairs.count + 7 + pieces], refs[Pairs.count + 7 + pieces :]
    rows = raw_ref.shape[0]
    unit_images(raw_ref, image_ref.at[pl.ds(rows, rows), :])
    products = dot_nt(unit_ref[...], image_ref[rows:, :])
    image_ref[:rows, :] = own_image_ref[...]
    weight_ref[:, :rows] = own_weight_ref[...]
    pairs.weigh(products[rows:, :], 1, 3, weight_ref, rows, rows)
    text_sum_body(1, weight_ref, image_ref, acc_ref, *text_refs)
    pairs.weigh(products[:rows, :], 0, 3, weight_ref, 0, rows)
    total = dot_tn(weight_ref[:, rows:], unit_ref[...]).astype(jnp.bfloat16)
    start = 0
    for ref in sum_refs:
        ref[...] = total[start : start + ref.shape[0], :]
        start += ref.shape[0]


def text_sum_body(half, weight_ref, image_ref, acc_ref, *out_refs):
    rows = weight_ref.shape[0] // CORES
    size = out_refs[0].shape[0]
    part = pl.ds(half * rows, rows)
    acc = acc_ref[part, :] + jnp.dot(
        weight_ref[part, :], image_ref[...], preferred_element_type=jnp.float32
    )
    for at, ref in enumerate(out_refs):
        ref[...] = acc[at * size : (at + 1) * size, :].astype(ref.dtype)


def second_sum_body(weight_ref, unit_ref, add_ref, out_ref, add_out_ref):
    rows = out_ref.shape[0]
    out_ref[...] = dot_tn(weight_ref[:, rows:], unit_ref[...])
    add_out_ref[...] = add_ref[...]


def own_sum_body(weight_ref, unit_ref, add_ref, out_ref):
    out_ref[...] = dot_tn(weight_ref[...], unit_ref[...]) + add_ref[...].astype(jnp.float32)


def all_body(tiles, chips, *refs):
    pairs = Pairs(refs, tiles)
    own_ref, other_ref, piece_ref = refs[Pairs.count : Pairs.count + 3]
    outs = refs[Pairs.count + 3 :]
    spread_ref, acc_ref, acc_piece_refs = outs[0], outs[1], outs[2 : 2 + ACC_PIECES]
    image_ref, weight_ref = outs[2 + ACC_PIECES :]
    rows = own_ref.shape[0]
    unit_images(piece_ref, image_ref)
    for half, text_ref in enumerate((own_ref, other_ref)):
        for chip in range(chips):
            products = dot_nt(text_ref[...], image_ref[pl.ds(chip * rows, rows), :])
            pairs.weigh(
                products, half, chip, weight_ref, half * rows, chip * rows, None if half else "search"
            )
        acc = jnp.dot(
            weight_ref[pl.ds(half * rows, rows), :],
            image_ref[...],
            preferred_element_type=jnp.float32,
        )
        if half == 0:
            acc_ref[...] = acc
            continue
        size = rows // ACC_PIECES
        for at, ref in enumerate(acc_piece_refs):
            ref[...] = acc[at * size : (at + 1) * size, :].astype(jnp.bfloat16)
    for chip in range(chips):
        columns = pl.ds(chip * rows, rows)
        total = dot_tn(weight_ref[pl.ds(0, rows), columns], own_ref[...])
        total += dot_tn(weight_ref[pl.ds(rows, rows), columns], other_ref[...])
        spread_ref[columns, :] = total.astype(jnp.bfloat16)


def relay_body(start, sum_ref, in_ref, out_ref):
    part = sum_ref[pl.ds(start, in_ref.shape[0]), :]
    out_ref[...] = (part + in_ref[...].astype(jnp.float32)).astype(jnp.bfloat16)


def text_grad_body(chunks, *refs):
    scale_ref, raw_refs, acc_ref = refs[0], refs[1 : 1 + chunks], refs[1 + chunks]
    add_refs, out_refs = refs[2 + chunks : -chunks], refs[-chunks:]
    place = lax.axis_index("tp")
    rows, width = raw_refs[0].shape
    size = add_refs[0].shape[0]
    for first in range(0, rows, STEP):
        part = pl.ds(first, STEP)
        scales = scale_ref[part, :1]
        raws = [ref[part, :].astype(jnp.float32) for ref in raw_refs]
        accs = []
        for k in range(chunks):
            features = feature_slice(place ^ far_first(k, chunks), width)
            added = add_refs[first // size][pl.ds(first % size, STEP), features]
            accs.append(acc_ref[part, features] + added.astype(jnp.float32))
        inner = sum(jnp.sum(x * a, axis=-1, keepdims=True) for x, a in zip(raws, accs))
        inner = inner * scales * scales
        for k in range(chunks):
            out_refs[k][part, :] = (scales * (accs[k] - raws[k] * inner)).astype(jnp.bfloat16)


def arrived_body(*refs):
    out_ref = refs[-1]
    out_ref[...] = sum(ref[: out_ref.shape[0], : out_ref.shape[1]] for ref in refs[:-1])


def finish_rows(start, count, raw_ref, scale_ref, sum_ref, add_ref, grad_ref, out_ref, sems, copies):
    for block in range(0, count, TILE // 2):
        for first in range(block, block + TILE // 2, STEP):
            part = pl.ds(start + first, STEP)
            raw = raw_ref[part, :].astype(jnp.float32)
            scales = scale_ref[part, :1]
            acc = sum_ref[part, :]
            if add_ref is not None:
                acc = acc + add_ref[pl.ds(first, STEP), :].astype(jnp.float32)
            inner = jnp.sum(raw * acc, axis=-1, keepdims=True) * scales * scales
            grad_ref[part, :] = (scales * (acc - raw * inner)).astype(jnp.bfloat16)
        part = pl.ds(start + block, TILE // 2)
        copies.append(
            pltpu.make_async_copy(
                grad_ref.at[part, :], out_ref.at[part, :], sems.at[len(copies)]
            )
        )
        copies[-1].start()


def finish_body(chunks, adds, *refs):
    part_refs, (raw_ref, scale_ref, sum_ref) = refs[:chunks], refs[chunks : chunks + 3]
    add_refs = refs[chunks + 3 : chunks + 3 + adds]
    text_ref, image_ref, grad_ref, sems = refs[-4:]
    place = lax.axis_index("tp")
    rows = part_refs[0].shape[0]
    copies = []
    for k in range(chunks):
        peer = place ^ far_first(k, chunks)
        for first in range(0, rows, TILE):
            block = pl.ds(pl.multiple_of(peer * rows + first, TILE), TILE)
            copies.append(
                pltpu.make_async_copy(
                    part_refs[k].at[pl.ds(first, TILE), :],
                    text_ref.at[block, :],
                    sems.at[len(copies)],
                )
            )
            copies[-1].start()
    start = 0
    for add_ref in add_refs or [None]:
        count = rows if add_ref is None else add_ref.shape[0]
        finish_rows(
            start, count, raw_ref, scale_ref, sum_ref, add_ref, grad_ref, image_ref, sems, copies
        )
        start += count
    for copy in copies:
        copy.wait()


def swap(value, axis, bits):
    count = lax.axis_size(axis)
    return lax.ppermute(value, axis, [(i, i ^ bits) for i in range(count)])


def swap_near(value, which):
    count = lax.axis_size("blk")
    return lax.ppermute(value, "blk", [(i, i ^ neighbour_bits(i)[which]) for i in range(count)])


def swap_chunks(chunks):
    count = len(chunks)
    return chunks[:1] + [swap(chunks[k], "tp", far_first(k, count)) for k in range(1, count)]


def per_device(text_emb, image_emb, logit_scale, logit_bias, bucket, positive, blocks):
    groups = lax.axis_size("tp")
    shards = lax.axis_size("blk")
    chips = shards // CORES
    rows, embed = image_emb.shape
    tiles = rows // TILE
    width = text_emb.shape[1]
    square = chips == 4

    def bf16(count, columns=embed):
        return struct((count, columns), jnp.bfloat16)

    def f32(count, columns=embed):
        return struct((count, columns), jnp.float32)

    def i32(count, columns):
        return struct((count, columns), jnp.int32)

    picked = call_kernel(pick_body, [bf16(rows, width)] * groups, [text_emb], limit=8)
    text_raw = swap_chunks(picked)
    if square:
        from_second = swap_near(image_emb, 1)
    else:
        same_core = [[chip * CORES + core for chip in range(chips)] for core in range(CORES)]
        gathered = lax.all_gather(
            image_emb, "blk", axis=0, tiled=True, axis_index_groups=same_core
        )
        _, image_raw, image_scales = call_kernel(
            own_images_body, [bf16(rows), bf16(rows), f32(rows, TILE)], [image_emb], limit=8
        )
    lists = call_kernel(
        functools.partial(list_body, groups, tiles, chips),
        [
            f32(2, TILE),
            f32(CORES * tiles * chips * tiles, TILE),
            i32(chips * tiles, TILE),
            i32(CORES * rows, TILE),
            f32(rows, TILE),
            f32(chips, TILE),
        ],
        [
            logit_scale,
            logit_bias,
            blocks.transpose(2, 1, 0),
            bucket.reshape(-1, TILE),
            positive.reshape(-1, TILE),
        ],
        scalars=3,
        limit=8,
    )
    if square:
        own_images, image_raw, image_scales = call_kernel(
            own_images_body, [bf16(rows), bf16(rows), f32(rows, TILE)], [image_emb], limit=8
        )
        image_sent, own_images = lax.optimization_barrier((image_emb, own_images))
        from_first = swap_near(image_sent, 0)
        from_second, own_images, *lists = lax.optimization_barrier(
            (from_second, own_images, *lists)
        )
        from_far = swap_near(from_second, 0)
        second_images = call_kernel(
            unit_images_body, [bf16(rows)], [from_second], flops=WAIT_FLOPS // 2, limit=8
        )[0]
        near_images = call_kernel(
            near_images_body, [bf16(3 * rows)], [from_first, second_images, own_images], limit=8
        )[0]
        text_raw[-1], near_images = lax.optimization_barrier((text_raw[-1], near_images))
    text_own, text_scales, *pieces = call_kernel(
        functools.partial(unit_text_body, groups),
        [bf16(rows), f32(rows, TILE)] + [bf16(rows // TEXT_PIECES)] * TEXT_PIECES,
        text_raw,
        limit=8,
    )
    text_other = [swap(piece, "blk", 1) for piece in pieces]
    unit_flops = 2 * rows * rows * embed

    def finish_text(acc_own, acc_other):
        parts = call_kernel(
            functools.partial(text_grad_body, groups),
            [bf16(rows, width)] * groups,
            [text_scales] + text_raw + [acc_own] + [swap(piece, "blk", 1) for piece in acc_other],
            limit=16,
        )
        return swap_chunks(parts)

    def finish(text_parts, total, pieces):
        arrived = call_kernel(
            arrived_body,
            [struct((16, TILE), jnp.bfloat16)],
            text_parts[1:],
            flops=WAIT_FLOPS,
            limit=8,
        )
        return tuple(
            call_kernel(
                functools.partial(finish_body, groups, len(pieces)),
                [bf16(groups * rows, width), bf16(rows)],
                text_parts + [image_raw, image_scales, total] + pieces + arrived,
                outs_anywhere=True,
                scratch=[
                    pltpu.VMEM((rows, embed), jnp.bfloat16),
                    pltpu.SemaphoreType.DMA(((groups + 2) * tiles,)),
                ],
                limit=8,
            )
        )

    if not square:
        columns = gathered.shape[0]
        spread, acc_own, *acc_other = call_kernel(
            functools.partial(all_body, tiles, chips),
            [bf16(columns), f32(rows)] + [bf16(rows // ACC_PIECES)] * ACC_PIECES,
            lists + [text_own, jnp.concatenate(text_other), gathered],
            scratch=[
                pltpu.VMEM((columns, embed), jnp.bfloat16),
                pltpu.VMEM((2 * rows, columns), jnp.bfloat16),
            ],
            flops=6 * chips * unit_flops,
            limit=56,
        )
        text_parts = finish_text(acc_own, acc_other)
        parts = lax.all_to_all(
            spread, "blk", split_axis=0, concat_axis=0, tiled=True, axis_index_groups=same_core
        )
        total = jnp.sum(parts.reshape(-1, rows, embed).astype(jnp.float32), axis=0)
        return finish(text_parts, total, [])

    own_weights, near_weights = call_kernel(
        functools.partial(near_own_body, tiles),
        [bf16(rows, rows), bf16(rows, 2 * rows)],
        lists + [text_own, near_images],
        limit=16,
    )
    units, first_weights, first_sum = call_kernel(
        functools.partial(first_sum_body, tiles),
        [bf16(2 * rows), bf16(2 * rows, rows), bf16(rows)],
        lists + [text_own, near_images, near_weights] + text_other,
        limit=16,
    )
    image_add = swap_near(first_sum, 0)
    own_weights, acc, near_weights = call_kernel(
        functools.partial(near_sum_body, tiles),
        [bf16(2 * rows, rows), f32(2 * rows), bf16(2 * rows, 2 * rows)],
        lists + [units, near_images, own_weights, near_weights, first_weights],
        limit=24,
    )
    own_weights, from_far = lax.optimization_barrier((own_weights, from_far))
    sizes = [rows - TILE, TILE]
    far_weights, far_images, *rest = call_kernel(
        functools.partial(far_body, tiles, len(sizes)),
        [bf16(2 * rows, 2 * rows), bf16(2 * rows)]
        + [bf16(size) for size in sizes]
        + [bf16(rows // ACC_PIECES)] * ACC_PIECES,
        lists + [units, own_images, own_weights, from_far, acc],
        limit=24,
    )
    far_sum, acc_other = rest[: len(sizes)], rest[len(sizes) :]
    acc_own = call_kernel(
        functools.partial(text_sum_body, 0),
        [f32(rows)],
        [far_weights, far_images, acc],
        limit=16,
    )[0]
    text_parts = finish_text(acc_own, acc_other)
    near_weights, text_parts[0] = lax.optimization_barrier((near_weights, text_parts[0]))
    second_sum, image_add = call_kernel(
        second_sum_body,
        [f32(rows), bf16(rows)],
        [near_weights, units, image_add],
        limit=16,
    )
    image_last = []
    far_in = [swap_near(piece, 0) for piece in far_sum]
    for size, start, piece in zip(sizes, (0, sizes[0]), far_in):
        relayed = call_kernel(
            functools.partial(relay_body, start), [bf16(size)], [second_sum, piece], limit=8
        )[0]
        image_last.append(swap_near(relayed, 1))
        second_sum, relayed = lax.optimization_barrier((second_sum, relayed))
    own_weights, relayed = lax.optimization_barrier((own_weights, relayed))
    base = call_kernel(
        own_sum_body, [f32(rows)], [own_weights, units, image_add], moved=0, limit=16
    )[0]
    return finish(text_parts, base, image_last)


def solution(mesh):
    in_specs = (P("blk", "tp"), P(("blk", "tp"), None), P(), P(), P(), P(), P())
    out_specs = (P("blk", "tp"), P(("blk", "tp"), None))
    return jax.shard_map(
        per_device, mesh=mesh, in_specs=in_specs, out_specs=out_specs, check_vma=False
    )
```

```python
import functools
import math

import jax
import jax.numpy as jnp
from jax import lax
from jax.experimental import pallas as pl
from jax.experimental.pallas import tpu as pltpu
from jax.sharding import PartitionSpec as P

TILE = 128
SLOTS = 3
WAIT_FLOPS = 20_000_000_000
TEXT_PIECES = 3
ACC_PIECES = 2
STEP = 32
CORES = 2
EPS = 1e-06
LOG2E = math.log2(math.e)
MIB = 1024 * 1024

VMEM_SPEC = pl.BlockSpec(memory_space=pltpu.VMEM)
ANY_SPEC = pl.BlockSpec(memory_space=pl.ANY)
SMEM_SPEC = pl.BlockSpec(memory_space=pltpu.SMEM)


def call_kernel(
    body,
    outs,
    operands,
    scalars=0,
    anywhere=(),
    outs_anywhere=False,
    scratch=(),
    flops=0,
    moved=None,
    aliases=None,
    limit=24,
):
    if moved is None:
        moved = sum(x.size * x.dtype.itemsize for x in operands)
        moved += sum(math.prod(o.shape) * o.dtype.itemsize for o in outs)
    specs = [SMEM_SPEC] * scalars + [VMEM_SPEC] * (len(operands) - scalars)
    for at in anywhere:
        specs[at] = ANY_SPEC
    return list(
        pl.pallas_call(
            body,
            out_shape=outs,
            in_specs=specs,
            out_specs=[ANY_SPEC if outs_anywhere else VMEM_SPEC] * len(outs),
            scratch_shapes=list(scratch),
            input_output_aliases=aliases or {},
            compiler_params=pltpu.CompilerParams(vmem_limit_bytes=limit * MIB),
            cost_estimate=pl.CostEstimate(flops=flops, bytes_accessed=moved, transcendentals=0),
        )(*operands)
    )


def struct(shape, dtype):
    return jax.ShapeDtypeStruct(shape, dtype)


def row_scales(square_sum):
    return lax.rsqrt(square_sum + EPS)


def column_of(row):
    return jnp.broadcast_to(row, (TILE, TILE)).T


def dot_nt(left, right):
    return lax.dot_general(
        left, right, (((1,), (1,)), ((), ())), preferred_element_type=jnp.float32
    )


def dot_tn(left, right):
    return lax.dot_general(
        left, right, (((0,), (0,)), ((), ())), preferred_element_type=jnp.float32
    )


def far_first(k, chunks):
    if chunks > 2 and k in (1, 2):
        return chunks - 3 + k
    return (chunks - k) % chunks


def feature_slice(peer, width):
    return pl.ds(pl.multiple_of(peer * width, width), width)


def pick_body(text_ref, *out_refs):
    place = lax.axis_index("tp")
    rows = out_refs[0].shape[0]
    for k, out_ref in enumerate(out_refs):
        peer = place ^ far_first(k, len(out_refs))
        out_ref[...] = text_ref[pl.ds(pl.multiple_of(peer * rows, rows), rows), :]


def unit_text_body(chunks, *refs):
    chunk_refs, (unit_ref, scale_ref) = refs[:chunks], refs[chunks : chunks + 2]
    piece_refs = refs[chunks + 2 :]
    place = lax.axis_index("tp")
    rows, width = chunk_refs[0].shape
    for first in range(0, rows, STEP):
        part = pl.ds(first, STEP)
        parts = [ref[part, :].astype(jnp.float32) for ref in chunk_refs]
        scales = row_scales(sum(jnp.sum(x * x, axis=-1, keepdims=True) for x in parts))
        scale_ref[part, :] = jnp.broadcast_to(scales, (STEP, TILE))
        for k, x in enumerate(parts):
            unit_ref[part, feature_slice(place ^ far_first(k, chunks), width)] = (x * scales).astype(jnp.bfloat16)
    split_rows(unit_ref, piece_refs)


def split_rows(whole_ref, piece_refs):
    for at, ref in enumerate(piece_refs):
        ref[...] = whole_ref[pl.ds(at * ref.shape[0], ref.shape[0]), :]


def join_rows(piece_refs, whole_ref):
    for at, ref in enumerate(piece_refs):
        whole_ref[pl.ds(at * ref.shape[0], ref.shape[0]), :] = ref[...]


def unit_images(ref, image_ref, scale_ref=None):
    for first in range(0, ref.shape[0], STEP):
        part = pl.ds(first, STEP)
        values = ref[part, :].astype(jnp.float32)
        scales = row_scales(jnp.sum(values * values, axis=-1, keepdims=True))
        image_ref[part, :] = (values * scales).astype(jnp.bfloat16)
        if scale_ref is not None:
            scale_ref[part, :] = jnp.broadcast_to(scales, (STEP, TILE))


def unit_images_body(raw_ref, out_ref):
    unit_images(raw_ref, out_ref)


def own_images_body(raw_ref, out_ref, raw_out_ref, scale_ref):
    unit_images(raw_ref, out_ref, scale_ref)
    raw_out_ref[...] = raw_ref[...]


def near_images_body(first_ref, second_unit_ref, own_unit_ref, out_ref):
    rows = first_ref.shape[0]
    unit_images(first_ref, out_ref)
    out_ref[rows : 2 * rows, :] = second_unit_ref[...]
    out_ref[2 * rows :, :] = own_unit_ref[...]


def neighbour_bits(shard):
    core = shard % CORES
    return 2 << core, 4 >> core


def list_body(groups, tiles, chips, *refs):
    scale_ref, bias_ref, blocks_ref, bucket_ref, positive_ref = refs[:5]
    line_ref, amount_ref, column_ref, row_ref, match_ref, own_ref = refs[5:]
    here, place = lax.axis_index("blk"), lax.axis_index("tp")
    scale = scale_ref[0]
    line_ref[pl.ds(0, 1), :] = jnp.full((1, TILE), -scale * LOG2E, jnp.float32)
    line_ref[pl.ds(1, 1), :] = jnp.full((1, TILE), -bias_ref[0] * LOG2E, jnp.float32)
    if chips == 4:
        first, second = neighbour_bits(here)
        shards = [here, here ^ first, here ^ second, here ^ 6]
    else:
        shards = [chip * CORES + here % CORES for chip in range(chips)]
    count = len(shards) * tiles

    def first_tile(shard):
        return (shard * groups + place) * tiles

    for n, shard in enumerate(shards):
        own_ref[pl.ds(n, 1), :] = jnp.full((1, TILE), jnp.where(shard == here, 1.0, 0.0))
        for j in range(tiles):
            column_ref[pl.ds(n * tiles + j, 1), :] = bucket_ref[pl.ds(first_tile(shard) + j, 1), :]
    for at in range(CORES * tiles):
        tile = first_tile(here ^ (at // tiles)) + at % tiles
        row_ref[pl.ds(at * TILE, TILE), :] = column_of(bucket_ref[pl.ds(tile, 1), :])
        if at < tiles:
            ids = lax.broadcasted_iota(jnp.int32, (1, TILE), 1) + tile * TILE
            matched = column_of(positive_ref[pl.ds(tile, 1), :]) == ids
            match_ref[pl.ds(at * TILE, TILE), :] = jnp.where(matched, 1.0, 0.0)
        for n, shard in enumerate(shards):
            entries = [blocks_ref[slot, shard, tile] for slot in range(SLOTS)]
            for j in range(tiles):
                listed = sum(jnp.where(entry == j, 1.0, 0.0) for entry in entries)
                amount_ref[pl.ds(at * count + n * tiles + j, 1), :] = jnp.full(
                    (1, TILE), scale * listed, jnp.float32
                )


class Pairs:
    count = 6

    def __init__(self, refs, tiles):
        self.line_ref, self.amount_ref, self.column_ref = refs[:3]
        self.row_ref, self.match_ref, self.own_ref = refs[3:6]
        self.tiles = tiles

    def weigh(self, products, half, group, weight_ref, top, left, own=None):
        tiles = self.tiles
        slope, offset = self.line_ref[pl.ds(0, 1), :], self.line_ref[pl.ds(1, 1), :]
        count = self.column_ref.shape[0]
        for a in range(tiles):
            at = half * tiles + a
            row_bucket = self.row_ref[pl.ds(at * TILE, TILE), :]
            for j in range(tiles):
                n = group * tiles + j
                amount = self.amount_ref[pl.ds(at * count + n, 1), :]
                power = (
                    products[a * TILE : (a + 1) * TILE, j * TILE : (j + 1) * TILE] * slope + offset
                )
                factor = jnp.where(row_bucket == self.column_ref[pl.ds(n, 1), :], amount, 0.0)
                if own and a == j:
                    match = self.match_ref[pl.ds(a * TILE, TILE), :]
                    if own == "search":
                        match = match * self.own_ref[pl.ds(group, 1), :]
                    power = jnp.where(match > 0.0, -power, power)
                    factor = jnp.where(match > 0.0, -amount, factor)
                inverse = pl.reciprocal(1.0 + jnp.exp2(power), approx=True)
                weight_ref[pl.ds(top + a * TILE, TILE), pl.ds(left + j * TILE, TILE)] = (
                    factor * inverse
                ).astype(jnp.bfloat16)


def near_own_body(tiles, *refs):
    pairs = Pairs(refs, tiles)
    unit_ref, image_ref, own_weight_ref, weight_ref = refs[Pairs.count :]
    rows = unit_ref.shape[0]
    products = dot_nt(unit_ref[...], image_ref[...])
    pairs.weigh(products[:, :rows], 0, 1, weight_ref, 0, 0)
    pairs.weigh(products[:, rows : 2 * rows], 0, 2, weight_ref, 0, rows)
    pairs.weigh(products[:, 2 * rows :], 0, 0, own_weight_ref, 0, 0, "diagonal")


def first_sum_body(tiles, *refs):
    pairs = Pairs(refs, tiles)
    own_unit_ref, near_image_ref, weight_in_ref = refs[Pairs.count : Pairs.count + 3]
    piece_refs = refs[Pairs.count + 3 : Pairs.count + 3 + TEXT_PIECES]
    unit_ref, weight_ref, sum_ref = refs[Pairs.count + 3 + TEXT_PIECES :]
    rows = own_unit_ref.shape[0]
    for at, ref in enumerate(piece_refs):
        unit_ref[pl.ds(rows + at * ref.shape[0], ref.shape[0]), :] = ref[...]
    unit_ref[:rows, :] = own_unit_ref[...]
    weight_ref[:rows, :] = weight_in_ref[:, :rows]
    products = dot_nt(unit_ref[rows:, :], near_image_ref[pl.ds(0, rows), :])
    pairs.weigh(products, 1, 1, weight_ref, rows, 0)
    sum_ref[...] = dot_tn(weight_ref[...], unit_ref[...]).astype(jnp.bfloat16)


def near_sum_body(tiles, *refs):
    pairs = Pairs(refs, tiles)
    unit_ref, image_ref, own_weight_in_ref, weight_in_ref, first_ref = refs[
        Pairs.count : Pairs.count + 5
    ]
    own_weight_ref, acc_ref, weight_ref = refs[Pairs.count + 5 :]
    rows = first_ref.shape[1]
    products = dot_nt(unit_ref[rows:, :], image_ref[rows:, :])
    own_weight_ref[:rows, :] = own_weight_in_ref[...]
    weight_ref[:, :rows] = first_ref[...]
    weight_ref[:rows, rows:] = weight_in_ref[:, rows:]
    pairs.weigh(products[:, :rows], 1, 2, weight_ref, rows, rows)
    pairs.weigh(products[:, rows:], 1, 0, own_weight_ref, rows, 0)
    acc_ref[...] = jnp.dot(
        weight_ref[...], image_ref[: 2 * rows, :], preferred_element_type=jnp.float32
    )


def far_body(tiles, pieces, *refs):
    pairs = Pairs(refs, tiles)
    unit_ref, own_image_ref, own_weight_ref, raw_ref, acc_ref = refs[Pairs.count : Pairs.count + 5]
    weight_ref, image_ref = refs[Pairs.count + 5 : Pairs.count + 7]
    sum_refs, text_refs = refs[Pairs.count + 7 : Pairs.count + 7 + pieces], refs[Pairs.count + 7 + pieces :]
    rows = raw_ref.shape[0]
    unit_images(raw_ref, image_ref.at[pl.ds(rows, rows), :])
    products = dot_nt(unit_ref[...], image_ref[rows:, :])
    image_ref[:rows, :] = own_image_ref[...]
    weight_ref[:, :rows] = own_weight_ref[...]
    pairs.weigh(products[rows:, :], 1, 3, weight_ref, rows, rows)
    text_sum_body(1, weight_ref, image_ref, acc_ref, *text_refs)
    pairs.weigh(products[:rows, :], 0, 3, weight_ref, 0, rows)
    total = dot_tn(weight_ref[:, rows:], unit_ref[...]).astype(jnp.bfloat16)
    start = 0
    for ref in sum_refs:
        ref[...] = total[start : start + ref.shape[0], :]
        start += ref.shape[0]


def text_sum_body(half, weight_ref, image_ref, acc_ref, *out_refs):
    rows = weight_ref.shape[0] // CORES
    size = out_refs[0].shape[0]
    part = pl.ds(half * rows, rows)
    acc = acc_ref[part, :] + jnp.dot(
        weight_ref[part, :], image_ref[...], preferred_element_type=jnp.float32
    )
    for at, ref in enumerate(out_refs):
        ref[...] = acc[at * size : (at + 1) * size, :].astype(ref.dtype)


def second_sum_body(weight_ref, unit_ref, add_ref, out_ref, add_out_ref):
    rows = out_ref.shape[0]
    out_ref[...] = dot_tn(weight_ref[:, rows:], unit_ref[...])
    add_out_ref[...] = add_ref[...]


def own_sum_body(weight_ref, unit_ref, add_ref, out_ref):
    out_ref[...] = dot_tn(weight_ref[...], unit_ref[...]) + add_ref[...].astype(jnp.float32)


def all_body(tiles, chips, *refs):
    pairs = Pairs(refs, tiles)
    own_ref, other_ref, piece_ref = refs[Pairs.count : Pairs.count + 3]
    outs = refs[Pairs.count + 3 :]
    spread_ref, acc_ref, acc_piece_refs = outs[0], outs[1], outs[2 : 2 + ACC_PIECES]
    image_ref, weight_ref = outs[2 + ACC_PIECES :]
    rows = own_ref.shape[0]
    unit_images(piece_ref, image_ref)
    for half, text_ref in enumerate((own_ref, other_ref)):
        for chip in range(chips):
            products = dot_nt(text_ref[...], image_ref[pl.ds(chip * rows, rows), :])
            pairs.weigh(
                products, half, chip, weight_ref, half * rows, chip * rows, None if half else "search"
            )
        acc = jnp.dot(
            weight_ref[pl.ds(half * rows, rows), :],
            image_ref[...],
            preferred_element_type=jnp.float32,
        )
        if half == 0:
            acc_ref[...] = acc
            continue
        size = rows // ACC_PIECES
        for at, ref in enumerate(acc_piece_refs):
            ref[...] = acc[at * size : (at + 1) * size, :].astype(jnp.bfloat16)
    for chip in range(chips):
        columns = pl.ds(chip * rows, rows)
        total = dot_tn(weight_ref[pl.ds(0, rows), columns], own_ref[...])
        total += dot_tn(weight_ref[pl.ds(rows, rows), columns], other_ref[...])
        spread_ref[columns, :] = total.astype(jnp.bfloat16)


def relay_body(start, sum_ref, in_ref, out_ref):
    part = sum_ref[pl.ds(start, in_ref.shape[0]), :]
    out_ref[...] = (part + in_ref[...].astype(jnp.float32)).astype(jnp.bfloat16)


def text_grad_body(chunks, *refs):
    scale_ref, raw_refs, acc_ref = refs[0], refs[1 : 1 + chunks], refs[1 + chunks]
    add_refs, out_refs = refs[2 + chunks : -chunks], refs[-chunks:]
    place = lax.axis_index("tp")
    rows, width = raw_refs[0].shape
    size = add_refs[0].shape[0]
    for first in range(0, rows, STEP):
        part = pl.ds(first, STEP)
        scales = scale_ref[part, :1]
        raws = [ref[part, :].astype(jnp.float32) for ref in raw_refs]
        accs = []
        for k in range(chunks):
            features = feature_slice(place ^ far_first(k, chunks), width)
            added = add_refs[first // size][pl.ds(first % size, STEP), features]
            accs.append(acc_ref[part, features] + added.astype(jnp.float32))
        inner = sum(jnp.sum(x * a, axis=-1, keepdims=True) for x, a in zip(raws, accs))
        inner = inner * scales * scales
        for k in range(chunks):
            out_refs[k][part, :] = (scales * (accs[k] - raws[k] * inner)).astype(jnp.bfloat16)


def arrived_body(*refs):
    out_ref = refs[-1]
    out_ref[...] = sum(ref[: out_ref.shape[0], : out_ref.shape[1]] for ref in refs[:-1])


def finish_rows(start, count, raw_ref, scale_ref, sum_ref, add_ref, grad_ref, out_ref, sems, copies):
    for block in range(0, count, TILE // 2):
        for first in range(block, block + TILE // 2, STEP):
            part = pl.ds(start + first, STEP)
            raw = raw_ref[part, :].astype(jnp.float32)
            scales = scale_ref[part, :1]
            acc = sum_ref[part, :]
            if add_ref is not None:
                acc = acc + add_ref[pl.ds(first, STEP), :].astype(jnp.float32)
            inner = jnp.sum(raw * acc, axis=-1, keepdims=True) * scales * scales
            grad_ref[part, :] = (scales * (acc - raw * inner)).astype(jnp.bfloat16)
        part = pl.ds(start + block, TILE // 2)
        copies.append(
            pltpu.make_async_copy(
                grad_ref.at[part, :], out_ref.at[part, :], sems.at[len(copies)]
            )
        )
        copies[-1].start()


def own_block_body(part_ref, out_ref, sem):
    rows = part_ref.shape[0]
    block = pl.ds(pl.multiple_of(lax.axis_index("tp") * rows, rows), rows)
    copy = pltpu.make_async_copy(part_ref, out_ref.at[block, :], sem)
    copy.start()
    copy.wait()


def finish_body(chunks, adds, *refs):
    part_refs, (raw_ref, scale_ref, sum_ref) = refs[:chunks], refs[chunks : chunks + 3]
    add_refs = refs[chunks + 3 : chunks + 3 + adds]
    text_ref, image_ref, grad_ref, sems = refs[-4:]
    place = lax.axis_index("tp")
    rows = part_refs[0].shape[0]
    copies = []
    for k in range(1, chunks):
        peer = place ^ far_first(k, chunks)
        for first in range(0, rows, TILE):
            block = pl.ds(pl.multiple_of(peer * rows + first, TILE), TILE)
            copies.append(
                pltpu.make_async_copy(
                    part_refs[k].at[pl.ds(first, TILE), :],
                    text_ref.at[block, :],
                    sems.at[len(copies)],
                )
            )
            copies[-1].start()
    start = 0
    for add_ref in add_refs or [None]:
        count = rows if add_ref is None else add_ref.shape[0]
        finish_rows(
            start, count, raw_ref, scale_ref, sum_ref, add_ref, grad_ref, image_ref, sems, copies
        )
        start += count
    for copy in copies:
        copy.wait()


def swap(value, axis, bits):
    count = lax.axis_size(axis)
    return lax.ppermute(value, axis, [(i, i ^ bits) for i in range(count)])


def swap_near(value, which):
    count = lax.axis_size("blk")
    return lax.ppermute(value, "blk", [(i, i ^ neighbour_bits(i)[which]) for i in range(count)])


def swap_chunks(chunks):
    count = len(chunks)
    return chunks[:1] + [swap(chunks[k], "tp", far_first(k, count)) for k in range(1, count)]


def per_device(text_emb, image_emb, logit_scale, logit_bias, bucket, positive, blocks):
    groups = lax.axis_size("tp")
    shards = lax.axis_size("blk")
    chips = shards // CORES
    rows, embed = image_emb.shape
    tiles = rows // TILE
    width = text_emb.shape[1]
    square = chips == 4

    def bf16(count, columns=embed):
        return struct((count, columns), jnp.bfloat16)

    def f32(count, columns=embed):
        return struct((count, columns), jnp.float32)

    def i32(count, columns):
        return struct((count, columns), jnp.int32)

    picked = call_kernel(pick_body, [bf16(rows, width)] * groups, [text_emb], limit=8)
    text_raw = swap_chunks(picked)
    if square:
        from_second = swap_near(image_emb, 1)
    else:
        same_core = [[chip * CORES + core for chip in range(chips)] for core in range(CORES)]
        gathered = lax.all_gather(
            image_emb, "blk", axis=0, tiled=True, axis_index_groups=same_core
        )
        _, image_raw, image_scales = call_kernel(
            own_images_body, [bf16(rows), bf16(rows), f32(rows, TILE)], [image_emb], limit=8
        )
    lists = call_kernel(
        functools.partial(list_body, groups, tiles, chips),
        [
            f32(2, TILE),
            f32(CORES * tiles * chips * tiles, TILE),
            i32(chips * tiles, TILE),
            i32(CORES * rows, TILE),
            f32(rows, TILE),
            f32(chips, TILE),
        ],
        [
            logit_scale,
            logit_bias,
            blocks.transpose(2, 1, 0),
            bucket.reshape(-1, TILE),
            positive.reshape(-1, TILE),
        ],
        scalars=3,
        limit=8,
    )
    if square:
        own_images, image_raw, image_scales = call_kernel(
            own_images_body, [bf16(rows), bf16(rows), f32(rows, TILE)], [image_emb], limit=8
        )
        image_sent, own_images = lax.optimization_barrier((image_emb, own_images))
        from_first = swap_near(image_sent, 0)
        from_second, own_images, *lists = lax.optimization_barrier(
            (from_second, own_images, *lists)
        )
        from_far = swap_near(from_second, 0)
        second_images = call_kernel(
            unit_images_body, [bf16(rows)], [from_second], flops=WAIT_FLOPS // 2, limit=8
        )[0]
        near_images = call_kernel(
            near_images_body, [bf16(3 * rows)], [from_first, second_images, own_images], limit=8
        )[0]
        text_raw[-1], near_images = lax.optimization_barrier((text_raw[-1], near_images))
    text_own, text_scales, *pieces = call_kernel(
        functools.partial(unit_text_body, groups),
        [bf16(rows), f32(rows, TILE)] + [bf16(rows // TEXT_PIECES)] * TEXT_PIECES,
        text_raw,
        limit=8,
    )
    text_other = [swap(piece, "blk", 1) for piece in pieces]
    unit_flops = 2 * rows * rows * embed

    def finish_text(acc_own, acc_other):
        parts = call_kernel(
            functools.partial(text_grad_body, groups),
            [bf16(rows, width)] * groups,
            [text_scales] + text_raw + [acc_own] + [swap(piece, "blk", 1) for piece in acc_other],
            limit=16,
        )
        return swap_chunks(parts)

    def finish(text_parts, total, pieces):
        text_own_block = call_kernel(
            own_block_body,
            [bf16(groups * rows, width)],
            text_parts[:1],
            outs_anywhere=True,
            scratch=[pltpu.SemaphoreType.DMA],
            moved=0,
            limit=8,
        )[0]
        arrived = call_kernel(
            arrived_body,
            [struct((16, TILE), jnp.bfloat16)],
            text_parts[1:],
            flops=WAIT_FLOPS,
            limit=8,
        )
        return tuple(
            call_kernel(
                functools.partial(finish_body, groups, len(pieces)),
                [bf16(groups * rows, width), bf16(rows)],
                text_parts
                + [image_raw, image_scales, total]
                + pieces
                + arrived
                + [text_own_block],
                anywhere=(groups + 4 + len(pieces),),
                aliases={groups + 4 + len(pieces): 0},
                outs_anywhere=True,
                scratch=[
                    pltpu.VMEM((rows, embed), jnp.bfloat16),
                    pltpu.SemaphoreType.DMA(((groups + 2) * tiles,)),
                ],
                limit=8,
            )
        )

    if not square:
        columns = gathered.shape[0]
        spread, acc_own, *acc_other = call_kernel(
            functools.partial(all_body, tiles, chips),
            [bf16(columns), f32(rows)] + [bf16(rows // ACC_PIECES)] * ACC_PIECES,
            lists + [text_own, jnp.concatenate(text_other), gathered],
            scratch=[
                pltpu.VMEM((columns, embed), jnp.bfloat16),
                pltpu.VMEM((2 * rows, columns), jnp.bfloat16),
            ],
            flops=6 * chips * unit_flops,
            limit=56,
        )
        text_parts = finish_text(acc_own, acc_other)
        parts = lax.all_to_all(
            spread, "blk", split_axis=0, concat_axis=0, tiled=True, axis_index_groups=same_core
        )
        total = jnp.sum(parts.reshape(-1, rows, embed).astype(jnp.float32), axis=0)
        return finish(text_parts, total, [])

    own_weights, near_weights = call_kernel(
        functools.partial(near_own_body, tiles),
        [bf16(rows, rows), bf16(rows, 2 * rows)],
        lists + [text_own, near_images],
        limit=16,
    )
    units, first_weights, first_sum = call_kernel(
        functools.partial(first_sum_body, tiles),
        [bf16(2 * rows), bf16(2 * rows, rows), bf16(rows)],
        lists + [text_own, near_images, near_weights] + text_other,
        limit=16,
    )
    image_add = swap_near(first_sum, 0)
    own_weights, acc, near_weights = call_kernel(
        functools.partial(near_sum_body, tiles),
        [bf16(2 * rows, rows), f32(2 * rows), bf16(2 * rows, 2 * rows)],
        lists + [units, near_images, own_weights, near_weights, first_weights],
        limit=24,
    )
    own_weights, from_far = lax.optimization_barrier((own_weights, from_far))
    sizes = [rows - TILE, TILE]
    far_weights, far_images, *rest = call_kernel(
        functools.partial(far_body, tiles, len(sizes)),
        [bf16(2 * rows, 2 * rows), bf16(2 * rows)]
        + [bf16(size) for size in sizes]
        + [bf16(rows // ACC_PIECES)] * ACC_PIECES,
        lists + [units, own_images, own_weights, from_far, acc],
        limit=24,
    )
    far_sum, acc_other = rest[: len(sizes)], rest[len(sizes) :]
    acc_own = call_kernel(
        functools.partial(text_sum_body, 0),
        [f32(rows)],
        [far_weights, far_images, acc],
        limit=16,
    )[0]
    text_parts = finish_text(acc_own, acc_other)
    near_weights, text_parts[0] = lax.optimization_barrier((near_weights, text_parts[0]))
    second_sum, image_add = call_kernel(
        second_sum_body,
        [f32(rows), bf16(rows)],
        [near_weights, units, image_add],
        limit=16,
    )
    image_last = []
    far_in = [swap_near(piece, 0) for piece in far_sum]
    for size, start, piece in zip(sizes, (0, sizes[0]), far_in):
        relayed = call_kernel(
            functools.partial(relay_body, start), [bf16(size)], [second_sum, piece], limit=8
        )[0]
        image_last.append(swap_near(relayed, 1))
        second_sum, relayed = lax.optimization_barrier((second_sum, relayed))
    own_weights, relayed = lax.optimization_barrier((own_weights, relayed))
    base = call_kernel(
        own_sum_body, [f32(rows)], [own_weights, units, image_add], moved=0, limit=16
    )[0]
    text_parts[0], base = lax.optimization_barrier((text_parts[0], base))
    return finish(text_parts, base, image_last)


def solution(mesh):
    in_specs = (P("blk", "tp"), P(("blk", "tp"), None), P(), P(), P(), P(), P())
    out_specs = (P("blk", "tp"), P(("blk", "tp"), None))
    return jax.shard_map(
        per_device, mesh=mesh, in_specs=in_specs, out_specs=out_specs, check_vma=False
    )
```

```python
import functools
import math

import jax
import jax.numpy as jnp
from jax import lax
from jax.experimental import pallas as pl
from jax.experimental.pallas import tpu as pltpu
from jax.sharding import PartitionSpec as P

TILE = 128
SLOTS = 3
WAIT_FLOPS = 20_000_000_000
TEXT_PIECES = 3
ACC_PIECES = 2
STEP = 32
CORES = 2
EPS = 1e-06
LOG2E = math.log2(math.e)
MIB = 1024 * 1024

VMEM_SPEC = pl.BlockSpec(memory_space=pltpu.VMEM)
ANY_SPEC = pl.BlockSpec(memory_space=pl.ANY)
SMEM_SPEC = pl.BlockSpec(memory_space=pltpu.SMEM)


def call_kernel(
    body,
    outs,
    operands,
    scalars=0,
    anywhere=(),
    outs_anywhere=False,
    scratch=(),
    flops=0,
    moved=None,
    aliases=None,
    limit=24,
):
    if moved is None:
        moved = sum(x.size * x.dtype.itemsize for x in operands)
        moved += sum(math.prod(o.shape) * o.dtype.itemsize for o in outs)
    specs = [SMEM_SPEC] * scalars + [VMEM_SPEC] * (len(operands) - scalars)
    for at in anywhere:
        specs[at] = ANY_SPEC
    return list(
        pl.pallas_call(
            body,
            out_shape=outs,
            in_specs=specs,
            out_specs=[ANY_SPEC if outs_anywhere else VMEM_SPEC] * len(outs),
            scratch_shapes=list(scratch),
            input_output_aliases=aliases or {},
            compiler_params=pltpu.CompilerParams(vmem_limit_bytes=limit * MIB),
            cost_estimate=pl.CostEstimate(flops=flops, bytes_accessed=moved, transcendentals=0),
        )(*operands)
    )


def struct(shape, dtype):
    return jax.ShapeDtypeStruct(shape, dtype)


def row_scales(square_sum):
    return lax.rsqrt(square_sum + EPS)


def column_of(row):
    return jnp.broadcast_to(row, (TILE, TILE)).T


def dot_nt(left, right):
    return lax.dot_general(
        left, right, (((1,), (1,)), ((), ())), preferred_element_type=jnp.float32
    )


def dot_tn(left, right):
    return lax.dot_general(
        left, right, (((0,), (0,)), ((), ())), preferred_element_type=jnp.float32
    )


def far_first(k, chunks):
    if chunks > 2 and k in (1, 2):
        return chunks - 3 + k
    return (chunks - k) % chunks


def feature_slice(peer, width):
    return pl.ds(pl.multiple_of(peer * width, width), width)


def pick_body(text_ref, *out_refs):
    place = lax.axis_index("tp")
    rows = out_refs[0].shape[0]
    for k, out_ref in enumerate(out_refs):
        peer = place ^ far_first(k, len(out_refs))
        out_ref[...] = text_ref[pl.ds(pl.multiple_of(peer * rows, rows), rows), :]


def unit_text_body(chunks, *refs):
    chunk_refs, (unit_ref, scale_ref) = refs[:chunks], refs[chunks : chunks + 2]
    piece_refs = refs[chunks + 2 :]
    place = lax.axis_index("tp")
    rows, width = chunk_refs[0].shape
    for first in range(0, rows, STEP):
        part = pl.ds(first, STEP)
        parts = [ref[part, :].astype(jnp.float32) for ref in chunk_refs]
        scales = row_scales(sum(jnp.sum(x * x, axis=-1, keepdims=True) for x in parts))
        scale_ref[part, :] = jnp.broadcast_to(scales, (STEP, TILE))
        for k, x in enumerate(parts):
            unit_ref[part, feature_slice(place ^ far_first(k, chunks), width)] = (x * scales).astype(jnp.bfloat16)
    split_rows(unit_ref, piece_refs)


def split_rows(whole_ref, piece_refs):
    for at, ref in enumerate(piece_refs):
        ref[...] = whole_ref[pl.ds(at * ref.shape[0], ref.shape[0]), :]


def join_rows(piece_refs, whole_ref):
    for at, ref in enumerate(piece_refs):
        whole_ref[pl.ds(at * ref.shape[0], ref.shape[0]), :] = ref[...]


def unit_images(ref, image_ref, scale_ref=None):
    for first in range(0, ref.shape[0], STEP):
        part = pl.ds(first, STEP)
        values = ref[part, :].astype(jnp.float32)
        scales = row_scales(jnp.sum(values * values, axis=-1, keepdims=True))
        image_ref[part, :] = (values * scales).astype(jnp.bfloat16)
        if scale_ref is not None:
            scale_ref[part, :] = jnp.broadcast_to(scales, (STEP, TILE))


def unit_images_body(raw_ref, out_ref):
    unit_images(raw_ref, out_ref)


def own_images_body(raw_ref, out_ref, raw_out_ref, scale_ref):
    unit_images(raw_ref, out_ref, scale_ref)
    raw_out_ref[...] = raw_ref[...]


def near_images_body(first_ref, second_unit_ref, own_unit_ref, out_ref):
    rows = first_ref.shape[0]
    unit_images(first_ref, out_ref)
    out_ref[rows : 2 * rows, :] = second_unit_ref[...]
    out_ref[2 * rows :, :] = own_unit_ref[...]


def neighbour_bits(shard):
    core = shard % CORES
    return 2 << core, 4 >> core


def list_body(groups, tiles, chips, *refs):
    scale_ref, bias_ref, blocks_ref, bucket_ref, positive_ref = refs[:5]
    line_ref, amount_ref, column_ref, row_ref, match_ref, own_ref = refs[5:]
    here, place = lax.axis_index("blk"), lax.axis_index("tp")
    scale = scale_ref[0]
    line_ref[pl.ds(0, 1), :] = jnp.full((1, TILE), -scale * LOG2E, jnp.float32)
    line_ref[pl.ds(1, 1), :] = jnp.full((1, TILE), -bias_ref[0] * LOG2E, jnp.float32)
    if chips == 4:
        first, second = neighbour_bits(here)
        shards = [here, here ^ first, here ^ second, here ^ 6]
    else:
        shards = [chip * CORES + here % CORES for chip in range(chips)]
    count = len(shards) * tiles

    def first_tile(shard):
        return (shard * groups + place) * tiles

    for n, shard in enumerate(shards):
        own_ref[pl.ds(n, 1), :] = jnp.full((1, TILE), jnp.where(shard == here, 1.0, 0.0))
        for j in range(tiles):
            column_ref[pl.ds(n * tiles + j, 1), :] = bucket_ref[pl.ds(first_tile(shard) + j, 1), :]
    for at in range(CORES * tiles):
        tile = first_tile(here ^ (at // tiles)) + at % tiles
        row_ref[pl.ds(at * TILE, TILE), :] = column_of(bucket_ref[pl.ds(tile, 1), :])
        if at < tiles:
            ids = lax.broadcasted_iota(jnp.int32, (1, TILE), 1) + tile * TILE
            matched = column_of(positive_ref[pl.ds(tile, 1), :]) == ids
            match_ref[pl.ds(at * TILE, TILE), :] = jnp.where(matched, 1.0, 0.0)
        for n, shard in enumerate(shards):
            entries = [blocks_ref[slot, shard, tile] for slot in range(SLOTS)]
            for j in range(tiles):
                listed = sum(jnp.where(entry == j, 1.0, 0.0) for entry in entries)
                amount_ref[pl.ds(at * count + n * tiles + j, 1), :] = jnp.full(
                    (1, TILE), scale * listed, jnp.float32
                )


class Pairs:
    count = 6

    def __init__(self, refs, tiles):
        self.line_ref, self.amount_ref, self.column_ref = refs[:3]
        self.row_ref, self.match_ref, self.own_ref = refs[3:6]
        self.tiles = tiles

    def weigh(self, products, half, group, weight_ref, top, left, own=None):
        tiles = self.tiles
        slope, offset = self.line_ref[pl.ds(0, 1), :], self.line_ref[pl.ds(1, 1), :]
        count = self.column_ref.shape[0]
        for a in range(tiles):
            at = half * tiles + a
            row_bucket = self.row_ref[pl.ds(at * TILE, TILE), :]
            for j in range(tiles):
                n = group * tiles + j
                amount = self.amount_ref[pl.ds(at * count + n, 1), :]
                power = (
                    products[a * TILE : (a + 1) * TILE, j * TILE : (j + 1) * TILE] * slope + offset
                )
                factor = jnp.where(row_bucket == self.column_ref[pl.ds(n, 1), :], amount, 0.0)
                if own and a == j:
                    match = self.match_ref[pl.ds(a * TILE, TILE), :]
                    if own == "search":
                        match = match * self.own_ref[pl.ds(group, 1), :]
                    power = jnp.where(match > 0.0, -power, power)
                    factor = jnp.where(match > 0.0, -amount, factor)
                inverse = pl.reciprocal(1.0 + jnp.exp2(power), approx=True)
                weight_ref[pl.ds(top + a * TILE, TILE), pl.ds(left + j * TILE, TILE)] = (
                    factor * inverse
                ).astype(jnp.bfloat16)


def near_own_body(tiles, *refs):
    pairs = Pairs(refs, tiles)
    unit_ref, image_ref, own_weight_ref, weight_ref = refs[Pairs.count :]
    rows = unit_ref.shape[0]
    products = dot_nt(unit_ref[...], image_ref[...])
    pairs.weigh(products[:, :rows], 0, 1, weight_ref, 0, 0)
    pairs.weigh(products[:, rows : 2 * rows], 0, 2, weight_ref, 0, rows)
    pairs.weigh(products[:, 2 * rows :], 0, 0, own_weight_ref, 0, 0, "diagonal")


def first_sum_body(tiles, *refs):
    pairs = Pairs(refs, tiles)
    own_unit_ref, near_image_ref, weight_in_ref = refs[Pairs.count : Pairs.count + 3]
    piece_refs = refs[Pairs.count + 3 : Pairs.count + 3 + TEXT_PIECES]
    unit_ref, weight_ref, sum_ref = refs[Pairs.count + 3 + TEXT_PIECES :]
    rows = own_unit_ref.shape[0]
    for at, ref in enumerate(piece_refs):
        unit_ref[pl.ds(rows + at * ref.shape[0], ref.shape[0]), :] = ref[...]
    unit_ref[:rows, :] = own_unit_ref[...]
    weight_ref[:rows, :] = weight_in_ref[:, :rows]
    products = dot_nt(unit_ref[rows:, :], near_image_ref[pl.ds(0, rows), :])
    pairs.weigh(products, 1, 1, weight_ref, rows, 0)
    sum_ref[...] = dot_tn(weight_ref[...], unit_ref[...]).astype(jnp.bfloat16)


def near_sum_body(tiles, *refs):
    pairs = Pairs(refs, tiles)
    unit_ref, image_ref, own_weight_in_ref, weight_in_ref, first_ref = refs[
        Pairs.count : Pairs.count + 5
    ]
    own_weight_ref, acc_ref, weight_ref = refs[Pairs.count + 5 :]
    rows = first_ref.shape[1]
    products = dot_nt(unit_ref[rows:, :], image_ref[rows:, :])
    own_weight_ref[:rows, :] = own_weight_in_ref[...]
    weight_ref[:, :rows] = first_ref[...]
    weight_ref[:rows, rows:] = weight_in_ref[:, rows:]
    pairs.weigh(products[:, :rows], 1, 2, weight_ref, rows, rows)
    pairs.weigh(products[:, rows:], 1, 0, own_weight_ref, rows, 0)
    acc_ref[...] = jnp.dot(
        weight_ref[...], image_ref[: 2 * rows, :], preferred_element_type=jnp.float32
    )


def far_body(tiles, pieces, *refs):
    pairs = Pairs(refs, tiles)
    unit_ref, own_image_ref, own_weight_ref, raw_ref, acc_ref = refs[Pairs.count : Pairs.count + 5]
    weight_ref, image_ref = refs[Pairs.count + 5 : Pairs.count + 7]
    sum_refs, text_refs = refs[Pairs.count + 7 : Pairs.count + 7 + pieces], refs[Pairs.count + 7 + pieces :]
    rows = raw_ref.shape[0]
    unit_images(raw_ref, image_ref.at[pl.ds(rows, rows), :])
    products = dot_nt(unit_ref[...], image_ref[rows:, :])
    image_ref[:rows, :] = own_image_ref[...]
    weight_ref[:, :rows] = own_weight_ref[...]
    pairs.weigh(products[rows:, :], 1, 3, weight_ref, rows, rows)
    text_sum_body(1, weight_ref, image_ref, acc_ref, *text_refs)
    pairs.weigh(products[:rows, :], 0, 3, weight_ref, 0, rows)
    total = dot_tn(weight_ref[:, rows:], unit_ref[...]).astype(jnp.bfloat16)
    start = 0
    for ref in sum_refs:
        ref[...] = total[start : start + ref.shape[0], :]
        start += ref.shape[0]


def text_sum_body(half, weight_ref, image_ref, acc_ref, *out_refs):
    rows = weight_ref.shape[0] // CORES
    size = out_refs[0].shape[0]
    part = pl.ds(half * rows, rows)
    acc = acc_ref[part, :] + jnp.dot(
        weight_ref[part, :], image_ref[...], preferred_element_type=jnp.float32
    )
    for at, ref in enumerate(out_refs):
        ref[...] = acc[at * size : (at + 1) * size, :].astype(ref.dtype)


def second_sum_body(weight_ref, unit_ref, add_ref, out_ref, add_out_ref):
    rows = out_ref.shape[0]
    out_ref[...] = dot_tn(weight_ref[:, rows:], unit_ref[...])
    add_out_ref[...] = add_ref[...]


def own_sum_body(weight_ref, unit_ref, add_ref, out_ref):
    out_ref[...] = dot_tn(weight_ref[...], unit_ref[...]) + add_ref[...].astype(jnp.float32)


def all_body(tiles, chips, *refs):
    pairs = Pairs(refs, tiles)
    own_ref, other_ref, piece_ref = refs[Pairs.count : Pairs.count + 3]
    outs = refs[Pairs.count + 3 :]
    spread_ref, acc_ref, acc_piece_refs = outs[0], outs[1], outs[2 : 2 + ACC_PIECES]
    image_ref, weight_ref = outs[2 + ACC_PIECES :]
    rows = own_ref.shape[0]
    unit_images(piece_ref, image_ref)
    for half, text_ref in enumerate((own_ref, other_ref)):
        for chip in range(chips):
            products = dot_nt(text_ref[...], image_ref[pl.ds(chip * rows, rows), :])
            pairs.weigh(
                products, half, chip, weight_ref, half * rows, chip * rows, None if half else "search"
            )
        acc = jnp.dot(
            weight_ref[pl.ds(half * rows, rows), :],
            image_ref[...],
            preferred_element_type=jnp.float32,
        )
        if half == 0:
            acc_ref[...] = acc
            continue
        size = rows // ACC_PIECES
        for at, ref in enumerate(acc_piece_refs):
            ref[...] = acc[at * size : (at + 1) * size, :].astype(jnp.bfloat16)
    for chip in range(chips):
        columns = pl.ds(chip * rows, rows)
        total = dot_tn(weight_ref[pl.ds(0, rows), columns], own_ref[...])
        total += dot_tn(weight_ref[pl.ds(rows, rows), columns], other_ref[...])
        spread_ref[columns, :] = total.astype(jnp.bfloat16)


def relay_body(start, sum_ref, in_ref, out_ref):
    part = sum_ref[pl.ds(start, in_ref.shape[0]), :]
    out_ref[...] = (part + in_ref[...].astype(jnp.float32)).astype(jnp.bfloat16)


def text_grad_body(chunks, *refs):
    scale_ref, raw_refs, acc_ref = refs[0], refs[1 : 1 + chunks], refs[1 + chunks]
    add_refs, out_refs = refs[2 + chunks : -chunks], refs[-chunks:]
    place = lax.axis_index("tp")
    rows, width = raw_refs[0].shape
    size = add_refs[0].shape[0]
    for first in range(0, rows, STEP):
        part = pl.ds(first, STEP)
        scales = scale_ref[part, :1]
        raws = [ref[part, :].astype(jnp.float32) for ref in raw_refs]
        accs = []
        for k in range(chunks):
            features = feature_slice(place ^ far_first(k, chunks), width)
            added = add_refs[first // size][pl.ds(first % size, STEP), features]
            accs.append(acc_ref[part, features] + added.astype(jnp.float32))
        inner = sum(jnp.sum(x * a, axis=-1, keepdims=True) for x, a in zip(raws, accs))
        inner = inner * scales * scales
        for k in range(chunks):
            out_refs[k][part, :] = (scales * (accs[k] - raws[k] * inner)).astype(jnp.bfloat16)


def arrived_body(*refs):
    out_ref = refs[-1]
    out_ref[...] = sum(ref[: out_ref.shape[0], : out_ref.shape[1]] for ref in refs[:-1])


def finish_rows(start, count, raw_ref, scale_ref, sum_ref, add_ref, grad_ref, out_ref, sems, copies):
    for block in range(0, count, TILE // 2):
        for first in range(block, block + TILE // 2, STEP):
            part = pl.ds(start + first, STEP)
            raw = raw_ref[part, :].astype(jnp.float32)
            scales = scale_ref[part, :1]
            acc = sum_ref[part, :]
            if add_ref is not None:
                acc = acc + add_ref[pl.ds(first, STEP), :].astype(jnp.float32)
            inner = jnp.sum(raw * acc, axis=-1, keepdims=True) * scales * scales
            grad_ref[part, :] = (scales * (acc - raw * inner)).astype(jnp.bfloat16)
        part = pl.ds(start + block, TILE // 2)
        copies.append(
            pltpu.make_async_copy(
                grad_ref.at[part, :], out_ref.at[part, :], sems.at[len(copies)]
            )
        )
        copies[-1].start()


def own_block_body(part_ref, out_ref, sem):
    rows = part_ref.shape[0]
    block = pl.ds(pl.multiple_of(lax.axis_index("tp") * rows, rows), rows)
    copy = pltpu.make_async_copy(part_ref, out_ref.at[block, :], sem)
    copy.start()
    copy.wait()


def finish_body(chunks, adds, *refs):
    part_refs, (raw_ref, scale_ref, sum_ref) = refs[:chunks], refs[chunks : chunks + 3]
    add_refs = refs[chunks + 3 : chunks + 3 + adds]
    text_ref, image_ref, grad_ref, sems = refs[-4:]
    place = lax.axis_index("tp")
    rows = part_refs[0].shape[0]
    copies = []
    for k in range(1, chunks):
        peer = place ^ far_first(k, chunks)
        for first in range(0, rows, TILE):
            block = pl.ds(pl.multiple_of(peer * rows + first, TILE), TILE)
            copies.append(
                pltpu.make_async_copy(
                    part_refs[k].at[pl.ds(first, TILE), :],
                    text_ref.at[block, :],
                    sems.at[len(copies)],
                )
            )
            copies[-1].start()
    start = 0
    for add_ref in add_refs or [None]:
        count = rows if add_ref is None else add_ref.shape[0]
        finish_rows(
            start, count, raw_ref, scale_ref, sum_ref, add_ref, grad_ref, image_ref, sems, copies
        )
        start += count
    for copy in copies:
        copy.wait()


def swap(value, axis, bits):
    count = lax.axis_size(axis)
    return lax.ppermute(value, axis, [(i, i ^ bits) for i in range(count)])


def swap_near(value, which):
    count = lax.axis_size("blk")
    return lax.ppermute(value, "blk", [(i, i ^ neighbour_bits(i)[which]) for i in range(count)])


def swap_chunks(chunks):
    count = len(chunks)
    return chunks[:1] + [swap(chunks[k], "tp", far_first(k, count)) for k in range(1, count)]


def per_device(text_emb, image_emb, logit_scale, logit_bias, bucket, positive, blocks):
    groups = lax.axis_size("tp")
    shards = lax.axis_size("blk")
    chips = shards // CORES
    rows, embed = image_emb.shape
    tiles = rows // TILE
    width = text_emb.shape[1]
    square = chips == 4

    def bf16(count, columns=embed):
        return struct((count, columns), jnp.bfloat16)

    def f32(count, columns=embed):
        return struct((count, columns), jnp.float32)

    def i32(count, columns):
        return struct((count, columns), jnp.int32)

    picked = call_kernel(pick_body, [bf16(rows, width)] * groups, [text_emb], limit=8)
    text_raw = swap_chunks(picked)
    if square:
        from_second = swap_near(image_emb, 1)
    else:
        same_core = [[chip * CORES + core for chip in range(chips)] for core in range(CORES)]
        gathered = lax.all_gather(
            image_emb, "blk", axis=0, tiled=True, axis_index_groups=same_core
        )
        _, image_raw, image_scales = call_kernel(
            own_images_body, [bf16(rows), bf16(rows), f32(rows, TILE)], [image_emb], limit=8
        )
    lists = call_kernel(
        functools.partial(list_body, groups, tiles, chips),
        [
            f32(2, TILE),
            f32(CORES * tiles * chips * tiles, TILE),
            i32(chips * tiles, TILE),
            i32(CORES * rows, TILE),
            f32(rows, TILE),
            f32(chips, TILE),
        ],
        [
            logit_scale,
            logit_bias,
            blocks.transpose(2, 1, 0),
            bucket.reshape(-1, TILE),
            positive.reshape(-1, TILE),
        ],
        scalars=3,
        limit=8,
    )
    if square:
        own_images, image_raw, image_scales = call_kernel(
            own_images_body, [bf16(rows), bf16(rows), f32(rows, TILE)], [image_emb], limit=8
        )
        image_sent, own_images = lax.optimization_barrier((image_emb, own_images))
        from_first = swap_near(image_sent, 0)
        from_second, own_images, *lists = lax.optimization_barrier(
            (from_second, own_images, *lists)
        )
        from_far = swap_near(from_second, 0)
        second_images = call_kernel(
            unit_images_body, [bf16(rows)], [from_second], flops=WAIT_FLOPS // 2, limit=8
        )[0]
        near_images = call_kernel(
            near_images_body, [bf16(3 * rows)], [from_first, second_images, own_images], limit=8
        )[0]
        text_raw[-1], near_images = lax.optimization_barrier((text_raw[-1], near_images))
    text_own, text_scales, *pieces = call_kernel(
        functools.partial(unit_text_body, groups),
        [bf16(rows), f32(rows, TILE)] + [bf16(rows // TEXT_PIECES)] * TEXT_PIECES,
        text_raw,
        limit=8,
    )
    text_other = [swap(piece, "blk", 1) for piece in pieces]
    unit_flops = 2 * rows * rows * embed

    def finish_text(acc_own, acc_other):
        parts = call_kernel(
            functools.partial(text_grad_body, groups),
            [bf16(rows, width)] * groups,
            [text_scales] + text_raw + [acc_own] + [swap(piece, "blk", 1) for piece in acc_other],
            limit=16,
        )
        return swap_chunks(parts)

    def finish(text_parts, total, pieces):
        text_own_block = call_kernel(
            own_block_body,
            [bf16(groups * rows, width)],
            text_parts[:1],
            outs_anywhere=True,
            scratch=[pltpu.SemaphoreType.DMA],
            moved=0,
            limit=8,
        )[0]
        arrived = call_kernel(
            arrived_body,
            [struct((16, TILE), jnp.bfloat16)],
            text_parts[1:],
            flops=WAIT_FLOPS,
            limit=8,
        )
        return tuple(
            call_kernel(
                functools.partial(finish_body, groups, len(pieces)),
                [bf16(groups * rows, width), bf16(rows)],
                text_parts
                + [image_raw, image_scales, total]
                + pieces
                + arrived
                + [text_own_block],
                anywhere=(groups + 4 + len(pieces),),
                aliases={groups + 4 + len(pieces): 0},
                outs_anywhere=True,
                scratch=[
                    pltpu.VMEM((rows, embed), jnp.bfloat16),
                    pltpu.SemaphoreType.DMA(((groups + 2) * tiles,)),
                ],
                limit=8,
            )
        )

    if not square:
        columns = gathered.shape[0]
        spread, acc_own, *acc_other = call_kernel(
            functools.partial(all_body, tiles, chips),
            [bf16(columns), f32(rows)] + [bf16(rows // ACC_PIECES)] * ACC_PIECES,
            lists + [text_own, jnp.concatenate(text_other), gathered],
            scratch=[
                pltpu.VMEM((columns, embed), jnp.bfloat16),
                pltpu.VMEM((2 * rows, columns), jnp.bfloat16),
            ],
            flops=6 * chips * unit_flops,
            limit=56,
        )
        text_parts = finish_text(acc_own, acc_other)
        parts = lax.all_to_all(
            spread, "blk", split_axis=0, concat_axis=0, tiled=True, axis_index_groups=same_core
        )
        total = jnp.sum(parts.reshape(-1, rows, embed).astype(jnp.float32), axis=0)
        return finish(text_parts, total, [])

    own_weights, near_weights = call_kernel(
        functools.partial(near_own_body, tiles),
        [bf16(rows, rows), bf16(rows, 2 * rows)],
        lists + [text_own, near_images],
        limit=16,
    )
    units, first_weights, first_sum = call_kernel(
        functools.partial(first_sum_body, tiles),
        [bf16(2 * rows), bf16(2 * rows, rows), bf16(rows)],
        lists + [text_own, near_images, near_weights] + text_other,
        limit=16,
    )
    image_add = swap_near(first_sum, 0)
    own_weights, acc, near_weights = call_kernel(
        functools.partial(near_sum_body, tiles),
        [bf16(2 * rows, rows), f32(2 * rows), bf16(2 * rows, 2 * rows)],
        lists + [units, near_images, own_weights, near_weights, first_weights],
        limit=24,
    )
    own_weights, from_far = lax.optimization_barrier((own_weights, from_far))
    sizes = [rows // 2] * 2
    far_weights, far_images, *rest = call_kernel(
        functools.partial(far_body, tiles, len(sizes)),
        [bf16(2 * rows, 2 * rows), bf16(2 * rows)]
        + [bf16(size) for size in sizes]
        + [bf16(rows // ACC_PIECES)] * ACC_PIECES,
        lists + [units, own_images, own_weights, from_far, acc],
        limit=24,
    )
    far_sum, acc_other = rest[: len(sizes)], rest[len(sizes) :]
    acc_own = call_kernel(
        functools.partial(text_sum_body, 0),
        [f32(rows)],
        [far_weights, far_images, acc],
        limit=16,
    )[0]
    text_parts = finish_text(acc_own, acc_other)
    near_weights, text_parts[0] = lax.optimization_barrier((near_weights, text_parts[0]))
    second_sum, image_add = call_kernel(
        second_sum_body,
        [f32(rows), bf16(rows)],
        [near_weights, units, image_add],
        limit=16,
    )
    image_last = []
    far_in = [swap_near(piece, 0) for piece in far_sum]
    for size, start, piece in zip(sizes, (0, sizes[0]), far_in):
        relayed = call_kernel(
            functools.partial(relay_body, start), [bf16(size)], [second_sum, piece], limit=8
        )[0]
        image_last.append(swap_near(relayed, 1))
        second_sum, relayed = lax.optimization_barrier((second_sum, relayed))
    own_weights, relayed = lax.optimization_barrier((own_weights, relayed))
    base = call_kernel(
        own_sum_body, [f32(rows)], [own_weights, units, image_add], moved=0, limit=16
    )[0]
    text_parts[0], base = lax.optimization_barrier((text_parts[0], base))
    return finish(text_parts, base, image_last)


def solution(mesh):
    in_specs = (P("blk", "tp"), P(("blk", "tp"), None), P(), P(), P(), P(), P())
    out_specs = (P("blk", "tp"), P(("blk", "tp"), None))
    return jax.shard_map(
        per_device, mesh=mesh, in_specs=in_specs, out_specs=out_specs, check_vma=False
    )
```

```python
import functools
import math

import jax
import jax.numpy as jnp
from jax import lax
from jax.experimental import pallas as pl
from jax.experimental.pallas import tpu as pltpu
from jax.sharding import PartitionSpec as P

TILE = 128
SLOTS = 3
WAIT_FLOPS = 20_000_000_000
TEXT_PIECES = 3
ACC_PIECES = 2
STEP = 16
CORES = 2
EPS = 1e-06
LOG2E = math.log2(math.e)
MIB = 1024 * 1024

VMEM_SPEC = pl.BlockSpec(memory_space=pltpu.VMEM)
ANY_SPEC = pl.BlockSpec(memory_space=pl.ANY)
SMEM_SPEC = pl.BlockSpec(memory_space=pltpu.SMEM)


def call_kernel(
    body,
    outs,
    operands,
    scalars=0,
    anywhere=(),
    outs_anywhere=False,
    scratch=(),
    flops=0,
    moved=None,
    aliases=None,
    limit=24,
):
    if moved is None:
        moved = sum(x.size * x.dtype.itemsize for x in operands)
        moved += sum(math.prod(o.shape) * o.dtype.itemsize for o in outs)
    specs = [SMEM_SPEC] * scalars + [VMEM_SPEC] * (len(operands) - scalars)
    for at in anywhere:
        specs[at] = ANY_SPEC
    return list(
        pl.pallas_call(
            body,
            out_shape=outs,
            in_specs=specs,
            out_specs=[ANY_SPEC if outs_anywhere else VMEM_SPEC] * len(outs),
            scratch_shapes=list(scratch),
            input_output_aliases=aliases or {},
            compiler_params=pltpu.CompilerParams(vmem_limit_bytes=limit * MIB),
            cost_estimate=pl.CostEstimate(flops=flops, bytes_accessed=moved, transcendentals=0),
        )(*operands)
    )


def struct(shape, dtype):
    return jax.ShapeDtypeStruct(shape, dtype)


def row_scales(square_sum):
    return lax.rsqrt(square_sum + EPS)


def column_of(row):
    return jnp.broadcast_to(row, (TILE, TILE)).T


def dot_nt(left, right):
    return lax.dot_general(
        left, right, (((1,), (1,)), ((), ())), preferred_element_type=jnp.float32
    )


def dot_tn(left, right):
    return lax.dot_general(
        left, right, (((0,), (0,)), ((), ())), preferred_element_type=jnp.float32
    )


def far_first(k, chunks):
    if chunks > 2 and k in (1, 2):
        return chunks - 3 + k
    return (chunks - k) % chunks


def feature_slice(peer, width):
    return pl.ds(pl.multiple_of(peer * width, width), width)


def pick_body(text_ref, *out_refs):
    place = lax.axis_index("tp")
    rows = out_refs[0].shape[0]
    for k, out_ref in enumerate(out_refs):
        peer = place ^ far_first(k, len(out_refs))
        out_ref[...] = text_ref[pl.ds(pl.multiple_of(peer * rows, rows), rows), :]


def unit_text_body(chunks, *refs):
    chunk_refs, (unit_ref, scale_ref) = refs[:chunks], refs[chunks : chunks + 2]
    piece_refs = refs[chunks + 2 :]
    place = lax.axis_index("tp")
    rows, width = chunk_refs[0].shape
    for first in range(0, rows, STEP):
        part = pl.ds(first, STEP)
        parts = [ref[part, :].astype(jnp.float32) for ref in chunk_refs]
        scales = row_scales(sum(jnp.sum(x * x, axis=-1, keepdims=True) for x in parts))
        scale_ref[part, :] = jnp.broadcast_to(scales, (STEP, TILE))
        for k, x in enumerate(parts):
            unit_ref[part, feature_slice(place ^ far_first(k, chunks), width)] = (x * scales).astype(jnp.bfloat16)
    split_rows(unit_ref, piece_refs)


def split_rows(whole_ref, piece_refs):
    for at, ref in enumerate(piece_refs):
        ref[...] = whole_ref[pl.ds(at * ref.shape[0], ref.shape[0]), :]


def join_rows(piece_refs, whole_ref):
    for at, ref in enumerate(piece_refs):
        whole_ref[pl.ds(at * ref.shape[0], ref.shape[0]), :] = ref[...]


def unit_images(ref, image_ref, scale_ref=None):
    for first in range(0, ref.shape[0], STEP):
        part = pl.ds(first, STEP)
        values = ref[part, :].astype(jnp.float32)
        scales = row_scales(jnp.sum(values * values, axis=-1, keepdims=True))
        image_ref[part, :] = (values * scales).astype(jnp.bfloat16)
        if scale_ref is not None:
            scale_ref[part, :] = jnp.broadcast_to(scales, (STEP, TILE))


def unit_images_body(raw_ref, out_ref):
    unit_images(raw_ref, out_ref)


def own_images_body(raw_ref, out_ref, raw_out_ref, scale_ref):
    unit_images(raw_ref, out_ref, scale_ref)
    raw_out_ref[...] = raw_ref[...]


def near_images_body(first_ref, second_unit_ref, own_unit_ref, out_ref):
    rows = first_ref.shape[0]
    unit_images(first_ref, out_ref)
    out_ref[rows : 2 * rows, :] = second_unit_ref[...]
    out_ref[2 * rows :, :] = own_unit_ref[...]


def neighbour_bits(shard):
    core = shard % CORES
    return 2 << core, 4 >> core


def list_body(groups, tiles, chips, *refs):
    scale_ref, bias_ref, blocks_ref, bucket_ref, positive_ref = refs[:5]
    line_ref, amount_ref, column_ref, row_ref, match_ref, own_ref = refs[5:]
    here, place = lax.axis_index("blk"), lax.axis_index("tp")
    scale = scale_ref[0]
    line_ref[pl.ds(0, 1), :] = jnp.full((1, TILE), -scale * LOG2E, jnp.float32)
    line_ref[pl.ds(1, 1), :] = jnp.full((1, TILE), -bias_ref[0] * LOG2E, jnp.float32)
    if chips == 4:
        first, second = neighbour_bits(here)
        shards = [here, here ^ first, here ^ second, here ^ 6]
    else:
        shards = [chip * CORES + here % CORES for chip in range(chips)]
    count = len(shards) * tiles

    def first_tile(shard):
        return (shard * groups + place) * tiles

    for n, shard in enumerate(shards):
        own_ref[pl.ds(n, 1), :] = jnp.full((1, TILE), jnp.where(shard == here, 1.0, 0.0))
        for j in range(tiles):
            column_ref[pl.ds(n * tiles + j, 1), :] = bucket_ref[pl.ds(first_tile(shard) + j, 1), :]
    for at in range(CORES * tiles):
        tile = first_tile(here ^ (at // tiles)) + at % tiles
        row_ref[pl.ds(at * TILE, TILE), :] = column_of(bucket_ref[pl.ds(tile, 1), :])
        if at < tiles:
            ids = lax.broadcasted_iota(jnp.int32, (1, TILE), 1) + tile * TILE
            matched = column_of(positive_ref[pl.ds(tile, 1), :]) == ids
            match_ref[pl.ds(at * TILE, TILE), :] = jnp.where(matched, 1.0, 0.0)
        for n, shard in enumerate(shards):
            entries = [blocks_ref[slot, shard, tile] for slot in range(SLOTS)]
            for j in range(tiles):
                listed = sum(jnp.where(entry == j, 1.0, 0.0) for entry in entries)
                amount_ref[pl.ds(at * count + n * tiles + j, 1), :] = jnp.full(
                    (1, TILE), scale * listed, jnp.float32
                )


class Pairs:
    count = 6

    def __init__(self, refs, tiles):
        self.line_ref, self.amount_ref, self.column_ref = refs[:3]
        self.row_ref, self.match_ref, self.own_ref = refs[3:6]
        self.tiles = tiles

    def weigh(self, products, half, group, weight_ref, top, left, own=None):
        tiles = self.tiles
        slope, offset = self.line_ref[pl.ds(0, 1), :], self.line_ref[pl.ds(1, 1), :]
        count = self.column_ref.shape[0]
        for a in range(tiles):
            at = half * tiles + a
            row_bucket = self.row_ref[pl.ds(at * TILE, TILE), :]
            for j in range(tiles):
                n = group * tiles + j
                amount = self.amount_ref[pl.ds(at * count + n, 1), :]
                power = (
                    products[a * TILE : (a + 1) * TILE, j * TILE : (j + 1) * TILE] * slope + offset
                )
                factor = jnp.where(row_bucket == self.column_ref[pl.ds(n, 1), :], amount, 0.0)
                if own and a == j:
                    match = self.match_ref[pl.ds(a * TILE, TILE), :]
                    if own == "search":
                        match = match * self.own_ref[pl.ds(group, 1), :]
                    power = jnp.where(match > 0.0, -power, power)
                    factor = jnp.where(match > 0.0, -amount, factor)
                inverse = pl.reciprocal(1.0 + jnp.exp2(power), approx=True)
                weight_ref[pl.ds(top + a * TILE, TILE), pl.ds(left + j * TILE, TILE)] = (
                    factor * inverse
                ).astype(jnp.bfloat16)


def near_own_body(tiles, *refs):
    pairs = Pairs(refs, tiles)
    unit_ref, image_ref, own_weight_ref, weight_ref = refs[Pairs.count :]
    rows = unit_ref.shape[0]
    products = dot_nt(unit_ref[...], image_ref[...])
    pairs.weigh(products[:, :rows], 0, 1, weight_ref, 0, 0)
    pairs.weigh(products[:, rows : 2 * rows], 0, 2, weight_ref, 0, rows)
    pairs.weigh(products[:, 2 * rows :], 0, 0, own_weight_ref, 0, 0, "diagonal")


def first_sum_body(tiles, *refs):
    pairs = Pairs(refs, tiles)
    own_unit_ref, near_image_ref, weight_in_ref = refs[Pairs.count : Pairs.count + 3]
    piece_refs = refs[Pairs.count + 3 : Pairs.count + 3 + TEXT_PIECES]
    unit_ref, weight_ref, sum_ref = refs[Pairs.count + 3 + TEXT_PIECES :]
    rows = own_unit_ref.shape[0]
    for at, ref in enumerate(piece_refs):
        unit_ref[pl.ds(rows + at * ref.shape[0], ref.shape[0]), :] = ref[...]
    unit_ref[:rows, :] = own_unit_ref[...]
    weight_ref[:rows, :] = weight_in_ref[:, :rows]
    products = dot_nt(unit_ref[rows:, :], near_image_ref[pl.ds(0, rows), :])
    pairs.weigh(products, 1, 1, weight_ref, rows, 0)
    sum_ref[...] = dot_tn(weight_ref[...], unit_ref[...]).astype(jnp.bfloat16)


def near_sum_body(tiles, *refs):
    pairs = Pairs(refs, tiles)
    unit_ref, image_ref, own_weight_in_ref, weight_in_ref, first_ref = refs[
        Pairs.count : Pairs.count + 5
    ]
    own_weight_ref, acc_ref, weight_ref = refs[Pairs.count + 5 :]
    rows = first_ref.shape[1]
    products = dot_nt(unit_ref[rows:, :], image_ref[rows:, :])
    own_weight_ref[:rows, :] = own_weight_in_ref[...]
    weight_ref[:, :rows] = first_ref[...]
    weight_ref[:rows, rows:] = weight_in_ref[:, rows:]
    pairs.weigh(products[:, :rows], 1, 2, weight_ref, rows, rows)
    pairs.weigh(products[:, rows:], 1, 0, own_weight_ref, rows, 0)
    acc_ref[...] = jnp.dot(
        weight_ref[...], image_ref[: 2 * rows, :], preferred_element_type=jnp.float32
    )


def far_body(tiles, pieces, *refs):
    pairs = Pairs(refs, tiles)
    unit_ref, own_image_ref, own_weight_ref, raw_ref, acc_ref = refs[Pairs.count : Pairs.count + 5]
    weight_ref, image_ref = refs[Pairs.count + 5 : Pairs.count + 7]
    sum_refs, text_refs = refs[Pairs.count + 7 : Pairs.count + 7 + pieces], refs[Pairs.count + 7 + pieces :]
    rows = raw_ref.shape[0]
    unit_images(raw_ref, image_ref.at[pl.ds(rows, rows), :])
    products = dot_nt(unit_ref[...], image_ref[rows:, :])
    image_ref[:rows, :] = own_image_ref[...]
    weight_ref[:, :rows] = own_weight_ref[...]
    pairs.weigh(products[rows:, :], 1, 3, weight_ref, rows, rows)
    text_sum_body(1, weight_ref, image_ref, acc_ref, *text_refs)
    pairs.weigh(products[:rows, :], 0, 3, weight_ref, 0, rows)
    total = dot_tn(weight_ref[:, rows:], unit_ref[...]).astype(jnp.bfloat16)
    start = 0
    for ref in sum_refs:
        ref[...] = total[start : start + ref.shape[0], :]
        start += ref.shape[0]


def text_sum_body(half, weight_ref, image_ref, acc_ref, *out_refs):
    rows = weight_ref.shape[0] // CORES
    size = out_refs[0].shape[0]
    part = pl.ds(half * rows, rows)
    acc = acc_ref[part, :] + jnp.dot(
        weight_ref[part, :], image_ref[...], preferred_element_type=jnp.float32
    )
    for at, ref in enumerate(out_refs):
        ref[...] = acc[at * size : (at + 1) * size, :].astype(ref.dtype)


def second_sum_body(weight_ref, unit_ref, add_ref, out_ref, add_out_ref):
    rows = out_ref.shape[0]
    out_ref[...] = dot_tn(weight_ref[:, rows:], unit_ref[...])
    add_out_ref[...] = add_ref[...]


def own_sum_body(weight_ref, unit_ref, add_ref, out_ref):
    out_ref[...] = dot_tn(weight_ref[...], unit_ref[...]) + add_ref[...].astype(jnp.float32)


def all_body(tiles, chips, *refs):
    pairs = Pairs(refs, tiles)
    own_ref, other_ref, piece_ref = refs[Pairs.count : Pairs.count + 3]
    outs = refs[Pairs.count + 3 :]
    spread_ref, acc_ref, acc_piece_refs = outs[0], outs[1], outs[2 : 2 + ACC_PIECES]
    image_ref, weight_ref = outs[2 + ACC_PIECES :]
    rows = own_ref.shape[0]
    unit_images(piece_ref, image_ref)
    for half, text_ref in enumerate((own_ref, other_ref)):
        for chip in range(chips):
            products = dot_nt(text_ref[...], image_ref[pl.ds(chip * rows, rows), :])
            pairs.weigh(
                products, half, chip, weight_ref, half * rows, chip * rows, None if half else "search"
            )
        acc = jnp.dot(
            weight_ref[pl.ds(half * rows, rows), :],
            image_ref[...],
            preferred_element_type=jnp.float32,
        )
        if half == 0:
            acc_ref[...] = acc
            continue
        size = rows // ACC_PIECES
        for at, ref in enumerate(acc_piece_refs):
            ref[...] = acc[at * size : (at + 1) * size, :].astype(jnp.bfloat16)
    for chip in range(chips):
        columns = pl.ds(chip * rows, rows)
        total = dot_tn(weight_ref[pl.ds(0, rows), columns], own_ref[...])
        total += dot_tn(weight_ref[pl.ds(rows, rows), columns], other_ref[...])
        spread_ref[columns, :] = total.astype(jnp.bfloat16)


def relay_body(start, sum_ref, in_ref, out_ref):
    part = sum_ref[pl.ds(start, in_ref.shape[0]), :]
    out_ref[...] = (part + in_ref[...].astype(jnp.float32)).astype(jnp.bfloat16)


def text_grad_body(chunks, *refs):
    scale_ref, raw_refs, acc_ref = refs[0], refs[1 : 1 + chunks], refs[1 + chunks]
    add_refs, out_refs = refs[2 + chunks : -chunks], refs[-chunks:]
    place = lax.axis_index("tp")
    rows, width = raw_refs[0].shape
    size = add_refs[0].shape[0]
    for first in range(0, rows, STEP):
        part = pl.ds(first, STEP)
        scales = scale_ref[part, :1]
        raws = [ref[part, :].astype(jnp.float32) for ref in raw_refs]
        accs = []
        for k in range(chunks):
            features = feature_slice(place ^ far_first(k, chunks), width)
            added = add_refs[first // size][pl.ds(first % size, STEP), features]
            accs.append(acc_ref[part, features] + added.astype(jnp.float32))
        inner = sum(jnp.sum(x * a, axis=-1, keepdims=True) for x, a in zip(raws, accs))
        inner = inner * scales * scales
        for k in range(chunks):
            out_refs[k][part, :] = (scales * (accs[k] - raws[k] * inner)).astype(jnp.bfloat16)


def arrived_body(*refs):
    out_ref = refs[-1]
    out_ref[...] = sum(ref[: out_ref.shape[0], : out_ref.shape[1]] for ref in refs[:-1])


def finish_rows(start, count, raw_ref, scale_ref, sum_ref, add_ref, grad_ref, out_ref, sems, copies):
    for block in range(0, count, TILE // 2):
        for first in range(block, block + TILE // 2, STEP):
            part = pl.ds(start + first, STEP)
            raw = raw_ref[part, :].astype(jnp.float32)
            scales = scale_ref[part, :1]
            acc = sum_ref[part, :]
            if add_ref is not None:
                acc = acc + add_ref[pl.ds(first, STEP), :].astype(jnp.float32)
            inner = jnp.sum(raw * acc, axis=-1, keepdims=True) * scales * scales
            grad_ref[part, :] = (scales * (acc - raw * inner)).astype(jnp.bfloat16)
        part = pl.ds(start + block, TILE // 2)
        copies.append(
            pltpu.make_async_copy(
                grad_ref.at[part, :], out_ref.at[part, :], sems.at[len(copies)]
            )
        )
        copies[-1].start()


def own_block_body(part_ref, out_ref, sem):
    rows = part_ref.shape[0]
    block = pl.ds(pl.multiple_of(lax.axis_index("tp") * rows, rows), rows)
    copy = pltpu.make_async_copy(part_ref, out_ref.at[block, :], sem)
    copy.start()
    copy.wait()


def finish_body(chunks, adds, *refs):
    part_refs, (raw_ref, scale_ref, sum_ref) = refs[:chunks], refs[chunks : chunks + 3]
    add_refs = refs[chunks + 3 : chunks + 3 + adds]
    text_ref, image_ref, grad_ref, sems = refs[-4:]
    place = lax.axis_index("tp")
    rows = part_refs[0].shape[0]
    copies = []
    for k in range(1, chunks):
        peer = place ^ far_first(k, chunks)
        for first in range(0, rows, TILE):
            block = pl.ds(pl.multiple_of(peer * rows + first, TILE), TILE)
            copies.append(
                pltpu.make_async_copy(
                    part_refs[k].at[pl.ds(first, TILE), :],
                    text_ref.at[block, :],
                    sems.at[len(copies)],
                )
            )
            copies[-1].start()
    start = 0
    for add_ref in add_refs or [None]:
        count = rows if add_ref is None else add_ref.shape[0]
        finish_rows(
            start, count, raw_ref, scale_ref, sum_ref, add_ref, grad_ref, image_ref, sems, copies
        )
        start += count
    for copy in copies:
        copy.wait()


def swap(value, axis, bits):
    count = lax.axis_size(axis)
    return lax.ppermute(value, axis, [(i, i ^ bits) for i in range(count)])


def swap_near(value, which):
    count = lax.axis_size("blk")
    return lax.ppermute(value, "blk", [(i, i ^ neighbour_bits(i)[which]) for i in range(count)])


def swap_chunks(chunks):
    count = len(chunks)
    return chunks[:1] + [swap(chunks[k], "tp", far_first(k, count)) for k in range(1, count)]


def per_device(text_emb, image_emb, logit_scale, logit_bias, bucket, positive, blocks):
    groups = lax.axis_size("tp")
    shards = lax.axis_size("blk")
    chips = shards // CORES
    rows, embed = image_emb.shape
    tiles = rows // TILE
    width = text_emb.shape[1]
    square = chips == 4

    def bf16(count, columns=embed):
        return struct((count, columns), jnp.bfloat16)

    def f32(count, columns=embed):
        return struct((count, columns), jnp.float32)

    def i32(count, columns):
        return struct((count, columns), jnp.int32)

    picked = call_kernel(pick_body, [bf16(rows, width)] * groups, [text_emb], limit=8)
    text_raw = swap_chunks(picked)
    if square:
        from_second = swap_near(image_emb, 1)
    else:
        same_core = [[chip * CORES + core for chip in range(chips)] for core in range(CORES)]
        gathered = lax.all_gather(
            image_emb, "blk", axis=0, tiled=True, axis_index_groups=same_core
        )
        _, image_raw, image_scales = call_kernel(
            own_images_body, [bf16(rows), bf16(rows), f32(rows, TILE)], [image_emb], limit=8
        )
    lists = call_kernel(
        functools.partial(list_body, groups, tiles, chips),
        [
            f32(2, TILE),
            f32(CORES * tiles * chips * tiles, TILE),
            i32(chips * tiles, TILE),
            i32(CORES * rows, TILE),
            f32(rows, TILE),
            f32(chips, TILE),
        ],
        [
            logit_scale,
            logit_bias,
            blocks.transpose(2, 1, 0),
            bucket.reshape(-1, TILE),
            positive.reshape(-1, TILE),
        ],
        scalars=3,
        limit=8,
    )
    if square:
        own_images, image_raw, image_scales = call_kernel(
            own_images_body, [bf16(rows), bf16(rows), f32(rows, TILE)], [image_emb], limit=8
        )
        image_sent, own_images = lax.optimization_barrier((image_emb, own_images))
        from_first = swap_near(image_sent, 0)
        from_second, own_images, *lists = lax.optimization_barrier(
            (from_second, own_images, *lists)
        )
        from_far = swap_near(from_second, 0)
        second_images = call_kernel(
            unit_images_body, [bf16(rows)], [from_second], flops=WAIT_FLOPS // 2, limit=8
        )[0]
        near_images = call_kernel(
            near_images_body, [bf16(3 * rows)], [from_first, second_images, own_images], limit=8
        )[0]
        text_raw[-1], near_images = lax.optimization_barrier((text_raw[-1], near_images))
    text_own, text_scales, *pieces = call_kernel(
        functools.partial(unit_text_body, groups),
        [bf16(rows), f32(rows, TILE)] + [bf16(rows // TEXT_PIECES)] * TEXT_PIECES,
        text_raw,
        limit=8,
    )
    text_other = [swap(piece, "blk", 1) for piece in pieces]
    unit_flops = 2 * rows * rows * embed

    def finish_text(acc_own, acc_other):
        parts = call_kernel(
            functools.partial(text_grad_body, groups),
            [bf16(rows, width)] * groups,
            [text_scales] + text_raw + [acc_own] + [swap(piece, "blk", 1) for piece in acc_other],
            limit=16,
        )
        return swap_chunks(parts)

    def finish(text_parts, total, pieces):
        text_own_block = call_kernel(
            own_block_body,
            [bf16(groups * rows, width)],
            text_parts[:1],
            outs_anywhere=True,
            scratch=[pltpu.SemaphoreType.DMA],
            moved=0,
            limit=8,
        )[0]
        arrived = call_kernel(
            arrived_body,
            [struct((16, TILE), jnp.bfloat16)],
            text_parts[1:],
            flops=WAIT_FLOPS,
            limit=8,
        )
        return tuple(
            call_kernel(
                functools.partial(finish_body, groups, len(pieces)),
                [bf16(groups * rows, width), bf16(rows)],
                text_parts
                + [image_raw, image_scales, total]
                + pieces
                + arrived
                + [text_own_block],
                anywhere=(groups + 4 + len(pieces),),
                aliases={groups + 4 + len(pieces): 0},
                outs_anywhere=True,
                scratch=[
                    pltpu.VMEM((rows, embed), jnp.bfloat16),
                    pltpu.SemaphoreType.DMA(((groups + 2) * tiles,)),
                ],
                limit=8,
            )
        )

    if not square:
        columns = gathered.shape[0]
        spread, acc_own, *acc_other = call_kernel(
            functools.partial(all_body, tiles, chips),
            [bf16(columns), f32(rows)] + [bf16(rows // ACC_PIECES)] * ACC_PIECES,
            lists + [text_own, jnp.concatenate(text_other), gathered],
            scratch=[
                pltpu.VMEM((columns, embed), jnp.bfloat16),
                pltpu.VMEM((2 * rows, columns), jnp.bfloat16),
            ],
            flops=6 * chips * unit_flops,
            limit=56,
        )
        text_parts = finish_text(acc_own, acc_other)
        parts = lax.all_to_all(
            spread, "blk", split_axis=0, concat_axis=0, tiled=True, axis_index_groups=same_core
        )
        total = jnp.sum(parts.reshape(-1, rows, embed).astype(jnp.float32), axis=0)
        return finish(text_parts, total, [])

    own_weights, near_weights = call_kernel(
        functools.partial(near_own_body, tiles),
        [bf16(rows, rows), bf16(rows, 2 * rows)],
        lists + [text_own, near_images],
        limit=16,
    )
    units, first_weights, first_sum = call_kernel(
        functools.partial(first_sum_body, tiles),
        [bf16(2 * rows), bf16(2 * rows, rows), bf16(rows)],
        lists + [text_own, near_images, near_weights] + text_other,
        limit=16,
    )
    image_add = swap_near(first_sum, 0)
    own_weights, acc, near_weights = call_kernel(
        functools.partial(near_sum_body, tiles),
        [bf16(2 * rows, rows), f32(2 * rows), bf16(2 * rows, 2 * rows)],
        lists + [units, near_images, own_weights, near_weights, first_weights],
        limit=24,
    )
    own_weights, from_far = lax.optimization_barrier((own_weights, from_far))
    sizes = [rows - TILE, TILE]
    far_weights, far_images, *rest = call_kernel(
        functools.partial(far_body, tiles, len(sizes)),
        [bf16(2 * rows, 2 * rows), bf16(2 * rows)]
        + [bf16(size) for size in sizes]
        + [bf16(rows // ACC_PIECES)] * ACC_PIECES,
        lists + [units, own_images, own_weights, from_far, acc],
        limit=24,
    )
    far_sum, acc_other = rest[: len(sizes)], rest[len(sizes) :]
    acc_own = call_kernel(
        functools.partial(text_sum_body, 0),
        [f32(rows)],
        [far_weights, far_images, acc],
        limit=16,
    )[0]
    text_parts = finish_text(acc_own, acc_other)
    near_weights, text_parts[0] = lax.optimization_barrier((near_weights, text_parts[0]))
    second_sum, image_add = call_kernel(
        second_sum_body,
        [f32(rows), bf16(rows)],
        [near_weights, units, image_add],
        limit=16,
    )
    image_last = []
    far_in = [swap_near(piece, 0) for piece in far_sum]
    for size, start, piece in zip(sizes, (0, sizes[0]), far_in):
        relayed = call_kernel(
            functools.partial(relay_body, start), [bf16(size)], [second_sum, piece], limit=8
        )[0]
        image_last.append(swap_near(relayed, 1))
        second_sum, relayed = lax.optimization_barrier((second_sum, relayed))
    own_weights, relayed = lax.optimization_barrier((own_weights, relayed))
    base = call_kernel(
        own_sum_body, [f32(rows)], [own_weights, units, image_add], moved=0, limit=16
    )[0]
    text_parts[0], base = lax.optimization_barrier((text_parts[0], base))
    return finish(text_parts, base, image_last)


def solution(mesh):
    in_specs = (P("blk", "tp"), P(("blk", "tp"), None), P(), P(), P(), P(), P())
    out_specs = (P("blk", "tp"), P(("blk", "tp"), None))
    return jax.shard_map(
        per_device, mesh=mesh, in_specs=in_specs, out_specs=out_specs, check_vma=False
    )
```
